32 devices in a mesh: det: 8 (over z, x), exp: 4 (over y, core).
Axes of the slice: x: 2, y: 2, z: 4, core: 2. Of those that a mesh axis runs over, the one named last changes fastest.
Arguments:
- template: bfloat16 [256, 128, 128], P('det'), may hold values from -4 to 4
- template_var: bfloat16 [256, 128, 128], P('det'), may hold values from 2 to 32
- science: bfloat16 [4, 2048, 1024], P('exp', 'det'), may hold values from -10 to 10
- science_var: bfloat16 [4, 2048, 1024], P('exp', 'det'), may hold values from 0.5 to 2
- routes_src: int32 [4, 128], P('exp', 'det'), may hold values from 0 to 7, as said below
- routes_blk: int32 [4, 128], P('exp', 'det'), may hold values from 0 to 31
- stamp_rows: int32 [4, 32], P('exp', 'det'), may hold values from 0 to 128
- stamp_cols: int32 [4, 32], P('exp', 'det'), may hold values from 0 to 896
- basis_col: bfloat16 [40, 21], replicated, may hold values from -1.25 to 1.25
- basis_row: bfloat16 [40, 21], replicated, may hold values from -1.25 to 1.25
- psf_col: float32 [4, 21], P('exp'), may hold values from 0.05 to 0.5
- psf_row: float32 [4, 21], P('exp'), may hold values from 0.05 to 0.5
Outputs:
- significance: float32 [256, 128, 128], P('det')
- psf_score: float32 [4, 2048, 1024], P('exp', 'det')
- coefficients: float32 [4, 328], P('exp', 'det')
The draws below stay inside these ranges and needn't reach their ends.
Inputs may be any that keep to these rules, and one draw needn't show every extreme that they name: `routes_src`: within the 16 blocks of one device, at most 2 take their template from one owner, and on every device some owner supplies exactly 2 of them.
All inputs are finite; a program needn't handle non-finite values.
Results may differ from the reference program's by a relative error of at most 0.0085.
Values may be sent and summed in bfloat16 or wider, within the bound.
No kernel may reach another device: no remote copies, remote signals or barrier semaphores. Data moves between devices by JAX's collectives and lax.ppermute only.
A program may use at most 128 MiB of HBM per device.

```python
import math
import jax
import jax.numpy as jnp
from jax import lax

PIX = 128
KW = 21
NBASIS = 40
BY = 2
BX = 8
TB = 32
NS = 4
EXPOSURES = 4
DETECTORS = 8
CAP = 2


def routes_of(key):
    base = jax.random.fold_in(key, 11)
    key_hot, key_forced, key_score, key_order, key_block = jax.random.split(base, 5)
    blocks_dev = BY * BX
    devices_all = EXPOSURES * DETECTORS
    slot_total = DETECTORS * CAP
    popular = (jax.random.permutation(key_hot, DETECTORS) < max(1, DETECTORS // 8)).astype(jnp.int32)
    slot_owner = jnp.arange(slot_total, dtype=jnp.int32) // CAP
    forced = jax.random.randint(key_forced, (devices_all, 1), 0, DETECTORS)
    noise_score = jax.random.randint(key_score, (devices_all, slot_total), 0, 2 ** 12)
    priority = noise_score + popular[slot_owner][None, :] * 2 ** 13 + (slot_owner[None, :] == forced).astype(jnp.int32) * 2 ** 14
    distinct = priority * slot_total + jnp.arange(slot_total, dtype=jnp.int32)[None, :]
    picked = lax.top_k(distinct, blocks_dev)[1]
    shuffle_key = jax.random.randint(key_order, (devices_all, blocks_dev), 0, 2 ** 12) * blocks_dev + jnp.arange(blocks_dev, dtype=jnp.int32)[None, :]
    ordering = jnp.argsort(shuffle_key, axis=1, stable=True)
    placed = jnp.take_along_axis(picked, ordering, axis=1)
    sources = (placed // CAP).reshape(EXPOSURES, DETECTORS * blocks_dev).astype(jnp.int32)
    indices = jax.random.randint(key_block, (EXPOSURES, DETECTORS * blocks_dev), 0, TB).astype(jnp.int32)
    return (sources, indices)


def template_of(key):
    base = jax.random.fold_in(key, 23)
    key_value = jax.random.fold_in(base, 0)
    return jnp.clip(jax.random.normal(key_value, (DETECTORS * TB, PIX, PIX)), -4.0, 4.0)


def draw_template(key, part):
    return template_of(key).astype(jnp.bfloat16)


def draw_routes_src(key, part):
    return routes_of(key)[0]


def draw_routes_blk(key, part):
    return routes_of(key)[1]


def draw_science(key, part):
    frames = template_of(key).astype(jnp.bfloat16).astype(jnp.float32)
    sources, indices = routes_of(key)
    picked = frames[(sources * TB + indices).reshape(-1)]
    base = jax.random.fold_in(key, 37)
    key_gain, key_offset, key_noise = jax.random.split(base, 3)
    blocks_all = EXPOSURES * DETECTORS * BY * BX
    gains = jax.random.uniform(key_gain, (blocks_all, 1, 1), minval=0.5, maxval=1.5)
    offsets = jax.random.uniform(key_offset, (EXPOSURES * DETECTORS, 1, 1, 1), minval=-1.0, maxval=1.0)
    noise = 0.5 * jnp.clip(jax.random.normal(key_noise, (blocks_all, PIX, PIX)), -4.0, 4.0)
    picture = (gains * picked + noise).reshape(EXPOSURES * DETECTORS, BY * BX, PIX, PIX) + offsets
    shaped = picture.reshape(EXPOSURES, DETECTORS, BY, BX, PIX, PIX).transpose(0, 1, 2, 4, 3, 5)
    return shaped.reshape(EXPOSURES, DETECTORS * BY * PIX, BX * PIX).astype(jnp.bfloat16)


def place_ends(values, rng, smallest, high):
    place = [jax.random.randint(jax.random.fold_in(rng, axis), (), 0, length) for axis, length in enumerate(values.shape)]
    widest = values.shape.index(max(values.shape))
    next_to = place[:widest] + [(place[widest] + 1) % values.shape[widest]] + place[widest + 1:]
    return values.at[tuple(place)].set(smallest).at[tuple(next_to)].set(high)


def shard_levels(stream_key, dims, shards, least, top_value):
    gain = 1.0
    for axis_at, parts in shards:
        heights = jax.random.uniform(jax.random.fold_in(jax.random.fold_in(stream_key, 6), axis_at), (parts,), jnp.float32, least / len(shards), top_value / len(shards))
        gain = gain * jnp.repeat(jnp.exp(heights), dims[axis_at] // parts).reshape((-1,) + (1,) * (len(dims) - 1 - axis_at))
    return gain


def normal_values(own_key, dims, spread, most, kind=jnp.bfloat16):
    result = spread * jax.random.normal(own_key, dims, jnp.float32)
    return jnp.clip(result, min=-most, max=most).astype(kind)


def setup_inputs(seed: int = 0) -> dict:
    seeds = jax.random.split(jax.random.key(seed), 13)
    template = draw_template(jax.random.fold_in(seeds[12], 71), 0)
    template_var = jnp.clip(jnp.exp(math.log(32.0) - 2.7725887 * jax.random.uniform(seeds[1], (DETECTORS * TB, PIX, PIX), jnp.float32) ** shard_levels(seeds[1], (DETECTORS * TB, PIX, PIX), ((0, 8),), -0.2, 0.2)), 2.0, 32.0).astype(jnp.bfloat16)
    science = draw_science(jax.random.fold_in(seeds[12], 71), 0)
    science_var = jnp.clip(jnp.exp(math.log(2.0) - 1.3862944 * jax.random.uniform(seeds[3], (EXPOSURES, DETECTORS * BY * PIX, BX * PIX), jnp.float32) ** shard_levels(seeds[3], (EXPOSURES, DETECTORS * BY * PIX, BX * PIX), ((0, 4), (1, 8)), -0.2, 0.2)), 0.5, 2.0).astype(jnp.bfloat16)
    routes_src = draw_routes_src(jax.random.fold_in(seeds[12], 71), 0)
    routes_blk = draw_routes_blk(jax.random.fold_in(seeds[12], 71), 0)
    stamp_rows = place_ends(jax.random.randint(seeds[6], (EXPOSURES, DETECTORS * NS), 0, (BY - 1) * PIX + 1), jax.random.fold_in(seeds[6], 1), 0, (BY - 1) * PIX).astype(jnp.int32)
    stamp_cols = place_ends(jax.random.randint(seeds[7], (EXPOSURES, DETECTORS * NS), 0, (BX - 1) * PIX + 1), jax.random.fold_in(seeds[7], 1), 0, (BX - 1) * PIX).astype(jnp.int32)
    basis_col = normal_values(seeds[8], (NBASIS, KW), KW ** -0.5, 1.25)
    basis_row = normal_values(seeds[9], (NBASIS, KW), KW ** -0.5, 1.25)
    psf_col = jnp.clip(jnp.exp(math.log(0.5) - 2.3025851 * jax.random.uniform(seeds[10], (EXPOSURES, KW), jnp.float32) ** shard_levels(seeds[10], (EXPOSURES, KW), ((0, 4),), -0.2, 0.2)), 0.05, 0.5)
    psf_row = jnp.clip(jnp.exp(math.log(0.5) - 2.3025851 * jax.random.uniform(seeds[11], (EXPOSURES, KW), jnp.float32) ** shard_levels(seeds[11], (EXPOSURES, KW), ((0, 4),), -0.2, 0.2)), 0.05, 0.5)
    return dict(template=template, template_var=template_var, science=science, science_var=science_var, routes_src=routes_src, routes_blk=routes_blk, stamp_rows=stamp_rows, stamp_cols=stamp_cols, basis_col=basis_col, basis_row=basis_row, psf_col=psf_col, psf_row=psf_row)


precise_mode = lax.Precision.HIGHEST
ridge_term = 0.01

def band_stack(filters, block_side):
    kernel_taps = filters.shape[1]
    inputs = jnp.arange(block_side + kernel_taps - 1)[:, None, None]
    outputs = jnp.arange(block_side)[None, :, None]
    offsets = jnp.arange(kernel_taps)[None, None, :]
    select = (inputs - outputs == offsets).astype(jnp.float32)
    return jnp.einsum('ni,rvi->nrv', filters.astype(jnp.float32), select, precision=precise_mode)

def column_windows(padded, block_side, kernel_taps):
    height_all, padded_span = padded.shape
    count_blocks = (padded_span - kernel_taps + 1) // block_side
    extended = jnp.pad(padded, ((0, 0), (0, (count_blocks + 1) * block_side - padded_span)))
    tiled_rows = extended.reshape(height_all, count_blocks + 1, block_side)
    return jnp.concatenate([tiled_rows[:, :count_blocks], tiled_rows[:, 1:, :kernel_taps - 1]], axis=2)

def row_windows(padded, block_side, kernel_taps):
    padded_span, across = padded.shape
    count_blocks = (padded_span - kernel_taps + 1) // block_side
    extended = jnp.pad(padded, ((0, (count_blocks + 1) * block_side - padded_span), (0, 0)))
    tiled_rows = extended.reshape(count_blocks + 1, block_side, across)
    return jnp.concatenate([tiled_rows[:count_blocks], tiled_rows[1:, :kernel_taps - 1]], axis=1)

def to_image(blocks, block_rows, block_cols):
    block_side = blocks.shape[-1]
    shaped = blocks.reshape(block_rows, block_cols, block_side, block_side).transpose(0, 2, 1, 3)
    return shaped.reshape(block_rows * block_side, block_cols * block_side)

def to_blocks(picture, block_side):
    height_all, across = picture.shape
    shaped = picture.reshape(height_all // block_side, block_side, across // block_side, block_side)
    return shaped.transpose(0, 2, 1, 3).reshape(-1, block_side, block_side)

def fit_kernel(frame_img, science_img, variance_img, rows_at, cols_at, basis_col, basis_row, block_side):
    kernel_taps = basis_col.shape[1]
    margin = kernel_taps // 2
    padded = jnp.pad(frame_img, margin)
    stamp_side = block_side + kernel_taps - 1

    def cut_stamp(top_row, left_col):
        return (lax.dynamic_slice(padded, (top_row, left_col), (stamp_side, stamp_side)), lax.dynamic_slice(science_img, (top_row, left_col), (block_side, block_side)), lax.dynamic_slice(variance_img, (top_row, left_col), (block_side, block_side)))
    stamps, science_cut, variance_cut = jax.vmap(cut_stamp)(rows_at, cols_at)
    col_bands = band_stack(basis_col, block_side).astype(jnp.bfloat16).astype(jnp.float32)
    row_bands = band_stack(basis_row, block_side).astype(jnp.bfloat16).astype(jnp.float32)
    vertical = jnp.einsum('kru,srx->skux', col_bands, stamps.astype(jnp.float32), precision=precise_mode).astype(jnp.bfloat16)
    design = jnp.einsum('skux,kxv->skuv', vertical.astype(jnp.float32), row_bands, precision=precise_mode)
    weight = 1.0 / variance_cut.astype(jnp.float32)
    science_f = science_cut.astype(jnp.float32)
    weighted = design * weight[:, None]
    pixel_count = rows_at.shape[0] * block_side * block_side
    gram_matrix = jnp.einsum('skuv,sluv->kl', weighted, design, precision=precise_mode)
    cross_terms = lax.optimization_barrier(jnp.sum(weighted, axis=(0, 2, 3)))
    weight_total = jnp.sum(weight)
    right_basis = jnp.einsum('skuv,suv->k', weighted, science_f, precision=precise_mode)
    right_back = jnp.sum(weight * science_f)
    upper = jnp.concatenate([gram_matrix, cross_terms[:, None]], axis=1)
    lower = jnp.concatenate([cross_terms, weight_total[None]])[None, :]
    normal = jnp.concatenate([upper, lower], axis=0) / pixel_count
    normal = normal + ridge_term * jnp.eye(normal.shape[0], dtype=jnp.float32)
    right_side = jnp.concatenate([right_basis, right_back[None]]) / pixel_count
    factor = jnp.linalg.cholesky(normal)
    return jax.scipy.linalg.cho_solve((factor, True), right_side)

def apply_kernel(frame_img, kernel_bf, block_side):
    kernel_taps = kernel_bf.shape[0]
    height_all = frame_img.shape[0]
    padded = jnp.pad(frame_img, kernel_taps // 2)
    windows = column_windows(padded, block_side, kernel_taps).astype(jnp.float32)
    kernel_bands = band_stack(kernel_bf, block_side)

    def add_row(offset, running):
        row_slab = lax.dynamic_slice_in_dim(windows, offset, height_all, 0)
        return running + jnp.einsum('ycr,rv->ycv', row_slab, kernel_bands[offset], precision=precise_mode)
    start = jnp.zeros((height_all, windows.shape[1], block_side), jnp.float32)
    return lax.fori_loop(0, kernel_taps, add_row, start).reshape(height_all, -1)

def correlate_psf(difference, psf_down, psf_across, block_side):
    kernel_taps = psf_down.shape[0]
    margin = kernel_taps // 2
    height_all, across = difference.shape
    data = difference.astype(jnp.float32)
    across_band = band_stack(psf_across[None, :], block_side)[0]
    windows = column_windows(jnp.pad(data, ((0, 0), (margin, margin))), block_side, kernel_taps)
    sideways = jnp.einsum('ycr,rv->ycv', windows, across_band, precision=precise_mode).reshape(height_all, across)
    down_band = band_stack(psf_down[None, :], block_side)[0]
    stacked = row_windows(jnp.pad(sideways, ((margin, margin), (0, 0))), block_side, kernel_taps)
    return jnp.einsum('brw,ru->buw', stacked, down_band, precision=precise_mode).reshape(height_all, across)

def reference(template, template_var, science, science_var, routes_src, routes_blk, stamp_rows, stamp_cols, basis_col, basis_row, psf_col, psf_row):
    blocks_dev = BY * BX
    height_all = BY * PIX
    across = BX * PIX
    source_ids = (routes_src * TB + routes_blk).reshape(-1).astype(jnp.int32)
    frames = template[source_ids].reshape(EXPOSURES * DETECTORS, blocks_dev, PIX, PIX)
    frame_vars = template_var[source_ids].reshape(EXPOSURES * DETECTORS, blocks_dev, PIX, PIX)
    science_all = science.reshape(EXPOSURES * DETECTORS, height_all, across)
    variance_all = science_var.reshape(EXPOSURES * DETECTORS, height_all, across)
    rows_all = stamp_rows.reshape(EXPOSURES * DETECTORS, NS)
    cols_all = stamp_cols.reshape(EXPOSURES * DETECTORS, NS)
    psf_downs = jnp.repeat(psf_col, DETECTORS, axis=0)
    psf_acrosses = jnp.repeat(psf_row, DETECTORS, axis=0)

    def process_detector(inputs):
        frame_blocks, tvar_blocks, science_img, variance_img, rows_at, cols_at, psf_down, psf_across = inputs
        frame_img = to_image(frame_blocks, BY, BX)
        fitted = fit_kernel(frame_img, science_img, variance_img, rows_at, cols_at, basis_col, basis_row, PIX)
        kernel = jnp.einsum('k,ki,kj->ij', fitted[:NBASIS], basis_col.astype(jnp.float32), basis_row.astype(jnp.float32), precision=precise_mode)
        kernel_sum = jnp.sum(kernel)
        matched = apply_kernel(frame_img, kernel.astype(jnp.bfloat16), PIX)
        difference = (science_img.astype(jnp.float32) - matched - fitted[NBASIS]).astype(jnp.bfloat16)
        scored = correlate_psf(difference, psf_down, psf_across, PIX)
        diff_blocks = to_blocks(difference, PIX)
        var_blocks = to_blocks(variance_img, PIX).astype(jnp.float32) + kernel_sum * kernel_sum * tvar_blocks.astype(jnp.float32)
        return (fitted, diff_blocks, var_blocks, scored)
    fitted_all, diff_all, var_all, scored_all = lax.map(process_detector, (frames, frame_vars, science_all, variance_all, rows_all, cols_all, psf_downs, psf_acrosses))
    diff_total = jax.ops.segment_sum(diff_all.reshape(-1, PIX, PIX).astype(jnp.float32), source_ids, num_segments=DETECTORS * TB)
    var_total = jax.ops.segment_sum(var_all.reshape(-1, PIX, PIX), source_ids, num_segments=DETECTORS * TB)
    significance = diff_total / jnp.sqrt(jnp.maximum(var_total, 1.0))
    return (significance, scored_all.reshape(EXPOSURES, DETECTORS * height_all, across), fitted_all.reshape(EXPOSURES, DETECTORS * (NBASIS + 1)))
```

```python
import functools

import jax
import jax.numpy as jnp
from jax import lax
from jax.experimental import pallas as pl
from jax.experimental.pallas import tpu as pltpu
from jax.sharding import PartitionSpec as P

ridge_term = 0.01
bf16 = jnp.bfloat16
f32 = jnp.float32
vmem = functools.partial(pl.BlockSpec, memory_space=pltpu.VMEM)
smem = functools.partial(pl.BlockSpec, memory_space=pltpu.SMEM)
limit = 56 * 1024 * 1024


def up(value, step):
    return -(-value // step) * step


def cost(flops, moved):
    return pl.CostEstimate(flops=flops, bytes_accessed=moved, transcendentals=0)


def route_body(src, blk, request, slot_of, sender, count, *, peers, exps, capacity):
    def clear_count(p, carry):
        count[p] = 0
        return carry

    def clear_slot(s, carry):
        sender[s] = 0
        for e in range(exps):
            request[(s // capacity) * exps + e, 0, s % capacity] = 0
        return carry

    lax.fori_loop(0, peers, clear_count, 0)
    lax.fori_loop(0, peers * capacity, clear_slot, 0)
    for b in range(src.shape[1]):
        owner = src[0, b]
        place = count[owner]
        count[owner] = place + 1
        slot_of[b] = owner * capacity + place
        sender[owner * capacity + place] = b
        for e in range(exps):
            request[owner * exps + e, 0, place] = blk[0, b] + 1


def route_tables(routes_src, routes_blk, peers, exps, capacity):
    body = functools.partial(route_body, peers=peers, exps=exps, capacity=capacity)
    return pl.pallas_call(
        body,
        out_shape=(
            jax.ShapeDtypeStruct((peers * exps, 1, capacity), jnp.int32),
            jax.ShapeDtypeStruct((routes_src.shape[1],), jnp.int32),
            jax.ShapeDtypeStruct((peers * capacity,), jnp.int32),
        ),
        in_specs=[smem()] * 2,
        out_specs=(smem(), smem(), smem()),
        scratch_shapes=[pltpu.SMEM((peers,), jnp.int32)],
        name="route_tables",
    )(routes_src, routes_blk)


def pick_body(incoming, me, template, out, sems, *, exps, capacity):
    slots = out.shape[0]

    def copy(s):
        wanted = incoming[(s // capacity) * exps + me[0], s % capacity]
        block = jnp.maximum(wanted - 1, 0)
        return pltpu.make_async_copy(template.at[block], out.at[s], sems.at[s])

    for s in range(slots):
        copy(s).start()
    for s in range(slots):
        copy(s).wait()


def pick_blocks(incoming, me, template, slots, exps, capacity):
    return pl.pallas_call(
        functools.partial(pick_body, exps=exps, capacity=capacity),
        out_shape=jax.ShapeDtypeStruct((slots,) + template.shape[1:], template.dtype),
        in_specs=[smem(), smem(), pl.BlockSpec(memory_space=pl.ANY)],
        out_specs=pl.BlockSpec(memory_space=pl.ANY),
        scratch_shapes=[pltpu.SemaphoreType.DMA((slots,))],
        name="pick_blocks",
    )(incoming, me, template)


def store_parts(sender, image, out, side, exps, capacity, across_blocks):
    part = side // exps
    slots = sender.shape[0]

    def one(s, carry):
        b = sender[s]
        top = pl.multiple_of((b // across_blocks) * side, side)
        left = pl.multiple_of((b % across_blocks) * side, side)
        block = image[pl.ds(top, side), pl.ds(left, side)].astype(bf16)
        row = pl.multiple_of((s % capacity) * part, part)
        for q in range(exps):
            out[(s // capacity) * exps + q, pl.ds(row, part), :] = block[q * part : (q + 1) * part]
        return carry

    lax.fori_loop(0, slots, one, 0, unroll=True if slots <= 32 else 4)


def send_body(sender, image, out, *, side, exps, capacity, across_blocks):
    store_parts(sender, image, out, side, exps, capacity, across_blocks)


def send_parts(sender, image, side, peers, exps, capacity):
    part = side // exps
    body = functools.partial(
        send_body, side=side, exps=exps, capacity=capacity, across_blocks=image.shape[1] // side
    )
    return pl.pallas_call(
        body,
        out_shape=jax.ShapeDtypeStruct((peers * exps, capacity * part, side), bf16),
        in_specs=[smem(), vmem()],
        out_specs=vmem(),
        compiler_params=pltpu.CompilerParams(vmem_limit_bytes=limit),
        name="send_parts",
    )(sender, image)


def fit_body(
    slot_of,
    sender,
    rows_at,
    cols_at,
    arrived,
    science,
    variance,
    col_bands,
    row_bands,
    col_t,
    row_rev,
    coef_out,
    payload,
    diff_out,
    frame,
    image_f,
    var_f,
    vert,
    design,
    windows,
    bands,
    matched,
    roots,
    *,
    side,
    exps,
    capacity,
    count,
    taps,
):
    high, wide = science.shape
    across_blocks = wide // side
    margin = taps // 2
    stamps = rows_at.shape[1]
    span_r = up(side + taps - 1, 16)
    padded_k = up(count + 2, 16)
    load_r = span_r
    part = side // exps

    frame[...] = jnp.zeros(frame.shape, f32)
    for b in range(slot_of.shape[0]):
        top = margin + (b // across_blocks) * side
        left = margin + (b % across_blocks) * side
        frame[top : top + side, left : left + side] = arrived[slot_of[b]].astype(f32)
    image_f[...] = jnp.zeros(image_f.shape, f32)
    var_f[...] = jnp.ones(var_f.shape, f32)
    image_f[:high, :wide] = science[...].astype(f32)
    var_f[:high, :wide] = variance[...].astype(f32)

    def cut(ref, top, left, height):
        down = pl.multiple_of((top // 8) * 8, 8)
        over = pl.multiple_of((left // side) * side, side)
        tile = ref[pl.ds(down, height), pl.ds(over, 3 * side)]
        tile = pltpu.roll(tile, lax.rem(3 * side - (left - over), 3 * side), 1)[:, : 2 * side]
        return pltpu.roll(tile, lax.rem(height - (top - down), height), 0)

    cuts = []
    for s in range(stamps):
        top = rows_at[0, s]
        left = cols_at[0, s]
        cuts.append(cut(frame, top, left, load_r).astype(bf16))
        science_cut = cut(image_f, top, left, side + 8)[:side, :side]
        weight_root = lax.rsqrt(cut(var_f, top, left, side + 8)[:side, :side])
        design[pl.ds(s * side * padded_k + count, side, stride=padded_k), :] = weight_root
        design[pl.ds(s * side * padded_k + count + 1, side, stride=padded_k), :] = (
            weight_root * science_cut
        )
        for extra in range(count + 2, padded_k):
            design[pl.ds(s * side * padded_k + extra, side, stride=padded_k), :] = jnp.zeros(
                (side, side), f32
            )
        roots[s * side : (s + 1) * side, :] = weight_root

    group = 4
    for k in range(0, count, group):
        filters = col_bands[k * side : (k + group) * side, :]
        for s in range(stamps):
            out = jnp.dot(filters, cuts[s], preferred_element_type=f32).astype(bf16)
            for a in range(group):
                vert[k + a, s * side : (s + 1) * side, :] = out[a * side : (a + 1) * side]

    for k in range(count):
        out = jnp.dot(vert[k], row_bands[k], preferred_element_type=f32)
        design[pl.ds(k, stamps * side, stride=padded_k), :] = out * roots[...]

    lines = 16

    def gram_step(step, total):
        start = pl.multiple_of(step * lines * padded_k, lines * padded_k)
        rows = design[pl.ds(start, lines * padded_k), :]
        tops = []
        lows = []
        for j in range(lines):
            line = rows[j * padded_k : (j + 1) * padded_k]
            top = line.astype(bf16)
            tops.append(top)
            lows.append((line - top.astype(f32)).astype(bf16))
        both = jnp.concatenate(
            [jnp.concatenate(tops, axis=1), jnp.concatenate(lows, axis=1)], axis=0
        )
        return total + lax.dot_general(
            both, both, (((1,), (1,)), ((), ())), preferred_element_type=f32
        )

    gram = lax.fori_loop(
        0, stamps * side // lines, gram_step, jnp.zeros((2 * padded_k, 2 * padded_k), f32)
    )
    folded = gram[:padded_k] + gram[padded_k:]
    folded = jnp.concatenate([folded, jnp.zeros((padded_k, side - 2 * padded_k), f32)], axis=1)
    folded = folded + pltpu.roll(folded, side - padded_k, 1)
    sub = lax.broadcasted_iota(jnp.int32, (padded_k, side), 0)
    lane = lax.broadcasted_iota(jnp.int32, (padded_k, side), 1)
    size = count + 1
    system = folded / (stamps * side * side)
    system = jnp.where((sub < size) & (lane <= size), system, 0.0)
    system = system + jnp.where((sub == lane) & (sub < size), ridge_term, 0.0)

    for k in range(size):
        row = system[k : k + 1, :]
        factor = system[:, k : k + 1] * (1.0 / row[:, k : k + 1])
        factor = jnp.where(sub[:, :1] == k, 0.0, factor)
        system = system - factor * row
    pivot = jnp.sum(jnp.where(sub == lane, system, 0.0), axis=1, keepdims=True)
    solved = system[:, size : size + 1] / jnp.where(sub[:, :1] < size, pivot, 1.0)
    coef_out[...] = jnp.sum(jnp.where(sub == lane, solved, 0.0), axis=0, keepdims=True)
    background = solved[count : count + 1, :]
    basis_coef = jnp.where(sub[:, :1] < count, solved, 0.0)

    scaled = basis_coef * row_rev[...]
    kernel = jnp.zeros((col_t.shape[0], side), f32)
    for _ in range(3):
        piece = scaled.astype(bf16)
        scaled = scaled - piece.astype(f32)
        kernel = kernel + jnp.dot(col_t[...], piece, preferred_element_type=f32)
    kernel_sum = jnp.sum(jnp.sum(kernel, axis=1, keepdims=True), axis=0, keepdims=True)
    rounded = kernel.astype(bf16).astype(f32)

    zero_band = jnp.zeros((side, side), bf16)

    def band(i):
        if i < 0 or i >= taps:
            return zero_band
        line = jnp.broadcast_to(rounded[i : i + 1, :], (side, side))
        return pltpu.roll(line, 0, 1, stride=1, stride_axis=0).astype(bf16)

    pairs = (taps + 2) // 2
    made = {i: band(i) for i in range(-1, 2 * pairs)}
    for q in range(pairs):
        for a in range(2):
            for b in range(2):
                bands[
                    q * 2 * side + a * side : q * 2 * side + (a + 1) * side,
                    b * side : (b + 1) * side,
                ] = made[2 * q + a - b]

    step = side - taps + 1
    rows_half = high // 2
    for c in range(windows.shape[0]):
        windows[c] = frame[:, c * step : c * step + side]
    for c in range(windows.shape[0]):
        lhs = jnp.concatenate(
            [
                windows[c, pl.ds(row, rows_half, stride=2), :].astype(bf16)
                for row in range(2 * pairs)
            ],
            axis=1,
        )
        out = jnp.dot(lhs, bands[...], preferred_element_type=f32)
        windows[c, pl.ds(0, rows_half, stride=2), :] = out[:, :side]
        windows[c, pl.ds(1, rows_half, stride=2), :] = out[:, side:]
        keep = min(step, wide - c * step)
        matched[:, c * step : c * step + keep] = windows[c, :high, :keep]
    image_f[:high, :wide] = image_f[:high, :wide] - matched[:, :wide] - background
    difference = image_f[:high, :wide].astype(bf16)
    diff_out[...] = difference

    store_parts(sender, diff_out, payload, side, exps, capacity, across_blocks)
    line_at = lax.broadcasted_iota(jnp.int32, (16, side), 0)
    trailer = jnp.zeros((16, side), f32)
    rest = kernel_sum
    for p in range(3):
        piece = rest.astype(bf16).astype(f32)
        rest = rest - piece
        trailer = jnp.where(line_at == p, piece, trailer)
    trailer = trailer.astype(bf16)

    def put(d, carry):
        payload[d, capacity * part :, :] = trailer
        return carry

    lax.fori_loop(0, payload.shape[0], put, 0, unroll=4)


def fit_and_subtract(
    slot_of,
    sender,
    rows_at,
    cols_at,
    arrived,
    science,
    variance,
    col_bands,
    row_bands,
    col_t,
    row_rev,
    peers,
    exps,
    capacity,
    count,
    taps,
):
    side = arrived.shape[1]
    high, wide = science.shape
    stamps = rows_at.shape[1]
    padded_k = up(count + 2, 16)
    part = side // exps
    pairs = (taps + 2) // 2
    step = side - taps + 1
    wins = -(-wide // step)
    tall = up(high - side + 8 + up(side + taps - 1, 16), 16)
    tall = max(tall, up(high + 2 * pairs, 16))
    broad = wide + 2 * side
    body = functools.partial(
        fit_body, side=side, exps=exps, capacity=capacity, count=count, taps=taps
    )
    return pl.pallas_call(
        body,
        out_shape=(
            jax.ShapeDtypeStruct((1, side), f32),
            jax.ShapeDtypeStruct((peers * exps, capacity * part + 16, side), bf16),
            jax.ShapeDtypeStruct((high, wide), bf16),
        ),
        in_specs=[smem()] * 4 + [vmem()] * 7,
        out_specs=(vmem(), vmem(), vmem()),
        scratch_shapes=[
            pltpu.VMEM((tall, broad), f32),
            pltpu.VMEM((high + 8, broad), f32),
            pltpu.VMEM((high + 8, broad), f32),
            pltpu.VMEM((count, stamps * side, 2 * side), bf16),
            pltpu.VMEM((stamps * side * padded_k, side), f32),
            pltpu.VMEM((wins, tall, side), f32),
            pltpu.VMEM((pairs * 2 * side, 2 * side), bf16),
            pltpu.VMEM((high, wide), f32),
            pltpu.VMEM((stamps * side, side), f32),
        ],
        compiler_params=pltpu.CompilerParams(vmem_limit_bytes=limit),
        cost_estimate=cost(5_000_000_000, 8_000_000),
        name="fit_and_subtract",
    )(
        slot_of,
        sender,
        rows_at,
        cols_at,
        arrived,
        science,
        variance,
        col_bands,
        row_bands,
        col_t,
        row_rev,
    )


def split2(value):
    top = value.astype(bf16)
    return top, (value - top.astype(f32)).astype(bf16)


def psf_body(diff, down, over, out, padded, sideways, *, side, taps):
    high, wide = diff.shape
    margin = taps // 2
    span = up(side + taps - 1, 16)
    padded[...] = jnp.zeros(padded.shape, f32)
    padded[:, margin : margin + wide] = diff[...].astype(f32)
    line = jnp.broadcast_to(over[...], (2 * side, 2 * side))
    band = pltpu.roll(line, 0, 1, stride=1, stride_axis=0)[:, :side]
    both = jnp.concatenate(split2(band), axis=1)
    sideways[...] = jnp.zeros(sideways.shape, f32)
    for c in range(wide // side):
        window = padded[:, c * side : (c + 2) * side].astype(bf16)
        got = jnp.dot(window, both, preferred_element_type=f32)
        sideways[margin : margin + high, c * side : (c + 1) * side] = got[:, :side] + got[:, side:]
    line = jnp.broadcast_to(down[...], (side, 2 * side))
    band = pltpu.roll(line, 0, 1, stride=1, stride_axis=0)[:, :span]
    top, low = split2(band)
    for r in range(high // side):
        data_top, data_low = split2(sideways[r * side : r * side + span, :])
        got = jnp.dot(top, data_top, preferred_element_type=f32)
        got = got + jnp.dot(top, data_low, preferred_element_type=f32)
        got = got + jnp.dot(low, data_top, preferred_element_type=f32)
        out[r * side : (r + 1) * side, :] = got


def correlate(diff, down, over_rev, side, taps):
    high, wide = diff.shape
    span = up(side + taps - 1, 16)
    return pl.pallas_call(
        functools.partial(psf_body, side=side, taps=taps),
        out_shape=jax.ShapeDtypeStruct((high, wide), f32),
        in_specs=[vmem()] * 3,
        out_specs=vmem(),
        scratch_shapes=[
            pltpu.VMEM((high, wide + side), f32),
            pltpu.VMEM((high - side + span, wide), f32),
        ],
        compiler_params=pltpu.CompilerParams(vmem_limit_bytes=limit),
        cost_estimate=cost(2_000_000_000, 2_000_000),
        name="correlate",
    )(diff, down, over_rev)


def variance_body(incoming, parts, out, *, part, capacity):
    out[...] = jnp.zeros(out.shape, f32)

    def one(j, carry):
        block = incoming[j // capacity, j % capacity] - 1

        @pl.when(block >= 0)
        def _():
            row = pl.multiple_of((j % capacity) * part, part)
            out[block] += parts[j // capacity, pl.ds(row, part), :].astype(f32)

        return carry

    lax.fori_loop(0, parts.shape[0] * capacity, one, 0)


def sum_variance(incoming, parts, tract, part, capacity):
    return pl.pallas_call(
        functools.partial(variance_body, part=part, capacity=capacity),
        out_shape=jax.ShapeDtypeStruct((tract, part, parts.shape[2]), f32),
        in_specs=[smem(), vmem()],
        out_specs=vmem(),
        compiler_params=pltpu.CompilerParams(vmem_limit_bytes=limit),
        name="sum_variance",
    )(incoming, parts)


def combine_body(incoming, parts, var_sum, var_template, out, total, gain, *, part, capacity):
    total[...] = jnp.zeros(total.shape, f32)
    gain[...] = jnp.zeros(gain.shape, f32)

    def one(j, carry):
        block = incoming[j // capacity, j % capacity] - 1

        @pl.when(block >= 0)
        def _():
            row = pl.multiple_of((j % capacity) * part, part)
            total[block] += parts[j // capacity, pl.ds(row, part), :].astype(f32)
            tail = parts[j // capacity, capacity * part :, :].astype(f32)
            kernel_sum = tail[0:1] + tail[1:2] + tail[2:3]
            gain[block] += jnp.broadcast_to(kernel_sum * kernel_sum, gain.shape[1:])

        return carry

    lax.fori_loop(0, parts.shape[0] * capacity, one, 0)
    for t in range(out.shape[0]):
        variance = var_sum[t] + gain[t, 0:1, :] * var_template[t].astype(f32)
        out[t] = (total[t] * lax.rsqrt(jnp.maximum(variance, 1.0))).astype(bf16)


def combine(incoming, parts, var_sum, var_template, part, capacity):
    tract, _, side = var_sum.shape
    return pl.pallas_call(
        functools.partial(combine_body, part=part, capacity=capacity),
        out_shape=jax.ShapeDtypeStruct((tract, part, side), bf16),
        in_specs=[smem(), vmem(), vmem(), vmem()],
        out_specs=vmem(),
        scratch_shapes=[
            pltpu.VMEM((tract, part, side), f32),
            pltpu.VMEM((tract, 8, side), f32),
        ],
        compiler_params=pltpu.CompilerParams(vmem_limit_bytes=limit),
        name="combine",
    )(incoming, parts, var_sum, var_template)


def join_body(places, *refs, part):
    out = refs[-1]
    for d, ref in enumerate(refs[:-1]):
        row = pl.multiple_of(places[d] * part, part)
        out[:, pl.ds(row, part), :] = ref[...].astype(f32)


def join_parts(places, parts):
    tract, part, side = parts[0].shape
    exps = len(parts)
    chunk = 8
    grid_spec = pltpu.PrefetchScalarGridSpec(
        num_scalar_prefetch=1,
        grid=(tract // chunk,),
        in_specs=[pl.BlockSpec((chunk, part, side), lambda i, _: (i, 0, 0))] * exps,
        out_specs=pl.BlockSpec((chunk, part * exps, side), lambda i, _: (i, 0, 0)),
    )
    return pl.pallas_call(
        functools.partial(join_body, part=part),
        out_shape=jax.ShapeDtypeStruct((tract, part * exps, side), f32),
        grid_spec=grid_spec,
        name="join_parts",
    )(places, *parts)


def local(
    template,
    template_var,
    science,
    science_var,
    routes_src,
    routes_blk,
    stamp_rows,
    stamp_cols,
    basis_col,
    basis_row,
    psf_col,
    psf_row,
):
    peers = lax.axis_size("det")
    exps = lax.axis_size("exp")
    me = lax.axis_index("exp").astype(jnp.int32)
    tract, side, _ = template.shape
    science_img = science[0]
    variance_img = science_var[0]
    blocks_dev = routes_src.shape[1]
    count, taps = basis_col.shape
    capacity = max(2, -(-blocks_dev // peers))
    slots = peers * capacity
    part = side // exps

    request, slot_of, sender = route_tables(routes_src, routes_blk, peers, exps, capacity)
    incoming = lax.all_to_all(
        request, ("det", "exp"), split_axis=0, concat_axis=0, tiled=True
    ).reshape(peers * exps, capacity)
    picked = pick_blocks(incoming, me[None], template, slots, exps, capacity)
    arrived = lax.all_to_all(picked, "det", split_axis=0, concat_axis=0, tiled=True)

    span = up(side + taps - 1, 16)
    padded_k = up(count + 2, 16)
    offset = jnp.arange(span)[None, :] - jnp.arange(side)[:, None]
    hot = (offset[:, :, None] == jnp.arange(taps)).astype(bf16)
    col_bands = jnp.einsum("ki,uri->kur", basis_col, hot, preferred_element_type=f32)
    col_bands = col_bands.astype(bf16).reshape(count * side, span)
    offset = jnp.arange(2 * side)[:, None] - jnp.arange(side)[None, :]
    hot = (offset[:, :, None] == jnp.arange(taps)).astype(bf16)
    row_bands = jnp.einsum("kj,xvj->kxv", basis_row, hot, preferred_element_type=f32)
    row_bands = row_bands.astype(bf16)
    col_t = jnp.pad(basis_col.T, ((0, up(taps, 16) - taps), (0, padded_k - count)))
    row_rev = jnp.pad(
        basis_row.astype(f32)[:, ::-1], ((0, padded_k - count), (side - taps, 0))
    )
    row_rev = jnp.roll(row_rev, 1, axis=1)
    over_rev = jnp.roll(jnp.pad(psf_row[:, ::-1], ((0, 0), (2 * side - taps, 0))), 1, axis=1)
    down = jnp.pad(psf_col, ((0, 0), (0, 2 * side - taps)))

    var_parts = send_parts(sender, variance_img, side, peers, exps, capacity)
    var_back = lax.all_to_all(
        var_parts, ("det", "exp"), split_axis=0, concat_axis=0, tiled=True
    )

    coef, payload, difference = fit_and_subtract(
        slot_of,
        sender,
        stamp_rows,
        stamp_cols,
        arrived,
        science_img,
        variance_img,
        col_bands,
        row_bands,
        col_t,
        row_rev,
        peers,
        exps,
        capacity,
        count,
        taps,
    )
    diff_back = lax.all_to_all(payload, ("det", "exp"), split_axis=0, concat_axis=0, tiled=True)
    scored = correlate(difference, down, over_rev, side, taps)
    var_sum = sum_variance(incoming, var_back, tract, part, capacity)
    var_template = lax.dynamic_slice_in_dim(template_var, me * part, part, 1)
    mine = combine(incoming, diff_back, var_sum, var_template, part, capacity)

    if exps & (exps - 1) == 0:
        held = [mine]
        reach = exps // 2
        gaps = [0]
        while reach:
            pairs = [(e, e ^ reach) for e in range(exps)]
            held = held + [lax.ppermute(h, "exp", pairs) for h in held]
            gaps = gaps + [g ^ reach for g in gaps]
            reach //= 2
        places = jnp.stack([me ^ g for g in gaps])
    else:
        held = [mine]
        for gap in range(1, exps):
            pairs = [(e, (e + gap) % exps) for e in range(exps)]
            held.append(lax.ppermute(mine, "exp", pairs))
        places = jnp.stack([(me - g) % exps for g in range(exps)])
    significance = join_parts(places, held)
    return (significance, scored[None], coef[:, : count + 1])


def solution(mesh):
    placed = (
        P("det", None, None),
        P("det", None, None),
        P("exp", "det", None),
        P("exp", "det", None),
        P("exp", "det"),
        P("exp", "det"),
        P("exp", "det"),
        P("exp", "det"),
        P(),
        P(),
        P("exp", None),
        P("exp", None),
    )
    return jax.shard_map(
        local,
        mesh=mesh,
        in_specs=placed,
        out_specs=(P("det", None, None), P("exp", "det", None), P("exp", "det")),
        check_vma=False,
    )
```

```python
import functools

import jax
import jax.numpy as jnp
from jax import lax
from jax.experimental import pallas as pl
from jax.experimental.pallas import tpu as pltpu
from jax.sharding import PartitionSpec as P

ridge_term = 0.01
bf16 = jnp.bfloat16
f32 = jnp.float32
vmem = functools.partial(pl.BlockSpec, memory_space=pltpu.VMEM)
smem = functools.partial(pl.BlockSpec, memory_space=pltpu.SMEM)
mib = 1024 * 1024
trailer_rows = 8


def up(value, step):
    return -(-value // step) * step


def cost(flops, moved):
    return pl.CostEstimate(flops=flops, bytes_accessed=moved, transcendentals=0)


def route_body(src, blk, request, slot_of, sender, count, *, peers, capacity):
    def clear_count(p, carry):
        count[p] = 0
        return carry

    def clear_slot(s, carry):
        sender[s] = 0
        request[s // capacity, 0, s % capacity] = 0
        return carry

    lax.fori_loop(0, peers, clear_count, 0, unroll=peers <= 16)
    lax.fori_loop(0, peers * capacity, clear_slot, 0, unroll=peers <= 16)
    for b in range(src.shape[1]):
        owner = src[0, b]
        place = count[owner]
        count[owner] = place + 1
        slot_of[b] = owner * capacity + place
        sender[owner * capacity + place] = b
        request[owner, 0, place] = blk[0, b] + 1


def route_tables(routes_src, routes_blk, peers, capacity):
    return pl.pallas_call(
        functools.partial(route_body, peers=peers, capacity=capacity),
        out_shape=(
            jax.ShapeDtypeStruct((peers, 1, capacity), jnp.int32),
            jax.ShapeDtypeStruct((routes_src.shape[1],), jnp.int32),
            jax.ShapeDtypeStruct((peers * capacity,), jnp.int32),
        ),
        in_specs=[smem()] * 2,
        out_specs=(smem(), smem(), smem()),
        scratch_shapes=[pltpu.SMEM((peers,), jnp.int32)],
        name="route_tables",
    )(routes_src, routes_blk)


def pick_body(incoming, template, out, *, capacity):
    def one(s, carry):
        block = jnp.maximum(incoming[s // capacity, 0, s % capacity] - 1, 0)
        out[s] = template[block]
        return carry

    lax.fori_loop(0, out.shape[0], one, 0, unroll=True if out.shape[0] <= 32 else 4)


def pick_blocks(incoming, template, slots, capacity):
    return pl.pallas_call(
        functools.partial(pick_body, capacity=capacity),
        out_shape=jax.ShapeDtypeStruct((slots,) + template.shape[1:], template.dtype),
        in_specs=[smem(), vmem()],
        out_specs=vmem(),
        compiler_params=pltpu.CompilerParams(vmem_limit_bytes=16 * mib),
        name="pick_blocks",
    )(incoming, template)


def store_parts(sender, image, out, side, exps, capacity, across_blocks):
    part = side // exps
    slots = sender.shape[0]

    def one(s, carry):
        b = sender[s]
        top = pl.multiple_of((b // across_blocks) * side, side)
        left = pl.multiple_of((b % across_blocks) * side, side)
        block = image[pl.ds(top, side), pl.ds(left, side)].astype(bf16)
        row = pl.multiple_of((s % capacity) * part, part)
        for q in range(exps):
            out[(s // capacity) * exps + q, pl.ds(row, part), :] = block[q * part : (q + 1) * part]
        return carry

    lax.fori_loop(0, slots, one, 0, unroll=True if slots <= 32 else 4)


def send_body(sender, request, image, out, *, side, exps, capacity, across_blocks):
    store_parts(sender, image, out, side, exps, capacity, across_blocks)
    part = side // exps
    lane = lax.broadcasted_iota(jnp.int32, (trailer_rows, side), 1)

    def put(p, carry):
        line = jnp.zeros((trailer_rows, side), f32)
        for c in range(capacity):
            line = jnp.where(lane == c, request[p, 0, c].astype(f32), line)
        for q in range(exps):
            out[p * exps + q, capacity * part :, :] = line.astype(bf16)
        return carry

    lax.fori_loop(0, request.shape[0], put, 0)


def send_parts(sender, request, image, side, exps, capacity):
    part = side // exps
    peers = request.shape[0]
    body = functools.partial(
        send_body, side=side, exps=exps, capacity=capacity, across_blocks=image.shape[1] // side
    )
    return pl.pallas_call(
        body,
        out_shape=jax.ShapeDtypeStruct(
            (peers * exps, capacity * part + trailer_rows, side), bf16
        ),
        in_specs=[smem(), smem(), vmem()],
        out_specs=vmem(),
        compiler_params=pltpu.CompilerParams(vmem_limit_bytes=16 * mib),
        name="send_parts",
    )(sender, request, image)


def cut(ref, top, left, height, side):
    down = pl.multiple_of((top // 8) * 8, 8)
    over = pl.multiple_of((left // side) * side, side)
    tile = ref[pl.ds(down, height), pl.ds(over, 3 * side)]
    tile = pltpu.roll(tile, lax.rem(3 * side - (left - over), 3 * side), 1)[:, : 2 * side]
    return pltpu.roll(tile, lax.rem(height - (top - down), height), 0)


def prepare_body(
    rows_at, cols_at, science, variance, col, rev, col_out, row_out, root_out, data_out, image, var
):
    side = rev.shape[1]
    high, wide = science.shape
    sub = lax.broadcasted_iota(jnp.int32, (side, side), 0)
    lane = lax.broadcasted_iota(jnp.int32, (side, side), 1)
    for k in range(row_out.shape[0]):
        line = jnp.broadcast_to(col[k : k + 1, :], (side, side))
        line = pltpu.roll(line, 0, 1, stride=1, stride_axis=0)
        rows = slice(k * side, (k + 1) * side)
        col_out[rows, :side] = jnp.where(lane >= sub, line, 0.0).astype(bf16)
        col_out[rows, side:] = jnp.where(lane < sub, line, 0.0).astype(bf16)
        line = jnp.broadcast_to(rev[k : k + 1, :], (side, side))
        line = pltpu.roll(line, 0, 1, stride=1, stride_axis=0)
        row_out[k, :side, :] = jnp.where(lane <= sub, line, 0.0).astype(bf16)
        row_out[k, side:, :] = jnp.where(lane > sub, line, 0.0).astype(bf16)
    image[:, wide:] = jnp.zeros((image.shape[0], image.shape[1] - wide), f32)
    image[high:, :wide] = jnp.zeros((image.shape[0] - high, wide), f32)
    image[:high, :wide] = science[...].astype(f32)
    var[:, wide:] = jnp.ones((var.shape[0], var.shape[1] - wide), f32)
    var[high:, :wide] = jnp.ones((var.shape[0] - high, wide), f32)
    var[:high, :wide] = variance[...].astype(f32)
    for s in range(rows_at.shape[1]):
        top = rows_at[0, s]
        left = cols_at[0, s]
        root = lax.rsqrt(cut(var, top, left, side + 8, side)[:side, :side])
        root_out[s * side : (s + 1) * side, :] = root
        data = cut(image, top, left, side + 8, side)[:side, :side]
        data_out[s * side : (s + 1) * side, :] = data * root


def prepare(rows_at, cols_at, science, variance, col, rev, count):
    side = rev.shape[1]
    high, wide = science.shape
    stamps = rows_at.shape[1]
    return pl.pallas_call(
        prepare_body,
        out_shape=(
            jax.ShapeDtypeStruct((count * side, 2 * side), bf16),
            jax.ShapeDtypeStruct((count, 2 * side, side), bf16),
            jax.ShapeDtypeStruct((stamps * side, side), f32),
            jax.ShapeDtypeStruct((stamps * side, side), f32),
        ),
        in_specs=[smem()] * 2 + [vmem()] * 4,
        out_specs=(vmem(),) * 4,
        scratch_shapes=[pltpu.VMEM((high + 8, wide + 2 * side), f32)] * 2,
        compiler_params=pltpu.CompilerParams(vmem_limit_bytes=24 * mib),
        name="prepare",
    )(rows_at, cols_at, science, variance, col, rev)


def normal_body(
    slot_of,
    rows_at,
    cols_at,
    arrived,
    col_bands,
    row_bands,
    roots,
    data,
    gram_out,
    windows,
    frame,
    vert,
    design,
    *,
    across_blocks,
    taps,
):
    count, _, side = row_bands.shape
    margin = taps // 2
    stamps = rows_at.shape[1]
    span = up(side + taps - 1, 16)
    padded_k = gram_out.shape[1]
    lines_all = stamps * side

    frame[...] = jnp.zeros(frame.shape, f32)
    for b in range(slot_of.shape[0]):
        top = margin + (b // across_blocks) * side
        left = margin + (b % across_blocks) * side
        frame[top : top + side, left : left + side] = arrived[slot_of[b]].astype(f32)

    cuts = []
    for s in range(stamps):
        cuts.append(cut(frame, rows_at[0, s], cols_at[0, s], span, side).astype(bf16))
    design[pl.ds(count, lines_all, stride=padded_k), :] = roots[...]
    design[pl.ds(count + 1, lines_all, stride=padded_k), :] = data[...]
    for extra in range(count + 2, padded_k):
        design[pl.ds(extra, lines_all, stride=padded_k), :] = jnp.zeros((lines_all, side), f32)

    group = vert.shape[0]
    for k in range(0, count, group):
        filters = col_bands[k * side : (k + group) * side, :span]
        for s in range(stamps):
            out = jnp.dot(filters, cuts[s], preferred_element_type=f32).astype(bf16)
            for a in range(group):
                vert[a, s * side : (s + 1) * side, :] = out[a * side : (a + 1) * side]
        for a in range(group):
            out = jnp.dot(vert[a], row_bands[k + a], preferred_element_type=f32)
            design[pl.ds(k + a, lines_all, stride=padded_k), :] = out * roots[...]

    lines = 16

    def gram_step(step, total):
        start = pl.multiple_of(step * lines * padded_k, lines * padded_k)
        rows = design[pl.ds(start, lines * padded_k), :]
        tops = []
        lows = []
        for j in range(lines):
            line = rows[j * padded_k : (j + 1) * padded_k]
            top = line.astype(bf16)
            tops.append(top)
            lows.append((line - top.astype(f32)).astype(bf16))
        tops = jnp.concatenate(tops, axis=1)
        both = jnp.concatenate([tops, jnp.concatenate(lows, axis=1)], axis=0)
        return total + lax.dot_general(
            both, tops, (((1,), (1,)), ((), ())), preferred_element_type=f32
        )

    gram_out[...] = lax.fori_loop(
        0, lines_all // lines, gram_step, jnp.zeros((2 * padded_k, padded_k), f32)
    )
    step = side - taps + 1
    for c in range(windows.shape[0]):
        windows[c] = frame[:, c * step : c * step + side]


def normal_matrix(
    slot_of, rows_at, cols_at, arrived, col_bands, row_bands, roots, data, high, wide, taps
):
    count, _, side = row_bands.shape
    stamps = rows_at.shape[1]
    padded_k = up(count + 2, 16)
    pairs = (taps + 2) // 2
    tall = up(high - side + 8 + up(side + taps - 1, 16), 16)
    tall = max(tall, up(high + 2 * pairs, 16))
    wins = -(-wide // (side - taps + 1))
    group = next(g for g in (4, 2, 1) if count % g == 0)
    return pl.pallas_call(
        functools.partial(normal_body, across_blocks=wide // side, taps=taps),
        out_shape=(
            jax.ShapeDtypeStruct((2 * padded_k, padded_k), f32),
            jax.ShapeDtypeStruct((wins, tall, side), f32),
        ),
        in_specs=[smem()] * 3 + [vmem()] * 5,
        out_specs=(vmem(),) * 2,
        scratch_shapes=[
            pltpu.VMEM((tall, wide + 2 * side), f32),
            pltpu.VMEM((group, stamps * side, 2 * side), bf16),
            pltpu.VMEM((stamps * side * padded_k, side), f32),
        ],
        compiler_params=pltpu.CompilerParams(vmem_limit_bytes=36 * mib),
        cost_estimate=cost(10_000_000_000, 8_000_000),
        name="normal_matrix",
    )(slot_of, rows_at, cols_at, arrived, col_bands, row_bands, roots, data)


def subtract_body(
    sender,
    gram,
    frames,
    science,
    col_t,
    row_rev,
    coef_out,
    payload,
    diff_out,
    windows,
    image,
    bands,
    *,
    exps,
    capacity,
    count,
    taps,
    pixels,
):
    side = frames.shape[2]
    high, wide = science.shape
    padded_k = gram.shape[1]
    part = side // exps
    size = count + 1

    square = jnp.concatenate(
        [gram[...], jnp.zeros((2 * padded_k, side - padded_k), f32)], axis=1
    )
    cross = square[padded_k:]
    mirror = jnp.concatenate([cross, jnp.zeros((side - padded_k, side), f32)], axis=0).T
    system = (square[:padded_k] + cross + mirror[:padded_k]) / pixels
    sub = lax.broadcasted_iota(jnp.int32, (padded_k, side), 0)
    lane = lax.broadcasted_iota(jnp.int32, (padded_k, side), 1)
    system = jnp.where((sub < size) & (lane <= size), system, 0.0)
    system = system + jnp.where((sub == lane) & (sub < size), ridge_term, 0.0)

    for k in range(size):
        row = system[k : k + 1, :]
        factor = system[:, k : k + 1] * (1.0 / row[:, k : k + 1])
        factor = jnp.where(sub[:, :1] == k, 0.0, factor)
        system = system - factor * row
    pivot = jnp.sum(jnp.where(sub == lane, system, 0.0), axis=1, keepdims=True)
    solved = system[:, size : size + 1] / jnp.where(sub[:, :1] < size, pivot, 1.0)
    coef_out[...] = jnp.sum(jnp.where(sub == lane, solved, 0.0), axis=0, keepdims=True)
    background = solved[count : count + 1, :]
    basis_coef = jnp.where(sub[:, :1] < count, solved, 0.0)

    scaled = basis_coef * row_rev[...]
    kernel = jnp.zeros((col_t.shape[0], side), f32)
    for _ in range(3):
        piece = scaled.astype(bf16)
        scaled = scaled - piece.astype(f32)
        kernel = kernel + jnp.dot(col_t[...], piece, preferred_element_type=f32)
    kernel_sum = jnp.sum(jnp.sum(kernel, axis=1, keepdims=True), axis=0, keepdims=True)
    rounded = kernel.astype(bf16).astype(f32)

    zero_band = jnp.zeros((side, side), bf16)

    def band(i):
        if i < 0 or i >= taps:
            return zero_band
        line = jnp.broadcast_to(rounded[i : i + 1, :], (side, side))
        return pltpu.roll(line, 0, 1, stride=1, stride_axis=0).astype(bf16)

    pairs = (taps + 2) // 2
    made = {i: band(i) for i in range(-1, 2 * pairs)}
    for q in range(pairs):
        for a in range(2):
            for b in range(2):
                bands[
                    q * 2 * side + a * side : q * 2 * side + (a + 1) * side,
                    b * side : (b + 1) * side,
                ] = made[2 * q + a - b]

    step = side - taps + 1
    rows_half = high // 2
    for c in range(windows.shape[0]):
        lhs = jnp.concatenate(
            [
                frames[c, pl.ds(row, rows_half, stride=2), :].astype(bf16)
                for row in range(2 * pairs)
            ],
            axis=1,
        )
        out = jnp.dot(lhs, bands[...], preferred_element_type=f32)
        windows[c, pl.ds(0, rows_half, stride=2), :] = out[:, :side]
        windows[c, pl.ds(1, rows_half, stride=2), :] = out[:, side:]
        keep = min(step, wide - c * step)
        image[:, c * step : c * step + keep] = windows[c, :, :keep]
    diff_out[...] = (science[...].astype(f32) - image[...] - background).astype(bf16)

    store_parts(sender, diff_out, payload, side, exps, capacity, wide // side)
    line_at = lax.broadcasted_iota(jnp.int32, (trailer_rows, side), 0)
    trailer = jnp.zeros((trailer_rows, side), f32)
    rest = kernel_sum
    for p in range(3):
        piece = rest.astype(bf16).astype(f32)
        rest = rest - piece
        trailer = jnp.where(line_at == p, piece, trailer)
    trailer = trailer.astype(bf16)

    def put(d, carry):
        payload[d, capacity * part :, :] = trailer
        return carry

    lax.fori_loop(0, payload.shape[0], put, 0, unroll=4)


def subtract(
    sender, gram, frames, science, col_t, row_rev, peers, exps, capacity, count, taps, pixels
):
    wins, _, side = frames.shape
    high, wide = science.shape
    part = side // exps
    pairs = (taps + 2) // 2
    body = functools.partial(
        subtract_body, exps=exps, capacity=capacity, count=count, taps=taps, pixels=pixels
    )
    return pl.pallas_call(
        body,
        out_shape=(
            jax.ShapeDtypeStruct((1, side), f32),
            jax.ShapeDtypeStruct(
                (peers * exps, capacity * part + trailer_rows, side), bf16
            ),
            jax.ShapeDtypeStruct((high, wide), bf16),
        ),
        in_specs=[smem()] + [vmem()] * 5,
        out_specs=(vmem(), vmem(), vmem()),
        scratch_shapes=[
            pltpu.VMEM((wins, high, side), f32),
            pltpu.VMEM((high, wide), f32),
            pltpu.VMEM((pairs * 2 * side, 2 * side), bf16),
        ],
        compiler_params=pltpu.CompilerParams(vmem_limit_bytes=24 * mib),
        cost_estimate=cost(5_000_000_000, 4_000_000),
        name="subtract",
    )(sender, gram, frames, science, col_t, row_rev)


def split2(value):
    top = value.astype(bf16)
    return top, (value - top.astype(f32)).astype(bf16)


def psf_body(diff, down, over, out, padded, sideways, *, side, taps):
    high, wide = diff.shape
    margin = taps // 2
    span = up(side + taps - 1, 16)
    padded[...] = jnp.zeros(padded.shape, f32)
    padded[:, margin : margin + wide] = diff[...].astype(f32)
    line = jnp.broadcast_to(over[...], (2 * side, 2 * side))
    band = pltpu.roll(line, 0, 1, stride=1, stride_axis=0)[:, :side]
    both = jnp.concatenate(split2(band), axis=1)
    sideways[...] = jnp.zeros(sideways.shape, f32)
    for c in range(wide // side):
        window = padded[:, c * side : (c + 2) * side].astype(bf16)
        got = jnp.dot(window, both, preferred_element_type=f32)
        sideways[margin : margin + high, c * side : (c + 1) * side] = got[:, :side] + got[:, side:]
    line = jnp.broadcast_to(down[...], (side, 2 * side))
    band = pltpu.roll(line, 0, 1, stride=1, stride_axis=0)[:, :span]
    top, low = split2(band)
    for r in range(high // side):
        data_top, data_low = split2(sideways[r * side : r * side + span, :])
        got = jnp.dot(top, data_top, preferred_element_type=f32)
        got = got + jnp.dot(top, data_low, preferred_element_type=f32)
        got = got + jnp.dot(low, data_top, preferred_element_type=f32)
        out[r * side : (r + 1) * side, :] = got


def correlate(diff, down, over_rev, side, taps):
    high, wide = diff.shape
    span = up(side + taps - 1, 16)
    return pl.pallas_call(
        functools.partial(psf_body, side=side, taps=taps),
        out_shape=jax.ShapeDtypeStruct((high, wide), f32),
        in_specs=[vmem()] * 3,
        out_specs=vmem(),
        scratch_shapes=[
            pltpu.VMEM((high, wide + side), f32),
            pltpu.VMEM((high - side + span, wide), f32),
        ],
        compiler_params=pltpu.CompilerParams(vmem_limit_bytes=16 * mib),
        cost_estimate=cost(2_000_000_000, 2_000_000),
        name="correlate",
    )(diff, down, over_rev)


def variance_body(table, parts, out, total, *, part, capacity):
    total[...] = jnp.zeros(total.shape, f32)
    tract = out.shape[0]

    def one(j, carry):
        block = table[j // capacity, j % capacity] - 1
        block = jnp.where(block < 0, tract, block)
        row = pl.multiple_of((j % capacity) * part, part)
        total[block] += parts[j // capacity, pl.ds(row, part), :].astype(f32)
        return carry

    lax.fori_loop(0, parts.shape[0] * capacity, one, 0, unroll=8)
    out[...] = total[:tract]


def sum_variance(table, parts, tract, part, capacity):
    side = parts.shape[2]
    return pl.pallas_call(
        functools.partial(variance_body, part=part, capacity=capacity),
        out_shape=jax.ShapeDtypeStruct((tract, part, side), f32),
        in_specs=[smem(), vmem()],
        out_specs=vmem(),
        scratch_shapes=[pltpu.VMEM((tract + 1, part, side), f32)],
        compiler_params=pltpu.CompilerParams(vmem_limit_bytes=16 * mib),
        name="sum_variance",
    )(table, parts)


def combine_body(table, parts, var_sum, var_template, out, total, gain, *, part, capacity):
    total[...] = jnp.zeros(total.shape, f32)
    gain[...] = jnp.zeros(gain.shape, f32)
    tract = out.shape[0]

    def one(d, carry):
        tail = parts[d, capacity * part :, :].astype(f32)
        kernel_sum = tail[0:1] + tail[1:2] + tail[2:3]
        square = jnp.broadcast_to(kernel_sum * kernel_sum, gain.shape[1:])
        for c in range(capacity):
            block = table[d, c] - 1
            block = jnp.where(block < 0, tract, block)
            total[block] += parts[d, c * part : (c + 1) * part, :].astype(f32)
            gain[block] += square
        return carry

    lax.fori_loop(0, parts.shape[0], one, 0, unroll=4)
    for t in range(tract):
        variance = var_sum[t] + gain[t, 0:1, :] * var_template[t].astype(f32)
        out[t] = (total[t] * lax.rsqrt(jnp.maximum(variance, 1.0))).astype(bf16)


def combine(table, parts, var_sum, var_template, part, capacity):
    tract, _, side = var_sum.shape
    return pl.pallas_call(
        functools.partial(combine_body, part=part, capacity=capacity),
        out_shape=jax.ShapeDtypeStruct((tract, part, side), bf16),
        in_specs=[smem(), vmem(), vmem(), vmem()],
        out_specs=vmem(),
        scratch_shapes=[
            pltpu.VMEM((tract + 1, part, side), f32),
            pltpu.VMEM((tract + 1, 8, side), f32),
        ],
        compiler_params=pltpu.CompilerParams(vmem_limit_bytes=16 * mib),
        name="combine",
    )(table, parts, var_sum, var_template)


def join_body(places, *refs, part, chunk):
    out, held, sems = refs[-3:]
    copies = []
    for i in range(out.shape[0] // chunk):
        blocks = pl.ds(i * chunk, chunk)
        for d, ref in enumerate(refs[:-3]):
            row = pl.multiple_of(places[d] * part, part)
            held[blocks, pl.ds(row, part), :] = ref[blocks].astype(f32)
        copies.append(pltpu.make_async_copy(held.at[blocks], out.at[blocks], sems.at[i]))
        copies[-1].start()
    for copy in copies:
        copy.wait()


def join_parts(places, parts):
    tract, part, side = parts[0].shape
    exps = len(parts)
    chunk = 8 if tract % 8 == 0 else tract
    return pl.pallas_call(
        functools.partial(join_body, part=part, chunk=chunk),
        out_shape=jax.ShapeDtypeStruct((tract, part * exps, side), f32),
        in_specs=[smem()] + [vmem()] * exps,
        out_specs=pl.BlockSpec(memory_space=pl.ANY),
        scratch_shapes=[
            pltpu.VMEM((tract, part * exps, side), f32),
            pltpu.SemaphoreType.DMA((tract // chunk,)),
        ],
        compiler_params=pltpu.CompilerParams(vmem_limit_bytes=16 * mib),
        name="join_parts",
    )(places, *parts)


def local(
    template,
    template_var,
    science,
    science_var,
    routes_src,
    routes_blk,
    stamp_rows,
    stamp_cols,
    basis_col,
    basis_row,
    psf_col,
    psf_row,
):
    peers = lax.axis_size("det")
    exps = lax.axis_size("exp")
    me = lax.axis_index("exp").astype(jnp.int32)
    tract, side, _ = template.shape
    science_img = science[0]
    variance_img = science_var[0]
    blocks_dev = routes_src.shape[1]
    count, taps = basis_col.shape
    capacity = max(2, -(-blocks_dev // peers))
    slots = peers * capacity
    part = side // exps

    request, slot_of, sender = route_tables(routes_src, routes_blk, peers, capacity)
    incoming = lax.all_to_all(request, "det", split_axis=0, concat_axis=0, tiled=True)
    picked = pick_blocks(incoming, template, slots, capacity)
    arrived = lax.all_to_all(picked, "det", split_axis=0, concat_axis=0, tiled=True)

    padded_k = up(count + 2, 16)
    col_t = jnp.pad(basis_col.T, ((0, up(taps, 16) - taps), (0, padded_k - count)))
    col = jnp.pad(basis_col.astype(f32), ((0, padded_k - count), (0, side - taps)))
    row_rev = jnp.pad(
        basis_row.astype(f32)[:, ::-1], ((0, padded_k - count), (side - taps, 0))
    )
    row_rev = jnp.roll(row_rev, 1, axis=1)
    over_rev = jnp.roll(jnp.pad(psf_row[:, ::-1], ((0, 0), (2 * side - taps, 0))), 1, axis=1)
    down = jnp.pad(psf_col, ((0, 0), (0, 2 * side - taps)))
    col_bands, row_bands, roots, data = prepare(
        stamp_rows, stamp_cols, science_img, variance_img, col, row_rev, count
    )
    sender_late, col_bands, row_bands, col_t, over_rev, down = lax.optimization_barrier(
        (sender, col_bands, row_bands, col_t, over_rev, down)
    )
    var_parts = send_parts(sender_late, request, variance_img, side, exps, capacity)
    var_back = lax.all_to_all(
        var_parts, ("det", "exp"), split_axis=0, concat_axis=0, tiled=True
    )
    table = var_back[:, capacity * part, :capacity].astype(f32).astype(jnp.int32)

    gram, frames = normal_matrix(
        slot_of,
        stamp_rows,
        stamp_cols,
        arrived,
        col_bands,
        row_bands,
        roots,
        data,
        science_img.shape[0],
        science_img.shape[1],
        taps,
    )
    coef, payload, difference = subtract(
        sender,
        gram,
        frames,
        science_img,
        col_t,
        row_rev,
        peers,
        exps,
        capacity,
        count,
        taps,
        stamp_rows.shape[1] * side * side,
    )
    diff_back = lax.all_to_all(payload, ("det", "exp"), split_axis=0, concat_axis=0, tiled=True)
    scored = correlate(difference, down, over_rev, side, taps)
    var_sum = sum_variance(table, var_back, tract, part, capacity)
    var_template = lax.dynamic_slice_in_dim(template_var, me * part, part, 1)
    var_sum, scored = lax.optimization_barrier((var_sum, scored))
    mine = combine(table, diff_back, var_sum, var_template, part, capacity)

    if exps & (exps - 1) == 0:
        held = [mine]
        reach = exps // 2
        gaps = [0]
        while reach:
            pairs = [(e, e ^ reach) for e in range(exps)]
            held = held + [lax.ppermute(h, "exp", pairs) for h in held]
            gaps = gaps + [g ^ reach for g in gaps]
            reach //= 2
        places = jnp.stack([me ^ g for g in gaps])
    else:
        held = [mine]
        for gap in range(1, exps):
            pairs = [(e, (e + gap) % exps) for e in range(exps)]
            held.append(lax.ppermute(mine, "exp", pairs))
        places = jnp.stack([(me - g) % exps for g in range(exps)])
    significance = join_parts(places, held)
    return (significance, scored[None], coef[:, : count + 1])


def solution(mesh):
    placed = (
        P("det", None, None),
        P("det", None, None),
        P("exp", "det", None),
        P("exp", "det", None),
        P("exp", "det"),
        P("exp", "det"),
        P("exp", "det"),
        P("exp", "det"),
        P(),
        P(),
        P("exp", None),
        P("exp", None),
    )
    return jax.shard_map(
        local,
        mesh=mesh,
        in_specs=placed,
        out_specs=(P("det", None, None), P("exp", "det", None), P("exp", "det")),
        check_vma=False,
    )
```

```python
import functools

import jax
import jax.numpy as jnp
from jax import lax
from jax.experimental import pallas as pl
from jax.experimental.pallas import tpu as pltpu
from jax.sharding import PartitionSpec as P

ridge_term = 0.01
bf16 = jnp.bfloat16
f32 = jnp.float32
vmem = functools.partial(pl.BlockSpec, memory_space=pltpu.VMEM)
smem = functools.partial(pl.BlockSpec, memory_space=pltpu.SMEM)
mib = 1024 * 1024
trailer_rows = 8


def up(value, step):
    return -(-value // step) * step


def cost(flops, moved):
    return pl.CostEstimate(flops=flops, bytes_accessed=moved, transcendentals=0)


def by_permutes(peers):
    return peers <= 8 and peers & (peers - 1) == 0


def permute(value, axis, size, distance):
    return lax.ppermute(value, axis, [(p, p ^ distance) for p in range(size)])


def route_body(me, src, blk, slot_of, sender, request, *rest, peers, capacity):
    outs, count = rest[:-1], rest[-1]

    def clear_count(p, carry):
        count[p] = 0
        return carry

    def clear_slot(s, carry):
        sender[s] = 0
        request[s // capacity, 0, s % capacity] = 0
        return carry

    lax.fori_loop(0, peers, clear_count, 0, unroll=peers <= 16)
    lax.fori_loop(0, peers * capacity, clear_slot, 0, unroll=peers <= 16)
    for b in range(src.shape[1]):
        owner = src[0, b]
        place = count[owner]
        count[owner] = place + 1
        slot_of[b] = owner * capacity + place
        sender[owner * capacity + place] = b
        request[owner, 0, place] = blk[0, b] + 1
    for distance, out in enumerate(outs):
        lane = lax.broadcasted_iota(jnp.int32, out.shape, 1)
        line = jnp.zeros(out.shape, jnp.int32)
        for c in range(capacity):
            line = jnp.where(lane == c, request[me[0] ^ distance, 0, c], line)
        out[...] = line


def route_tables(me, routes_src, routes_blk, peers, capacity):
    extra = peers if by_permutes(peers) else 0
    return pl.pallas_call(
        functools.partial(route_body, peers=peers, capacity=capacity),
        out_shape=(
            jax.ShapeDtypeStruct((routes_src.shape[1],), jnp.int32),
            jax.ShapeDtypeStruct((peers * capacity,), jnp.int32),
            jax.ShapeDtypeStruct((peers, 1, capacity), jnp.int32),
        )
        + (jax.ShapeDtypeStruct((8, 128), jnp.int32),) * extra,
        in_specs=[smem()] * 3,
        out_specs=(smem(),) * 3 + (vmem(),) * extra,
        scratch_shapes=[pltpu.SMEM((peers,), jnp.int32)],
        name="route_tables",
    )(me, routes_src, routes_blk)


def pick_body(*refs, capacity):
    sems = refs[-1]
    groups = (len(refs) - 2) // 2
    asked, template, outs = refs[:groups], refs[groups], refs[groups + 1 : -1]
    copies = []
    for ask, out in zip(asked, outs):
        table = ask[...] if groups > 1 else None
        for s in range(out.shape[0]):
            if groups > 1:
                wanted = table[0, s]
            else:
                wanted = ask[s // capacity, 0, s % capacity]
            block = jnp.maximum(wanted - 1, 0)
            copies.append(
                pltpu.make_async_copy(template.at[block], out.at[s], sems.at[len(copies)])
            )
            copies[-1].start()
    for copy in copies:
        copy.wait()


def pick_blocks(asked, template, slots, capacity):
    groups = len(asked)
    each = slots // groups
    return pl.pallas_call(
        functools.partial(pick_body, capacity=capacity),
        out_shape=(jax.ShapeDtypeStruct((each,) + template.shape[1:], template.dtype),) * groups,
        in_specs=[vmem() if groups > 1 else smem()] * groups
        + [pl.BlockSpec(memory_space=pltpu.HBM)],
        out_specs=(vmem(),) * groups,
        scratch_shapes=[pltpu.SemaphoreType.DMA((slots,))],
        compiler_params=pltpu.CompilerParams(vmem_limit_bytes=16 * mib),
        name="pick_blocks",
    )(*asked, template)


def store_parts(sender, image, out, side, exps, capacity, across_blocks):
    part = side // exps
    slots = sender.shape[0]

    def one(s, carry):
        b = sender[s]
        top = pl.multiple_of((b // across_blocks) * side, side)
        left = pl.multiple_of((b % across_blocks) * side, side)
        block = image[pl.ds(top, side), pl.ds(left, side)].astype(bf16)
        row = pl.multiple_of((s % capacity) * part, part)
        for q in range(exps):
            out[(s // capacity) * exps + q, pl.ds(row, part), :] = block[q * part : (q + 1) * part]
        return carry

    lax.fori_loop(0, slots, one, 0, unroll=True if slots <= 32 else 4)


def store_requests(request, out, side, exps, capacity):
    lane = lax.broadcasted_iota(jnp.int32, (trailer_rows, side), 1)

    def put(p, carry):
        line = jnp.zeros((trailer_rows, side), f32)
        for c in range(capacity):
            line = jnp.where(lane == c, request[p, 0, c].astype(f32), line)
        for q in range(exps):
            out[p * exps + q, out.shape[1] - trailer_rows :, :] = line.astype(bf16)
        return carry

    lax.fori_loop(0, request.shape[0], put, 0)


def cut(ref, top, left, height, side):
    down = pl.multiple_of((top // 8) * 8, 8)
    over = pl.multiple_of((left // side) * side, side)
    tile = ref[pl.ds(down, height), pl.ds(over, 3 * side)]
    tile = pltpu.roll(tile, lax.rem(3 * side - (left - over), 3 * side), 1)[:, : 2 * side]
    return pltpu.roll(tile, lax.rem(height - (top - down), height), 0)


def prepare_body(
    sender,
    request,
    rows_at,
    cols_at,
    science,
    variance,
    col,
    rev,
    parts_out,
    col_out,
    row_out,
    root_out,
    data_out,
    image,
    var,
    *,
    exps,
    capacity,
):
    side = rev.shape[1]
    high, wide = science.shape
    store_parts(sender, variance, parts_out, side, exps, capacity, wide // side)
    store_requests(request, parts_out, side, exps, capacity)
    sub = lax.broadcasted_iota(jnp.int32, (side, side), 0)
    lane = lax.broadcasted_iota(jnp.int32, (side, side), 1)
    for k in range(row_out.shape[0]):
        line = jnp.broadcast_to(col[k : k + 1, :], (side, side))
        line = pltpu.roll(line, 0, 1, stride=1, stride_axis=0)
        rows = slice(k * side, (k + 1) * side)
        col_out[rows, :side] = jnp.where(lane >= sub, line, 0.0).astype(bf16)
        col_out[rows, side:] = jnp.where(lane < sub, line, 0.0).astype(bf16)
        line = jnp.broadcast_to(rev[k : k + 1, :], (side, side))
        line = pltpu.roll(line, 0, 1, stride=1, stride_axis=0)
        row_out[k, :side, :] = jnp.where(lane <= sub, line, 0.0).astype(bf16)
        row_out[k, side:, :] = jnp.where(lane > sub, line, 0.0).astype(bf16)
    image[:, wide:] = jnp.zeros((image.shape[0], image.shape[1] - wide), f32)
    image[high:, :wide] = jnp.zeros((image.shape[0] - high, wide), f32)
    image[:high, :wide] = science[...].astype(f32)
    var[:, wide:] = jnp.ones((var.shape[0], var.shape[1] - wide), f32)
    var[high:, :wide] = jnp.ones((var.shape[0] - high, wide), f32)
    var[:high, :wide] = variance[...].astype(f32)
    for s in range(rows_at.shape[1]):
        top = rows_at[0, s]
        left = cols_at[0, s]
        root = lax.rsqrt(cut(var, top, left, side + 8, side)[:side, :side])
        root_out[s * side : (s + 1) * side, :] = root
        data = cut(image, top, left, side + 8, side)[:side, :side]
        data_out[s * side : (s + 1) * side, :] = data * root


def prepare(
    sender, request, rows_at, cols_at, science, variance, col, rev, count, exps, capacity
):
    side = rev.shape[1]
    high, wide = science.shape
    stamps = rows_at.shape[1]
    rows = capacity * (side // exps) + trailer_rows
    return pl.pallas_call(
        functools.partial(prepare_body, exps=exps, capacity=capacity),
        out_shape=(
            jax.ShapeDtypeStruct((request.shape[0] * exps, rows, side), bf16),
            jax.ShapeDtypeStruct((count * side, 2 * side), bf16),
            jax.ShapeDtypeStruct((count, 2 * side, side), bf16),
            jax.ShapeDtypeStruct((stamps * side, side), f32),
            jax.ShapeDtypeStruct((stamps * side, side), f32),
        ),
        in_specs=[smem()] * 4 + [vmem()] * 4,
        out_specs=(vmem(),) * 5,
        scratch_shapes=[pltpu.VMEM((high + 8, wide + 2 * side), f32)] * 2,
        compiler_params=pltpu.CompilerParams(vmem_limit_bytes=24 * mib),
        name="prepare",
    )(sender, request, rows_at, cols_at, science, variance, col, rev)


def normal_body(*refs, groups, across_blocks, taps):
    me, slot_of, rows_at, cols_at = refs[:4]
    arrived = refs[4 : 4 + groups]
    col_bands, row_bands, roots, data, gram_out, windows, frame, vert, design, stage = refs[
        4 + groups :
    ]
    count, _, side = row_bands.shape
    margin = taps // 2
    stamps = rows_at.shape[1]
    span = up(side + taps - 1, 16)
    padded_k = gram_out.shape[1]
    pitch = padded_k + 1
    lines_all = stamps * side

    frame[...] = jnp.zeros(frame.shape, f32)
    source = arrived[0]
    if groups > 1:
        source = stage
        each = arrived[0].shape[0]
        for distance in range(groups):
            for c in range(each):
                stage[(me[0] ^ distance) * each + c] = arrived[distance][c]
    for b in range(slot_of.shape[0]):
        top = margin + (b // across_blocks) * side
        left = margin + (b % across_blocks) * side
        frame[top : top + side, left : left + side] = source[slot_of[b]].astype(f32)

    cuts = []
    for s in range(stamps):
        cuts.append(cut(frame, rows_at[0, s], cols_at[0, s], span, side).astype(bf16))
    design[pl.ds(count, lines_all, stride=pitch), :] = roots[...]
    design[pl.ds(count + 1, lines_all, stride=pitch), :] = data[...]
    for extra in range(count + 2, padded_k):
        design[pl.ds(extra, lines_all, stride=pitch), :] = jnp.zeros((lines_all, side), f32)

    group = vert.shape[0]
    for k in range(0, count, group):
        filters = col_bands[k * side : (k + group) * side, :span]
        for s in range(stamps):
            out = jnp.dot(filters, cuts[s], preferred_element_type=f32).astype(bf16)
            for a in range(group):
                vert[a, s * side : (s + 1) * side, :] = out[a * side : (a + 1) * side]
        for a in range(group):
            out = jnp.dot(vert[a], row_bands[k + a], preferred_element_type=f32)
            design[pl.ds(k + a, lines_all, stride=pitch), :] = out * roots[...]

    lines = 16
    sets = 4

    def gram_step(step, total):
        start = pl.multiple_of(step * sets * lines * pitch, 8)
        tops = []
        lows = []
        for g in range(sets):
            top_set = []
            low_set = []
            for j in range(lines):
                line = design[pl.ds(start + (g * lines + j) * pitch, padded_k), :]
                top = line.astype(bf16)
                top_set.append(top)
                low_set.append((line - top.astype(f32)).astype(bf16))
            tops.append(jnp.concatenate(top_set, axis=1))
            lows.append(jnp.concatenate(low_set, axis=1))
        right = jnp.concatenate(tops, axis=0)
        left = jnp.concatenate([right] + lows, axis=0)
        return total + lax.dot_general(
            left, right, (((1,), (1,)), ((), ())), preferred_element_type=f32
        )

    total = lax.fori_loop(
        0,
        lines_all // (lines * sets),
        gram_step,
        jnp.zeros((2 * sets * padded_k, sets * padded_k), f32),
    )
    for h in range(2):
        part = jnp.zeros((padded_k, padded_k), f32)
        for g in range(sets):
            first = (h * sets + g) * padded_k
            part = part + total[first : first + padded_k, g * padded_k : (g + 1) * padded_k]
        gram_out[h * padded_k : (h + 1) * padded_k, :] = part

    step = side - taps + 1
    half = windows.shape[2]
    for c in range(windows.shape[0]):
        stage_rows = frame[:, c * step : c * step + side]
        design[: stage_rows.shape[0], :] = stage_rows
        for parity in range(2):
            windows[c, parity] = design[pl.ds(parity, half, stride=2), :]


def normal_matrix(
    me, slot_of, rows_at, cols_at, arrived, col_bands, row_bands, roots, data, high, wide, taps
):
    count, _, side = row_bands.shape
    stamps = rows_at.shape[1]
    padded_k = up(count + 2, 16)
    pairs = (taps + 2) // 2
    tall = up(high - side + 8 + up(side + taps - 1, 16), 16)
    tall = max(tall, up(high + 2 * pairs, 16))
    wins = -(-wide // (side - taps + 1))
    group = next(g for g in (4, 2, 1) if count % g == 0)
    groups = len(arrived)
    slots = sum(a.shape[0] for a in arrived) if groups > 1 else 1
    return pl.pallas_call(
        functools.partial(normal_body, groups=groups, across_blocks=wide // side, taps=taps),
        out_shape=(
            jax.ShapeDtypeStruct((2 * padded_k, padded_k), f32),
            jax.ShapeDtypeStruct((wins, 2, tall // 2, side), f32),
        ),
        in_specs=[smem()] * 4 + [vmem()] * (groups + 4),
        out_specs=(vmem(),) * 2,
        scratch_shapes=[
            pltpu.VMEM((tall, wide + 2 * side), f32),
            pltpu.VMEM((group, stamps * side, 2 * side), bf16),
            pltpu.VMEM((stamps * side * (padded_k + 1), side), f32),
            pltpu.VMEM((slots, side, side), bf16),
        ],
        compiler_params=pltpu.CompilerParams(vmem_limit_bytes=36 * mib),
        cost_estimate=cost(10_000_000_000, 8_000_000),
        name="normal_matrix",
    )(me, slot_of, rows_at, cols_at, *arrived, col_bands, row_bands, roots, data)


def subtract_body(
    sender,
    gram,
    frames,
    science,
    col_t,
    row_rev,
    coef_out,
    payload,
    diff_out,
    window,
    image,
    bands,
    total,
    *,
    exps,
    capacity,
    count,
    taps,
    pixels,
):
    side = frames.shape[3]
    high, wide = science.shape
    padded_k = gram.shape[1]
    part = side // exps
    size = count + 1

    square = jnp.concatenate(
        [gram[...], jnp.zeros((2 * padded_k, side - padded_k), f32)], axis=1
    )
    cross = square[padded_k:]
    mirror = jnp.concatenate([cross, jnp.zeros((side - padded_k, side), f32)], axis=0).T
    system = (square[:padded_k] + cross + mirror[:padded_k]) / pixels
    sub = lax.broadcasted_iota(jnp.int32, (padded_k, side), 0)
    lane = lax.broadcasted_iota(jnp.int32, (padded_k, side), 1)
    system = jnp.where((sub < size) & (lane <= size), system, 0.0)
    system = system + jnp.where((sub == lane) & (sub < size), ridge_term, 0.0)

    for k in range(size):
        row = system[k : k + 1, :]
        factor = system[:, k : k + 1] * (1.0 / row[:, k : k + 1])
        factor = jnp.where(sub[:, :1] == k, 0.0, factor)
        system = system - factor * row
    pivot = jnp.sum(jnp.where(sub == lane, system, 0.0), axis=1, keepdims=True)
    solved = system[:, size : size + 1] / jnp.where(sub[:, :1] < size, pivot, 1.0)
    coef_out[...] = jnp.sum(jnp.where(sub == lane, solved, 0.0), axis=0, keepdims=True)
    background = solved[count : count + 1, :]
    basis_coef = jnp.where(sub[:, :1] < count, solved, 0.0)

    scaled = basis_coef * row_rev[...]
    kernel = jnp.zeros((col_t.shape[0], side), f32)
    for _ in range(3):
        piece = scaled.astype(bf16)
        scaled = scaled - piece.astype(f32)
        kernel = kernel + jnp.dot(col_t[...], piece, preferred_element_type=f32)
    kernel_sum = jnp.sum(jnp.sum(kernel, axis=1, keepdims=True), axis=0, keepdims=True)
    rounded = kernel.astype(bf16).astype(f32)

    zero_band = jnp.zeros((side, side), bf16)

    def band(i):
        if i < 0 or i >= taps:
            return zero_band
        line = jnp.broadcast_to(rounded[i : i + 1, :], (side, side))
        return pltpu.roll(line, 0, 1, stride=1, stride_axis=0).astype(bf16)

    pairs = (taps + 2) // 2
    made = {i: band(i) for i in range(-1, 2 * pairs)}
    for q in range(pairs):
        for a in range(2):
            for b in range(2):
                bands[
                    q * 2 * side + a * side : q * 2 * side + (a + 1) * side,
                    b * side : (b + 1) * side,
                ] = made[2 * q + a - b]

    step = side - taps + 1
    rows_half = high // 2
    wins = frames.shape[0]
    for q in range(pairs):
        lhs = jnp.concatenate(
            [
                jnp.concatenate(
                    [frames[c, a, q : q + rows_half, :].astype(bf16) for a in range(2)], axis=1
                )
                for c in range(wins)
            ],
            axis=0,
        )
        out = jnp.dot(
            lhs, bands[q * 2 * side : (q + 1) * 2 * side, :], preferred_element_type=f32
        )
        if q:
            out = out + total[...]
        if q < pairs - 1:
            total[...] = out
    for c in range(wins):
        rows = out[c * rows_half : (c + 1) * rows_half]
        window[c, pl.ds(0, rows_half, stride=2), :] = rows[:, :side]
        window[c, pl.ds(1, rows_half, stride=2), :] = rows[:, side:]
        keep = min(step, wide - c * step)
        image[:, c * step : c * step + keep] = window[c, :, :keep]
    diff_out[...] = (science[...].astype(f32) - image[...] - background).astype(bf16)

    store_parts(sender, diff_out, payload, side, exps, capacity, wide // side)
    line_at = lax.broadcasted_iota(jnp.int32, (trailer_rows, side), 0)
    trailer = jnp.zeros((trailer_rows, side), f32)
    rest = kernel_sum
    for p in range(3):
        piece = rest.astype(bf16).astype(f32)
        rest = rest - piece
        trailer = jnp.where(line_at == p, piece, trailer)
    trailer = trailer.astype(bf16)

    def put(d, carry):
        payload[d, capacity * part :, :] = trailer
        return carry

    lax.fori_loop(0, payload.shape[0], put, 0, unroll=4)


def subtract(
    sender, gram, frames, science, col_t, row_rev, peers, exps, capacity, count, taps, pixels
):
    wins, _, _, side = frames.shape
    high, wide = science.shape
    part = side // exps
    pairs = (taps + 2) // 2
    body = functools.partial(
        subtract_body, exps=exps, capacity=capacity, count=count, taps=taps, pixels=pixels
    )
    return pl.pallas_call(
        body,
        out_shape=(
            jax.ShapeDtypeStruct((1, side), f32),
            jax.ShapeDtypeStruct(
                (peers * exps, capacity * part + trailer_rows, side), bf16
            ),
            jax.ShapeDtypeStruct((high, wide), bf16),
        ),
        in_specs=[smem()] + [vmem()] * 5,
        out_specs=(vmem(), vmem(), vmem()),
        scratch_shapes=[
            pltpu.VMEM((wins, high, side), f32),
            pltpu.VMEM((high, wide), f32),
            pltpu.VMEM((pairs * 2 * side, 2 * side), bf16),
            pltpu.VMEM((wins * high // 2, 2 * side), f32),
        ],
        compiler_params=pltpu.CompilerParams(vmem_limit_bytes=24 * mib),
        cost_estimate=cost(5_000_000_000, 4_000_000),
        name="subtract",
    )(sender, gram, frames, science, col_t, row_rev)


def split2(value):
    top = value.astype(bf16)
    return top, (value - top.astype(f32)).astype(bf16)


def score_body(
    table,
    diff,
    down,
    over,
    parts,
    out,
    var_out,
    padded,
    sideways,
    var_total,
    *,
    side,
    taps,
    part,
    capacity,
):
    add_variance(table, parts, var_out, var_total, part, capacity)
    high, wide = diff.shape
    margin = taps // 2
    span = up(side + taps - 1, 16)
    padded[...] = jnp.zeros(padded.shape, f32)
    padded[:, margin : margin + wide] = diff[...].astype(f32)
    line = jnp.broadcast_to(over[...], (2 * side, 2 * side))
    band = pltpu.roll(line, 0, 1, stride=1, stride_axis=0)[:, :side]
    both = jnp.concatenate(split2(band), axis=1)
    sideways[...] = jnp.zeros(sideways.shape, f32)
    for c in range(wide // side):
        window = padded[:, c * side : (c + 2) * side].astype(bf16)
        got = jnp.dot(window, both, preferred_element_type=f32)
        sideways[margin : margin + high, c * side : (c + 1) * side] = got[:, :side] + got[:, side:]
    line = jnp.broadcast_to(down[...], (side, 2 * side))
    band = pltpu.roll(line, 0, 1, stride=1, stride_axis=0)[:, :span]
    top, low = split2(band)
    for r in range(high // side):
        data_top, data_low = split2(sideways[r * side : r * side + span, :])
        got = jnp.dot(top, data_top, preferred_element_type=f32)
        got = got + jnp.dot(top, data_low, preferred_element_type=f32)
        got = got + jnp.dot(low, data_top, preferred_element_type=f32)
        out[r * side : (r + 1) * side, :] = got


def score(table, diff, down, over_rev, parts, side, taps, tract, part, capacity):
    high, wide = diff.shape
    span = up(side + taps - 1, 16)
    return pl.pallas_call(
        functools.partial(score_body, side=side, taps=taps, part=part, capacity=capacity),
        out_shape=(
            jax.ShapeDtypeStruct((high, wide), f32),
            jax.ShapeDtypeStruct((tract, part, side), f32),
        ),
        in_specs=[smem()] + [vmem()] * 4,
        out_specs=(vmem(),) * 2,
        scratch_shapes=[
            pltpu.VMEM((high, wide + side), f32),
            pltpu.VMEM((high - side + span, wide), f32),
            pltpu.VMEM((tract + 1, part, side), f32),
        ],
        compiler_params=pltpu.CompilerParams(vmem_limit_bytes=24 * mib),
        cost_estimate=cost(2_000_000_000, 2_000_000),
        name="score",
    )(table, diff, down, over_rev, parts)


def add_variance(table, parts, out, total, part, capacity):
    total[...] = jnp.zeros(total.shape, f32)
    tract = out.shape[0]

    def one(j, carry):
        block = table[j // capacity, j % capacity] - 1
        block = jnp.where(block < 0, tract, block)
        row = pl.multiple_of((j % capacity) * part, part)
        total[block] += parts[j // capacity, pl.ds(row, part), :].astype(f32)
        return carry

    lax.fori_loop(0, parts.shape[0] * capacity, one, 0, unroll=8)
    out[...] = total[:tract]


def combine_body(table, parts, var_sum, var_template, out, total, gain, *, part, capacity):
    total[...] = jnp.zeros(total.shape, f32)
    gain[...] = jnp.zeros(gain.shape, f32)
    tract = out.shape[0]

    def one(d, carry):
        tail = parts[d, capacity * part :, :].astype(f32)
        kernel_sum = tail[0:1] + tail[1:2] + tail[2:3]
        square = jnp.broadcast_to(kernel_sum * kernel_sum, gain.shape[1:])
        for c in range(capacity):
            block = table[d, c] - 1
            block = jnp.where(block < 0, tract, block)
            total[block] += parts[d, c * part : (c + 1) * part, :].astype(f32)
            gain[block] += square
        return carry

    lax.fori_loop(0, parts.shape[0], one, 0, unroll=4)
    for t in range(tract):
        variance = var_sum[t] + gain[t, 0:1, :] * var_template[t].astype(f32)
        out[t] = (total[t] * lax.rsqrt(jnp.maximum(variance, 1.0))).astype(bf16)


def combine(table, parts, var_sum, var_template, part, capacity):
    tract, _, side = var_sum.shape
    return pl.pallas_call(
        functools.partial(combine_body, part=part, capacity=capacity),
        out_shape=jax.ShapeDtypeStruct((tract, part, side), bf16),
        in_specs=[smem(), vmem(), vmem(), vmem()],
        out_specs=vmem(),
        scratch_shapes=[
            pltpu.VMEM((tract + 1, part, side), f32),
            pltpu.VMEM((tract + 1, 8, side), f32),
        ],
        compiler_params=pltpu.CompilerParams(vmem_limit_bytes=16 * mib),
        name="combine",
    )(table, parts, var_sum, var_template)


def join_body(places, *refs, part, chunk):
    out, held, sems = refs[-3:]
    copies = []
    for i in range(out.shape[0] // chunk):
        blocks = pl.ds(i * chunk, chunk)
        for d, ref in enumerate(refs[:-3]):
            row = pl.multiple_of(places[d] * part, part)
            held[blocks, pl.ds(row, part), :] = ref[blocks].astype(f32)
        copies.append(pltpu.make_async_copy(held.at[blocks], out.at[blocks], sems.at[i]))
        copies[-1].start()
    for copy in copies:
        copy.wait()


def join_parts(places, parts):
    tract, part, side = parts[0].shape
    exps = len(parts)
    chunk = 8 if tract % 8 == 0 else tract
    return pl.pallas_call(
        functools.partial(join_body, part=part, chunk=chunk),
        out_shape=jax.ShapeDtypeStruct((tract, part * exps, side), f32),
        in_specs=[smem()] + [vmem()] * exps,
        out_specs=pl.BlockSpec(memory_space=pl.ANY),
        scratch_shapes=[
            pltpu.VMEM((tract, part * exps, side), f32),
            pltpu.SemaphoreType.DMA((tract // chunk,)),
        ],
        compiler_params=pltpu.CompilerParams(vmem_limit_bytes=16 * mib),
        name="join_parts",
    )(places, *parts)


def local(
    template,
    template_var,
    science,
    science_var,
    routes_src,
    routes_blk,
    stamp_rows,
    stamp_cols,
    basis_col,
    basis_row,
    psf_col,
    psf_row,
):
    peers = lax.axis_size("det")
    exps = lax.axis_size("exp")
    me = lax.axis_index("exp").astype(jnp.int32)
    tract, side, _ = template.shape
    science_img = science[0]
    variance_img = science_var[0]
    blocks_dev = routes_src.shape[1]
    count, taps = basis_col.shape
    capacity = max(2, -(-blocks_dev // peers))
    slots = peers * capacity
    part = side // exps

    mine_det = lax.axis_index("det").astype(jnp.int32)[None]
    slot_of, sender, request, *asks = route_tables(
        mine_det, routes_src, routes_blk, peers, capacity
    )
    if by_permutes(peers):
        asked = [a if d == 0 else permute(a, "det", peers, d) for d, a in enumerate(asks)]
        picked = pick_blocks(asked, template, slots, capacity)
        arrived = [a if d == 0 else permute(a, "det", peers, d) for d, a in enumerate(picked)]
    else:
        asked = lax.all_to_all(request, "det", split_axis=0, concat_axis=0, tiled=True)
        picked = pick_blocks([asked], template, slots, capacity)
        arrived = [lax.all_to_all(picked[0], "det", split_axis=0, concat_axis=0, tiled=True)]

    padded_k = up(count + 2, 16)
    col_t = jnp.pad(basis_col.T, ((0, up(taps, 16) - taps), (0, padded_k - count)))
    col = jnp.pad(basis_col.astype(f32), ((0, padded_k - count), (0, side - taps)))
    row_rev = jnp.pad(
        basis_row.astype(f32)[:, ::-1], ((0, padded_k - count), (side - taps, 0))
    )
    row_rev = jnp.roll(row_rev, 1, axis=1)
    over_rev = jnp.roll(jnp.pad(psf_row[:, ::-1], ((0, 0), (2 * side - taps, 0))), 1, axis=1)
    down = jnp.pad(psf_col, ((0, 0), (0, 2 * side - taps)))
    var_parts, col_bands, row_bands, roots, data = prepare(
        sender,
        request,
        stamp_rows,
        stamp_cols,
        science_img,
        variance_img,
        col,
        row_rev,
        count,
        exps,
        capacity,
    )
    var_back = lax.all_to_all(
        var_parts, ("det", "exp"), split_axis=0, concat_axis=0, tiled=True
    )
    table = var_back[:, capacity * part, :capacity].astype(f32).astype(jnp.int32)

    gram, frames = normal_matrix(
        mine_det,
        slot_of,
        stamp_rows,
        stamp_cols,
        arrived,
        col_bands,
        row_bands,
        roots,
        data,
        science_img.shape[0],
        science_img.shape[1],
        taps,
    )
    coef, payload, difference = subtract(
        sender,
        gram,
        frames,
        science_img,
        col_t,
        row_rev,
        peers,
        exps,
        capacity,
        count,
        taps,
        stamp_rows.shape[1] * side * side,
    )
    diff_back = lax.all_to_all(payload, ("det", "exp"), split_axis=0, concat_axis=0, tiled=True)
    scored, var_sum = score(
        table, difference, down, over_rev, var_back, side, taps, tract, part, capacity
    )
    var_template = lax.dynamic_slice_in_dim(template_var, me * part, part, 1)
    mine = combine(table, diff_back, var_sum, var_template, part, capacity)

    if exps & (exps - 1) == 0:
        held = [mine]
        reach = exps // 2
        gaps = [0]
        while reach:
            pairs = [(e, e ^ reach) for e in range(exps)]
            held = held + [lax.ppermute(h, "exp", pairs) for h in held]
            gaps = gaps + [g ^ reach for g in gaps]
            reach //= 2
        places = jnp.stack([me ^ g for g in gaps])
    else:
        held = [mine]
        for gap in range(1, exps):
            pairs = [(e, (e + gap) % exps) for e in range(exps)]
            held.append(lax.ppermute(mine, "exp", pairs))
        places = jnp.stack([(me - g) % exps for g in range(exps)])
    significance = join_parts(places, held)
    return (significance, scored[None], coef[:, : count + 1])


def solution(mesh):
    placed = (
        P("det", None, None),
        P("det", None, None),
        P("exp", "det", None),
        P("exp", "det", None),
        P("exp", "det"),
        P("exp", "det"),
        P("exp", "det"),
        P("exp", "det"),
        P(),
        P(),
        P("exp", None),
        P("exp", None),
    )
    return jax.shard_map(
        local,
        mesh=mesh,
        in_specs=placed,
        out_specs=(P("det", None, None), P("exp", "det", None), P("exp", "det")),
        check_vma=False,
    )
```

```python
import functools

import jax
import jax.numpy as jnp
from jax import lax
from jax.experimental import pallas as pl
from jax.experimental.pallas import tpu as pltpu
from jax.sharding import PartitionSpec as P

ridge_term = 0.01
bf16 = jnp.bfloat16
f32 = jnp.float32
vmem = functools.partial(pl.BlockSpec, memory_space=pltpu.VMEM)
smem = functools.partial(pl.BlockSpec, memory_space=pltpu.SMEM)
mib = 1024 * 1024
trailer_rows = 8


def up(value, step):
    return -(-value // step) * step


def cost(flops, moved):
    return pl.CostEstimate(flops=flops, bytes_accessed=moved, transcendentals=0)


def route_body(src, blk, slot_of, sender, request, count, *, peers, capacity):
    def clear_count(p, carry):
        count[p] = 0
        return carry

    def clear_slot(s, carry):
        sender[s] = 0
        request[s // capacity, 0, s % capacity] = 0
        return carry

    lax.fori_loop(0, peers, clear_count, 0, unroll=peers <= 16)
    lax.fori_loop(0, peers * capacity, clear_slot, 0, unroll=peers <= 16)
    for b in range(src.shape[1]):
        owner = src[0, b]
        place = count[owner]
        count[owner] = place + 1
        slot_of[b] = owner * capacity + place
        sender[owner * capacity + place] = b
        request[owner, 0, place] = blk[0, b] + 1


def route_tables(routes_src, routes_blk, peers, capacity):
    return pl.pallas_call(
        functools.partial(route_body, peers=peers, capacity=capacity),
        out_shape=(
            jax.ShapeDtypeStruct((routes_src.shape[1],), jnp.int32),
            jax.ShapeDtypeStruct((peers * capacity,), jnp.int32),
            jax.ShapeDtypeStruct((peers, 1, capacity), jnp.int32),
        ),
        in_specs=[smem()] * 2,
        out_specs=(smem(),) * 3,
        scratch_shapes=[pltpu.SMEM((peers,), jnp.int32)],
        name="route_tables",
    )(routes_src, routes_blk)


def pick_body(asked, template, out, sems, *, capacity):
    copies = []
    for s in range(out.shape[0]):
        block = jnp.maximum(asked[s // capacity, 0, s % capacity] - 1, 0)
        copies.append(pltpu.make_async_copy(template.at[block], out.at[s], sems.at[s]))
        copies[-1].start()
    for copy in copies:
        copy.wait()


def pick_blocks(asked, template, slots, capacity):
    return pl.pallas_call(
        functools.partial(pick_body, capacity=capacity),
        out_shape=jax.ShapeDtypeStruct((slots,) + template.shape[1:], template.dtype),
        in_specs=[smem(), pl.BlockSpec(memory_space=pl.ANY)],
        out_specs=vmem(),
        scratch_shapes=[pltpu.SemaphoreType.DMA((slots,))],
        compiler_params=pltpu.CompilerParams(vmem_limit_bytes=60 * mib),
        name="pick_blocks",
    )(asked, template)


def store_parts(sender, image, out, side, exps, capacity, across_blocks):
    part = side // exps
    slots = sender.shape[0]

    def one(s, carry):
        b = sender[s]
        top = pl.multiple_of((b // across_blocks) * side, side)
        left = pl.multiple_of((b % across_blocks) * side, side)
        block = image[pl.ds(top, side), pl.ds(left, side)].astype(bf16)
        row = pl.multiple_of((s % capacity) * part, part)
        for q in range(exps):
            out[(s // capacity) * exps + q, pl.ds(row, part), :] = block[q * part : (q + 1) * part]
        return carry

    lax.fori_loop(0, slots, one, 0, unroll=True if slots <= 32 else 4)


def store_requests(request, out, side, exps, capacity):
    lane = lax.broadcasted_iota(jnp.int32, (trailer_rows, side), 1)

    def put(p, carry):
        line = jnp.zeros((trailer_rows, side), f32)
        for c in range(capacity):
            line = jnp.where(lane == c, request[p, 0, c].astype(f32), line)
        for q in range(exps):
            out[p * exps + q, out.shape[1] - trailer_rows :, :] = line.astype(bf16)
        return carry

    lax.fori_loop(0, request.shape[0], put, 0)


def cut(ref, top, left, height, side):
    down = pl.multiple_of((top // 8) * 8, 8)
    over = pl.multiple_of((left // side) * side, side)
    tile = ref[pl.ds(down, height), pl.ds(over, 3 * side)]
    tile = pltpu.roll(tile, lax.rem(3 * side - (left - over), 3 * side), 1)[:, : 2 * side]
    return pltpu.roll(tile, lax.rem(height - (top - down), height), 0)


def prepare_body(
    sender,
    request,
    rows_at,
    cols_at,
    science,
    variance,
    parts_out,
    root_out,
    data_out,
    image,
    var,
    *,
    exps,
    capacity,
):
    side = root_out.shape[1]
    high, wide = science.shape
    store_parts(sender, variance, parts_out, side, exps, capacity, wide // side)
    store_requests(request, parts_out, side, exps, capacity)
    image[:, wide:] = jnp.zeros((image.shape[0], image.shape[1] - wide), f32)
    image[high:, :wide] = jnp.zeros((image.shape[0] - high, wide), f32)
    image[:high, :wide] = science[...].astype(f32)
    var[:, wide:] = jnp.ones((var.shape[0], var.shape[1] - wide), f32)
    var[high:, :wide] = jnp.ones((var.shape[0] - high, wide), f32)
    var[:high, :wide] = variance[...].astype(f32)
    for s in range(rows_at.shape[1]):
        top = rows_at[0, s]
        left = cols_at[0, s]
        root = lax.rsqrt(cut(var, top, left, side + 8, side)[:side, :side])
        root_out[s * side : (s + 1) * side, :] = root
        data = cut(image, top, left, side + 8, side)[:side, :side]
        data_out[s * side : (s + 1) * side, :] = data * root


def prepare(sender, request, rows_at, cols_at, science, variance, side, exps, capacity):
    high, wide = science.shape
    stamps = rows_at.shape[1]
    rows = capacity * (side // exps) + trailer_rows
    return pl.pallas_call(
        functools.partial(prepare_body, exps=exps, capacity=capacity),
        out_shape=(
            jax.ShapeDtypeStruct((request.shape[0] * exps, rows, side), bf16),
            jax.ShapeDtypeStruct((stamps * side, side), f32),
            jax.ShapeDtypeStruct((stamps * side, side), f32),
        ),
        in_specs=[smem()] * 4 + [vmem()] * 2,
        out_specs=(vmem(),) * 3,
        scratch_shapes=[pltpu.VMEM((high + 8, wide + 2 * side), f32)] * 2,
        compiler_params=pltpu.CompilerParams(vmem_limit_bytes=24 * mib),
        name="prepare",
    )(sender, request, rows_at, cols_at, science, variance)


def normal_body(
    slot_of,
    rows_at,
    cols_at,
    arrived,
    col,
    row_rev,
    roots,
    data,
    gram_out,
    windows,
    frame,
    vert,
    design,
    *,
    count,
    across_blocks,
    taps,
):
    side = row_rev.shape[1]
    margin = taps // 2
    stamps = rows_at.shape[1]
    span = up(side + taps - 1, 16)
    padded_k = gram_out.shape[1]
    pitch = padded_k + 1
    lines_all = stamps * side
    sub = lax.broadcasted_iota(jnp.int32, (side, side), 0)
    lane = lax.broadcasted_iota(jnp.int32, (side, side), 1)

    frame[...] = jnp.zeros(frame.shape, f32)
    for b in range(slot_of.shape[0]):
        top = margin + (b // across_blocks) * side
        left = margin + (b % across_blocks) * side
        frame[top : top + side, left : left + side] = arrived[slot_of[b]].astype(f32)

    cuts = []
    for s in range(stamps):
        cuts.append(cut(frame, rows_at[0, s], cols_at[0, s], span, side).astype(bf16))
    design[pl.ds(count, lines_all, stride=pitch), :] = roots[...]
    design[pl.ds(count + 1, lines_all, stride=pitch), :] = data[...]
    for extra in range(count + 2, padded_k):
        design[pl.ds(extra, lines_all, stride=pitch), :] = jnp.zeros((lines_all, side), f32)

    group = vert.shape[0]
    for k in range(0, count, group):
        filters = []
        for a in range(group):
            line = jnp.broadcast_to(col[k + a : k + a + 1, :], (side, side))
            line = pltpu.roll(line, 0, 1, stride=1, stride_axis=0)
            first = jnp.where(lane >= sub, line, 0.0).astype(bf16)
            second = jnp.where(lane < sub, line, 0.0).astype(bf16)
            filters.append(jnp.concatenate([first, second[:, : span - side]], axis=1))
        filters = jnp.concatenate(filters, axis=0)
        for s in range(stamps):
            out = jnp.dot(filters, cuts[s], preferred_element_type=f32).astype(bf16)
            for a in range(group):
                vert[a, s * side : (s + 1) * side, :] = out[a * side : (a + 1) * side]
        for a in range(group):
            line = jnp.broadcast_to(row_rev[k + a : k + a + 1, :], (side, side))
            line = pltpu.roll(line, 0, 1, stride=1, stride_axis=0)
            first = jnp.where(lane <= sub, line, 0.0).astype(bf16)
            second = jnp.where(lane > sub, line, 0.0).astype(bf16)
            band = jnp.concatenate([first, second], axis=0)
            out = jnp.dot(vert[a], band, preferred_element_type=f32)
            design[pl.ds(k + a, lines_all, stride=pitch), :] = out * roots[...]

    lines = 16
    sets = 4

    def gram_step(step, total):
        start = pl.multiple_of(step * sets * lines * pitch, 8)
        tops = []
        lows = []
        for g in range(sets):
            top_set = []
            low_set = []
            for j in range(lines):
                line = design[pl.ds(start + (g * lines + j) * pitch, padded_k), :]
                top = line.astype(bf16)
                top_set.append(top)
                low_set.append((line - top.astype(f32)).astype(bf16))
            tops.append(jnp.concatenate(top_set, axis=1))
            lows.append(jnp.concatenate(low_set, axis=1))
        right = jnp.concatenate(tops, axis=0)
        left = jnp.concatenate([right] + lows, axis=0)
        return total + lax.dot_general(
            left, right, (((1,), (1,)), ((), ())), preferred_element_type=f32
        )

    total = lax.fori_loop(
        0,
        lines_all // (lines * sets),
        gram_step,
        jnp.zeros((2 * sets * padded_k, sets * padded_k), f32),
    )
    for h in range(2):
        part = jnp.zeros((padded_k, padded_k), f32)
        for g in range(sets):
            first = (h * sets + g) * padded_k
            part = part + total[first : first + padded_k, g * padded_k : (g + 1) * padded_k]
        gram_out[h * padded_k : (h + 1) * padded_k, :] = part

    step = side - taps + 1
    half = windows.shape[2]
    for c in range(windows.shape[0]):
        stage_rows = frame[:, c * step : c * step + side]
        design[: stage_rows.shape[0], :] = stage_rows
        for parity in range(2):
            windows[c, parity] = design[pl.ds(parity, half, stride=2), :]


def normal_matrix(
    slot_of, rows_at, cols_at, arrived, col, row_rev, roots, data, high, wide, count, taps
):
    side = row_rev.shape[1]
    stamps = rows_at.shape[1]
    padded_k = up(count + 2, 16)
    pairs = (taps + 2) // 2
    tall = up(high - side + 8 + up(side + taps - 1, 16), 16)
    tall = max(tall, up(high + 2 * pairs, 16))
    wins = -(-wide // (side - taps + 1))
    group = next(g for g in (4, 2, 1) if count % g == 0)
    return pl.pallas_call(
        functools.partial(normal_body, count=count, across_blocks=wide // side, taps=taps),
        out_shape=(
            jax.ShapeDtypeStruct((2 * padded_k, padded_k), f32),
            jax.ShapeDtypeStruct((wins, 2, tall // 2, side), f32),
        ),
        in_specs=[smem()] * 3 + [vmem()] * 5,
        out_specs=(vmem(),) * 2,
        scratch_shapes=[
            pltpu.VMEM((tall, wide + 2 * side), f32),
            pltpu.VMEM((group, stamps * side, 2 * side), bf16),
            pltpu.VMEM((stamps * side * (padded_k + 1), side), f32),
        ],
        compiler_params=pltpu.CompilerParams(vmem_limit_bytes=36 * mib),
        cost_estimate=cost(10_000_000_000, 8_000_000),
        name="normal_matrix",
    )(slot_of, rows_at, cols_at, arrived, col, row_rev, roots, data)


def subtract_body(
    sender,
    gram,
    frames,
    science,
    col_t,
    row_rev,
    coef_out,
    payload,
    window,
    image,
    bands,
    total,
    *,
    exps,
    capacity,
    count,
    taps,
    pixels,
):
    side = frames.shape[3]
    high, wide = science.shape
    padded_k = gram.shape[1]
    part = side // exps
    size = count + 1

    square = jnp.concatenate(
        [gram[...], jnp.zeros((2 * padded_k, side - padded_k), f32)], axis=1
    )
    cross = square[padded_k:]
    mirror = jnp.concatenate([cross, jnp.zeros((side - padded_k, side), f32)], axis=0).T
    system = (square[:padded_k] + cross + mirror[:padded_k]) / pixels
    sub = lax.broadcasted_iota(jnp.int32, (padded_k, side), 0)
    lane = lax.broadcasted_iota(jnp.int32, (padded_k, side), 1)
    system = jnp.where((sub < size) & (lane <= size), system, 0.0)
    system = system + jnp.where((sub == lane) & (sub < size), ridge_term, 0.0)

    for k in range(0, size, 4):
        block = range(min(4, size - k))
        cols = [jnp.broadcast_to(system[:, k + j : k + j + 1], system.shape) for j in block]
        rows = [system[k + j : k + j + 1, :] for j in block]
        core = [[cols[j][k + i : k + i + 1, :] for j in block] for i in block]
        for j in block:
            inverse = 1.0 / core[j][j]
            factor = jnp.where(sub == k + j, 0.0, cols[j] * inverse)
            system = system - factor * rows[j]
            for i in block[j + 1 :]:
                scale = core[i][j] * inverse
                rows[i] = rows[i] - scale * rows[j]
                for l in block[j + 1 :]:
                    core[i][l] = core[i][l] - scale * core[j][l]
                cols[i] = cols[i] - factor * core[j][i]
    pivot = jnp.sum(jnp.where(sub == lane, system, 0.0), axis=1, keepdims=True)
    solved = system[:, size : size + 1] / jnp.where(sub[:, :1] < size, pivot, 1.0)
    coef_out[...] = jnp.sum(jnp.where(sub == lane, solved, 0.0), axis=0, keepdims=True)
    background = solved[count : count + 1, :]
    basis_coef = jnp.where(sub[:, :1] < count, solved, 0.0)

    scaled = basis_coef * row_rev[...]
    kernel = jnp.zeros((col_t.shape[0], side), f32)
    for _ in range(3):
        piece = scaled.astype(bf16)
        scaled = scaled - piece.astype(f32)
        kernel = kernel + jnp.dot(col_t[...], piece, preferred_element_type=f32)
    kernel_sum = jnp.sum(jnp.sum(kernel, axis=1, keepdims=True), axis=0, keepdims=True)
    rounded = kernel.astype(bf16).astype(f32)

    zero_band = jnp.zeros((side, side), bf16)

    def band(i):
        if i < 0 or i >= taps:
            return zero_band
        line = jnp.broadcast_to(rounded[i : i + 1, :], (side, side))
        return pltpu.roll(line, 0, 1, stride=1, stride_axis=0).astype(bf16)

    pairs = (taps + 2) // 2
    made = {i: band(i) for i in range(-1, 2 * pairs)}
    for q in range(pairs):
        for a in range(2):
            for b in range(2):
                bands[
                    q * 2 * side + a * side : q * 2 * side + (a + 1) * side,
                    b * side : (b + 1) * side,
                ] = made[2 * q + a - b]

    step = side - taps + 1
    rows_half = high // 2
    wins = frames.shape[0]
    for q in range(pairs):
        lhs = jnp.concatenate(
            [
                jnp.concatenate(
                    [frames[c, a, q : q + rows_half, :].astype(bf16) for a in range(2)], axis=1
                )
                for c in range(wins)
            ],
            axis=0,
        )
        out = jnp.dot(
            lhs, bands[q * 2 * side : (q + 1) * 2 * side, :], preferred_element_type=f32
        )
        if q:
            out = out + total[...]
        if q < pairs - 1:
            total[...] = out
    for c in range(wins):
        rows = out[c * rows_half : (c + 1) * rows_half]
        window[c, pl.ds(0, rows_half, stride=2), :] = rows[:, :side]
        window[c, pl.ds(1, rows_half, stride=2), :] = rows[:, side:]
        keep = min(step, wide - c * step)
        image[:, c * step : c * step + keep] = window[c, :, :keep]
    image[...] = science[...].astype(f32) - image[...] - background

    store_parts(sender, image, payload, side, exps, capacity, wide // side)
    line_at = lax.broadcasted_iota(jnp.int32, (trailer_rows, side), 0)
    trailer = jnp.zeros((trailer_rows, side), f32)
    rest = kernel_sum
    for p in range(3):
        piece = rest.astype(bf16).astype(f32)
        rest = rest - piece
        trailer = jnp.where(line_at == p, piece, trailer)
    trailer = trailer.astype(bf16)

    def put(d, carry):
        payload[d, capacity * part :, :] = trailer
        return carry

    lax.fori_loop(0, payload.shape[0], put, 0, unroll=4)


def subtract(
    sender, gram, frames, science, col_t, row_rev, peers, exps, capacity, count, taps, pixels
):
    wins, _, _, side = frames.shape
    high, wide = science.shape
    part = side // exps
    pairs = (taps + 2) // 2
    body = functools.partial(
        subtract_body, exps=exps, capacity=capacity, count=count, taps=taps, pixels=pixels
    )
    return pl.pallas_call(
        body,
        out_shape=(
            jax.ShapeDtypeStruct((1, side), f32),
            jax.ShapeDtypeStruct(
                (peers * exps, capacity * part + trailer_rows, side), bf16
            ),
        ),
        in_specs=[smem()] + [vmem()] * 5,
        out_specs=(vmem(), vmem()),
        scratch_shapes=[
            pltpu.VMEM((wins, high, side), f32),
            pltpu.VMEM((high, wide), f32),
            pltpu.VMEM((pairs * 2 * side, 2 * side), bf16),
            pltpu.VMEM((wins * high // 2, 2 * side), f32),
        ],
        compiler_params=pltpu.CompilerParams(vmem_limit_bytes=24 * mib),
        cost_estimate=cost(5_000_000_000, 4_000_000),
        name="subtract",
    )(sender, gram, frames, science, col_t, row_rev)


def split2(value):
    top = value.astype(bf16)
    return top, (value - top.astype(f32)).astype(bf16)


def score_body(
    table,
    slot_of,
    payload,
    down,
    over,
    parts,
    out,
    var_out,
    padded,
    sideways,
    var_total,
    *,
    side,
    taps,
    part,
    capacity,
):
    add_variance(table, parts, var_out, var_total, part, capacity)
    high, wide = out.shape
    margin = taps // 2
    span = up(side + taps - 1, 16)
    across_blocks = wide // side
    exps = side // part
    padded[...] = jnp.zeros(padded.shape, f32)
    for b in range(slot_of.shape[0]):
        slot = slot_of[b]
        row = pl.multiple_of((slot % capacity) * part, part)
        left = margin + (b % across_blocks) * side
        for q in range(exps):
            top = (b // across_blocks) * side + q * part
            block = payload[(slot // capacity) * exps + q, pl.ds(row, part), :]
            padded[top : top + part, left : left + side] = block.astype(f32)
    line = jnp.broadcast_to(over[...], (2 * side, 2 * side))
    band = pltpu.roll(line, 0, 1, stride=1, stride_axis=0)[:, :side]
    both = jnp.concatenate(split2(band), axis=1)
    sideways[...] = jnp.zeros(sideways.shape, f32)
    for c in range(wide // side):
        window = padded[:, c * side : (c + 2) * side].astype(bf16)
        got = jnp.dot(window, both, preferred_element_type=f32)
        sideways[margin : margin + high, c * side : (c + 1) * side] = got[:, :side] + got[:, side:]
    line = jnp.broadcast_to(down[...], (side, 2 * side))
    band = pltpu.roll(line, 0, 1, stride=1, stride_axis=0)[:, :span]
    top, low = split2(band)
    for r in range(high // side):
        data_top, data_low = split2(sideways[r * side : r * side + span, :])
        got = jnp.dot(top, data_top, preferred_element_type=f32)
        got = got + jnp.dot(top, data_low, preferred_element_type=f32)
        got = got + jnp.dot(low, data_top, preferred_element_type=f32)
        out[r * side : (r + 1) * side, :] = got


def score(
    table, slot_of, payload, down, over_rev, parts, high, wide, taps, tract, part, capacity
):
    side = payload.shape[2]
    span = up(side + taps - 1, 16)
    return pl.pallas_call(
        functools.partial(score_body, side=side, taps=taps, part=part, capacity=capacity),
        out_shape=(
            jax.ShapeDtypeStruct((high, wide), f32),
            jax.ShapeDtypeStruct((tract, part, side), f32),
        ),
        in_specs=[smem()] * 2 + [vmem()] * 4,
        out_specs=(vmem(),) * 2,
        scratch_shapes=[
            pltpu.VMEM((high, wide + side), f32),
            pltpu.VMEM((high - side + span, wide), f32),
            pltpu.VMEM((tract + 1, part, side), f32),
        ],
        compiler_params=pltpu.CompilerParams(vmem_limit_bytes=24 * mib),
        cost_estimate=cost(2_000_000_000, 2_000_000),
        name="score",
    )(table, slot_of, payload, down, over_rev, parts)


def add_variance(table, parts, out, total, part, capacity):
    total[...] = jnp.zeros(total.shape, f32)
    tract = out.shape[0]

    def one(j, carry):
        block = table[j // capacity, j % capacity] - 1
        block = jnp.where(block < 0, tract, block)
        row = pl.multiple_of((j % capacity) * part, part)
        total[block] += parts[j // capacity, pl.ds(row, part), :].astype(f32)
        return carry

    lax.fori_loop(0, parts.shape[0] * capacity, one, 0, unroll=8)
    out[...] = total[:tract]


def combine_body(table, parts, var_sum, var_template, out, total, gain, *, part, capacity):
    total[...] = jnp.zeros(total.shape, f32)
    gain[...] = jnp.zeros(gain.shape, f32)
    tract = out.shape[0]

    def one(d, carry):
        tail = parts[d, capacity * part :, :].astype(f32)
        kernel_sum = tail[0:1] + tail[1:2] + tail[2:3]
        square = jnp.broadcast_to(kernel_sum * kernel_sum, gain.shape[1:])
        for c in range(capacity):
            block = table[d, c] - 1
            block = jnp.where(block < 0, tract, block)
            total[block] += parts[d, c * part : (c + 1) * part, :].astype(f32)
            gain[block] += square
        return carry

    lax.fori_loop(0, parts.shape[0], one, 0, unroll=4)
    for t in range(tract):
        variance = var_sum[t] + gain[t, 0:1, :] * var_template[t].astype(f32)
        out[t] = (total[t] * lax.rsqrt(jnp.maximum(variance, 1.0))).astype(bf16)


def combine(table, parts, var_sum, var_template, part, capacity):
    tract, _, side = var_sum.shape
    return pl.pallas_call(
        functools.partial(combine_body, part=part, capacity=capacity),
        out_shape=jax.ShapeDtypeStruct((tract, part, side), bf16),
        in_specs=[smem(), vmem(), vmem(), vmem()],
        out_specs=vmem(),
        scratch_shapes=[
            pltpu.VMEM((tract + 1, part, side), f32),
            pltpu.VMEM((tract + 1, 8, side), f32),
        ],
        compiler_params=pltpu.CompilerParams(vmem_limit_bytes=16 * mib),
        name="combine",
    )(table, parts, var_sum, var_template)


def join_body(places, *refs, part, chunk):
    out, held, sems = refs[-3:]
    copies = []
    for i in range(out.shape[0] // chunk):
        blocks = pl.ds(i * chunk, chunk)
        for d, ref in enumerate(refs[:-3]):
            row = pl.multiple_of(places[d] * part, part)
            held[blocks, pl.ds(row, part), :] = ref[blocks].astype(f32)
        copies.append(pltpu.make_async_copy(held.at[blocks], out.at[blocks], sems.at[i]))
        copies[-1].start()
    for copy in copies:
        copy.wait()


def join_parts(places, parts):
    tract, part, side = parts[0].shape
    exps = len(parts)
    chunk = 8 if tract % 8 == 0 else tract
    return pl.pallas_call(
        functools.partial(join_body, part=part, chunk=chunk),
        out_shape=jax.ShapeDtypeStruct((tract, part * exps, side), f32),
        in_specs=[smem()] + [vmem()] * exps,
        out_specs=pl.BlockSpec(memory_space=pl.ANY),
        scratch_shapes=[
            pltpu.VMEM((tract, part * exps, side), f32),
            pltpu.SemaphoreType.DMA((tract // chunk,)),
        ],
        compiler_params=pltpu.CompilerParams(vmem_limit_bytes=16 * mib),
        name="join_parts",
    )(places, *parts)


def local(
    template,
    template_var,
    science,
    science_var,
    routes_src,
    routes_blk,
    stamp_rows,
    stamp_cols,
    basis_col,
    basis_row,
    psf_col,
    psf_row,
):
    peers = lax.axis_size("det")
    exps = lax.axis_size("exp")
    me = lax.axis_index("exp").astype(jnp.int32)
    tract, side, _ = template.shape
    science_img = science[0]
    variance_img = science_var[0]
    blocks_dev = routes_src.shape[1]
    count, taps = basis_col.shape
    capacity = max(2, -(-blocks_dev // peers))
    slots = peers * capacity
    part = side // exps

    slot_of, sender, request = route_tables(routes_src, routes_blk, peers, capacity)
    asked = lax.all_to_all(request, "det", split_axis=0, concat_axis=0, tiled=True)
    picked = pick_blocks(asked, template, slots, capacity)
    arrived = lax.all_to_all(picked, "det", split_axis=0, concat_axis=0, tiled=True)

    padded_k = up(count + 2, 16)
    col_t = jnp.pad(basis_col.T, ((0, up(taps, 16) - taps), (0, padded_k - count)))
    col = jnp.pad(basis_col.astype(f32), ((0, padded_k - count), (0, side - taps)))
    row_rev = jnp.pad(
        basis_row.astype(f32)[:, ::-1], ((0, padded_k - count), (side - taps, 0))
    )
    row_rev = jnp.roll(row_rev, 1, axis=1)
    over_rev = jnp.roll(jnp.pad(psf_row[:, ::-1], ((0, 0), (2 * side - taps, 0))), 1, axis=1)
    down = jnp.pad(psf_col, ((0, 0), (0, 2 * side - taps)))
    var_parts, roots, data = prepare(
        sender, request, stamp_rows, stamp_cols, science_img, variance_img, side, exps, capacity
    )
    var_back = lax.all_to_all(
        var_parts, ("det", "exp"), split_axis=0, concat_axis=0, tiled=True
    )
    table = var_back[:, capacity * part, :capacity].astype(f32).astype(jnp.int32)

    high, wide = science_img.shape
    gram, frames = normal_matrix(
        slot_of,
        stamp_rows,
        stamp_cols,
        arrived,
        col,
        row_rev,
        roots,
        data,
        high,
        wide,
        count,
        taps,
    )
    coef, payload = subtract(
        sender,
        gram,
        frames,
        science_img,
        col_t,
        row_rev,
        peers,
        exps,
        capacity,
        count,
        taps,
        stamp_rows.shape[1] * side * side,
    )
    diff_back = lax.all_to_all(payload, ("det", "exp"), split_axis=0, concat_axis=0, tiled=True)
    scored, var_sum = score(
        table,
        slot_of,
        payload,
        down,
        over_rev,
        var_back,
        high,
        wide,
        taps,
        tract,
        part,
        capacity,
    )
    var_template = lax.dynamic_slice_in_dim(template_var, me * part, part, 1)
    mine = combine(table, diff_back, var_sum, var_template, part, capacity)

    if exps & (exps - 1) == 0:
        held = [mine]
        reach = exps // 2
        gaps = [0]
        while reach:
            pairs = [(e, e ^ reach) for e in range(exps)]
            held = held + [lax.ppermute(h, "exp", pairs) for h in held]
            gaps = gaps + [g ^ reach for g in gaps]
            reach //= 2
        places = jnp.stack([me ^ g for g in gaps])
    else:
        held = [mine]
        for gap in range(1, exps):
            pairs = [(e, (e + gap) % exps) for e in range(exps)]
            held.append(lax.ppermute(mine, "exp", pairs))
        places = jnp.stack([(me - g) % exps for g in range(exps)])
    significance = join_parts(places, held)
    return (significance, scored[None], coef[:, : count + 1])


def solution(mesh):
    placed = (
        P("det", None, None),
        P("det", None, None),
        P("exp", "det", None),
        P("exp", "det", None),
        P("exp", "det"),
        P("exp", "det"),
        P("exp", "det"),
        P("exp", "det"),
        P(),
        P(),
        P("exp", None),
        P("exp", None),
    )
    return jax.shard_map(
        local,
        mesh=mesh,
        in_specs=placed,
        out_specs=(P("det", None, None), P("exp", "det", None), P("exp", "det")),
        check_vma=False,
    )
```

```python
import functools

import jax
import jax.numpy as jnp
from jax import lax
from jax.experimental import pallas as pl
from jax.experimental.pallas import tpu as pltpu
from jax.sharding import PartitionSpec as P

ridge_term = 0.01
bf16 = jnp.bfloat16
f32 = jnp.float32
vmem = functools.partial(pl.BlockSpec, memory_space=pltpu.VMEM)
smem = functools.partial(pl.BlockSpec, memory_space=pltpu.SMEM)
mib = 1024 * 1024
trailer_rows = 8


def up(value, step):
    return -(-value // step) * step


def cost(flops, moved):
    return pl.CostEstimate(flops=flops, bytes_accessed=moved, transcendentals=0)


def route_body(src, blk, slot_of, sender, request, count, *, peers, capacity):
    def clear_count(p, carry):
        count[p] = 0
        return carry

    def clear_slot(s, carry):
        sender[s] = 0
        request[s // capacity, 0, s % capacity] = 0
        return carry

    lax.fori_loop(0, peers, clear_count, 0, unroll=peers <= 16)
    lax.fori_loop(0, peers * capacity, clear_slot, 0, unroll=peers <= 16)
    for b in range(src.shape[1]):
        owner = src[0, b]
        place = count[owner]
        count[owner] = place + 1
        slot_of[b] = owner * capacity + place
        sender[owner * capacity + place] = b
        request[owner, 0, place] = blk[0, b] + 1


def route_tables(routes_src, routes_blk, peers, capacity):
    return pl.pallas_call(
        functools.partial(route_body, peers=peers, capacity=capacity),
        out_shape=(
            jax.ShapeDtypeStruct((routes_src.shape[1],), jnp.int32),
            jax.ShapeDtypeStruct((peers * capacity,), jnp.int32),
            jax.ShapeDtypeStruct((peers, 1, capacity), jnp.int32),
        ),
        in_specs=[smem()] * 2,
        out_specs=(smem(),) * 3,
        scratch_shapes=[pltpu.SMEM((peers,), jnp.int32)],
        name="route_tables",
    )(routes_src, routes_blk)


def pick_body(asked, template, earlier, out, *, capacity):
    del earlier

    def one(s, carry):
        block = jnp.maximum(asked[s // capacity, 0, s % capacity] - 1, 0)
        out[s] = template[block]
        return carry

    lax.fori_loop(0, out.shape[0], one, 0, unroll=True if out.shape[0] <= 32 else 4)


def pick_blocks(asked, template, earlier, slots, capacity):
    return pl.pallas_call(
        functools.partial(pick_body, capacity=capacity),
        out_shape=jax.ShapeDtypeStruct((slots,) + template.shape[1:], template.dtype),
        in_specs=[smem(), vmem(), pl.BlockSpec(memory_space=pl.ANY)],
        out_specs=vmem(),
        compiler_params=pltpu.CompilerParams(vmem_limit_bytes=16 * mib),
        name="pick_blocks",
    )(asked, template, earlier)


def store_parts(sender, image, out, side, exps, capacity, across_blocks):
    part = side // exps
    slots = sender.shape[0]

    def one(s, carry):
        b = sender[s]
        top = pl.multiple_of((b // across_blocks) * side, side)
        left = pl.multiple_of((b % across_blocks) * side, side)
        block = image[pl.ds(top, side), pl.ds(left, side)].astype(bf16)
        row = pl.multiple_of((s % capacity) * part, part)
        for q in range(exps):
            out[(s // capacity) * exps + q, pl.ds(row, part), :] = block[q * part : (q + 1) * part]
        return carry

    lax.fori_loop(0, slots, one, 0, unroll=True if slots <= 32 else 4)


def store_requests(request, out, side, exps, capacity):
    lane = lax.broadcasted_iota(jnp.int32, (trailer_rows, side), 1)

    def put(p, carry):
        line = jnp.zeros((trailer_rows, side), f32)
        for c in range(capacity):
            line = jnp.where(lane == c, request[p, 0, c].astype(f32), line)
        for q in range(exps):
            out[p * exps + q, out.shape[1] - trailer_rows :, :] = line.astype(bf16)
        return carry

    lax.fori_loop(0, request.shape[0], put, 0)


def cut(ref, top, left, height, side):
    down = pl.multiple_of((top // 8) * 8, 8)
    over = pl.multiple_of((left // side) * side, side)
    tile = ref[pl.ds(down, height), pl.ds(over, 3 * side)]
    tile = pltpu.roll(tile, lax.rem(3 * side - (left - over), 3 * side), 1)[:, : 2 * side]
    return pltpu.roll(tile, lax.rem(height - (top - down), height), 0)


def prepare_body(sender, request, variance, out, *, side, exps, capacity):
    store_parts(sender, variance, out, side, exps, capacity, variance.shape[1] // side)
    store_requests(request, out, side, exps, capacity)


def prepare(sender, request, variance, side, exps, capacity):
    rows = capacity * (side // exps) + trailer_rows
    return pl.pallas_call(
        functools.partial(prepare_body, side=side, exps=exps, capacity=capacity),
        out_shape=jax.ShapeDtypeStruct((request.shape[0] * exps, rows, side), bf16),
        in_specs=[smem()] * 2 + [vmem()],
        out_specs=vmem(),
        compiler_params=pltpu.CompilerParams(vmem_limit_bytes=16 * mib),
        cost_estimate=cost(0, 3_000_000),
        name="prepare",
    )(sender, request, variance)


def normal_body(
    slot_of,
    rows_at,
    cols_at,
    arrived,
    col,
    row_rev,
    science,
    variance,
    gram_out,
    windows,
    frame,
    vert,
    design,
    image,
    var,
    roots,
    *,
    count,
    across_blocks,
    taps,
):
    side = row_rev.shape[1]
    margin = taps // 2
    stamps = rows_at.shape[1]
    span = up(side + taps - 1, 16)
    padded_k = gram_out.shape[1]
    pitch = padded_k + 1
    lines_all = stamps * side
    sub = lax.broadcasted_iota(jnp.int32, (side, side), 0)
    lane = lax.broadcasted_iota(jnp.int32, (side, side), 1)

    frame[...] = jnp.zeros(frame.shape, f32)
    for b in range(slot_of.shape[0]):
        top = margin + (b // across_blocks) * side
        left = margin + (b % across_blocks) * side
        frame[top : top + side, left : left + side] = arrived[slot_of[b]].astype(f32)

    cuts = []
    for s in range(stamps):
        cuts.append(cut(frame, rows_at[0, s], cols_at[0, s], span, side).astype(bf16))
    high, wide = science.shape
    image[:, wide:] = jnp.zeros((image.shape[0], image.shape[1] - wide), f32)
    image[high:, :wide] = jnp.zeros((image.shape[0] - high, wide), f32)
    image[:high, :wide] = science[...].astype(f32)
    var[:, wide:] = jnp.ones((var.shape[0], var.shape[1] - wide), f32)
    var[high:, :wide] = jnp.ones((var.shape[0] - high, wide), f32)
    var[:high, :wide] = variance[...].astype(f32)
    for s in range(stamps):
        top = rows_at[0, s]
        left = cols_at[0, s]
        root = lax.rsqrt(cut(var, top, left, side + 8, side)[:side, :side])
        roots[s * side : (s + 1) * side, :] = root
        place = pl.ds(s * side * pitch + count, side, stride=pitch)
        design[place, :] = root
        place = pl.ds(s * side * pitch + count + 1, side, stride=pitch)
        design[place, :] = root * cut(image, top, left, side + 8, side)[:side, :side]
    for extra in range(count + 2, padded_k):
        design[pl.ds(extra, lines_all, stride=pitch), :] = jnp.zeros((lines_all, side), f32)

    group = vert.shape[0]
    for k in range(0, count, group):
        filters = []
        for a in range(group):
            line = jnp.broadcast_to(col[k + a : k + a + 1, :], (side, side))
            line = pltpu.roll(line, 0, 1, stride=1, stride_axis=0)
            first = jnp.where(lane >= sub, line, 0.0).astype(bf16)
            second = jnp.where(lane < sub, line, 0.0).astype(bf16)
            filters.append(jnp.concatenate([first, second[:, : span - side]], axis=1))
        filters = jnp.concatenate(filters, axis=0)
        for s in range(stamps):
            out = jnp.dot(filters, cuts[s], preferred_element_type=f32).astype(bf16)
            for a in range(group):
                vert[a, s * side : (s + 1) * side, :] = out[a * side : (a + 1) * side]
        for a in range(group):
            line = jnp.broadcast_to(row_rev[k + a : k + a + 1, :], (side, side))
            line = pltpu.roll(line, 0, 1, stride=1, stride_axis=0)
            first = jnp.where(lane <= sub, line, 0.0).astype(bf16)
            second = jnp.where(lane > sub, line, 0.0).astype(bf16)
            band = jnp.concatenate([first, second], axis=0)
            out = jnp.dot(vert[a], band, preferred_element_type=f32)
            design[pl.ds(k + a, lines_all, stride=pitch), :] = out * roots[...]

    lines = 16
    sets = 4

    def gram_step(step, total):
        start = pl.multiple_of(step * sets * lines * pitch, 8)
        rows = []
        for g in range(sets):
            row = [
                design[pl.ds(start + (g * lines + j) * pitch, padded_k), :].astype(bf16)
                for j in range(lines)
            ]
            rows.append(jnp.concatenate(row, axis=1))
        both = jnp.concatenate(rows, axis=0)
        return total + lax.dot_general(
            both, both, (((1,), (1,)), ((), ())), preferred_element_type=f32
        )

    total = lax.fori_loop(
        0,
        lines_all // (lines * sets),
        gram_step,
        jnp.zeros((sets * padded_k, sets * padded_k), f32),
    )
    part = jnp.zeros((padded_k, padded_k), f32)
    for g in range(sets):
        rows = slice(g * padded_k, (g + 1) * padded_k)
        part = part + total[rows, rows]
    gram_out[...] = part

    step = side - taps + 1
    half = windows.shape[2]
    for c in range(windows.shape[0]):
        stage_rows = frame[:, c * step : c * step + side]
        design[: stage_rows.shape[0], :] = stage_rows
        for parity in range(2):
            windows[c, parity] = design[pl.ds(parity, half, stride=2), :]


def normal_matrix(
    slot_of, rows_at, cols_at, arrived, col, row_rev, science, variance, count, taps
):
    high, wide = science.shape
    side = row_rev.shape[1]
    stamps = rows_at.shape[1]
    padded_k = up(count + 2, 16)
    pairs = (taps + 2) // 2
    tall = up(high - side + 8 + up(side + taps - 1, 16), 16)
    tall = max(tall, up(high + 2 * pairs, 16))
    wins = -(-wide // (side - taps + 1))
    group = next(g for g in (4, 2, 1) if count % g == 0)
    return pl.pallas_call(
        functools.partial(normal_body, count=count, across_blocks=wide // side, taps=taps),
        out_shape=(
            jax.ShapeDtypeStruct((padded_k, padded_k), f32),
            jax.ShapeDtypeStruct((wins, 2, tall // 2, side), f32),
        ),
        in_specs=[smem()] * 3 + [vmem()] * 5,
        out_specs=(vmem(),) * 2,
        scratch_shapes=[
            pltpu.VMEM((tall, wide + 2 * side), f32),
            pltpu.VMEM((group, stamps * side, 2 * side), bf16),
            pltpu.VMEM((stamps * side * (padded_k + 1), side), f32),
            pltpu.VMEM((high + 8, wide + 2 * side), f32),
            pltpu.VMEM((high + 8, wide + 2 * side), f32),
            pltpu.VMEM((stamps * side, side), f32),
        ],
        compiler_params=pltpu.CompilerParams(vmem_limit_bytes=36 * mib),
        cost_estimate=cost(10_000_000_000, 8_000_000),
        name="normal_matrix",
    )(slot_of, rows_at, cols_at, arrived, col, row_rev, science, variance)


def subtract_body(
    sender,
    gram,
    frames,
    science,
    col_t,
    row_rev,
    coef_out,
    payload,
    window,
    image,
    bands,
    total,
    *,
    exps,
    capacity,
    count,
    taps,
    pixels,
):
    side = frames.shape[3]
    high, wide = science.shape
    padded_k = gram.shape[1]
    part = side // exps
    size = count + 1

    system = jnp.concatenate(
        [gram[...], jnp.zeros((padded_k, side - padded_k), f32)], axis=1
    ) / pixels
    sub = lax.broadcasted_iota(jnp.int32, (padded_k, side), 0)
    lane = lax.broadcasted_iota(jnp.int32, (padded_k, side), 1)
    system = jnp.where((sub < size) & (lane <= size), system, 0.0)
    system = system + jnp.where((sub == lane) & (sub < size), ridge_term, 0.0)

    for k in range(0, size, 4):
        block = range(min(4, size - k))
        cols = [jnp.broadcast_to(system[:, k + j : k + j + 1], system.shape) for j in block]
        rows = [system[k + j : k + j + 1, :] for j in block]
        core = [[cols[j][k + i : k + i + 1, :] for j in block] for i in block]
        for j in block:
            inverse = pl.reciprocal(core[j][j], approx=True)
            for _ in range(2):
                inverse = inverse * (2.0 - core[j][j] * inverse)
            factor = jnp.where(sub == k + j, 0.0, cols[j] * inverse)
            system = system - factor * rows[j]
            for i in block[j + 1 :]:
                scale = core[i][j] * inverse
                rows[i] = rows[i] - scale * rows[j]
                for l in block[j + 1 :]:
                    core[i][l] = core[i][l] - scale * core[j][l]
                cols[i] = cols[i] - factor * core[j][i]
    pivot = jnp.sum(jnp.where(sub == lane, system, 0.0), axis=1, keepdims=True)
    solved = system[:, size : size + 1] / jnp.where(sub[:, :1] < size, pivot, 1.0)
    coef_out[...] = jnp.sum(jnp.where(sub == lane, solved, 0.0), axis=0, keepdims=True)
    background = solved[count : count + 1, :]
    basis_coef = jnp.where(sub[:, :1] < count, solved, 0.0)

    scaled = basis_coef * row_rev[...]
    kernel = jnp.zeros((col_t.shape[0], side), f32)
    for _ in range(3):
        piece = scaled.astype(bf16)
        scaled = scaled - piece.astype(f32)
        kernel = kernel + jnp.dot(col_t[...], piece, preferred_element_type=f32)
    kernel_sum = jnp.sum(jnp.sum(kernel, axis=1, keepdims=True), axis=0, keepdims=True)
    rounded = kernel.astype(bf16).astype(f32)

    zero_band = jnp.zeros((side, side), bf16)

    def band(i):
        if i < 0 or i >= taps:
            return zero_band
        line = jnp.broadcast_to(rounded[i : i + 1, :], (side, side))
        return pltpu.roll(line, 0, 1, stride=1, stride_axis=0).astype(bf16)

    pairs = (taps + 2) // 2
    made = {i: band(i) for i in range(-1, 2 * pairs)}
    for q in range(pairs):
        for a in range(2):
            for b in range(2):
                bands[
                    q * 2 * side + a * side : q * 2 * side + (a + 1) * side,
                    b * side : (b + 1) * side,
                ] = made[2 * q + a - b]

    step = side - taps + 1
    rows_half = high // 2
    wins = frames.shape[0]
    for q in range(pairs):
        lhs = jnp.concatenate(
            [
                jnp.concatenate(
                    [frames[c, a, q : q + rows_half, :].astype(bf16) for a in range(2)], axis=1
                )
                for c in range(wins)
            ],
            axis=0,
        )
        out = jnp.dot(
            lhs, bands[q * 2 * side : (q + 1) * 2 * side, :], preferred_element_type=f32
        )
        if q:
            out = out + total[...]
        if q < pairs - 1:
            total[...] = out
    for c in range(wins):
        rows = out[c * rows_half : (c + 1) * rows_half]
        window[c, pl.ds(0, rows_half, stride=2), :] = rows[:, :side]
        window[c, pl.ds(1, rows_half, stride=2), :] = rows[:, side:]
        keep = min(step, wide - c * step)
        image[:, c * step : c * step + keep] = window[c, :, :keep]
    image[...] = science[...].astype(f32) - image[...] - background

    store_parts(sender, image, payload, side, exps, capacity, wide // side)
    line_at = lax.broadcasted_iota(jnp.int32, (trailer_rows, side), 0)
    trailer = jnp.zeros((trailer_rows, side), f32)
    rest = kernel_sum
    for p in range(3):
        piece = rest.astype(bf16).astype(f32)
        rest = rest - piece
        trailer = jnp.where(line_at == p, piece, trailer)
    trailer = trailer.astype(bf16)

    def put(d, carry):
        payload[d, capacity * part :, :] = trailer
        return carry

    lax.fori_loop(0, payload.shape[0], put, 0, unroll=4)


def subtract(
    sender, gram, frames, science, col_t, row_rev, peers, exps, capacity, count, taps, pixels
):
    wins, _, _, side = frames.shape
    high, wide = science.shape
    part = side // exps
    pairs = (taps + 2) // 2
    body = functools.partial(
        subtract_body, exps=exps, capacity=capacity, count=count, taps=taps, pixels=pixels
    )
    return pl.pallas_call(
        body,
        out_shape=(
            jax.ShapeDtypeStruct((1, side), f32),
            jax.ShapeDtypeStruct(
                (peers * exps, capacity * part + trailer_rows, side), bf16
            ),
        ),
        in_specs=[smem()] + [vmem()] * 5,
        out_specs=(vmem(), vmem()),
        scratch_shapes=[
            pltpu.VMEM((wins, high, side), f32),
            pltpu.VMEM((high, wide), f32),
            pltpu.VMEM((pairs * 2 * side, 2 * side), bf16),
            pltpu.VMEM((wins * high // 2, 2 * side), f32),
        ],
        compiler_params=pltpu.CompilerParams(vmem_limit_bytes=24 * mib),
        cost_estimate=cost(5_000_000_000, 4_000_000),
        name="subtract",
    )(sender, gram, frames, science, col_t, row_rev)


def split2(value):
    top = value.astype(bf16)
    return top, (value - top.astype(f32)).astype(bf16)


def score_body(
    table,
    slot_of,
    payload,
    down,
    over,
    parts,
    out,
    var_out,
    padded,
    sideways,
    var_total,
    *,
    side,
    taps,
    part,
    capacity,
):
    add_variance(table, parts, var_out, var_total, part, capacity)
    high, wide = out.shape
    margin = taps // 2
    span = up(side + taps - 1, 16)
    across_blocks = wide // side
    exps = side // part
    padded[...] = jnp.zeros(padded.shape, f32)
    for b in range(slot_of.shape[0]):
        slot = slot_of[b]
        row = pl.multiple_of((slot % capacity) * part, part)
        left = margin + (b % across_blocks) * side
        for q in range(exps):
            top = (b // across_blocks) * side + q * part
            block = payload[(slot // capacity) * exps + q, pl.ds(row, part), :]
            padded[top : top + part, left : left + side] = block.astype(f32)
    line = jnp.broadcast_to(over[...], (2 * side, 2 * side))
    band = pltpu.roll(line, 0, 1, stride=1, stride_axis=0)[:, :side]
    both = jnp.concatenate(split2(band), axis=1)
    sideways[...] = jnp.zeros(sideways.shape, f32)
    for c in range(wide // side):
        window = padded[:, c * side : (c + 2) * side].astype(bf16)
        got = jnp.dot(window, both, preferred_element_type=f32)
        sideways[margin : margin + high, c * side : (c + 1) * side] = got[:, :side] + got[:, side:]
    line = jnp.broadcast_to(down[...], (side, 2 * side))
    band = pltpu.roll(line, 0, 1, stride=1, stride_axis=0)[:, :span]
    top, low = split2(band)
    for r in range(high // side):
        data_top, data_low = split2(sideways[r * side : r * side + span, :])
        got = jnp.dot(top, data_top, preferred_element_type=f32)
        got = got + jnp.dot(top, data_low, preferred_element_type=f32)
        got = got + jnp.dot(low, data_top, preferred_element_type=f32)
        out[r * side : (r + 1) * side, :] = got


def score(
    table, slot_of, payload, down, over_rev, parts, high, wide, taps, tract, part, capacity
):
    side = payload.shape[2]
    span = up(side + taps - 1, 16)
    return pl.pallas_call(
        functools.partial(score_body, side=side, taps=taps, part=part, capacity=capacity),
        out_shape=(
            jax.ShapeDtypeStruct((high, wide), f32),
            jax.ShapeDtypeStruct((tract, part, side), f32),
        ),
        in_specs=[smem()] * 2 + [vmem()] * 4,
        out_specs=(vmem(),) * 2,
        scratch_shapes=[
            pltpu.VMEM((high, wide + side), f32),
            pltpu.VMEM((high - side + span, wide), f32),
            pltpu.VMEM((tract + 1, part, side), f32),
        ],
        compiler_params=pltpu.CompilerParams(vmem_limit_bytes=24 * mib),
        cost_estimate=cost(2_000_000_000, 2_000_000),
        name="score",
    )(table, slot_of, payload, down, over_rev, parts)


def add_variance(table, parts, out, total, part, capacity):
    total[...] = jnp.zeros(total.shape, f32)
    tract = out.shape[0]

    def one(j, carry):
        block = table[j // capacity, j % capacity] - 1
        block = jnp.where(block < 0, tract, block)
        row = pl.multiple_of((j % capacity) * part, part)
        total[block] += parts[j // capacity, pl.ds(row, part), :].astype(f32)
        return carry

    lax.fori_loop(0, parts.shape[0] * capacity, one, 0, unroll=8)
    out[...] = total[:tract]


def combine_body(table, parts, var_sum, var_template, out, total, gain, *, part, capacity):
    total[...] = jnp.zeros(total.shape, f32)
    gain[...] = jnp.zeros(gain.shape, f32)
    tract = out.shape[0]

    def one(d, carry):
        tail = parts[d, capacity * part :, :].astype(f32)
        kernel_sum = tail[0:1] + tail[1:2] + tail[2:3]
        square = jnp.broadcast_to(kernel_sum * kernel_sum, gain.shape[1:])
        for c in range(capacity):
            block = table[d, c] - 1
            block = jnp.where(block < 0, tract, block)
            total[block] += parts[d, c * part : (c + 1) * part, :].astype(f32)
            gain[block] += square
        return carry

    lax.fori_loop(0, parts.shape[0], one, 0, unroll=4)
    for t in range(tract):
        variance = var_sum[t] + gain[t, 0:1, :] * var_template[t].astype(f32)
        out[t] = (total[t] * lax.rsqrt(jnp.maximum(variance, 1.0))).astype(bf16)


def combine(table, parts, var_sum, var_template, part, capacity):
    tract, _, side = var_sum.shape
    return pl.pallas_call(
        functools.partial(combine_body, part=part, capacity=capacity),
        out_shape=jax.ShapeDtypeStruct((tract, part, side), bf16),
        in_specs=[smem(), vmem(), vmem(), vmem()],
        out_specs=vmem(),
        scratch_shapes=[
            pltpu.VMEM((tract + 1, part, side), f32),
            pltpu.VMEM((tract + 1, 8, side), f32),
        ],
        compiler_params=pltpu.CompilerParams(vmem_limit_bytes=16 * mib),
        name="combine",
    )(table, parts, var_sum, var_template)


def join_body(places, *refs, part, count, fresh):
    out, held, sems = refs[-3:]
    ins = refs[:count]
    copies = []
    for d, ref in enumerate(ins):
        held[d] = ref[...].astype(f32)
        row = pl.multiple_of(places[d] * part, part)
        copies.append(
            pltpu.make_async_copy(held.at[d], out.at[:, pl.ds(row, part), :], sems.at[d])
        )
        copies[-1].start()
    for copy in copies:
        copy.wait()


def join_parts(places, parts, whole, exps):
    tract, part, side = parts[0].shape
    count = len(parts)
    fresh = whole is None
    anywhere = pl.BlockSpec(memory_space=pl.ANY)
    return pl.pallas_call(
        functools.partial(join_body, part=part, count=count, fresh=fresh),
        out_shape=jax.ShapeDtypeStruct((tract, part * exps, side), f32),
        in_specs=[smem()] + [vmem()] * count + ([] if fresh else [anywhere]),
        out_specs=anywhere,
        scratch_shapes=[
            pltpu.VMEM((count, tract, part, side), f32),
            pltpu.SemaphoreType.DMA((count,)),
        ],
        input_output_aliases={} if fresh else {count + 1: 0},
        compiler_params=pltpu.CompilerParams(vmem_limit_bytes=16 * mib),
        name="join_parts",
    )(places, *parts, *([] if fresh else [whole]))


def local(
    template,
    template_var,
    science,
    science_var,
    routes_src,
    routes_blk,
    stamp_rows,
    stamp_cols,
    basis_col,
    basis_row,
    psf_col,
    psf_row,
):
    peers = lax.axis_size("det")
    exps = lax.axis_size("exp")
    me = lax.axis_index("exp").astype(jnp.int32)
    tract, side, _ = template.shape
    science_img = science[0]
    variance_img = science_var[0]
    blocks_dev = routes_src.shape[1]
    count, taps = basis_col.shape
    capacity = max(2, -(-blocks_dev // peers))
    slots = peers * capacity
    part = side // exps

    slot_of, sender, request = route_tables(routes_src, routes_blk, peers, capacity)
    asked = lax.all_to_all(request, "det", split_axis=0, concat_axis=0, tiled=True)
    var_parts = prepare(sender, request, variance_img, side, exps, capacity)
    picked = pick_blocks(asked, template, var_parts, slots, capacity)
    arrived = lax.all_to_all(picked, "det", split_axis=0, concat_axis=0, tiled=True)

    padded_k = up(count + 2, 16)
    col_t = jnp.pad(basis_col.T, ((0, up(taps, 16) - taps), (0, padded_k - count)))
    col = jnp.pad(basis_col.astype(f32), ((0, padded_k - count), (0, side - taps)))
    row_rev = jnp.pad(
        basis_row.astype(f32)[:, ::-1], ((0, padded_k - count), (side - taps, 0))
    )
    row_rev = jnp.roll(row_rev, 1, axis=1)
    over_rev = jnp.roll(jnp.pad(psf_row[:, ::-1], ((0, 0), (2 * side - taps, 0))), 1, axis=1)
    down = jnp.pad(psf_col, ((0, 0), (0, 2 * side - taps)))
    var_late, arrived = lax.optimization_barrier((var_parts, arrived))
    var_back = lax.all_to_all(
        var_late, ("det", "exp"), split_axis=0, concat_axis=0, tiled=True
    )
    table = var_back[:, capacity * part, :capacity].astype(f32).astype(jnp.int32)

    high, wide = science_img.shape
    gram, frames = normal_matrix(
        slot_of,
        stamp_rows,
        stamp_cols,
        arrived,
        col,
        row_rev,
        science_img,
        variance_img,
        count,
        taps,
    )
    coef, payload = subtract(
        sender,
        gram,
        frames,
        science_img,
        col_t,
        row_rev,
        peers,
        exps,
        capacity,
        count,
        taps,
        stamp_rows.shape[1] * side * side,
    )
    diff_back = lax.all_to_all(payload, ("det", "exp"), split_axis=0, concat_axis=0, tiled=True)
    scored, var_sum = score(
        table,
        slot_of,
        payload,
        down,
        over_rev,
        var_back,
        high,
        wide,
        taps,
        tract,
        part,
        capacity,
    )
    var_template = lax.dynamic_slice_in_dim(template_var, me * part, part, 1)
    mine = combine(table, diff_back, var_sum, var_template, part, capacity)

    if exps & (exps - 1) == 0:
        held = {0: mine}
        reach = exps // 2
        while reach:
            pairs = [(e, e ^ reach) for e in range(exps)]
            held.update({g ^ reach: lax.ppermute(h, "exp", pairs) for g, h in held.items()})
            reach //= 2
        there = {g: me ^ g for g in held}
    else:
        held = {0: mine}
        for gap in range(1, exps):
            pairs = [(e, (e + gap) % exps) for e in range(exps)]
            held[gap] = lax.ppermute(mine, "exp", pairs)
        there = {g: (me - g) % exps for g in held}
    first = max(1, exps // 2)
    significance = None
    for gaps in [list(range(first))] + [[g] for g in range(first, exps)]:
        places = jnp.stack([there[g] for g in gaps])
        significance = join_parts(places, [held[g] for g in gaps], significance, exps)
    return (significance, scored[None], coef[:, : count + 1])


def solution(mesh):
    placed = (
        P("det", None, None),
        P("det", None, None),
        P("exp", "det", None),
        P("exp", "det", None),
        P("exp", "det"),
        P("exp", "det"),
        P("exp", "det"),
        P("exp", "det"),
        P(),
        P(),
        P("exp", None),
        P("exp", None),
    )
    return jax.shard_map(
        local,
        mesh=mesh,
        in_specs=placed,
        out_specs=(P("det", None, None), P("exp", "det", None), P("exp", "det")),
        check_vma=False,
    )
```

```python
import functools

import jax
import jax.numpy as jnp
from jax import lax
from jax.experimental import pallas as pl
from jax.experimental.pallas import tpu as pltpu
from jax.sharding import PartitionSpec as P

ridge_term = 0.01
bf16 = jnp.bfloat16
f32 = jnp.float32
vmem = functools.partial(pl.BlockSpec, memory_space=pltpu.VMEM)
smem = functools.partial(pl.BlockSpec, memory_space=pltpu.SMEM)
mib = 1024 * 1024
trailer_rows = 8


def up(value, step):
    return -(-value // step) * step


def cost(flops, moved):
    return pl.CostEstimate(flops=flops, bytes_accessed=moved, transcendentals=0)


def route_body(src, blk, slot_of, sender, request, count, *, peers, capacity):
    def clear_count(p, carry):
        count[p] = 0
        return carry

    def clear_slot(s, carry):
        sender[s] = 0
        request[s // capacity, 0, s % capacity] = 0
        return carry

    lax.fori_loop(0, peers, clear_count, 0, unroll=peers <= 16)
    lax.fori_loop(0, peers * capacity, clear_slot, 0, unroll=peers <= 16)
    for b in range(src.shape[1]):
        owner = src[0, b]
        place = count[owner]
        count[owner] = place + 1
        slot_of[b] = owner * capacity + place
        sender[owner * capacity + place] = b
        request[owner, 0, place] = blk[0, b] + 1


def route_tables(routes_src, routes_blk, peers, capacity):
    return pl.pallas_call(
        functools.partial(route_body, peers=peers, capacity=capacity),
        out_shape=(
            jax.ShapeDtypeStruct((routes_src.shape[1],), jnp.int32),
            jax.ShapeDtypeStruct((peers * capacity,), jnp.int32),
            jax.ShapeDtypeStruct((peers, 1, capacity), jnp.int32),
        ),
        in_specs=[smem()] * 2,
        out_specs=(smem(),) * 3,
        scratch_shapes=[pltpu.SMEM((peers,), jnp.int32)],
        name="route_tables",
    )(routes_src, routes_blk)


def pick_body(asked, template, out, *, capacity):
    def one(s, carry):
        block = jnp.maximum(asked[s // capacity, 0, s % capacity] - 1, 0)
        out[s] = template[block]
        return carry

    lax.fori_loop(0, out.shape[0], one, 0, unroll=True if out.shape[0] <= 32 else 4)


def pick_blocks(asked, template, slots, capacity):
    return pl.pallas_call(
        functools.partial(pick_body, capacity=capacity),
        out_shape=jax.ShapeDtypeStruct((slots,) + template.shape[1:], template.dtype),
        in_specs=[smem(), vmem()],
        out_specs=vmem(),
        compiler_params=pltpu.CompilerParams(vmem_limit_bytes=16 * mib),
        name="pick_blocks",
    )(asked, template)


def store_parts(sender, image, out, side, exps, capacity, across_blocks):
    part = side // exps
    slots = sender.shape[0]
    peers = slots // capacity

    def one(s, carry):
        b = sender[s]
        top = pl.multiple_of((b // across_blocks) * side, side)
        left = pl.multiple_of((b % across_blocks) * side, side)
        block = image[pl.ds(top, side), pl.ds(left, side)].astype(bf16)
        row = pl.multiple_of((s % capacity) * part, part)
        for q in range(exps):
            out[q * peers + s // capacity, pl.ds(row, part), :] = block[q * part : (q + 1) * part]
        return carry

    lax.fori_loop(0, slots, one, 0, unroll=True if slots <= 32 else 4)


def store_requests(request, out, side, exps, capacity):
    lane = lax.broadcasted_iota(jnp.int32, (trailer_rows, side), 1)

    def put(p, carry):
        line = jnp.zeros((trailer_rows, side), f32)
        for c in range(capacity):
            line = jnp.where(lane == c, request[p, 0, c].astype(f32), line)
        for q in range(exps):
            out[q * request.shape[0] + p, out.shape[1] - trailer_rows :, :] = line.astype(bf16)
        return carry

    lax.fori_loop(0, request.shape[0], put, 0)


def cut(ref, top, left, height, side):
    down = pl.multiple_of((top // 8) * 8, 8)
    over = pl.multiple_of((left // side) * side, side)
    tile = ref[pl.ds(down, height), pl.ds(over, 3 * side)]
    tile = pltpu.roll(tile, lax.rem(3 * side - (left - over), 3 * side), 1)[:, : 2 * side]
    return pltpu.roll(tile, lax.rem(height - (top - down), height), 0)


def prepare_body(sender, request, variance, template, out, near, sem, *, side, exps, capacity):
    copy = pltpu.make_async_copy(template, near, sem)
    copy.start()
    store_parts(sender, variance, out, side, exps, capacity, variance.shape[1] // side)
    store_requests(request, out, side, exps, capacity)
    copy.wait()


def prepare(sender, request, variance, template, side, exps, capacity):
    rows = capacity * (side // exps) + trailer_rows
    return pl.pallas_call(
        functools.partial(prepare_body, side=side, exps=exps, capacity=capacity),
        out_shape=(
            jax.ShapeDtypeStruct((request.shape[0] * exps, rows, side), bf16),
            jax.ShapeDtypeStruct(template.shape, template.dtype),
        ),
        in_specs=[smem()] * 2 + [vmem(), pl.BlockSpec(memory_space=pl.ANY)],
        out_specs=(vmem(), vmem()),
        scratch_shapes=[pltpu.SemaphoreType.DMA(())],
        compiler_params=pltpu.CompilerParams(vmem_limit_bytes=16 * mib),
        cost_estimate=cost(0, 6_000_000),
        name="prepare",
    )(sender, request, variance, template)


def normal_body(
    slot_of,
    rows_at,
    cols_at,
    arrived,
    col,
    row_rev,
    science,
    variance,
    gram_out,
    windows,
    frame,
    vert,
    design,
    image,
    var,
    roots,
    window,
    *,
    count,
    across_blocks,
    taps,
):
    side = row_rev.shape[1]
    margin = taps // 2
    stamps = rows_at.shape[1]
    span = up(side + taps - 1, 16)
    padded_k = gram_out.shape[1]
    pitch = padded_k + 1
    lines_all = stamps * side
    sub = lax.broadcasted_iota(jnp.int32, (side, side), 0)
    lane = lax.broadcasted_iota(jnp.int32, (side, side), 1)

    frame[...] = jnp.zeros(frame.shape, f32)
    for b in range(slot_of.shape[0]):
        top = margin + (b // across_blocks) * side
        left = margin + (b % across_blocks) * side
        frame[top : top + side, left : left + side] = arrived[slot_of[b]].astype(f32)

    cuts = []
    for s in range(stamps):
        cuts.append(cut(frame, rows_at[0, s], cols_at[0, s], span, side).astype(bf16))
    high, wide = science.shape
    image[:, wide:] = jnp.zeros((image.shape[0], image.shape[1] - wide), f32)
    image[high:, :wide] = jnp.zeros((image.shape[0] - high, wide), f32)
    image[:high, :wide] = science[...].astype(f32)
    var[:, wide:] = jnp.ones((var.shape[0], var.shape[1] - wide), f32)
    var[high:, :wide] = jnp.ones((var.shape[0] - high, wide), f32)
    var[:high, :wide] = variance[...].astype(f32)
    for s in range(stamps):
        top = rows_at[0, s]
        left = cols_at[0, s]
        root = lax.rsqrt(cut(var, top, left, side + 8, side)[:side, :side])
        roots[s * side : (s + 1) * side, :] = root
        place = pl.ds(s * side * pitch + count, side, stride=pitch)
        design[place, :] = root
        place = pl.ds(s * side * pitch + count + 1, side, stride=pitch)
        design[place, :] = root * cut(image, top, left, side + 8, side)[:side, :side]
    for extra in range(count + 2, padded_k):
        design[pl.ds(extra, lines_all, stride=pitch), :] = jnp.zeros((lines_all, side), f32)

    group = vert.shape[0]
    step = side - taps + 1
    starts = list(range(0, count, group))
    for turn, k in enumerate(starts):
        for c in range(turn, windows.shape[0], len(starts)):
            window[...] = frame[:, c * step : c * step + side]
            for parity in range(2):
                place = pl.ds(parity, windows.shape[2], stride=2)
                windows[c, parity] = window[place, :]
        filters = []
        for a in range(group):
            line = jnp.broadcast_to(col[k + a : k + a + 1, :], (side, side))
            line = pltpu.roll(line, 0, 1, stride=1, stride_axis=0)
            first = jnp.where(lane >= sub, line, 0.0).astype(bf16)
            second = jnp.where(lane < sub, line, 0.0).astype(bf16)
            filters.append(jnp.concatenate([first, second[:, : span - side]], axis=1))
        filters = jnp.concatenate(filters, axis=0)
        for s in range(stamps):
            out = jnp.dot(filters, cuts[s], preferred_element_type=f32).astype(bf16)
            for a in range(group):
                vert[a, s * side : (s + 1) * side, :] = out[a * side : (a + 1) * side]
        for a in range(group):
            line = jnp.broadcast_to(row_rev[k + a : k + a + 1, :], (side, side))
            line = pltpu.roll(line, 0, 1, stride=1, stride_axis=0)
            first = jnp.where(lane <= sub, line, 0.0).astype(bf16)
            second = jnp.where(lane > sub, line, 0.0).astype(bf16)
            band = jnp.concatenate([first, second], axis=0)
            out = jnp.dot(vert[a], band, preferred_element_type=f32)
            design[pl.ds(k + a, lines_all, stride=pitch), :] = out * roots[...]

    lines = 16
    sets = 4

    def gram_step(step, total):
        start = pl.multiple_of(step * sets * lines * pitch, 8)
        rows = []
        for g in range(sets):
            row = [
                design[pl.ds(start + (g * lines + j) * pitch, padded_k), :].astype(bf16)
                for j in range(lines)
            ]
            rows.append(jnp.concatenate(row, axis=1))
        both = jnp.concatenate(rows, axis=0)
        return total + lax.dot_general(
            both, both, (((1,), (1,)), ((), ())), preferred_element_type=f32
        )

    total = lax.fori_loop(
        0,
        lines_all // (lines * sets),
        gram_step,
        jnp.zeros((sets * padded_k, sets * padded_k), f32),
    )
    part = jnp.zeros((padded_k, padded_k), f32)
    for g in range(sets):
        rows = slice(g * padded_k, (g + 1) * padded_k)
        part = part + total[rows, rows]
    gram_out[...] = part


def normal_matrix(
    slot_of, rows_at, cols_at, arrived, col, row_rev, science, variance, count, taps
):
    high, wide = science.shape
    side = row_rev.shape[1]
    stamps = rows_at.shape[1]
    padded_k = up(count + 2, 16)
    pairs = (taps + 2) // 2
    tall = up(high - side + 8 + up(side + taps - 1, 16), 16)
    tall = max(tall, up(high + 2 * pairs, 16))
    wins = -(-wide // (side - taps + 1))
    group = next(g for g in (4, 2, 1) if count % g == 0)
    return pl.pallas_call(
        functools.partial(normal_body, count=count, across_blocks=wide // side, taps=taps),
        out_shape=(
            jax.ShapeDtypeStruct((padded_k, padded_k), f32),
            jax.ShapeDtypeStruct((wins, 2, tall // 2, side), f32),
        ),
        in_specs=[smem()] * 3 + [vmem()] * 5,
        out_specs=(vmem(),) * 2,
        scratch_shapes=[
            pltpu.VMEM((tall, wide + 2 * side), f32),
            pltpu.VMEM((group, stamps * side, 2 * side), bf16),
            pltpu.VMEM((stamps * side * (padded_k + 1), side), f32),
            pltpu.VMEM((high + 8, wide + 2 * side), f32),
            pltpu.VMEM((high + 8, wide + 2 * side), f32),
            pltpu.VMEM((stamps * side, side), f32),
            pltpu.VMEM((tall, side), f32),
        ],
        compiler_params=pltpu.CompilerParams(vmem_limit_bytes=36 * mib),
        cost_estimate=cost(10_000_000_000, 8_000_000),
        name="normal_matrix",
    )(slot_of, rows_at, cols_at, arrived, col, row_rev, science, variance)


def subtract_body(
    sender,
    gram,
    frames,
    science,
    col_t,
    row_rev,
    coef_out,
    payload,
    window,
    image,
    bands,
    total,
    stacked,
    *,
    exps,
    capacity,
    count,
    taps,
    pixels,
):
    side = frames.shape[3]
    high, wide = science.shape
    padded_k = gram.shape[1]
    part = side // exps
    size = count + 1

    system = jnp.concatenate(
        [gram[...], jnp.zeros((padded_k, side - padded_k), f32)], axis=1
    ) / pixels
    sub = lax.broadcasted_iota(jnp.int32, (padded_k, side), 0)
    lane = lax.broadcasted_iota(jnp.int32, (padded_k, side), 1)
    system = jnp.where((sub < size) & (lane <= size), system, 0.0)
    system = system + jnp.where((sub == lane) & (sub < size), ridge_term, 0.0)

    pairs = (taps + 2) // 2
    rows_half = high // 2
    wins = frames.shape[0]

    def stack_rows(q):
        for c in range(wins):
            for a in range(2):
                stacked[q, c * rows_half : (c + 1) * rows_half, a * side : (a + 1) * side] = (
                    frames[c, a, q : q + rows_half, :].astype(bf16)
                )

    starts = list(range(0, size, 4))
    for step, k in enumerate(starts):
        for q in range(step, pairs, len(starts)):
            stack_rows(q)
        block = range(min(4, size - k))
        cols = [jnp.broadcast_to(system[:, k + j : k + j + 1], system.shape) for j in block]
        rows = [system[k + j : k + j + 1, :] for j in block]
        core = [[cols[j][k + i : k + i + 1, :] for j in block] for i in block]
        for j in block:
            inverse = 1.0 / core[j][j]
            factor = jnp.where(sub == k + j, 0.0, cols[j] * inverse)
            system = system - factor * rows[j]
            for i in block[j + 1 :]:
                scale = core[i][j] * inverse
                rows[i] = rows[i] - scale * rows[j]
                for l in block[j + 1 :]:
                    core[i][l] = core[i][l] - scale * core[j][l]
                cols[i] = cols[i] - factor * core[j][i]
    pivot = jnp.sum(jnp.where(sub == lane, system, 0.0), axis=1, keepdims=True)
    solved = system[:, size : size + 1] / jnp.where(sub[:, :1] < size, pivot, 1.0)
    coef_out[...] = jnp.sum(jnp.where(sub == lane, solved, 0.0), axis=0, keepdims=True)
    background = solved[count : count + 1, :]
    basis_coef = jnp.where(sub[:, :1] < count, solved, 0.0)

    scaled = basis_coef * row_rev[...]
    kernel = jnp.zeros((col_t.shape[0], side), f32)
    for _ in range(3):
        piece = scaled.astype(bf16)
        scaled = scaled - piece.astype(f32)
        kernel = kernel + jnp.dot(col_t[...], piece, preferred_element_type=f32)
    kernel_sum = jnp.sum(jnp.sum(kernel, axis=1, keepdims=True), axis=0, keepdims=True)
    rounded = kernel.astype(bf16).astype(f32)

    zero_band = jnp.zeros((side, side), bf16)

    def band(i):
        if i < 0 or i >= taps:
            return zero_band
        line = jnp.broadcast_to(rounded[i : i + 1, :], (side, side))
        return pltpu.roll(line, 0, 1, stride=1, stride_axis=0).astype(bf16)

    made = {i: band(i) for i in range(-1, 2 * pairs)}
    for q in range(pairs):
        for a in range(2):
            for b in range(2):
                bands[
                    q * 2 * side + a * side : q * 2 * side + (a + 1) * side,
                    b * side : (b + 1) * side,
                ] = made[2 * q + a - b]

    step = side - taps + 1
    for q in range(pairs):
        out = jnp.dot(
            stacked[q], bands[q * 2 * side : (q + 1) * 2 * side, :], preferred_element_type=f32
        )
        if q:
            out = out + total[...]
        if q < pairs - 1:
            total[...] = out
    for c in range(wins):
        rows = out[c * rows_half : (c + 1) * rows_half]
        window[c, pl.ds(0, rows_half, stride=2), :] = rows[:, :side]
        window[c, pl.ds(1, rows_half, stride=2), :] = rows[:, side:]
        keep = min(step, wide - c * step)
        image[:, c * step : c * step + keep] = window[c, :, :keep]
    image[...] = science[...].astype(f32) - image[...] - background

    store_parts(sender, image, payload, side, exps, capacity, wide // side)
    line_at = lax.broadcasted_iota(jnp.int32, (trailer_rows, side), 0)
    trailer = jnp.zeros((trailer_rows, side), f32)
    rest = kernel_sum
    for p in range(3):
        piece = rest.astype(bf16).astype(f32)
        rest = rest - piece
        trailer = jnp.where(line_at == p, piece, trailer)
    trailer = trailer.astype(bf16)

    def put(d, carry):
        payload[d, capacity * part :, :] = trailer
        return carry

    lax.fori_loop(0, payload.shape[0], put, 0, unroll=4)


def subtract(
    sender, gram, frames, science, col_t, row_rev, peers, exps, capacity, count, taps, pixels
):
    wins, _, _, side = frames.shape
    high, wide = science.shape
    part = side // exps
    pairs = (taps + 2) // 2
    body = functools.partial(
        subtract_body, exps=exps, capacity=capacity, count=count, taps=taps, pixels=pixels
    )
    return pl.pallas_call(
        body,
        out_shape=(
            jax.ShapeDtypeStruct((1, side), f32),
            jax.ShapeDtypeStruct(
                (peers * exps, capacity * part + trailer_rows, side), bf16
            ),
        ),
        in_specs=[smem()] + [vmem()] * 5,
        out_specs=(vmem(), vmem()),
        scratch_shapes=[
            pltpu.VMEM((wins, high, side), f32),
            pltpu.VMEM((high, wide), f32),
            pltpu.VMEM((pairs * 2 * side, 2 * side), bf16),
            pltpu.VMEM((wins * high // 2, 2 * side), f32),
            pltpu.VMEM((pairs, wins * high // 2, 2 * side), bf16),
        ],
        compiler_params=pltpu.CompilerParams(vmem_limit_bytes=32 * mib),
        cost_estimate=cost(5_000_000_000, 4_000_000),
        name="subtract",
    )(sender, gram, frames, science, col_t, row_rev)


def split2(value):
    top = value.astype(bf16)
    return top, (value - top.astype(f32)).astype(bf16)


def score_body(
    table,
    slot_of,
    payload,
    down,
    over,
    parts,
    out,
    var_out,
    padded,
    sideways,
    var_total,
    *,
    side,
    taps,
    part,
    capacity,
):
    add_variance(table, parts, var_out, var_total, part, capacity)
    high, wide = out.shape
    margin = taps // 2
    span = up(side + taps - 1, 16)
    across_blocks = wide // side
    exps = side // part
    peers = payload.shape[0] // exps
    padded[...] = jnp.zeros(padded.shape, f32)
    for b in range(slot_of.shape[0]):
        slot = slot_of[b]
        row = pl.multiple_of((slot % capacity) * part, part)
        left = margin + (b % across_blocks) * side
        for q in range(exps):
            top = (b // across_blocks) * side + q * part
            block = payload[q * peers + slot // capacity, pl.ds(row, part), :]
            padded[top : top + part, left : left + side] = block.astype(f32)
    line = jnp.broadcast_to(over[...], (2 * side, 2 * side))
    band = pltpu.roll(line, 0, 1, stride=1, stride_axis=0)[:, :side]
    both = jnp.concatenate(split2(band), axis=1)
    sideways[...] = jnp.zeros(sideways.shape, f32)
    for c in range(wide // side):
        window = padded[:, c * side : (c + 2) * side].astype(bf16)
        got = jnp.dot(window, both, preferred_element_type=f32)
        sideways[margin : margin + high, c * side : (c + 1) * side] = got[:, :side] + got[:, side:]
    line = jnp.broadcast_to(down[...], (side, 2 * side))
    band = pltpu.roll(line, 0, 1, stride=1, stride_axis=0)[:, :span]
    top, low = split2(band)
    for r in range(high // side):
        data_top, data_low = split2(sideways[r * side : r * side + span, :])
        got = jnp.dot(top, data_top, preferred_element_type=f32)
        got = got + jnp.dot(top, data_low, preferred_element_type=f32)
        got = got + jnp.dot(low, data_top, preferred_element_type=f32)
        out[r * side : (r + 1) * side, :] = got


def score(
    table, slot_of, payload, down, over_rev, parts, high, wide, taps, tract, part, capacity
):
    side = payload.shape[2]
    span = up(side + taps - 1, 16)
    return pl.pallas_call(
        functools.partial(score_body, side=side, taps=taps, part=part, capacity=capacity),
        out_shape=(
            jax.ShapeDtypeStruct((high, wide), f32),
            jax.ShapeDtypeStruct((tract, part, side), f32),
        ),
        in_specs=[smem()] * 2 + [vmem()] * 4,
        out_specs=(vmem(),) * 2,
        scratch_shapes=[
            pltpu.VMEM((high, wide + side), f32),
            pltpu.VMEM((high - side + span, wide), f32),
            pltpu.VMEM((tract + 1, part, side), f32),
        ],
        compiler_params=pltpu.CompilerParams(vmem_limit_bytes=24 * mib),
        cost_estimate=cost(2_000_000_000, 2_000_000),
        name="score",
    )(table, slot_of, payload, down, over_rev, parts)


def add_variance(table, parts, out, total, part, capacity):
    total[...] = jnp.zeros(total.shape, f32)
    tract = out.shape[0]

    def one(j, carry):
        block = table[j // capacity, j % capacity] - 1
        block = jnp.where(block < 0, tract, block)
        row = pl.multiple_of((j % capacity) * part, part)
        total[block] += parts[j // capacity, pl.ds(row, part), :].astype(f32)
        return carry

    lax.fori_loop(0, parts.shape[0] * capacity, one, 0, unroll=8)
    out[...] = total[:tract]


def combine_body(table, parts, var_sum, var_template, out, total, gain, *, part, capacity):
    total[...] = jnp.zeros(total.shape, f32)
    gain[...] = jnp.zeros(gain.shape, f32)
    tract = out.shape[0]

    def one(d, carry):
        tail = parts[d, capacity * part :, :].astype(f32)
        kernel_sum = tail[0:1] + tail[1:2] + tail[2:3]
        square = jnp.broadcast_to(kernel_sum * kernel_sum, gain.shape[1:])
        for c in range(capacity):
            block = table[d, c] - 1
            block = jnp.where(block < 0, tract, block)
            total[block] += parts[d, c * part : (c + 1) * part, :].astype(f32)
            gain[block] += square
        return carry

    lax.fori_loop(0, parts.shape[0], one, 0, unroll=4)
    for t in range(tract):
        variance = var_sum[t] + gain[t, 0:1, :] * var_template[t].astype(f32)
        out[t] = (total[t] * lax.rsqrt(jnp.maximum(variance, 1.0))).astype(bf16)


def combine(table, parts, var_sum, var_template, part, capacity):
    tract, _, side = var_sum.shape
    return pl.pallas_call(
        functools.partial(combine_body, part=part, capacity=capacity),
        out_shape=jax.ShapeDtypeStruct((tract, part, side), bf16),
        in_specs=[smem(), vmem(), vmem(), vmem()],
        out_specs=vmem(),
        scratch_shapes=[
            pltpu.VMEM((tract + 1, part, side), f32),
            pltpu.VMEM((tract + 1, 8, side), f32),
        ],
        compiler_params=pltpu.CompilerParams(vmem_limit_bytes=16 * mib),
        name="combine",
    )(table, parts, var_sum, var_template)


def join_body(places, *refs, part, count, fresh):
    out, held, sems = refs[-3:]
    ins = refs[:count]
    copies = []
    for d, ref in enumerate(ins):
        held[d] = ref[...].astype(f32)
        row = pl.multiple_of(places[d] * part, part)
        copies.append(
            pltpu.make_async_copy(held.at[d], out.at[:, pl.ds(row, part), :], sems.at[d])
        )
        copies[-1].start()
    for copy in copies:
        copy.wait()


def join_parts(places, parts, whole, exps):
    tract, part, side = parts[0].shape
    count = len(parts)
    fresh = whole is None
    anywhere = pl.BlockSpec(memory_space=pl.ANY)
    return pl.pallas_call(
        functools.partial(join_body, part=part, count=count, fresh=fresh),
        out_shape=jax.ShapeDtypeStruct((tract, part * exps, side), f32),
        in_specs=[smem()] + [vmem()] * count + ([] if fresh else [anywhere]),
        out_specs=anywhere,
        scratch_shapes=[
            pltpu.VMEM((count, tract, part, side), f32),
            pltpu.SemaphoreType.DMA((count,)),
        ],
        input_output_aliases={} if fresh else {count + 1: 0},
        compiler_params=pltpu.CompilerParams(vmem_limit_bytes=16 * mib),
        cost_estimate=cost(0, 3_000_000 * count),
        name="join_parts",
    )(places, *parts, *([] if fresh else [whole]))


def local(
    template,
    template_var,
    science,
    science_var,
    routes_src,
    routes_blk,
    stamp_rows,
    stamp_cols,
    basis_col,
    basis_row,
    psf_col,
    psf_row,
):
    peers = lax.axis_size("det")
    exps = lax.axis_size("exp")
    me = lax.axis_index("exp").astype(jnp.int32)
    tract, side, _ = template.shape
    science_img = science[0]
    variance_img = science_var[0]
    blocks_dev = routes_src.shape[1]
    count, taps = basis_col.shape
    capacity = max(2, -(-blocks_dev // peers))
    slots = peers * capacity
    part = side // exps

    slot_of, sender, request = route_tables(routes_src, routes_blk, peers, capacity)
    asked = lax.all_to_all(request, "det", split_axis=0, concat_axis=0, tiled=True)
    var_parts, near = prepare(sender, request, variance_img, template, side, exps, capacity)
    picked = pick_blocks(asked, near, slots, capacity)
    arrived = lax.all_to_all(picked, "det", split_axis=0, concat_axis=0, tiled=True)

    padded_k = up(count + 2, 16)
    col_t = jnp.pad(basis_col.T, ((0, up(taps, 16) - taps), (0, padded_k - count)))
    col = jnp.pad(basis_col.astype(f32), ((0, padded_k - count), (0, side - taps)))
    row_rev = jnp.pad(
        basis_row.astype(f32)[:, ::-1], ((0, padded_k - count), (side - taps, 0))
    )
    row_rev = jnp.roll(row_rev, 1, axis=1)
    over_rev = jnp.roll(jnp.pad(psf_row[:, ::-1], ((0, 0), (2 * side - taps, 0))), 1, axis=1)
    down = jnp.pad(psf_col, ((0, 0), (0, 2 * side - taps)))
    var_late, arrived = lax.optimization_barrier((var_parts, arrived))
    var_back = lax.all_to_all(
        var_late, ("exp", "det"), split_axis=0, concat_axis=0, tiled=True
    )
    table = var_back[:, capacity * part, :capacity].astype(f32).astype(jnp.int32)

    high, wide = science_img.shape
    gram, frames = normal_matrix(
        slot_of,
        stamp_rows,
        stamp_cols,
        arrived,
        col,
        row_rev,
        science_img,
        variance_img,
        count,
        taps,
    )
    coef, payload = subtract(
        sender,
        gram,
        frames,
        science_img,
        col_t,
        row_rev,
        peers,
        exps,
        capacity,
        count,
        taps,
        stamp_rows.shape[1] * side * side,
    )
    diff_back = lax.all_to_all(payload, ("exp", "det"), split_axis=0, concat_axis=0, tiled=True)
    scored, var_sum = score(
        table,
        slot_of,
        payload,
        down,
        over_rev,
        var_back,
        high,
        wide,
        taps,
        tract,
        part,
        capacity,
    )
    var_template = lax.dynamic_slice_in_dim(template_var, me * part, part, 1)
    mine = combine(table, diff_back, var_sum, var_template, part, capacity)

    if exps & (exps - 1) == 0:
        held = {0: mine}
        reach = exps // 2
        while reach:
            pairs = [(e, e ^ reach) for e in range(exps)]
            held.update({g ^ reach: lax.ppermute(h, "exp", pairs) for g, h in held.items()})
            reach //= 2
        there = {g: me ^ g for g in held}
    else:
        held = {0: mine}
        for gap in range(1, exps):
            pairs = [(e, (e + gap) % exps) for e in range(exps)]
            held[gap] = lax.ppermute(mine, "exp", pairs)
        there = {g: (me - g) % exps for g in held}
    first = max(1, exps // 2)
    significance = None
    for gaps in [list(range(first))] + [[g] for g in range(first, exps)]:
        places = jnp.stack([there[g] for g in gaps])
        significance = join_parts(places, [held[g] for g in gaps], significance, exps)
    return (significance, scored[None], coef[:, : count + 1])


def solution(mesh):
    placed = (
        P("det", None, None),
        P("det", None, None),
        P("exp", "det", None),
        P("exp", "det", None),
        P("exp", "det"),
        P("exp", "det"),
        P("exp", "det"),
        P("exp", "det"),
        P(),
        P(),
        P("exp", None),
        P("exp", None),
    )
    return jax.shard_map(
        local,
        mesh=mesh,
        in_specs=placed,
        out_specs=(P("det", None, None), P("exp", "det", None), P("exp", "det")),
        check_vma=False,
    )
```

```python
import functools

import jax
import jax.numpy as jnp
from jax import lax
from jax.experimental import pallas as pl
from jax.experimental.pallas import tpu as pltpu
from jax.sharding import PartitionSpec as P

ridge_term = 0.01
bf16 = jnp.bfloat16
f32 = jnp.float32
vmem = functools.partial(pl.BlockSpec, memory_space=pltpu.VMEM)
smem = functools.partial(pl.BlockSpec, memory_space=pltpu.SMEM)
mib = 1024 * 1024
trailer_rows = 8


def up(value, step):
    return -(-value // step) * step


def cost(flops, moved):
    return pl.CostEstimate(flops=flops, bytes_accessed=moved, transcendentals=0)


def route_body(src, blk, slot_of, sender, request, count, *, peers, capacity):
    def clear_count(p, carry):
        count[p] = 0
        return carry

    def clear_slot(s, carry):
        sender[s] = 0
        request[s // capacity, 0, s % capacity] = 0
        return carry

    lax.fori_loop(0, peers, clear_count, 0, unroll=peers <= 16)
    lax.fori_loop(0, peers * capacity, clear_slot, 0, unroll=peers <= 16)
    for b in range(src.shape[1]):
        owner = src[0, b]
        place = count[owner]
        count[owner] = place + 1
        slot_of[b] = owner * capacity + place
        sender[owner * capacity + place] = b
        request[owner, 0, place] = blk[0, b] + 1


def route_tables(routes_src, routes_blk, peers, capacity):
    return pl.pallas_call(
        functools.partial(route_body, peers=peers, capacity=capacity),
        out_shape=(
            jax.ShapeDtypeStruct((routes_src.shape[1],), jnp.int32),
            jax.ShapeDtypeStruct((peers * capacity,), jnp.int32),
            jax.ShapeDtypeStruct((peers, 1, capacity), jnp.int32),
        ),
        in_specs=[smem()] * 2,
        out_specs=(smem(),) * 3,
        scratch_shapes=[pltpu.SMEM((peers,), jnp.int32)],
        name="route_tables",
    )(routes_src, routes_blk)


def touch_body(template, out):
    out[...] = template[0, : out.shape[0], : out.shape[1]]


def touch(template):
    return pl.pallas_call(
        touch_body,
        out_shape=jax.ShapeDtypeStruct((16, 128), template.dtype),
        in_specs=[vmem()],
        out_specs=vmem(),
        compiler_params=pltpu.CompilerParams(vmem_limit_bytes=16 * mib),
        cost_estimate=cost(0, 4_000_000),
        name="touch",
    )(template)


def pick_body(asked, template, earlier, out, *, capacity):
    del earlier

    def one(s, carry):
        block = jnp.maximum(asked[s // capacity, 0, s % capacity] - 1, 0)
        out[s] = template[block]
        return carry

    lax.fori_loop(0, out.shape[0], one, 0, unroll=True if out.shape[0] <= 32 else 4)


def pick_blocks(asked, template, earlier, slots, capacity):
    return pl.pallas_call(
        functools.partial(pick_body, capacity=capacity),
        out_shape=jax.ShapeDtypeStruct((slots,) + template.shape[1:], template.dtype),
        in_specs=[smem(), vmem(), pl.BlockSpec(memory_space=pl.ANY)],
        out_specs=vmem(),
        compiler_params=pltpu.CompilerParams(vmem_limit_bytes=16 * mib),
        name="pick_blocks",
    )(asked, template, earlier)


def store_parts(sender, image, out, side, exps, capacity, across_blocks):
    part = side // exps
    slots = sender.shape[0]

    def one(s, carry):
        b = sender[s]
        top = pl.multiple_of((b // across_blocks) * side, side)
        left = pl.multiple_of((b % across_blocks) * side, side)
        block = image[pl.ds(top, side), pl.ds(left, side)].astype(bf16)
        row = pl.multiple_of((s % capacity) * part, part)
        for q in range(exps):
            out[(s // capacity) * exps + q, pl.ds(row, part), :] = block[q * part : (q + 1) * part]
        return carry

    lax.fori_loop(0, slots, one, 0, unroll=True if slots <= 32 else 4)


def store_requests(request, out, side, exps, capacity):
    lane = lax.broadcasted_iota(jnp.int32, (trailer_rows, side), 1)

    def put(p, carry):
        line = jnp.zeros((trailer_rows, side), f32)
        for c in range(capacity):
            line = jnp.where(lane == c, request[p, 0, c].astype(f32), line)
        for q in range(exps):
            out[p * exps + q, out.shape[1] - trailer_rows :, :] = line.astype(bf16)
        return carry

    lax.fori_loop(0, request.shape[0], put, 0)


def cut(ref, top, left, height, side):
    down = pl.multiple_of((top // 8) * 8, 8)
    over = pl.multiple_of((left // side) * side, side)
    tile = ref[pl.ds(down, height), pl.ds(over, 3 * side)]
    tile = pltpu.roll(tile, lax.rem(3 * side - (left - over), 3 * side), 1)[:, : 2 * side]
    return pltpu.roll(tile, lax.rem(height - (top - down), height), 0)


def prepare_body(sender, request, variance, earlier, out, *, side, exps, capacity):
    del earlier
    store_parts(sender, variance, out, side, exps, capacity, variance.shape[1] // side)
    store_requests(request, out, side, exps, capacity)


def prepare(sender, request, variance, earlier, side, exps, capacity):
    rows = capacity * (side // exps) + trailer_rows
    return pl.pallas_call(
        functools.partial(prepare_body, side=side, exps=exps, capacity=capacity),
        out_shape=jax.ShapeDtypeStruct((request.shape[0] * exps, rows, side), bf16),
        in_specs=[smem()] * 2 + [vmem(), pl.BlockSpec(memory_space=pl.ANY)],
        out_specs=vmem(),
        compiler_params=pltpu.CompilerParams(vmem_limit_bytes=16 * mib),
        cost_estimate=cost(0, 6_000_000),
        name="prepare",
    )(sender, request, variance, earlier)


def normal_body(
    slot_of,
    rows_at,
    cols_at,
    arrived,
    col,
    row_rev,
    science,
    variance,
    gram_out,
    windows,
    frame,
    vert,
    design,
    image,
    var,
    roots,
    window,
    *,
    count,
    across_blocks,
    taps,
):
    side = row_rev.shape[1]
    margin = taps // 2
    stamps = rows_at.shape[1]
    span = up(side + taps - 1, 16)
    padded_k = gram_out.shape[1]
    pitch = padded_k + 1
    lines_all = stamps * side
    sub = lax.broadcasted_iota(jnp.int32, (side, side), 0)
    lane = lax.broadcasted_iota(jnp.int32, (side, side), 1)

    frame[...] = jnp.zeros(frame.shape, f32)
    for b in range(slot_of.shape[0]):
        top = margin + (b // across_blocks) * side
        left = margin + (b % across_blocks) * side
        frame[top : top + side, left : left + side] = arrived[slot_of[b]].astype(f32)

    cuts = []
    for s in range(stamps):
        cuts.append(cut(frame, rows_at[0, s], cols_at[0, s], span, side).astype(bf16))
    high, wide = science.shape
    image[:, wide:] = jnp.zeros((image.shape[0], image.shape[1] - wide), f32)
    image[high:, :wide] = jnp.zeros((image.shape[0] - high, wide), f32)
    image[:high, :wide] = science[...].astype(f32)
    var[:, wide:] = jnp.ones((var.shape[0], var.shape[1] - wide), f32)
    var[high:, :wide] = jnp.ones((var.shape[0] - high, wide), f32)
    var[:high, :wide] = variance[...].astype(f32)
    for s in range(stamps):
        top = rows_at[0, s]
        left = cols_at[0, s]
        root = lax.rsqrt(cut(var, top, left, side + 8, side)[:side, :side])
        roots[s * side : (s + 1) * side, :] = root
        place = pl.ds(s * side * pitch + count, side, stride=pitch)
        design[place, :] = root
        place = pl.ds(s * side * pitch + count + 1, side, stride=pitch)
        design[place, :] = root * cut(image, top, left, side + 8, side)[:side, :side]
    for extra in range(count + 2, padded_k):
        design[pl.ds(extra, lines_all, stride=pitch), :] = jnp.zeros((lines_all, side), f32)

    group = vert.shape[0]
    step = side - taps + 1
    starts = list(range(0, count, group))
    for turn, k in enumerate(starts):
        for c in range(turn, windows.shape[0], len(starts)):
            window[...] = frame[:, c * step : c * step + side]
            for parity in range(2):
                place = pl.ds(parity, windows.shape[2], stride=2)
                windows[c, parity] = window[place, :]
        filters = []
        for a in range(group):
            line = jnp.broadcast_to(col[k + a : k + a + 1, :], (side, side))
            line = pltpu.roll(line, 0, 1, stride=1, stride_axis=0)
            first = jnp.where(lane >= sub, line, 0.0).astype(bf16)
            second = jnp.where(lane < sub, line, 0.0).astype(bf16)
            filters.append(jnp.concatenate([first, second[:, : span - side]], axis=1))
        filters = jnp.concatenate(filters, axis=0)
        for s in range(stamps):
            out = jnp.dot(filters, cuts[s], preferred_element_type=f32).astype(bf16)
            for a in range(group):
                vert[a, s * side : (s + 1) * side, :] = out[a * side : (a + 1) * side]
        for a in range(group):
            line = jnp.broadcast_to(row_rev[k + a : k + a + 1, :], (side, side))
            line = pltpu.roll(line, 0, 1, stride=1, stride_axis=0)
            first = jnp.where(lane <= sub, line, 0.0).astype(bf16)
            second = jnp.where(lane > sub, line, 0.0).astype(bf16)
            band = jnp.concatenate([first, second], axis=0)
            out = jnp.dot(vert[a], band, preferred_element_type=f32)
            design[pl.ds(k + a, lines_all, stride=pitch), :] = out * roots[...]

    lines = 16
    sets = 4

    def gram_step(step, total):
        start = pl.multiple_of(step * sets * lines * pitch, 8)
        rows = []
        for g in range(sets):
            row = [
                design[pl.ds(start + (g * lines + j) * pitch, padded_k), :].astype(bf16)
                for j in range(lines)
            ]
            rows.append(jnp.concatenate(row, axis=1))
        both = jnp.concatenate(rows, axis=0)
        return total + lax.dot_general(
            both, both, (((1,), (1,)), ((), ())), preferred_element_type=f32
        )

    total = lax.fori_loop(
        0,
        lines_all // (lines * sets),
        gram_step,
        jnp.zeros((sets * padded_k, sets * padded_k), f32),
    )
    part = jnp.zeros((padded_k, padded_k), f32)
    for g in range(sets):
        rows = slice(g * padded_k, (g + 1) * padded_k)
        part = part + total[rows, rows]
    gram_out[...] = part


def normal_matrix(
    slot_of, rows_at, cols_at, arrived, col, row_rev, science, variance, count, taps
):
    high, wide = science.shape
    side = row_rev.shape[1]
    stamps = rows_at.shape[1]
    padded_k = up(count + 2, 16)
    pairs = (taps + 2) // 2
    tall = up(high - side + 8 + up(side + taps - 1, 16), 16)
    tall = max(tall, up(high + 2 * pairs, 16))
    wins = -(-wide // (side - taps + 1))
    group = next(g for g in (4, 2, 1) if count % g == 0)
    return pl.pallas_call(
        functools.partial(normal_body, count=count, across_blocks=wide // side, taps=taps),
        out_shape=(
            jax.ShapeDtypeStruct((padded_k, padded_k), f32),
            jax.ShapeDtypeStruct((wins, 2, tall // 2, side), f32),
        ),
        in_specs=[smem()] * 3 + [vmem()] * 5,
        out_specs=(vmem(),) * 2,
        scratch_shapes=[
            pltpu.VMEM((tall, wide + 2 * side), f32),
            pltpu.VMEM((group, stamps * side, 2 * side), bf16),
            pltpu.VMEM((stamps * side * (padded_k + 1), side), f32),
            pltpu.VMEM((high + 8, wide + 2 * side), f32),
            pltpu.VMEM((high + 8, wide + 2 * side), f32),
            pltpu.VMEM((stamps * side, side), f32),
            pltpu.VMEM((tall, side), f32),
        ],
        compiler_params=pltpu.CompilerParams(vmem_limit_bytes=28 * mib),
        cost_estimate=cost(10_000_000_000, 8_000_000),
        name="normal_matrix",
    )(slot_of, rows_at, cols_at, arrived, col, row_rev, science, variance)


def subtract_body(
    sender,
    gram,
    frames,
    science,
    col_t,
    row_rev,
    coef_out,
    payload,
    window,
    image,
    bands,
    total,
    stacked,
    *,
    exps,
    capacity,
    count,
    taps,
    pixels,
):
    side = frames.shape[3]
    high, wide = science.shape
    padded_k = gram.shape[1]
    part = side // exps
    size = count + 1

    system = jnp.concatenate(
        [gram[...], jnp.zeros((padded_k, side - padded_k), f32)], axis=1
    ) / pixels
    sub = lax.broadcasted_iota(jnp.int32, (padded_k, side), 0)
    lane = lax.broadcasted_iota(jnp.int32, (padded_k, side), 1)
    system = jnp.where((sub < size) & (lane <= size), system, 0.0)
    system = system + jnp.where((sub == lane) & (sub < size), ridge_term, 0.0)

    pairs = (taps + 2) // 2
    rows_half = high // 2
    wins = frames.shape[0]

    def stack_rows(q):
        for c in range(wins):
            for a in range(2):
                stacked[q, c * rows_half : (c + 1) * rows_half, a * side : (a + 1) * side] = (
                    frames[c, a, q : q + rows_half, :].astype(bf16)
                )

    starts = list(range(0, size, 4))
    for step, k in enumerate(starts):
        for q in range(step, pairs, len(starts)):
            stack_rows(q)
        block = range(min(4, size - k))
        cols = [jnp.broadcast_to(system[:, k + j : k + j + 1], system.shape) for j in block]
        rows = [system[k + j : k + j + 1, :] for j in block]
        core = [[cols[j][k + i : k + i + 1, :] for j in block] for i in block]
        for j in block:
            inverse = 1.0 / core[j][j]
            factor = jnp.where(sub == k + j, 0.0, cols[j] * inverse)
            system = system - factor * rows[j]
            for i in block[j + 1 :]:
                scale = core[i][j] * inverse
                rows[i] = rows[i] - scale * rows[j]
                for l in block[j + 1 :]:
                    core[i][l] = core[i][l] - scale * core[j][l]
                cols[i] = cols[i] - factor * core[j][i]
    pivot = jnp.sum(jnp.where(sub == lane, system, 0.0), axis=1, keepdims=True)
    solved = system[:, size : size + 1] / jnp.where(sub[:, :1] < size, pivot, 1.0)
    coef_out[...] = jnp.sum(jnp.where(sub == lane, solved, 0.0), axis=0, keepdims=True)
    background = solved[count : count + 1, :]
    basis_coef = jnp.where(sub[:, :1] < count, solved, 0.0)

    scaled = basis_coef * row_rev[...]
    kernel = jnp.zeros((col_t.shape[0], side), f32)
    for _ in range(3):
        piece = scaled.astype(bf16)
        scaled = scaled - piece.astype(f32)
        kernel = kernel + jnp.dot(col_t[...], piece, preferred_element_type=f32)
    kernel_sum = jnp.sum(jnp.sum(kernel, axis=1, keepdims=True), axis=0, keepdims=True)
    rounded = kernel.astype(bf16).astype(f32)

    zero_band = jnp.zeros((side, side), bf16)

    def band(i):
        if i < 0 or i >= taps:
            return zero_band
        line = jnp.broadcast_to(rounded[i : i + 1, :], (side, side))
        return pltpu.roll(line, 0, 1, stride=1, stride_axis=0).astype(bf16)

    made = {i: band(i) for i in range(-1, 2 * pairs)}
    for q in range(pairs):
        for a in range(2):
            for b in range(2):
                bands[
                    q * 2 * side + a * side : q * 2 * side + (a + 1) * side,
                    b * side : (b + 1) * side,
                ] = made[2 * q + a - b]

    step = side - taps + 1
    for q in range(pairs):
        out = jnp.dot(
            stacked[q], bands[q * 2 * side : (q + 1) * 2 * side, :], preferred_element_type=f32
        )
        if q:
            out = out + total[...]
        if q < pairs - 1:
            total[...] = out
    for c in range(wins):
        rows = out[c * rows_half : (c + 1) * rows_half]
        window[c, pl.ds(0, rows_half, stride=2), :] = rows[:, :side]
        window[c, pl.ds(1, rows_half, stride=2), :] = rows[:, side:]
        keep = min(step, wide - c * step)
        image[:, c * step : c * step + keep] = window[c, :, :keep]
    image[...] = science[...].astype(f32) - image[...] - background

    store_parts(sender, image, payload, side, exps, capacity, wide // side)
    line_at = lax.broadcasted_iota(jnp.int32, (trailer_rows, side), 0)
    trailer = jnp.zeros((trailer_rows, side), f32)
    rest = kernel_sum
    for p in range(3):
        piece = rest.astype(bf16).astype(f32)
        rest = rest - piece
        trailer = jnp.where(line_at == p, piece, trailer)
    trailer = trailer.astype(bf16)

    def put(d, carry):
        payload[d, capacity * part :, :] = trailer
        return carry

    lax.fori_loop(0, payload.shape[0], put, 0, unroll=4)


def subtract(
    sender, gram, frames, science, col_t, row_rev, peers, exps, capacity, count, taps, pixels
):
    wins, _, _, side = frames.shape
    high, wide = science.shape
    part = side // exps
    pairs = (taps + 2) // 2
    body = functools.partial(
        subtract_body, exps=exps, capacity=capacity, count=count, taps=taps, pixels=pixels
    )
    return pl.pallas_call(
        body,
        out_shape=(
            jax.ShapeDtypeStruct((1, side), f32),
            jax.ShapeDtypeStruct(
                (peers * exps, capacity * part + trailer_rows, side), bf16
            ),
        ),
        in_specs=[smem()] + [vmem()] * 5,
        out_specs=(vmem(), vmem()),
        scratch_shapes=[
            pltpu.VMEM((wins, high, side), f32),
            pltpu.VMEM((high, wide), f32),
            pltpu.VMEM((pairs * 2 * side, 2 * side), bf16),
            pltpu.VMEM((wins * high // 2, 2 * side), f32),
            pltpu.VMEM((pairs, wins * high // 2, 2 * side), bf16),
        ],
        compiler_params=pltpu.CompilerParams(vmem_limit_bytes=24 * mib),
        cost_estimate=cost(5_000_000_000, 4_000_000),
        name="subtract",
    )(sender, gram, frames, science, col_t, row_rev)


def split2(value):
    top = value.astype(bf16)
    return top, (value - top.astype(f32)).astype(bf16)


def score_body(
    table,
    slot_of,
    payload,
    down,
    over,
    parts,
    out,
    var_out,
    padded,
    sideways,
    var_total,
    *,
    side,
    taps,
    part,
    capacity,
):
    add_variance(table, parts, var_out, var_total, part, capacity)
    high, wide = out.shape
    margin = taps // 2
    span = up(side + taps - 1, 16)
    across_blocks = wide // side
    exps = side // part
    padded[...] = jnp.zeros(padded.shape, f32)
    for b in range(slot_of.shape[0]):
        slot = slot_of[b]
        row = pl.multiple_of((slot % capacity) * part, part)
        left = margin + (b % across_blocks) * side
        for q in range(exps):
            top = (b // across_blocks) * side + q * part
            block = payload[(slot // capacity) * exps + q, pl.ds(row, part), :]
            padded[top : top + part, left : left + side] = block.astype(f32)
    line = jnp.broadcast_to(over[...], (2 * side, 2 * side))
    band = pltpu.roll(line, 0, 1, stride=1, stride_axis=0)[:, :side]
    both = jnp.concatenate(split2(band), axis=1)
    sideways[...] = jnp.zeros(sideways.shape, f32)
    for c in range(wide // side):
        window = padded[:, c * side : (c + 2) * side].astype(bf16)
        got = jnp.dot(window, both, preferred_element_type=f32)
        sideways[margin : margin + high, c * side : (c + 1) * side] = got[:, :side] + got[:, side:]
    line = jnp.broadcast_to(down[...], (side, 2 * side))
    band = pltpu.roll(line, 0, 1, stride=1, stride_axis=0)[:, :span]
    top, low = split2(band)
    for r in range(high // side):
        data_top, data_low = split2(sideways[r * side : r * side + span, :])
        got = jnp.dot(top, data_top, preferred_element_type=f32)
        got = got + jnp.dot(top, data_low, preferred_element_type=f32)
        got = got + jnp.dot(low, data_top, preferred_element_type=f32)
        out[r * side : (r + 1) * side, :] = got


def score(
    table, slot_of, payload, down, over_rev, parts, high, wide, taps, tract, part, capacity
):
    side = payload.shape[2]
    span = up(side + taps - 1, 16)
    return pl.pallas_call(
        functools.partial(score_body, side=side, taps=taps, part=part, capacity=capacity),
        out_shape=(
            jax.ShapeDtypeStruct((high, wide), f32),
            jax.ShapeDtypeStruct((tract, part, side), f32),
        ),
        in_specs=[smem()] * 2 + [vmem()] * 4,
        out_specs=(vmem(),) * 2,
        scratch_shapes=[
            pltpu.VMEM((high, wide + side), f32),
            pltpu.VMEM((high - side + span, wide), f32),
            pltpu.VMEM((tract + 1, part, side), f32),
        ],
        compiler_params=pltpu.CompilerParams(vmem_limit_bytes=24 * mib),
        cost_estimate=cost(2_000_000_000, 2_000_000),
        name="score",
    )(table, slot_of, payload, down, over_rev, parts)


def add_variance(table, parts, out, total, part, capacity):
    total[...] = jnp.zeros(total.shape, f32)
    tract = out.shape[0]

    def one(j, carry):
        block = table[j // capacity, j % capacity] - 1
        block = jnp.where(block < 0, tract, block)
        row = pl.multiple_of((j % capacity) * part, part)
        total[block] += parts[j // capacity, pl.ds(row, part), :].astype(f32)
        return carry

    lax.fori_loop(0, parts.shape[0] * capacity, one, 0, unroll=8)
    out[...] = total[:tract]


def combine_body(table, parts, var_sum, var_template, out, total, gain, *, part, capacity):
    total[...] = jnp.zeros(total.shape, f32)
    gain[...] = jnp.zeros(gain.shape, f32)
    tract = out.shape[0]

    def one(d, carry):
        tail = parts[d, capacity * part :, :].astype(f32)
        kernel_sum = tail[0:1] + tail[1:2] + tail[2:3]
        square = jnp.broadcast_to(kernel_sum * kernel_sum, gain.shape[1:])
        for c in range(capacity):
            block = table[d, c] - 1
            block = jnp.where(block < 0, tract, block)
            total[block] += parts[d, c * part : (c + 1) * part, :].astype(f32)
            gain[block] += square
        return carry

    lax.fori_loop(0, parts.shape[0], one, 0, unroll=4)
    for t in range(tract):
        variance = var_sum[t] + gain[t, 0:1, :] * var_template[t].astype(f32)
        out[t] = (total[t] * lax.rsqrt(jnp.maximum(variance, 1.0))).astype(bf16)


def combine(table, parts, var_sum, var_template, part, capacity):
    tract, _, side = var_sum.shape
    return pl.pallas_call(
        functools.partial(combine_body, part=part, capacity=capacity),
        out_shape=jax.ShapeDtypeStruct((tract, part, side), bf16),
        in_specs=[smem(), vmem(), vmem(), vmem()],
        out_specs=vmem(),
        scratch_shapes=[
            pltpu.VMEM((tract + 1, part, side), f32),
            pltpu.VMEM((tract + 1, 8, side), f32),
        ],
        compiler_params=pltpu.CompilerParams(vmem_limit_bytes=16 * mib),
        name="combine",
    )(table, parts, var_sum, var_template)


def join_body(places, *refs, part, count):
    ins = refs[:count]
    out, held, sems = refs[-3:]
    copies = []
    for d, ref in enumerate(ins):
        held[d] = ref[...].astype(f32)
        row = pl.multiple_of(places[d] * part, part)
        copies.append(
            pltpu.make_async_copy(held.at[d], out.at[:, pl.ds(row, part), :], sems.at[d])
        )
        copies[-1].start()
    for copy in copies:
        copy.wait()


def join_parts(places, parts, whole, exps):
    tract, part, side = parts[0].shape
    count = len(parts)
    fresh = whole is None
    anywhere = pl.BlockSpec(memory_space=pl.ANY)
    return pl.pallas_call(
        functools.partial(join_body, part=part, count=count),
        out_shape=jax.ShapeDtypeStruct((tract, part * exps, side), f32),
        in_specs=[smem()] + [vmem()] * count + ([] if fresh else [anywhere]),
        out_specs=anywhere,
        scratch_shapes=[
            pltpu.VMEM((count, tract, part, side), f32),
            pltpu.SemaphoreType.DMA((count,)),
        ],
        input_output_aliases={} if fresh else {count + 1: 0},
        compiler_params=pltpu.CompilerParams(vmem_limit_bytes=16 * mib),
        cost_estimate=cost(0, 3_000_000 * count),
        name="join_parts",
    )(places, *parts, *([] if fresh else [whole]))


def local(
    template,
    template_var,
    science,
    science_var,
    routes_src,
    routes_blk,
    stamp_rows,
    stamp_cols,
    basis_col,
    basis_row,
    psf_col,
    psf_row,
):
    peers = lax.axis_size("det")
    exps = lax.axis_size("exp")
    me = lax.axis_index("exp").astype(jnp.int32)
    tract, side, _ = template.shape
    science_img = science[0]
    variance_img = science_var[0]
    blocks_dev = routes_src.shape[1]
    count, taps = basis_col.shape
    capacity = max(2, -(-blocks_dev // peers))
    slots = peers * capacity
    part = side // exps

    slot_of, sender, request = route_tables(routes_src, routes_blk, peers, capacity)
    asked = lax.all_to_all(request, "det", split_axis=0, concat_axis=0, tiled=True)
    picked = pick_blocks(asked, template, touch(template), slots, capacity)
    var_parts = prepare(sender, request, variance_img, picked, side, exps, capacity)
    arrived = lax.all_to_all(picked, "det", split_axis=0, concat_axis=0, tiled=True)

    padded_k = up(count + 2, 16)
    col_t = jnp.pad(basis_col.T, ((0, up(taps, 16) - taps), (0, padded_k - count)))
    col = jnp.pad(basis_col.astype(f32), ((0, padded_k - count), (0, side - taps)))
    row_rev = jnp.pad(
        basis_row.astype(f32)[:, ::-1], ((0, padded_k - count), (side - taps, 0))
    )
    row_rev = jnp.roll(row_rev, 1, axis=1)
    over_rev = jnp.roll(jnp.pad(psf_row[:, ::-1], ((0, 0), (2 * side - taps, 0))), 1, axis=1)
    down = jnp.pad(psf_col, ((0, 0), (0, 2 * side - taps)))
    var_late, arrived = lax.optimization_barrier((var_parts, arrived))
    var_back = lax.all_to_all(
        var_late, ("det", "exp"), split_axis=0, concat_axis=0, tiled=True
    )
    table = var_back[:, capacity * part, :capacity].astype(f32).astype(jnp.int32)

    high, wide = science_img.shape
    gram, frames = normal_matrix(
        slot_of,
        stamp_rows,
        stamp_cols,
        arrived,
        col,
        row_rev,
        science_img,
        variance_img,
        count,
        taps,
    )
    coef, payload = subtract(
        sender,
        gram,
        frames,
        science_img,
        col_t,
        row_rev,
        peers,
        exps,
        capacity,
        count,
        taps,
        stamp_rows.shape[1] * side * side,
    )
    diff_back = lax.all_to_all(payload, ("det", "exp"), split_axis=0, concat_axis=0, tiled=True)
    scored, var_sum = score(
        table,
        slot_of,
        payload,
        down,
        over_rev,
        var_back,
        high,
        wide,
        taps,
        tract,
        part,
        capacity,
    )
    var_template = lax.dynamic_slice_in_dim(template_var, me * part, part, 1)
    mine = combine(table, diff_back, var_sum, var_template, part, capacity)

    def swap(value, distance):
        return lax.ppermute(value, "exp", [(e, e ^ distance) for e in range(exps)])

    def put(parts, whole):
        places = jnp.stack([there for there, _ in parts])
        return join_parts(places, [held for _, held in parts], whole, exps)

    if exps == 4:
        far = swap(mine, 2)
        near = swap(mine, 1)
        last = swap(far, 1)
        whole = put([(me, mine), (me ^ 1, near), (me ^ 2, far)], None)
        significance = put([(me ^ 3, last)], whole)
    else:
        parts = [(me, mine)]
        for gap in range(1, exps):
            pairs = [(e, (e + gap) % exps) for e in range(exps)]
            parts.append(((me - gap) % exps, lax.ppermute(mine, "exp", pairs)))
        significance = put(parts, None)
    return (significance, scored[None], coef[:, : count + 1])


def solution(mesh):
    placed = (
        P("det", None, None),
        P("det", None, None),
        P("exp", "det", None),
        P("exp", "det", None),
        P("exp", "det"),
        P("exp", "det"),
        P("exp", "det"),
        P("exp", "det"),
        P(),
        P(),
        P("exp", None),
        P("exp", None),
    )
    return jax.shard_map(
        local,
        mesh=mesh,
        in_specs=placed,
        out_specs=(P("det", None, None), P("exp", "det", None), P("exp", "det")),
        check_vma=False,
    )
```

```python
import functools

import jax
import jax.numpy as jnp
from jax import lax
from jax.experimental import pallas as pl
from jax.experimental.pallas import tpu as pltpu
from jax.sharding import PartitionSpec as P

ridge_term = 0.01
bf16 = jnp.bfloat16
f32 = jnp.float32
vmem = functools.partial(pl.BlockSpec, memory_space=pltpu.VMEM)
smem = functools.partial(pl.BlockSpec, memory_space=pltpu.SMEM)
mib = 1024 * 1024
trailer_rows = 8


def up(value, step):
    return -(-value // step) * step


def cost(flops, moved):
    return pl.CostEstimate(flops=flops, bytes_accessed=moved, transcendentals=0)


def route_body(src, blk, slot_of, sender, request, count, *, peers, capacity):
    def clear_count(p, carry):
        count[p] = 0
        return carry

    def clear_slot(s, carry):
        sender[s] = 0
        request[s // capacity, 0, s % capacity] = 0
        return carry

    lax.fori_loop(0, peers, clear_count, 0, unroll=peers <= 16)
    lax.fori_loop(0, peers * capacity, clear_slot, 0, unroll=peers <= 16)
    for b in range(src.shape[1]):
        owner = src[0, b]
        place = count[owner]
        count[owner] = place + 1
        slot_of[b] = owner * capacity + place
        sender[owner * capacity + place] = b
        request[owner, 0, place] = blk[0, b] + 1


def route_tables(routes_src, routes_blk, peers, capacity):
    return pl.pallas_call(
        functools.partial(route_body, peers=peers, capacity=capacity),
        out_shape=(
            jax.ShapeDtypeStruct((routes_src.shape[1],), jnp.int32),
            jax.ShapeDtypeStruct((peers * capacity,), jnp.int32),
            jax.ShapeDtypeStruct((peers, 1, capacity), jnp.int32),
        ),
        in_specs=[smem()] * 2,
        out_specs=(smem(),) * 3,
        scratch_shapes=[pltpu.SMEM((peers,), jnp.int32)],
        name="route_tables",
    )(routes_src, routes_blk)


def fetch_body(template, near, sem):
    copy = pltpu.make_async_copy(template, near, sem)
    copy.start()
    copy.wait()


def fetch(template):
    return pl.pallas_call(
        fetch_body,
        out_shape=jax.ShapeDtypeStruct(template.shape, template.dtype),
        in_specs=[pl.BlockSpec(memory_space=pl.ANY)],
        out_specs=vmem(),
        scratch_shapes=[pltpu.SemaphoreType.DMA(())],
        compiler_params=pltpu.CompilerParams(vmem_limit_bytes=16 * mib),
        cost_estimate=cost(0, 4_000_000),
        name="fetch",
    )(template)


def pick_body(asked, template, out, *, capacity):
    def one(s, carry):
        block = jnp.maximum(asked[s // capacity, 0, s % capacity] - 1, 0)
        out[s] = template[block]
        return carry

    lax.fori_loop(0, out.shape[0], one, 0, unroll=True if out.shape[0] <= 32 else 4)


def pick_blocks(asked, template, slots, capacity):
    return pl.pallas_call(
        functools.partial(pick_body, capacity=capacity),
        out_shape=jax.ShapeDtypeStruct((slots,) + template.shape[1:], template.dtype),
        in_specs=[smem(), vmem()],
        out_specs=vmem(),
        compiler_params=pltpu.CompilerParams(vmem_limit_bytes=16 * mib),
        name="pick_blocks",
    )(asked, template)


def store_parts(sender, image, out, side, exps, capacity, across_blocks):
    part = side // exps
    slots = sender.shape[0]

    def one(s, carry):
        b = sender[s]
        top = pl.multiple_of((b // across_blocks) * side, side)
        left = pl.multiple_of((b % across_blocks) * side, side)
        block = image[pl.ds(top, side), pl.ds(left, side)].astype(bf16)
        row = pl.multiple_of((s % capacity) * part, part)
        for q in range(exps):
            out[(s // capacity) * exps + q, pl.ds(row, part), :] = block[q * part : (q + 1) * part]
        return carry

    lax.fori_loop(0, slots, one, 0, unroll=True if slots <= 32 else 4)


def store_requests(request, out, side, exps, capacity):
    lane = lax.broadcasted_iota(jnp.int32, (trailer_rows, side), 1)

    def put(p, carry):
        line = jnp.zeros((trailer_rows, side), f32)
        for c in range(capacity):
            line = jnp.where(lane == c, request[p, 0, c].astype(f32), line)
        for q in range(exps):
            out[p * exps + q, out.shape[1] - trailer_rows :, :] = line.astype(bf16)
        return carry

    lax.fori_loop(0, request.shape[0], put, 0)


def cut(ref, top, left, height, side):
    down = pl.multiple_of((top // 8) * 8, 8)
    over = pl.multiple_of((left // side) * side, side)
    tile = ref[pl.ds(down, height), pl.ds(over, 3 * side)]
    tile = pltpu.roll(tile, lax.rem(3 * side - (left - over), 3 * side), 1)[:, : 2 * side]
    return pltpu.roll(tile, lax.rem(height - (top - down), height), 0)


def prepare_body(sender, request, variance, earlier, out, *, side, exps, capacity):
    del earlier
    store_parts(sender, variance, out, side, exps, capacity, variance.shape[1] // side)
    store_requests(request, out, side, exps, capacity)


def prepare(sender, request, variance, earlier, side, exps, capacity):
    rows = capacity * (side // exps) + trailer_rows
    return pl.pallas_call(
        functools.partial(prepare_body, side=side, exps=exps, capacity=capacity),
        out_shape=jax.ShapeDtypeStruct((request.shape[0] * exps, rows, side), bf16),
        in_specs=[smem()] * 2 + [vmem(), pl.BlockSpec(memory_space=pl.ANY)],
        out_specs=vmem(),
        compiler_params=pltpu.CompilerParams(vmem_limit_bytes=16 * mib),
        cost_estimate=cost(0, 6_000_000),
        name="prepare",
    )(sender, request, variance, earlier)


def normal_body(
    slot_of,
    rows_at,
    cols_at,
    arrived,
    col,
    row_rev,
    science,
    variance,
    gram_out,
    windows,
    frame,
    cuts,
    across,
    design,
    roots,
    window,
    *,
    count,
    across_blocks,
    taps,
):
    side = row_rev.shape[1]
    margin = taps // 2
    stamps = rows_at.shape[1]
    span = up(side + taps - 1, 16)
    padded_k = gram_out.shape[1]
    pitch = padded_k + 1
    lines_all = stamps * side
    sub = lax.broadcasted_iota(jnp.int32, (side, side), 0)
    lane = lax.broadcasted_iota(jnp.int32, (side, side), 1)

    high, wide = science.shape
    rows_off = up(margin, 8)
    frame[:rows_off, :] = jnp.zeros((rows_off, frame.shape[1]), f32)
    below = rows_off + high
    frame[below:, :] = jnp.zeros((frame.shape[0] - below, frame.shape[1]), f32)
    frame[rows_off:below, :side] = jnp.zeros((high, side), f32)
    after = side + wide
    frame[rows_off:below, after:] = jnp.zeros((high, frame.shape[1] - after), f32)
    for b in range(slot_of.shape[0]):
        top = rows_off + (b // across_blocks) * side
        left = side + (b % across_blocks) * side
        frame[top : top + side, left : left + side] = arrived[slot_of[b]].astype(f32)
    first_row = rows_off - margin
    first_col = side - margin

    def cut_image(ref, top, left):
        tall = min(high, side + 16)
        down = pl.multiple_of(jnp.minimum((top // 16) * 16, high - tall), 16)
        over = pl.multiple_of(jnp.minimum((left // side) * side, wide - 2 * side), side)
        tile = ref[pl.ds(down, tall), pl.ds(over, 2 * side)].astype(f32)
        tile = pltpu.roll(tile, lax.rem(2 * side - (left - over), 2 * side), 1)[:, :side]
        return pltpu.roll(tile, lax.rem(tall - (top - down), tall), 0)[:side]

    for s in range(stamps):
        top = rows_at[0, s]
        left = cols_at[0, s]
        tile = cut(frame, top + first_row, left + first_col, span, side)
        cuts[s * span : (s + 1) * span, :] = tile.astype(bf16)
        root = lax.rsqrt(cut_image(variance, top, left))
        roots[s * side : (s + 1) * side, :] = root
        place = pl.ds(s * side * pitch + count, side, stride=pitch)
        design[place, :] = root
        place = pl.ds(s * side * pitch + count + 1, side, stride=pitch)
        design[place, :] = root * cut_image(science, top, left)
    for extra in range(count + 2, padded_k):
        design[pl.ds(extra, lines_all, stride=pitch), :] = jnp.zeros((lines_all, side), f32)

    group = across.shape[1] // side
    step = side - taps + 1
    starts = list(range(0, count, group))
    for turn, k in enumerate(starts):
        for c in range(turn, windows.shape[0], len(starts)):
            left = first_col + c * step
            window[...] = frame[first_row : first_row + window.shape[0], left : left + side]
            for parity in range(2):
                place = pl.ds(parity, windows.shape[2], stride=2)
                windows[c, parity] = window[place, :]
        bands = []
        for a in range(group):
            line = jnp.broadcast_to(row_rev[k + a : k + a + 1, :], (side, side))
            line = pltpu.roll(line, 0, 1, stride=1, stride_axis=0)
            first = jnp.where(lane <= sub, line, 0.0).astype(bf16)
            second = jnp.where(lane > sub, line, 0.0).astype(bf16)
            bands.append(jnp.concatenate([first, second], axis=0))
        out = jnp.dot(cuts[...], jnp.concatenate(bands, axis=1), preferred_element_type=f32)
        across[...] = out.astype(bf16)
        for a in range(group):
            line = jnp.broadcast_to(col[k + a : k + a + 1, :], (side, side))
            line = pltpu.roll(line, 0, 1, stride=1, stride_axis=0)
            first = jnp.where(lane >= sub, line, 0.0).astype(bf16)
            second = jnp.where(lane < sub, line, 0.0).astype(bf16)
            band = jnp.concatenate([first, second[:, : span - side]], axis=1)
            for s in range(0, stamps, 2):
                members = range(s, min(s + 2, stamps))
                data = [
                    across[m * span : (m + 1) * span, a * side : (a + 1) * side] for m in members
                ]
                out = jnp.dot(band, jnp.concatenate(data, axis=1), preferred_element_type=f32)
                for h, m in enumerate(members):
                    place = pl.ds(m * side * pitch + k + a, side, stride=pitch)
                    design[place, :] = (
                        out[:, h * side : (h + 1) * side] * roots[m * side : (m + 1) * side, :]
                    )

    lines = 16
    sets = 4

    def gram_step(step, total):
        start = pl.multiple_of(step * sets * lines * pitch, 8)
        rows = []
        for g in range(sets):
            row = [
                design[pl.ds(start + (g * lines + j) * pitch, padded_k), :].astype(bf16)
                for j in range(lines)
            ]
            rows.append(jnp.concatenate(row, axis=1))
        both = jnp.concatenate(rows, axis=0)
        return total + lax.dot_general(
            both, both, (((1,), (1,)), ((), ())), preferred_element_type=f32
        )

    total = lax.fori_loop(
        0,
        lines_all // (lines * sets),
        gram_step,
        jnp.zeros((sets * padded_k, sets * padded_k), f32),
    )
    part = jnp.zeros((padded_k, padded_k), f32)
    for g in range(sets):
        rows = slice(g * padded_k, (g + 1) * padded_k)
        part = part + total[rows, rows]
    gram_out[...] = part


def normal_matrix(
    slot_of, rows_at, cols_at, arrived, col, row_rev, science, variance, count, taps
):
    high, wide = science.shape
    side = row_rev.shape[1]
    stamps = rows_at.shape[1]
    padded_k = up(count + 2, 16)
    pairs = (taps + 2) // 2
    span = up(side + taps - 1, 16)
    half = up(high // 2 + pairs, 8)
    tall = up(taps // 2, 8) + max(high - side + span, 2 * half)
    wins = -(-wide // (side - taps + 1))
    group = 2 if count % 2 == 0 else 1
    return pl.pallas_call(
        functools.partial(normal_body, count=count, across_blocks=wide // side, taps=taps),
        out_shape=(
            jax.ShapeDtypeStruct((padded_k, padded_k), f32),
            jax.ShapeDtypeStruct((wins, 2, half, side), f32),
        ),
        in_specs=[smem()] * 3 + [vmem()] * 5,
        out_specs=(vmem(),) * 2,
        scratch_shapes=[
            pltpu.VMEM((tall, wide + 2 * side), f32),
            pltpu.VMEM((stamps * span, 2 * side), bf16),
            pltpu.VMEM((stamps * span, group * side), bf16),
            pltpu.VMEM((stamps * side * (padded_k + 1), side), f32),
            pltpu.VMEM((stamps * side, side), f32),
            pltpu.VMEM((2 * half, side), f32),
        ],
        compiler_params=pltpu.CompilerParams(vmem_limit_bytes=28 * mib),
        cost_estimate=cost(10_000_000_000, 8_000_000),
        name="normal_matrix",
    )(slot_of, rows_at, cols_at, arrived, col, row_rev, science, variance)


def subtract_body(
    sender,
    gram,
    frames,
    science,
    col_t,
    row_rev,
    coef_out,
    payload,
    window,
    image,
    bands,
    total,
    stacked,
    *,
    exps,
    capacity,
    count,
    taps,
    pixels,
):
    side = frames.shape[3]
    high, wide = science.shape
    padded_k = gram.shape[1]
    part = side // exps
    size = count + 1

    system = jnp.concatenate(
        [gram[...], jnp.zeros((padded_k, side - padded_k), f32)], axis=1
    ) / pixels
    sub = lax.broadcasted_iota(jnp.int32, (padded_k, side), 0)
    lane = lax.broadcasted_iota(jnp.int32, (padded_k, side), 1)
    system = jnp.where((sub < size) & (lane <= size), system, 0.0)
    system = system + jnp.where((sub == lane) & (sub < size), ridge_term, 0.0)

    pairs = (taps + 2) // 2
    rows_half = high // 2
    wins = frames.shape[0]

    def stack_rows(q):
        for c in range(wins):
            for a in range(2):
                stacked[q, c * rows_half : (c + 1) * rows_half, a * side : (a + 1) * side] = (
                    frames[c, a, q : q + rows_half, :].astype(bf16)
                )

    starts = list(range(0, size, 4))
    for step, k in enumerate(starts):
        for q in range(step, pairs, len(starts)):
            stack_rows(q)
        block = range(min(4, size - k))
        cols = [jnp.broadcast_to(system[:, k + j : k + j + 1], system.shape) for j in block]
        rows = [system[k + j : k + j + 1, :] for j in block]
        core = [[cols[j][k + i : k + i + 1, :] for j in block] for i in block]
        for j in block:
            inverse = 1.0 / core[j][j]
            factor = jnp.where(sub == k + j, 0.0, cols[j] * inverse)
            system = system - factor * rows[j]
            for i in block[j + 1 :]:
                scale = core[i][j] * inverse
                rows[i] = rows[i] - scale * rows[j]
                for l in block[j + 1 :]:
                    core[i][l] = core[i][l] - scale * core[j][l]
                cols[i] = cols[i] - factor * core[j][i]
    pivot = jnp.sum(jnp.where(sub == lane, system, 0.0), axis=1, keepdims=True)
    solved = system[:, size : size + 1] / jnp.where(sub[:, :1] < size, pivot, 1.0)
    coef_out[...] = jnp.sum(jnp.where(sub == lane, solved, 0.0), axis=0, keepdims=True)
    background = solved[count : count + 1, :]
    basis_coef = jnp.where(sub[:, :1] < count, solved, 0.0)

    scaled = basis_coef * row_rev[...]
    kernel = jnp.zeros((col_t.shape[0], side), f32)
    for _ in range(3):
        piece = scaled.astype(bf16)
        scaled = scaled - piece.astype(f32)
        kernel = kernel + jnp.dot(col_t[...], piece, preferred_element_type=f32)
    kernel_sum = jnp.sum(jnp.sum(kernel, axis=1, keepdims=True), axis=0, keepdims=True)
    rounded = kernel.astype(bf16).astype(f32)

    zero_band = jnp.zeros((side, side), bf16)

    def band(i):
        if i < 0 or i >= taps:
            return zero_band
        line = jnp.broadcast_to(rounded[i : i + 1, :], (side, side))
        return pltpu.roll(line, 0, 1, stride=1, stride_axis=0).astype(bf16)

    made = {i: band(i) for i in range(-1, 2 * pairs)}
    for q in range(pairs):
        for a in range(2):
            for b in range(2):
                bands[
                    q * 2 * side + a * side : q * 2 * side + (a + 1) * side,
                    b * side : (b + 1) * side,
                ] = made[2 * q + a - b]

    step = side - taps + 1
    for q in range(pairs):
        out = jnp.dot(
            stacked[q], bands[q * 2 * side : (q + 1) * 2 * side, :], preferred_element_type=f32
        )
        if q:
            out = out + total[...]
        if q < pairs - 1:
            total[...] = out
    for c in range(wins):
        rows = out[c * rows_half : (c + 1) * rows_half]
        window[c, pl.ds(0, rows_half, stride=2), :] = rows[:, :side]
        window[c, pl.ds(1, rows_half, stride=2), :] = rows[:, side:]
        keep = min(step, wide - c * step)
        image[:, c * step : c * step + keep] = window[c, :, :keep]
    image[...] = science[...].astype(f32) - image[...] - background

    store_parts(sender, image, payload, side, exps, capacity, wide // side)
    line_at = lax.broadcasted_iota(jnp.int32, (trailer_rows, side), 0)
    trailer = jnp.zeros((trailer_rows, side), f32)
    rest = kernel_sum
    for p in range(3):
        piece = rest.astype(bf16).astype(f32)
        rest = rest - piece
        trailer = jnp.where(line_at == p, piece, trailer)
    trailer = trailer.astype(bf16)

    def put(d, carry):
        payload[d, capacity * part :, :] = trailer
        return carry

    lax.fori_loop(0, payload.shape[0], put, 0, unroll=4)


def subtract(
    sender, gram, frames, science, col_t, row_rev, peers, exps, capacity, count, taps, pixels
):
    wins, _, _, side = frames.shape
    high, wide = science.shape
    part = side // exps
    pairs = (taps + 2) // 2
    body = functools.partial(
        subtract_body, exps=exps, capacity=capacity, count=count, taps=taps, pixels=pixels
    )
    return pl.pallas_call(
        body,
        out_shape=(
            jax.ShapeDtypeStruct((1, side), f32),
            jax.ShapeDtypeStruct(
                (peers * exps, capacity * part + trailer_rows, side), bf16
            ),
        ),
        in_specs=[smem()] + [vmem()] * 5,
        out_specs=(vmem(), vmem()),
        scratch_shapes=[
            pltpu.VMEM((wins, high, side), f32),
            pltpu.VMEM((high, wide), f32),
            pltpu.VMEM((pairs * 2 * side, 2 * side), bf16),
            pltpu.VMEM((wins * high // 2, 2 * side), f32),
            pltpu.VMEM((pairs, wins * high // 2, 2 * side), bf16),
        ],
        compiler_params=pltpu.CompilerParams(vmem_limit_bytes=24 * mib),
        cost_estimate=cost(5_000_000_000, 4_000_000),
        name="subtract",
    )(sender, gram, frames, science, col_t, row_rev)


def split2(value):
    top = value.astype(bf16)
    return top, (value - top.astype(f32)).astype(bf16)


def score_body(
    table,
    slot_of,
    payload,
    down,
    over,
    parts,
    out,
    var_out,
    padded,
    sideways,
    var_total,
    *,
    side,
    taps,
    part,
    capacity,
):
    add_variance(table, parts, var_out, var_total, part, capacity)
    high, wide = out.shape
    margin = taps // 2
    span = up(side + taps - 1, 16)
    across_blocks = wide // side
    exps = side // part
    padded[...] = jnp.zeros(padded.shape, f32)
    for b in range(slot_of.shape[0]):
        slot = slot_of[b]
        row = pl.multiple_of((slot % capacity) * part, part)
        left = margin + (b % across_blocks) * side
        for q in range(exps):
            top = (b // across_blocks) * side + q * part
            block = payload[(slot // capacity) * exps + q, pl.ds(row, part), :]
            padded[top : top + part, left : left + side] = block.astype(f32)
    line = jnp.broadcast_to(over[...], (2 * side, 2 * side))
    band = pltpu.roll(line, 0, 1, stride=1, stride_axis=0)[:, :side]
    both = jnp.concatenate(split2(band), axis=1)
    sideways[...] = jnp.zeros(sideways.shape, f32)
    for c in range(wide // side):
        window = padded[:, c * side : (c + 2) * side].astype(bf16)
        got = jnp.dot(window, both, preferred_element_type=f32)
        sideways[margin : margin + high, c * side : (c + 1) * side] = got[:, :side] + got[:, side:]
    line = jnp.broadcast_to(down[...], (side, 2 * side))
    band = pltpu.roll(line, 0, 1, stride=1, stride_axis=0)[:, :span]
    top, low = split2(band)
    for r in range(high // side):
        data_top, data_low = split2(sideways[r * side : r * side + span, :])
        got = jnp.dot(top, data_top, preferred_element_type=f32)
        got = got + jnp.dot(top, data_low, preferred_element_type=f32)
        got = got + jnp.dot(low, data_top, preferred_element_type=f32)
        out[r * side : (r + 1) * side, :] = got


def score(
    table, slot_of, payload, down, over_rev, parts, high, wide, taps, tract, part, capacity
):
    side = payload.shape[2]
    span = up(side + taps - 1, 16)
    return pl.pallas_call(
        functools.partial(score_body, side=side, taps=taps, part=part, capacity=capacity),
        out_shape=(
            jax.ShapeDtypeStruct((high, wide), f32),
            jax.ShapeDtypeStruct((tract, part, side), f32),
        ),
        in_specs=[smem()] * 2 + [vmem()] * 4,
        out_specs=(vmem(),) * 2,
        scratch_shapes=[
            pltpu.VMEM((high, wide + side), f32),
            pltpu.VMEM((high - side + span, wide), f32),
            pltpu.VMEM((tract + 1, part, side), f32),
        ],
        compiler_params=pltpu.CompilerParams(vmem_limit_bytes=24 * mib),
        cost_estimate=cost(2_000_000_000, 2_000_000),
        name="score",
    )(table, slot_of, payload, down, over_rev, parts)


def add_variance(table, parts, out, total, part, capacity):
    total[...] = jnp.zeros(total.shape, f32)
    tract = out.shape[0]

    def one(j, carry):
        block = table[j // capacity, j % capacity] - 1
        block = jnp.where(block < 0, tract, block)
        row = pl.multiple_of((j % capacity) * part, part)
        total[block] += parts[j // capacity, pl.ds(row, part), :].astype(f32)
        return carry

    lax.fori_loop(0, parts.shape[0] * capacity, one, 0, unroll=8)
    out[...] = total[:tract]


def combine_body(table, parts, var_sum, var_template, out, total, gain, *, part, capacity):
    total[...] = jnp.zeros(total.shape, f32)
    gain[...] = jnp.zeros(gain.shape, f32)
    tract = out.shape[0]

    def one(d, carry):
        tail = parts[d, capacity * part :, :].astype(f32)
        kernel_sum = tail[0:1] + tail[1:2] + tail[2:3]
        square = jnp.broadcast_to(kernel_sum * kernel_sum, gain.shape[1:])
        for c in range(capacity):
            block = table[d, c] - 1
            block = jnp.where(block < 0, tract, block)
            total[block] += parts[d, c * part : (c + 1) * part, :].astype(f32)
            gain[block] += square
        return carry

    lax.fori_loop(0, parts.shape[0], one, 0, unroll=4)
    for t in range(tract):
        variance = var_sum[t] + gain[t, 0:1, :] * var_template[t].astype(f32)
        out[t] = (total[t] * lax.rsqrt(jnp.maximum(variance, 1.0))).astype(bf16)


def combine(table, parts, var_sum, var_template, part, capacity):
    tract, _, side = var_sum.shape
    return pl.pallas_call(
        functools.partial(combine_body, part=part, capacity=capacity),
        out_shape=jax.ShapeDtypeStruct((tract, part, side), bf16),
        in_specs=[smem(), vmem(), vmem(), vmem()],
        out_specs=vmem(),
        scratch_shapes=[
            pltpu.VMEM((tract + 1, part, side), f32),
            pltpu.VMEM((tract + 1, 8, side), f32),
        ],
        compiler_params=pltpu.CompilerParams(vmem_limit_bytes=16 * mib),
        name="combine",
    )(table, parts, var_sum, var_template)


def join_body(places, *refs, part, count):
    ins = refs[:count]
    out, held, sems = refs[-3:]
    copies = []
    for d, ref in enumerate(ins):
        held[d] = ref[...].astype(f32)
        row = pl.multiple_of(places[d] * part, part)
        copies.append(
            pltpu.make_async_copy(held.at[d], out.at[:, pl.ds(row, part), :], sems.at[d])
        )
        copies[-1].start()
    for copy in copies:
        copy.wait()


def join_parts(places, parts, whole, exps):
    tract, part, side = parts[0].shape
    count = len(parts)
    fresh = whole is None
    anywhere = pl.BlockSpec(memory_space=pl.ANY)
    return pl.pallas_call(
        functools.partial(join_body, part=part, count=count),
        out_shape=jax.ShapeDtypeStruct((tract, part * exps, side), f32),
        in_specs=[smem()] + [vmem()] * count + ([] if fresh else [anywhere]),
        out_specs=anywhere,
        scratch_shapes=[
            pltpu.VMEM((count, tract, part, side), f32),
            pltpu.SemaphoreType.DMA((count,)),
        ],
        input_output_aliases={} if fresh else {count + 1: 0},
        compiler_params=pltpu.CompilerParams(vmem_limit_bytes=16 * mib),
        cost_estimate=cost(0, 3_000_000 * count),
        name="join_parts",
    )(places, *parts, *([] if fresh else [whole]))


def local(
    template,
    template_var,
    science,
    science_var,
    routes_src,
    routes_blk,
    stamp_rows,
    stamp_cols,
    basis_col,
    basis_row,
    psf_col,
    psf_row,
):
    peers = lax.axis_size("det")
    exps = lax.axis_size("exp")
    me = lax.axis_index("exp").astype(jnp.int32)
    tract, side, _ = template.shape
    science_img = science[0]
    variance_img = science_var[0]
    blocks_dev = routes_src.shape[1]
    count, taps = basis_col.shape
    capacity = max(2, -(-blocks_dev // peers))
    slots = peers * capacity
    part = side // exps

    slot_of, sender, request = route_tables(routes_src, routes_blk, peers, capacity)
    asked = lax.all_to_all(request, "det", split_axis=0, concat_axis=0, tiled=True)
    picked = pick_blocks(asked, fetch(template), slots, capacity)
    var_parts = prepare(sender, request, variance_img, picked, side, exps, capacity)
    arrived = lax.all_to_all(picked, "det", split_axis=0, concat_axis=0, tiled=True)

    padded_k = up(count + 2, 16)
    col_t = jnp.pad(basis_col.T, ((0, up(taps, 16) - taps), (0, padded_k - count)))
    col = jnp.pad(basis_col.astype(f32), ((0, padded_k - count), (0, side - taps)))
    row_rev = jnp.pad(
        basis_row.astype(f32)[:, ::-1], ((0, padded_k - count), (side - taps, 0))
    )
    row_rev = jnp.roll(row_rev, 1, axis=1)
    over_rev = jnp.roll(jnp.pad(psf_row[:, ::-1], ((0, 0), (2 * side - taps, 0))), 1, axis=1)
    down = jnp.pad(psf_col, ((0, 0), (0, 2 * side - taps)))
    var_late, arrived = lax.optimization_barrier((var_parts, arrived))
    var_back = lax.all_to_all(
        var_late, ("det", "exp"), split_axis=0, concat_axis=0, tiled=True
    )
    table = var_back[:, capacity * part, :capacity].astype(f32).astype(jnp.int32)

    high, wide = science_img.shape
    gram, frames = normal_matrix(
        slot_of,
        stamp_rows,
        stamp_cols,
        arrived,
        col,
        row_rev,
        science_img,
        variance_img,
        count,
        taps,
    )
    coef, payload = subtract(
        sender,
        gram,
        frames,
        science_img,
        col_t,
        row_rev,
        peers,
        exps,
        capacity,
        count,
        taps,
        stamp_rows.shape[1] * side * side,
    )
    diff_back = lax.all_to_all(payload, ("det", "exp"), split_axis=0, concat_axis=0, tiled=True)
    scored, var_sum = score(
        table,
        slot_of,
        payload,
        down,
        over_rev,
        var_back,
        high,
        wide,
        taps,
        tract,
        part,
        capacity,
    )
    var_template = lax.dynamic_slice_in_dim(template_var, me * part, part, 1)
    mine = combine(table, diff_back, var_sum, var_template, part, capacity)

    def swap(value, distance):
        return lax.ppermute(value, "exp", [(e, e ^ distance) for e in range(exps)])

    def put(parts, whole):
        places = jnp.stack([there for there, _ in parts])
        return join_parts(places, [held for _, held in parts], whole, exps)

    if exps == 4:
        far = swap(mine, 2)
        near = swap(mine, 1)
        last = swap(far, 1)
        whole = put([(me, mine), (me ^ 1, near), (me ^ 2, far)], None)
        significance = put([(me ^ 3, last)], whole)
    else:
        parts = [(me, mine)]
        for gap in range(1, exps):
            pairs = [(e, (e + gap) % exps) for e in range(exps)]
            parts.append(((me - gap) % exps, lax.ppermute(mine, "exp", pairs)))
        significance = put(parts, None)
    return (significance, scored[None], coef[:, : count + 1])


def solution(mesh):
    placed = (
        P("det", None, None),
        P("det", None, None),
        P("exp", "det", None),
        P("exp", "det", None),
        P("exp", "det"),
        P("exp", "det"),
        P("exp", "det"),
        P("exp", "det"),
        P(),
        P(),
        P("exp", None),
        P("exp", None),
    )
    return jax.shard_map(
        local,
        mesh=mesh,
        in_specs=placed,
        out_specs=(P("det", None, None), P("exp", "det", None), P("exp", "det")),
        check_vma=False,
    )
```

```python
import functools

import jax
import jax.numpy as jnp
from jax import lax
from jax.experimental import pallas as pl
from jax.experimental.pallas import tpu as pltpu
from jax.sharding import PartitionSpec as P

ridge_term = 0.01
bf16 = jnp.bfloat16
f32 = jnp.float32
vmem = functools.partial(pl.BlockSpec, memory_space=pltpu.VMEM)
smem = functools.partial(pl.BlockSpec, memory_space=pltpu.SMEM)
mib = 1024 * 1024
trailer_rows = 8


def up(value, step):
    return -(-value // step) * step


def cost(flops, moved):
    return pl.CostEstimate(flops=flops, bytes_accessed=moved, transcendentals=0)


def route_body(src, blk, slot_of, sender, request, count, *, peers, capacity):
    def clear_count(p, carry):
        count[p] = 0
        return carry

    def clear_slot(s, carry):
        sender[s] = 0
        request[s // capacity, 0, s % capacity] = 0
        return carry

    lax.fori_loop(0, peers, clear_count, 0, unroll=peers <= 16)
    lax.fori_loop(0, peers * capacity, clear_slot, 0, unroll=peers <= 16)
    for b in range(src.shape[1]):
        owner = src[0, b]
        place = count[owner]
        count[owner] = place + 1
        slot_of[b] = owner * capacity + place
        sender[owner * capacity + place] = b
        request[owner, 0, place] = blk[0, b] + 1


def route_tables(routes_src, routes_blk, peers, capacity):
    return pl.pallas_call(
        functools.partial(route_body, peers=peers, capacity=capacity),
        out_shape=(
            jax.ShapeDtypeStruct((routes_src.shape[1],), jnp.int32),
            jax.ShapeDtypeStruct((peers * capacity,), jnp.int32),
            jax.ShapeDtypeStruct((peers, 1, capacity), jnp.int32),
        ),
        in_specs=[smem()] * 2,
        out_specs=(smem(),) * 3,
        scratch_shapes=[pltpu.SMEM((peers,), jnp.int32)],
        name="route_tables",
    )(routes_src, routes_blk)


def fetch_body(template, near, sem):
    copy = pltpu.make_async_copy(template, near, sem)
    copy.start()
    copy.wait()


def fetch(template):
    return pl.pallas_call(
        fetch_body,
        out_shape=jax.ShapeDtypeStruct(template.shape, template.dtype),
        in_specs=[pl.BlockSpec(memory_space=pl.ANY)],
        out_specs=vmem(),
        scratch_shapes=[pltpu.SemaphoreType.DMA(())],
        compiler_params=pltpu.CompilerParams(vmem_limit_bytes=16 * mib),
        cost_estimate=cost(0, 4_000_000),
        name="fetch",
    )(template)


def pick_body(asked, template, out, *, capacity):
    def one(s, carry):
        block = jnp.maximum(asked[s // capacity, 0, s % capacity] - 1, 0)
        out[s] = template[block]
        return carry

    lax.fori_loop(0, out.shape[0], one, 0, unroll=True if out.shape[0] <= 32 else 4)


def pick_blocks(asked, template, slots, capacity):
    return pl.pallas_call(
        functools.partial(pick_body, capacity=capacity),
        out_shape=jax.ShapeDtypeStruct((slots,) + template.shape[1:], template.dtype),
        in_specs=[smem(), vmem()],
        out_specs=vmem(),
        compiler_params=pltpu.CompilerParams(vmem_limit_bytes=16 * mib),
        name="pick_blocks",
    )(asked, template)


def store_parts(sender, image, out, side, exps, capacity, across_blocks):
    part = side // exps
    slots = sender.shape[0]

    def one(s, carry):
        b = sender[s]
        top = pl.multiple_of((b // across_blocks) * side, side)
        left = pl.multiple_of((b % across_blocks) * side, side)
        block = image[pl.ds(top, side), pl.ds(left, side)].astype(bf16)
        row = pl.multiple_of((s % capacity) * part, part)
        for q in range(exps):
            out[(s // capacity) * exps + q, pl.ds(row, part), :] = block[q * part : (q + 1) * part]
        return carry

    lax.fori_loop(0, slots, one, 0, unroll=True if slots <= 32 else 4)


def store_requests(request, out, side, exps, capacity):
    lane = lax.broadcasted_iota(jnp.int32, (trailer_rows, side), 1)

    def put(p, carry):
        line = jnp.zeros((trailer_rows, side), f32)
        for c in range(capacity):
            line = jnp.where(lane == c, request[p, 0, c].astype(f32), line)
        for q in range(exps):
            out[p * exps + q, out.shape[1] - trailer_rows :, :] = line.astype(bf16)
        return carry

    lax.fori_loop(0, request.shape[0], put, 0)


def cut(ref, top, left, height, side):
    down = pl.multiple_of((top // 8) * 8, 8)
    over = pl.multiple_of((left // side) * side, side)
    tile = ref[pl.ds(down, height), pl.ds(over, 3 * side)]
    tile = pltpu.roll(tile, lax.rem(3 * side - (left - over), 3 * side), 1)[:, : 2 * side]
    return pltpu.roll(tile, lax.rem(height - (top - down), height), 0)


def prepare_body(sender, request, variance, science, earlier, out, *, side, exps, capacity):
    del earlier, science
    store_parts(sender, variance, out, side, exps, capacity, variance.shape[1] // side)
    store_requests(request, out, side, exps, capacity)


def prepare(sender, request, variance, science, earlier, side, exps, capacity):
    rows = capacity * (side // exps) + trailer_rows
    return pl.pallas_call(
        functools.partial(prepare_body, side=side, exps=exps, capacity=capacity),
        out_shape=jax.ShapeDtypeStruct((request.shape[0] * exps, rows, side), bf16),
        in_specs=[smem()] * 2 + [vmem(), vmem(), pl.BlockSpec(memory_space=pl.ANY)],
        out_specs=vmem(),
        compiler_params=pltpu.CompilerParams(vmem_limit_bytes=16 * mib),
        cost_estimate=cost(0, 6_000_000),
        name="prepare",
    )(sender, request, variance, science, earlier)


def normal_body(
    slot_of,
    rows_at,
    cols_at,
    arrived,
    col,
    row_rev,
    science,
    variance,
    gram_out,
    windows,
    frame,
    cuts,
    vert,
    design,
    roots,
    window,
    *,
    count,
    across_blocks,
    taps,
):
    side = row_rev.shape[1]
    margin = taps // 2
    stamps = rows_at.shape[1]
    span = up(side + taps - 1, 16)
    padded_k = gram_out.shape[1]
    pitch = padded_k + 1
    lines_all = stamps * side
    sub = lax.broadcasted_iota(jnp.int32, (side, side), 0)
    lane = lax.broadcasted_iota(jnp.int32, (side, side), 1)

    high, wide = science.shape
    rows_off = up(margin, 8)
    frame[:rows_off, :] = jnp.zeros((rows_off, frame.shape[1]), f32)
    below = rows_off + high
    frame[below:, :] = jnp.zeros((frame.shape[0] - below, frame.shape[1]), f32)
    frame[rows_off:below, :side] = jnp.zeros((high, side), f32)
    after = side + wide
    frame[rows_off:below, after:] = jnp.zeros((high, frame.shape[1] - after), f32)
    for b in range(slot_of.shape[0]):
        top = rows_off + (b // across_blocks) * side
        left = side + (b % across_blocks) * side
        frame[top : top + side, left : left + side] = arrived[slot_of[b]].astype(f32)
    first_row = rows_off - margin
    first_col = side - margin

    def cut_image(ref, top, left):
        tall = min(high, side + 16)
        down = pl.multiple_of(jnp.minimum((top // 16) * 16, high - tall), 16)
        over = pl.multiple_of(jnp.minimum((left // side) * side, wide - 2 * side), side)
        tile = ref[pl.ds(down, tall), pl.ds(over, 2 * side)].astype(f32)
        tile = pltpu.roll(tile, lax.rem(2 * side - (left - over), 2 * side), 1)[:, :side]
        return pltpu.roll(tile, lax.rem(tall - (top - down), tall), 0)[:side]

    for s in range(stamps):
        top = rows_at[0, s]
        left = cols_at[0, s]
        tile = cut(frame, top + first_row, left + first_col, span, side)
        cuts[s * span : (s + 1) * span, :] = tile.astype(bf16)
        root = lax.rsqrt(cut_image(variance, top, left))
        roots[s * side : (s + 1) * side, :] = root
        place = pl.ds(s * side * pitch + count, side, stride=pitch)
        design[place, :] = root
        place = pl.ds(s * side * pitch + count + 1, side, stride=pitch)
        design[place, :] = root * cut_image(science, top, left)
    for extra in range(count + 2, padded_k):
        design[pl.ds(extra, lines_all, stride=pitch), :] = jnp.zeros((lines_all, side), f32)

    group = vert.shape[0]
    step = side - taps + 1
    starts = list(range(0, count, group))
    for turn, k in enumerate(starts):
        for c in range(turn, windows.shape[0], len(starts)):
            left = first_col + c * step
            window[...] = frame[first_row : first_row + window.shape[0], left : left + side]
            for parity in range(2):
                place = pl.ds(parity, windows.shape[2], stride=2)
                windows[c, parity] = window[place, :]
        filters = []
        for a in range(group):
            line = jnp.broadcast_to(col[k + a : k + a + 1, :], (side, side))
            line = pltpu.roll(line, 0, 1, stride=1, stride_axis=0)
            first = jnp.where(lane >= sub, line, 0.0).astype(bf16)
            second = jnp.where(lane < sub, line, 0.0).astype(bf16)
            filters.append(jnp.concatenate([first, second[:, : span - side]], axis=1))
        filters = jnp.concatenate(filters, axis=0)
        for s in range(stamps):
            out = jnp.dot(
                filters, cuts[s * span : (s + 1) * span, :], preferred_element_type=f32
            ).astype(bf16)
            for a in range(group):
                vert[a, s * side : (s + 1) * side, :] = out[a * side : (a + 1) * side]
        for a in range(group):
            line = jnp.broadcast_to(row_rev[k + a : k + a + 1, :], (side, side))
            line = pltpu.roll(line, 0, 1, stride=1, stride_axis=0)
            first = jnp.where(lane <= sub, line, 0.0).astype(bf16)
            second = jnp.where(lane > sub, line, 0.0).astype(bf16)
            band = jnp.concatenate([first, second], axis=0)
            out = jnp.dot(vert[a], band, preferred_element_type=f32)
            design[pl.ds(k + a, lines_all, stride=pitch), :] = out * roots[...]

    lines = 16
    sets = 4

    def gram_step(step, total):
        start = pl.multiple_of(step * sets * lines * pitch, 8)
        rows = []
        for g in range(sets):
            row = [
                design[pl.ds(start + (g * lines + j) * pitch, padded_k), :].astype(bf16)
                for j in range(lines)
            ]
            rows.append(jnp.concatenate(row, axis=1))
        both = jnp.concatenate(rows, axis=0)
        return total + lax.dot_general(
            both, both, (((1,), (1,)), ((), ())), preferred_element_type=f32
        )

    total = lax.fori_loop(
        0,
        lines_all // (lines * sets),
        gram_step,
        jnp.zeros((sets * padded_k, sets * padded_k), f32),
    )
    part = jnp.zeros((padded_k, padded_k), f32)
    for g in range(sets):
        rows = slice(g * padded_k, (g + 1) * padded_k)
        part = part + total[rows, rows]
    gram_out[...] = part


def normal_matrix(
    slot_of, rows_at, cols_at, arrived, col, row_rev, science, variance, count, taps
):
    high, wide = science.shape
    side = row_rev.shape[1]
    stamps = rows_at.shape[1]
    padded_k = up(count + 2, 16)
    pairs = (taps + 2) // 2
    span = up(side + taps - 1, 16)
    half = up(high // 2 + pairs, 8)
    tall = up(taps // 2, 8) + max(high - side + span, 2 * half)
    wins = -(-wide // (side - taps + 1))
    group = next(g for g in (8, 4, 2, 1) if count % g == 0)
    return pl.pallas_call(
        functools.partial(normal_body, count=count, across_blocks=wide // side, taps=taps),
        out_shape=(
            jax.ShapeDtypeStruct((padded_k, padded_k), f32),
            jax.ShapeDtypeStruct((wins, 2, half, side), f32),
        ),
        in_specs=[smem()] * 3 + [vmem()] * 5,
        out_specs=(vmem(),) * 2,
        scratch_shapes=[
            pltpu.VMEM((tall, wide + 2 * side), f32),
            pltpu.VMEM((stamps * span, 2 * side), bf16),
            pltpu.VMEM((group, stamps * side, 2 * side), bf16),
            pltpu.VMEM((stamps * side * (padded_k + 1), side), f32),
            pltpu.VMEM((stamps * side, side), f32),
            pltpu.VMEM((2 * half, side), f32),
        ],
        compiler_params=pltpu.CompilerParams(vmem_limit_bytes=28 * mib),
        cost_estimate=cost(10_000_000_000, 8_000_000),
        name="normal_matrix",
    )(slot_of, rows_at, cols_at, arrived, col, row_rev, science, variance)


def subtract_body(
    sender,
    gram,
    frames,
    science,
    col_t,
    row_rev,
    coef_out,
    payload,
    window,
    image,
    bands,
    total,
    stacked,
    *,
    exps,
    capacity,
    count,
    taps,
    pixels,
):
    side = frames.shape[3]
    high, wide = science.shape
    padded_k = gram.shape[1]
    part = side // exps
    size = count + 1

    system = jnp.concatenate(
        [gram[...], jnp.zeros((padded_k, side - padded_k), f32)], axis=1
    ) / pixels
    sub = lax.broadcasted_iota(jnp.int32, (padded_k, side), 0)
    lane = lax.broadcasted_iota(jnp.int32, (padded_k, side), 1)
    system = jnp.where((sub < size) & (lane <= size), system, 0.0)
    system = system + jnp.where((sub == lane) & (sub < size), ridge_term, 0.0)

    pairs = (taps + 2) // 2
    rows_half = high // 2
    wins = frames.shape[0]

    def stack_rows(q):
        for c in range(wins):
            for a in range(2):
                stacked[q, c * rows_half : (c + 1) * rows_half, a * side : (a + 1) * side] = (
                    frames[c, a, q : q + rows_half, :].astype(bf16)
                )

    starts = list(range(0, size, 8))
    for step, k in enumerate(starts):
        for q in range(step, pairs, len(starts)):
            stack_rows(q)
        block = range(min(8, size - k))
        cols = [jnp.broadcast_to(system[:, k + j : k + j + 1], system.shape) for j in block]
        rows = [system[k + j : k + j + 1, :] for j in block]
        core = [[cols[j][k + i : k + i + 1, :] for j in block] for i in block]
        for j in block:
            inverse = 1.0 / core[j][j]
            factor = jnp.where(sub == k + j, 0.0, cols[j] * inverse)
            system = system - factor * rows[j]
            for i in block[j + 1 :]:
                scale = core[i][j] * inverse
                rows[i] = rows[i] - scale * rows[j]
                for l in block[j + 1 :]:
                    core[i][l] = core[i][l] - scale * core[j][l]
                cols[i] = cols[i] - factor * core[j][i]
    pivot = jnp.sum(jnp.where(sub == lane, system, 0.0), axis=1, keepdims=True)
    solved = system[:, size : size + 1] / jnp.where(sub[:, :1] < size, pivot, 1.0)
    coef_out[...] = jnp.sum(jnp.where(sub == lane, solved, 0.0), axis=0, keepdims=True)
    background = solved[count : count + 1, :]
    basis_coef = jnp.where(sub[:, :1] < count, solved, 0.0)

    scaled = basis_coef * row_rev[...]
    kernel = jnp.zeros((col_t.shape[0], side), f32)
    for _ in range(3):
        piece = scaled.astype(bf16)
        scaled = scaled - piece.astype(f32)
        kernel = kernel + jnp.dot(col_t[...], piece, preferred_element_type=f32)
    kernel_sum = jnp.sum(jnp.sum(kernel, axis=1, keepdims=True), axis=0, keepdims=True)
    rounded = kernel.astype(bf16).astype(f32)

    zero_band = jnp.zeros((side, side), bf16)

    def band(i):
        if i < 0 or i >= taps:
            return zero_band
        line = jnp.broadcast_to(rounded[i : i + 1, :], (side, side))
        return pltpu.roll(line, 0, 1, stride=1, stride_axis=0).astype(bf16)

    made = {i: band(i) for i in range(-1, 2 * pairs)}
    for q in range(pairs):
        for a in range(2):
            for b in range(2):
                bands[
                    q * 2 * side + a * side : q * 2 * side + (a + 1) * side,
                    b * side : (b + 1) * side,
                ] = made[2 * q + a - b]

    step = side - taps + 1
    for q in range(pairs):
        out = jnp.dot(
            stacked[q], bands[q * 2 * side : (q + 1) * 2 * side, :], preferred_element_type=f32
        )
        if q:
            out = out + total[...]
        if q < pairs - 1:
            total[...] = out
    for c in range(wins):
        rows = out[c * rows_half : (c + 1) * rows_half]
        window[c, pl.ds(0, rows_half, stride=2), :] = rows[:, :side]
        window[c, pl.ds(1, rows_half, stride=2), :] = rows[:, side:]
        keep = min(step, wide - c * step)
        image[:, c * step : c * step + keep] = window[c, :, :keep]
    image[...] = science[...].astype(f32) - image[...] - background

    store_parts(sender, image, payload, side, exps, capacity, wide // side)
    line_at = lax.broadcasted_iota(jnp.int32, (trailer_rows, side), 0)
    trailer = jnp.zeros((trailer_rows, side), f32)
    rest = kernel_sum
    for p in range(3):
        piece = rest.astype(bf16).astype(f32)
        rest = rest - piece
        trailer = jnp.where(line_at == p, piece, trailer)
    trailer = trailer.astype(bf16)

    def put(d, carry):
        payload[d, capacity * part :, :] = trailer
        return carry

    lax.fori_loop(0, payload.shape[0], put, 0, unroll=4)


def subtract(
    sender, gram, frames, science, col_t, row_rev, peers, exps, capacity, count, taps, pixels
):
    wins, _, _, side = frames.shape
    high, wide = science.shape
    part = side // exps
    pairs = (taps + 2) // 2
    body = functools.partial(
        subtract_body, exps=exps, capacity=capacity, count=count, taps=taps, pixels=pixels
    )
    return pl.pallas_call(
        body,
        out_shape=(
            jax.ShapeDtypeStruct((1, side), f32),
            jax.ShapeDtypeStruct(
                (peers * exps, capacity * part + trailer_rows, side), bf16
            ),
        ),
        in_specs=[smem()] + [vmem()] * 5,
        out_specs=(vmem(), vmem()),
        scratch_shapes=[
            pltpu.VMEM((wins, high, side), f32),
            pltpu.VMEM((high, wide), f32),
            pltpu.VMEM((pairs * 2 * side, 2 * side), bf16),
            pltpu.VMEM((wins * high // 2, 2 * side), f32),
            pltpu.VMEM((pairs, wins * high // 2, 2 * side), bf16),
        ],
        compiler_params=pltpu.CompilerParams(vmem_limit_bytes=24 * mib),
        cost_estimate=cost(5_000_000_000, 4_000_000),
        name="subtract",
    )(sender, gram, frames, science, col_t, row_rev)


def split2(value):
    top = value.astype(bf16)
    return top, (value - top.astype(f32)).astype(bf16)


def score_body(
    table,
    slot_of,
    payload,
    down,
    over,
    parts,
    out,
    var_out,
    padded,
    sideways,
    var_total,
    *,
    side,
    taps,
    part,
    capacity,
):
    add_variance(table, parts, var_out, var_total, part, capacity)
    high, wide = out.shape
    margin = taps // 2
    span = up(side + taps - 1, 16)
    across_blocks = wide // side
    exps = side // part
    padded[...] = jnp.zeros(padded.shape, f32)
    for b in range(slot_of.shape[0]):
        slot = slot_of[b]
        row = pl.multiple_of((slot % capacity) * part, part)
        left = margin + (b % across_blocks) * side
        for q in range(exps):
            top = (b // across_blocks) * side + q * part
            block = payload[(slot // capacity) * exps + q, pl.ds(row, part), :]
            padded[top : top + part, left : left + side] = block.astype(f32)
    line = jnp.broadcast_to(over[...], (2 * side, 2 * side))
    band = pltpu.roll(line, 0, 1, stride=1, stride_axis=0)[:, :side]
    both = jnp.concatenate(split2(band), axis=1)
    sideways[...] = jnp.zeros(sideways.shape, f32)
    for c in range(wide // side):
        window = padded[:, c * side : (c + 2) * side].astype(bf16)
        got = jnp.dot(window, both, preferred_element_type=f32)
        sideways[margin : margin + high, c * side : (c + 1) * side] = got[:, :side] + got[:, side:]
    line = jnp.broadcast_to(down[...], (side, 2 * side))
    band = pltpu.roll(line, 0, 1, stride=1, stride_axis=0)[:, :span]
    top, low = split2(band)
    for r in range(high // side):
        data_top, data_low = split2(sideways[r * side : r * side + span, :])
        got = jnp.dot(top, data_top, preferred_element_type=f32)
        got = got + jnp.dot(top, data_low, preferred_element_type=f32)
        got = got + jnp.dot(low, data_top, preferred_element_type=f32)
        out[r * side : (r + 1) * side, :] = got


def score(
    table, slot_of, payload, down, over_rev, parts, high, wide, taps, tract, part, capacity
):
    side = payload.shape[2]
    span = up(side + taps - 1, 16)
    return pl.pallas_call(
        functools.partial(score_body, side=side, taps=taps, part=part, capacity=capacity),
        out_shape=(
            jax.ShapeDtypeStruct((high, wide), f32),
            jax.ShapeDtypeStruct((tract, part, side), f32),
        ),
        in_specs=[smem()] * 2 + [vmem()] * 4,
        out_specs=(vmem(),) * 2,
        scratch_shapes=[
            pltpu.VMEM((high, wide + side), f32),
            pltpu.VMEM((high - side + span, wide), f32),
            pltpu.VMEM((tract + 1, part, side), f32),
        ],
        compiler_params=pltpu.CompilerParams(vmem_limit_bytes=24 * mib),
        cost_estimate=cost(2_000_000_000, 2_000_000),
        name="score",
    )(table, slot_of, payload, down, over_rev, parts)


def add_variance(table, parts, out, total, part, capacity):
    total[...] = jnp.zeros(total.shape, f32)
    tract = out.shape[0]

    def one(j, carry):
        block = table[j // capacity, j % capacity] - 1
        block = jnp.where(block < 0, tract, block)
        row = pl.multiple_of((j % capacity) * part, part)
        total[block] += parts[j // capacity, pl.ds(row, part), :].astype(f32)
        return carry

    lax.fori_loop(0, parts.shape[0] * capacity, one, 0, unroll=8)
    out[...] = total[:tract]


def combine_body(table, parts, var_sum, var_template, out, total, gain, *, part, capacity):
    total[...] = jnp.zeros(total.shape, f32)
    gain[...] = jnp.zeros(gain.shape, f32)
    tract = out.shape[0]

    def one(d, carry):
        tail = parts[d, capacity * part :, :].astype(f32)
        kernel_sum = tail[0:1] + tail[1:2] + tail[2:3]
        square = jnp.broadcast_to(kernel_sum * kernel_sum, gain.shape[1:])
        for c in range(capacity):
            block = table[d, c] - 1
            block = jnp.where(block < 0, tract, block)
            total[block] += parts[d, c * part : (c + 1) * part, :].astype(f32)
            gain[block] += square
        return carry

    lax.fori_loop(0, parts.shape[0], one, 0, unroll=4)
    for t in range(tract):
        variance = var_sum[t] + gain[t, 0:1, :] * var_template[t].astype(f32)
        out[t] = (total[t] * lax.rsqrt(jnp.maximum(variance, 1.0))).astype(bf16)


def combine(table, parts, var_sum, var_template, part, capacity):
    tract, _, side = var_sum.shape
    return pl.pallas_call(
        functools.partial(combine_body, part=part, capacity=capacity),
        out_shape=jax.ShapeDtypeStruct((tract, part, side), bf16),
        in_specs=[smem(), vmem(), vmem(), vmem()],
        out_specs=vmem(),
        scratch_shapes=[
            pltpu.VMEM((tract + 1, part, side), f32),
            pltpu.VMEM((tract + 1, 8, side), f32),
        ],
        compiler_params=pltpu.CompilerParams(vmem_limit_bytes=16 * mib),
        name="combine",
    )(table, parts, var_sum, var_template)


def join_body(places, *refs, part, count):
    ins = refs[:count]
    out, held, sems = refs[-3:]
    copies = []
    for d, ref in enumerate(ins):
        held[d] = ref[...].astype(f32)
        row = pl.multiple_of(places[d] * part, part)
        copies.append(
            pltpu.make_async_copy(held.at[d], out.at[:, pl.ds(row, part), :], sems.at[d])
        )
        copies[-1].start()
    for copy in copies:
        copy.wait()


def join_parts(places, parts, whole, exps):
    tract, part, side = parts[0].shape
    count = len(parts)
    fresh = whole is None
    anywhere = pl.BlockSpec(memory_space=pl.ANY)
    return pl.pallas_call(
        functools.partial(join_body, part=part, count=count),
        out_shape=jax.ShapeDtypeStruct((tract, part * exps, side), f32),
        in_specs=[smem()] + [vmem()] * count + ([] if fresh else [anywhere]),
        out_specs=anywhere,
        scratch_shapes=[
            pltpu.VMEM((count, tract, part, side), f32),
            pltpu.SemaphoreType.DMA((count,)),
        ],
        input_output_aliases={} if fresh else {count + 1: 0},
        compiler_params=pltpu.CompilerParams(vmem_limit_bytes=16 * mib),
        cost_estimate=cost(0, 3_000_000 * count),
        name="join_parts",
    )(places, *parts, *([] if fresh else [whole]))


def local(
    template,
    template_var,
    science,
    science_var,
    routes_src,
    routes_blk,
    stamp_rows,
    stamp_cols,
    basis_col,
    basis_row,
    psf_col,
    psf_row,
):
    peers = lax.axis_size("det")
    exps = lax.axis_size("exp")
    me = lax.axis_index("exp").astype(jnp.int32)
    tract, side, _ = template.shape
    science_img = science[0]
    variance_img = science_var[0]
    blocks_dev = routes_src.shape[1]
    count, taps = basis_col.shape
    capacity = max(2, -(-blocks_dev // peers))
    slots = peers * capacity
    part = side // exps

    slot_of, sender, request = route_tables(routes_src, routes_blk, peers, capacity)
    asked = lax.all_to_all(request, "det", split_axis=0, concat_axis=0, tiled=True)
    picked = pick_blocks(asked, fetch(template), slots, capacity)
    var_parts = prepare(
        sender, request, variance_img, science_img, picked, side, exps, capacity
    )
    arrived = lax.all_to_all(picked, "det", split_axis=0, concat_axis=0, tiled=True)

    padded_k = up(count + 2, 16)
    col_t = jnp.pad(basis_col.T, ((0, up(taps, 16) - taps), (0, padded_k - count)))
    col = jnp.pad(basis_col.astype(f32), ((0, padded_k - count), (0, side - taps)))
    row_rev = jnp.pad(
        basis_row.astype(f32)[:, ::-1], ((0, padded_k - count), (side - taps, 0))
    )
    row_rev = jnp.roll(row_rev, 1, axis=1)
    over_rev = jnp.roll(jnp.pad(psf_row[:, ::-1], ((0, 0), (2 * side - taps, 0))), 1, axis=1)
    down = jnp.pad(psf_col, ((0, 0), (0, 2 * side - taps)))
    var_late, arrived = lax.optimization_barrier((var_parts, arrived))
    var_back = lax.all_to_all(
        var_late, ("det", "exp"), split_axis=0, concat_axis=0, tiled=True
    )
    table = var_back[:, capacity * part, :capacity].astype(f32).astype(jnp.int32)

    high, wide = science_img.shape
    gram, frames = normal_matrix(
        slot_of,
        stamp_rows,
        stamp_cols,
        arrived,
        col,
        row_rev,
        science_img,
        variance_img,
        count,
        taps,
    )
    coef, payload = subtract(
        sender,
        gram,
        frames,
        science_img,
        col_t,
        row_rev,
        peers,
        exps,
        capacity,
        count,
        taps,
        stamp_rows.shape[1] * side * side,
    )
    diff_back = lax.all_to_all(payload, ("det", "exp"), split_axis=0, concat_axis=0, tiled=True)
    scored, var_sum = score(
        table,
        slot_of,
        payload,
        down,
        over_rev,
        var_back,
        high,
        wide,
        taps,
        tract,
        part,
        capacity,
    )
    var_template = lax.dynamic_slice_in_dim(template_var, me * part, part, 1)
    mine = combine(table, diff_back, var_sum, var_template, part, capacity)

    def swap(value, distance):
        return lax.ppermute(value, "exp", [(e, e ^ distance) for e in range(exps)])

    def put(parts, whole):
        places = jnp.stack([there for there, _ in parts])
        return join_parts(places, [held for _, held in parts], whole, exps)

    if exps == 4:
        far = swap(mine, 2)
        near = swap(mine, 1)
        last = swap(far, 1)
        whole = put([(me, mine), (me ^ 1, near), (me ^ 2, far)], None)
        significance = put([(me ^ 3, last)], whole)
    else:
        parts = [(me, mine)]
        for gap in range(1, exps):
            pairs = [(e, (e + gap) % exps) for e in range(exps)]
            parts.append(((me - gap) % exps, lax.ppermute(mine, "exp", pairs)))
        significance = put(parts, None)
    return (significance, scored[None], coef[:, : count + 1])


def solution(mesh):
    placed = (
        P("det", None, None),
        P("det", None, None),
        P("exp", "det", None),
        P("exp", "det", None),
        P("exp", "det"),
        P("exp", "det"),
        P("exp", "det"),
        P("exp", "det"),
        P(),
        P(),
        P("exp", None),
        P("exp", None),
    )
    return jax.shard_map(
        local,
        mesh=mesh,
        in_specs=placed,
        out_specs=(P("det", None, None), P("exp", "det", None), P("exp", "det")),
        check_vma=False,
    )
```

```python
import functools

import jax
import jax.numpy as jnp
from jax import lax
from jax.experimental import pallas as pl
from jax.experimental.pallas import tpu as pltpu
from jax.sharding import PartitionSpec as P

ridge_term = 0.01
bf16 = jnp.bfloat16
f32 = jnp.float32
vmem = functools.partial(pl.BlockSpec, memory_space=pltpu.VMEM)
smem = functools.partial(pl.BlockSpec, memory_space=pltpu.SMEM)
mib = 1024 * 1024
trailer_rows = 8


def up(value, step):
    return -(-value // step) * step


def cost(flops, moved):
    return pl.CostEstimate(flops=flops, bytes_accessed=moved, transcendentals=0)


def distance(here, there, exps):
    if exps & (exps - 1) == 0:
        return here ^ there
    return lax.rem(here - there + exps, exps)


def from_exposure(value, gap, exps):
    if exps & (exps - 1) == 0:
        pairs = [(e, e ^ gap) for e in range(exps)]
    else:
        pairs = [(e, (e + gap) % exps) for e in range(exps)]
    return lax.ppermute(value, "exp", pairs)


def route_body(src, blk, slot_of, sender, request, count, *, peers, capacity):
    def clear_count(p, carry):
        count[p] = 0
        return carry

    def clear_slot(s, carry):
        sender[s] = 0
        request[s // capacity, 0, s % capacity] = 0
        return carry

    lax.fori_loop(0, peers, clear_count, 0, unroll=peers <= 16)
    lax.fori_loop(0, peers * capacity, clear_slot, 0, unroll=peers <= 16)
    for b in range(src.shape[1]):
        owner = src[0, b]
        place = count[owner]
        count[owner] = place + 1
        slot_of[b] = owner * capacity + place
        sender[owner * capacity + place] = b
        request[owner, 0, place] = blk[0, b] + 1


def route_tables(routes_src, routes_blk, peers, capacity):
    return pl.pallas_call(
        functools.partial(route_body, peers=peers, capacity=capacity),
        out_shape=(
            jax.ShapeDtypeStruct((routes_src.shape[1],), jnp.int32),
            jax.ShapeDtypeStruct((peers * capacity,), jnp.int32),
            jax.ShapeDtypeStruct((peers, 1, capacity), jnp.int32),
        ),
        in_specs=[smem()] * 2,
        out_specs=(smem(),) * 3,
        scratch_shapes=[pltpu.SMEM((peers,), jnp.int32)],
        name="route_tables",
    )(routes_src, routes_blk)


def fetch_body(template, near, sem):
    copy = pltpu.make_async_copy(template, near, sem)
    copy.start()
    copy.wait()


def fetch(template):
    return pl.pallas_call(
        fetch_body,
        out_shape=jax.ShapeDtypeStruct(template.shape, template.dtype),
        in_specs=[pl.BlockSpec(memory_space=pl.ANY)],
        out_specs=vmem(),
        scratch_shapes=[pltpu.SemaphoreType.DMA(())],
        compiler_params=pltpu.CompilerParams(vmem_limit_bytes=16 * mib),
        cost_estimate=cost(0, 4_000_000),
        name="fetch",
    )(template)


def pick_body(asked, template, out, *, capacity):
    def one(s, carry):
        block = jnp.maximum(asked[s // capacity, 0, s % capacity] - 1, 0)
        out[s] = template[block]
        return carry

    lax.fori_loop(0, out.shape[0], one, 0, unroll=True if out.shape[0] <= 32 else 4)


def pick_blocks(asked, template, slots, capacity):
    return pl.pallas_call(
        functools.partial(pick_body, capacity=capacity),
        out_shape=jax.ShapeDtypeStruct((slots,) + template.shape[1:], template.dtype),
        in_specs=[smem(), vmem()],
        out_specs=vmem(),
        compiler_params=pltpu.CompilerParams(vmem_limit_bytes=16 * mib),
        name="pick_blocks",
    )(asked, template)


def store_parts(sender, image, out, side, exps, capacity, across_blocks):
    part = side // exps
    slots = sender.shape[0]

    def one(s, carry):
        b = sender[s]
        top = pl.multiple_of((b // across_blocks) * side, side)
        left = pl.multiple_of((b % across_blocks) * side, side)
        block = image[pl.ds(top, side), pl.ds(left, side)].astype(bf16)
        row = pl.multiple_of((s % capacity) * part, part)
        for q in range(exps):
            out[(s // capacity) * exps + q, pl.ds(row, part), :] = block[q * part : (q + 1) * part]
        return carry

    lax.fori_loop(0, slots, one, 0, unroll=True if slots <= 32 else 4)


def cut(ref, top, left, height, side):
    down = pl.multiple_of((top // 8) * 8, 8)
    over = pl.multiple_of((left // side) * side, side)
    tile = ref[pl.ds(down, height), pl.ds(over, 3 * side)]
    tile = pltpu.roll(tile, lax.rem(3 * side - (left - over), 3 * side), 1)[:, : 2 * side]
    return pltpu.roll(tile, lax.rem(height - (top - down), height), 0)


def prepare_body(
    sender, variance, science, asked, earlier, out, asked_out, *, side, exps, capacity
):
    del earlier, science
    store_parts(sender, variance, out, side, exps, capacity, variance.shape[1] // side)
    asked_out[...] = asked[...]


def prepare(sender, variance, science, asked, earlier, side, exps, capacity):
    slots = sender.shape[0]
    part = side // exps
    return pl.pallas_call(
        functools.partial(prepare_body, side=side, exps=exps, capacity=capacity),
        out_shape=(
            jax.ShapeDtypeStruct((slots // capacity * exps, capacity * part, side), bf16),
            jax.ShapeDtypeStruct(asked.shape, asked.dtype),
        ),
        in_specs=[smem()] + [vmem()] * 3 + [pl.BlockSpec(memory_space=pl.ANY)],
        out_specs=(vmem(), vmem()),
        compiler_params=pltpu.CompilerParams(vmem_limit_bytes=16 * mib),
        cost_estimate=cost(0, 6_000_000),
        name="prepare",
    )(sender, variance, science, asked, earlier)


def normal_body(
    slot_of,
    rows_at,
    cols_at,
    arrived,
    col,
    row_rev,
    science,
    variance,
    gram_out,
    windows,
    frame,
    cuts,
    vert,
    design,
    roots,
    window,
    *,
    count,
    across_blocks,
    taps,
):
    side = row_rev.shape[1]
    margin = taps // 2
    stamps = rows_at.shape[1]
    span = up(side + taps - 1, 16)
    padded_k = gram_out.shape[1]
    pitch = (count + 2) | 1
    lines_all = stamps * side
    sub = lax.broadcasted_iota(jnp.int32, (side, side), 0)
    lane = lax.broadcasted_iota(jnp.int32, (side, side), 1)

    high, wide = science.shape
    rows_off = up(margin, 8)
    frame[:rows_off, :] = jnp.zeros((rows_off, frame.shape[1]), f32)
    below = rows_off + high
    frame[below:, :] = jnp.zeros((frame.shape[0] - below, frame.shape[1]), f32)
    frame[rows_off:below, :side] = jnp.zeros((high, side), f32)
    after = side + wide
    frame[rows_off:below, after:] = jnp.zeros((high, frame.shape[1] - after), f32)
    for b in range(slot_of.shape[0]):
        top = rows_off + (b // across_blocks) * side
        left = side + (b % across_blocks) * side
        frame[top : top + side, left : left + side] = arrived[slot_of[b]].astype(f32)
    first_row = rows_off - margin
    first_col = side - margin

    def cut_image(ref, top, left):
        tall = min(high, side + 16)
        down = pl.multiple_of(jnp.minimum((top // 16) * 16, high - tall), 16)
        over = pl.multiple_of(jnp.minimum((left // side) * side, wide - 2 * side), side)
        tile = ref[pl.ds(down, tall), pl.ds(over, 2 * side)].astype(f32)
        tile = pltpu.roll(tile, lax.rem(2 * side - (left - over), 2 * side), 1)[:, :side]
        return pltpu.roll(tile, lax.rem(tall - (top - down), tall), 0)[:side]

    for s in range(stamps):
        top = rows_at[0, s]
        left = cols_at[0, s]
        tile = cut(frame, top + first_row, left + first_col, span, side)
        cuts[s * span : (s + 1) * span, :] = tile.astype(bf16)
        root = lax.rsqrt(cut_image(variance, top, left))
        roots[s * side : (s + 1) * side, :] = root
        place = pl.ds(s * side * pitch + count, side, stride=pitch)
        design[place, :] = root
        place = pl.ds(s * side * pitch + count + 1, side, stride=pitch)
        design[place, :] = root * cut_image(science, top, left)
    design[lines_all * pitch :, :] = jnp.zeros((design.shape[0] - lines_all * pitch, side), f32)

    group = vert.shape[0]
    step = side - taps + 1
    starts = list(range(0, count, group))
    for turn, k in enumerate(starts):
        for c in range(turn, windows.shape[0], len(starts)):
            left = first_col + c * step
            window[...] = frame[first_row : first_row + window.shape[0], left : left + side]
            for parity in range(2):
                place = pl.ds(parity, windows.shape[2], stride=2)
                windows[c, parity] = window[place, :]
        filters = []
        for a in range(group):
            line = jnp.broadcast_to(col[k + a : k + a + 1, :], (side, side))
            line = pltpu.roll(line, 0, 1, stride=1, stride_axis=0)
            first = jnp.where(lane >= sub, line, 0.0).astype(bf16)
            second = jnp.where(lane < sub, line, 0.0).astype(bf16)
            filters.append(jnp.concatenate([first, second[:, : span - side]], axis=1))
        filters = jnp.concatenate(filters, axis=0)
        for s in range(stamps):
            out = jnp.dot(
                filters, cuts[s * span : (s + 1) * span, :], preferred_element_type=f32
            ).astype(bf16)
            for a in range(group):
                vert[a, s * side : (s + 1) * side, :] = out[a * side : (a + 1) * side]
        for a in range(group):
            line = jnp.broadcast_to(row_rev[k + a : k + a + 1, :], (side, side))
            line = pltpu.roll(line, 0, 1, stride=1, stride_axis=0)
            first = jnp.where(lane <= sub, line, 0.0).astype(bf16)
            second = jnp.where(lane > sub, line, 0.0).astype(bf16)
            band = jnp.concatenate([first, second], axis=0)
            out = jnp.dot(vert[a], band, preferred_element_type=f32)
            design[pl.ds(k + a, lines_all, stride=pitch), :] = out * roots[...]

    lines = 16
    sets = 4

    def gram_step(step, total):
        start = pl.multiple_of(step * sets * lines * pitch, 8)
        rows = []
        for g in range(sets):
            row = [
                design[pl.ds(start + (g * lines + j) * pitch, padded_k), :].astype(bf16)
                for j in range(lines)
            ]
            rows.append(jnp.concatenate(row, axis=1))
        both = jnp.concatenate(rows, axis=0)
        return total + lax.dot_general(
            both, both, (((1,), (1,)), ((), ())), preferred_element_type=f32
        )

    total = lax.fori_loop(
        0,
        lines_all // (lines * sets),
        gram_step,
        jnp.zeros((sets * padded_k, sets * padded_k), f32),
        unroll=2,
    )
    part = jnp.zeros((padded_k, padded_k), f32)
    for g in range(sets):
        rows = slice(g * padded_k, (g + 1) * padded_k)
        part = part + total[rows, rows]
    gram_out[...] = part


def normal_matrix(
    slot_of, rows_at, cols_at, arrived, col, row_rev, science, variance, count, taps
):
    high, wide = science.shape
    side = row_rev.shape[1]
    stamps = rows_at.shape[1]
    padded_k = up(count + 2, 16)
    pairs = (taps + 2) // 2
    span = up(side + taps - 1, 16)
    half = up(high // 2 + pairs, 8)
    tall = up(taps // 2, 8) + max(high - side + span, 2 * half)
    wins = -(-wide // (side - taps + 1))
    group = next(g for g in (8, 4, 2, 1) if count % g == 0)
    return pl.pallas_call(
        functools.partial(normal_body, count=count, across_blocks=wide // side, taps=taps),
        out_shape=(
            jax.ShapeDtypeStruct((padded_k, padded_k), f32),
            jax.ShapeDtypeStruct((wins, 2, half, side), f32),
        ),
        in_specs=[smem()] * 3 + [vmem()] * 5,
        out_specs=(vmem(),) * 2,
        scratch_shapes=[
            pltpu.VMEM((tall, wide + 2 * side), f32),
            pltpu.VMEM((stamps * span, 2 * side), bf16),
            pltpu.VMEM((group, stamps * side, 2 * side), bf16),
            pltpu.VMEM((up(stamps * side * ((count + 2) | 1) + padded_k, 8), side), f32),
            pltpu.VMEM((stamps * side, side), f32),
            pltpu.VMEM((2 * half, side), f32),
        ],
        compiler_params=pltpu.CompilerParams(vmem_limit_bytes=28 * mib),
        cost_estimate=cost(10_000_000_000, 8_000_000),
        name="normal_matrix",
    )(slot_of, rows_at, cols_at, arrived, col, row_rev, science, variance)


def subtract_body(
    sender,
    gram,
    frames,
    science,
    col_t,
    row_rev,
    coef_out,
    payload,
    window,
    image,
    bands,
    total,
    stacked,
    *,
    exps,
    capacity,
    count,
    taps,
    pixels,
):
    side = frames.shape[3]
    high, wide = science.shape
    padded_k = gram.shape[1]
    part = side // exps
    size = count + 1

    system = jnp.concatenate(
        [gram[...], jnp.zeros((padded_k, side - padded_k), f32)], axis=1
    ) / pixels
    sub = lax.broadcasted_iota(jnp.int32, (padded_k, side), 0)
    lane = lax.broadcasted_iota(jnp.int32, (padded_k, side), 1)
    system = jnp.where((sub < size) & (lane <= size), system, 0.0)
    system = system + jnp.where((sub == lane) & (sub < size), ridge_term, 0.0)

    pairs = (taps + 2) // 2
    rows_half = high // 2
    wins = frames.shape[0]

    def stack_rows(q):
        for c in range(wins):
            for a in range(2):
                stacked[q, c * rows_half : (c + 1) * rows_half, a * side : (a + 1) * side] = (
                    frames[c, a, q : q + rows_half, :].astype(bf16)
                )

    starts = list(range(0, size, 8))
    for step, k in enumerate(starts):
        for q in range(step, pairs, len(starts)):
            stack_rows(q)
        block = range(min(8, size - k))
        cols = [jnp.broadcast_to(system[:, k + j : k + j + 1], system.shape) for j in block]
        rows = [system[k + j : k + j + 1, :] for j in block]
        core = [[cols[j][k + i : k + i + 1, :] for j in block] for i in block]
        for j in block:
            inverse = 1.0 / core[j][j]
            factor = jnp.where(sub == k + j, 0.0, cols[j] * inverse)
            system = system - factor * rows[j]
            for i in block[j + 1 :]:
                scale = core[i][j] * inverse
                rows[i] = rows[i] - scale * rows[j]
                for l in block[j + 1 :]:
                    core[i][l] = core[i][l] - scale * core[j][l]
                cols[i] = cols[i] - factor * core[j][i]
    pivot = jnp.sum(jnp.where(sub == lane, system, 0.0), axis=1, keepdims=True)
    solved = system[:, size : size + 1] / jnp.where(sub[:, :1] < size, pivot, 1.0)
    coef_out[...] = jnp.sum(jnp.where(sub == lane, solved, 0.0), axis=0, keepdims=True)
    background = solved[count : count + 1, :]
    basis_coef = jnp.where(sub[:, :1] < count, solved, 0.0)

    scaled = basis_coef * row_rev[...]
    kernel = jnp.zeros((col_t.shape[0], side), f32)
    for _ in range(3):
        piece = scaled.astype(bf16)
        scaled = scaled - piece.astype(f32)
        kernel = kernel + jnp.dot(col_t[...], piece, preferred_element_type=f32)
    kernel_sum = jnp.sum(jnp.sum(kernel, axis=1, keepdims=True), axis=0, keepdims=True)
    rounded = kernel.astype(bf16).astype(f32)

    zero_band = jnp.zeros((side, side), bf16)

    def band(i):
        if i < 0 or i >= taps:
            return zero_band
        line = jnp.broadcast_to(rounded[i : i + 1, :], (side, side))
        return pltpu.roll(line, 0, 1, stride=1, stride_axis=0).astype(bf16)

    made = {i: band(i) for i in range(-1, 2 * pairs)}
    for q in range(pairs):
        for a in range(2):
            for b in range(2):
                bands[
                    q * 2 * side + a * side : q * 2 * side + (a + 1) * side,
                    b * side : (b + 1) * side,
                ] = made[2 * q + a - b]

    step = side - taps + 1
    for q in range(pairs):
        out = jnp.dot(
            stacked[q], bands[q * 2 * side : (q + 1) * 2 * side, :], preferred_element_type=f32
        )
        if q:
            out = out + total[...]
        if q < pairs - 1:
            total[...] = out
    for c in range(wins):
        rows = out[c * rows_half : (c + 1) * rows_half]
        window[c, pl.ds(0, rows_half, stride=2), :] = rows[:, :side]
        window[c, pl.ds(1, rows_half, stride=2), :] = rows[:, side:]
        keep = min(step, wide - c * step)
        image[:, c * step : c * step + keep] = window[c, :, :keep]
    image[...] = science[...].astype(f32) - image[...] - background

    store_parts(sender, image, payload, side, exps, capacity, wide // side)
    line_at = lax.broadcasted_iota(jnp.int32, (trailer_rows, side), 0)
    trailer = jnp.zeros((trailer_rows, side), f32)
    rest = kernel_sum
    for p in range(3):
        piece = rest.astype(bf16).astype(f32)
        rest = rest - piece
        trailer = jnp.where(line_at == p, piece, trailer)
    trailer = trailer.astype(bf16)

    def put(d, carry):
        payload[d, capacity * part :, :] = trailer
        return carry

    lax.fori_loop(0, payload.shape[0], put, 0, unroll=4)


def subtract(
    sender, gram, frames, science, col_t, row_rev, peers, exps, capacity, count, taps, pixels
):
    wins, _, _, side = frames.shape
    high, wide = science.shape
    part = side // exps
    pairs = (taps + 2) // 2
    body = functools.partial(
        subtract_body, exps=exps, capacity=capacity, count=count, taps=taps, pixels=pixels
    )
    return pl.pallas_call(
        body,
        out_shape=(
            jax.ShapeDtypeStruct((1, side), f32),
            jax.ShapeDtypeStruct(
                (peers * exps, capacity * part + trailer_rows, side), bf16
            ),
        ),
        in_specs=[smem()] + [vmem()] * 5,
        out_specs=(vmem(), vmem()),
        scratch_shapes=[
            pltpu.VMEM((wins, high, side), f32),
            pltpu.VMEM((high, wide), f32),
            pltpu.VMEM((pairs * 2 * side, 2 * side), bf16),
            pltpu.VMEM((wins * high // 2, 2 * side), f32),
            pltpu.VMEM((pairs, wins * high // 2, 2 * side), bf16),
        ],
        compiler_params=pltpu.CompilerParams(vmem_limit_bytes=24 * mib),
        cost_estimate=cost(5_000_000_000, 4_000_000),
        name="subtract",
    )(sender, gram, frames, science, col_t, row_rev)


def split2(value):
    top = value.astype(bf16)
    return top, (value - top.astype(f32)).astype(bf16)


def score_body(
    me,
    table,
    slot_of,
    payload,
    down,
    over,
    parts,
    out,
    var_out,
    padded,
    sideways,
    var_total,
    *,
    side,
    taps,
    part,
    capacity,
):
    add_variance(me, table, parts, var_out, var_total, part, capacity)
    high, wide = out.shape
    margin = taps // 2
    span = up(side + taps - 1, 16)
    across_blocks = wide // side
    exps = side // part
    padded[...] = jnp.zeros(padded.shape, f32)
    for b in range(slot_of.shape[0]):
        slot = slot_of[b]
        row = pl.multiple_of((slot % capacity) * part, part)
        left = margin + (b % across_blocks) * side
        for q in range(exps):
            top = (b // across_blocks) * side + q * part
            block = payload[(slot // capacity) * exps + q, pl.ds(row, part), :]
            padded[top : top + part, left : left + side] = block.astype(f32)
    line = jnp.broadcast_to(over[...], (2 * side, 2 * side))
    band = pltpu.roll(line, 0, 1, stride=1, stride_axis=0)[:, :side]
    both = jnp.concatenate(split2(band), axis=1)
    sideways[...] = jnp.zeros(sideways.shape, f32)
    for c in range(wide // side):
        window = padded[:, c * side : (c + 2) * side].astype(bf16)
        got = jnp.dot(window, both, preferred_element_type=f32)
        sideways[margin : margin + high, c * side : (c + 1) * side] = got[:, :side] + got[:, side:]
    line = jnp.broadcast_to(down[...], (side, 2 * side))
    band = pltpu.roll(line, 0, 1, stride=1, stride_axis=0)[:, :span]
    top, low = split2(band)
    for r in range(high // side):
        data_top, data_low = split2(sideways[r * side : r * side + span, :])
        got = jnp.dot(top, data_top, preferred_element_type=f32)
        got = got + jnp.dot(top, data_low, preferred_element_type=f32)
        got = got + jnp.dot(low, data_top, preferred_element_type=f32)
        out[r * side : (r + 1) * side, :] = got


def score(
    me, table, slot_of, payload, down, over_rev, parts, high, wide, taps, tract, part, capacity
):
    side = payload.shape[2]
    span = up(side + taps - 1, 16)
    return pl.pallas_call(
        functools.partial(score_body, side=side, taps=taps, part=part, capacity=capacity),
        out_shape=(
            jax.ShapeDtypeStruct((high, wide), f32),
            jax.ShapeDtypeStruct((tract, part, side), f32),
        ),
        in_specs=[smem()] * 3 + [vmem()] * 4,
        out_specs=(vmem(),) * 2,
        scratch_shapes=[
            pltpu.VMEM((high, wide + side), f32),
            pltpu.VMEM((high - side + span, wide), f32),
            pltpu.VMEM((tract + 1, part, side), f32),
        ],
        compiler_params=pltpu.CompilerParams(vmem_limit_bytes=24 * mib),
        cost_estimate=cost(2_000_000_000, 2_000_000),
        name="score",
    )(me, table, slot_of, payload, down, over_rev, parts)


def wanted_block(me, table, d, c, tract):
    exps = table.shape[0]
    block = table[distance(me[0], lax.rem(d, exps), exps), d // exps, c] - 1
    return jnp.where(block < 0, tract, block)


def add_variance(me, table, parts, out, total, part, capacity):
    total[...] = jnp.zeros(total.shape, f32)
    tract = out.shape[0]

    def one(d, carry):
        for c in range(capacity):
            block = wanted_block(me, table, d, c, tract)
            total[block] += parts[d, c * part : (c + 1) * part, :].astype(f32)
        return carry

    lax.fori_loop(0, parts.shape[0], one, 0, unroll=4)
    out[...] = total[:tract]


def combine_body(
    me, table, parts, var_sum, var_template, out, total, gain, *, part, capacity
):
    total[...] = jnp.zeros(total.shape, f32)
    gain[...] = jnp.zeros(gain.shape, f32)
    tract = out.shape[0]

    def one(d, carry):
        tail = parts[d, capacity * part :, :].astype(f32)
        kernel_sum = tail[0:1] + tail[1:2] + tail[2:3]
        square = jnp.broadcast_to(kernel_sum * kernel_sum, gain.shape[1:])
        for c in range(capacity):
            block = wanted_block(me, table, d, c, tract)
            total[block] += parts[d, c * part : (c + 1) * part, :].astype(f32)
            gain[block] += square
        return carry

    lax.fori_loop(0, parts.shape[0], one, 0, unroll=4)
    for t in range(tract):
        variance = var_sum[t] + gain[t, 0:1, :] * var_template[t].astype(f32)
        out[t] = (total[t] * lax.rsqrt(jnp.maximum(variance, 1.0))).astype(bf16)


def combine(me, table, parts, var_sum, var_template, part, capacity):
    tract, _, side = var_sum.shape
    return pl.pallas_call(
        functools.partial(combine_body, part=part, capacity=capacity),
        out_shape=jax.ShapeDtypeStruct((tract, part, side), bf16),
        in_specs=[smem(), smem(), vmem(), vmem(), vmem()],
        out_specs=vmem(),
        scratch_shapes=[
            pltpu.VMEM((tract + 1, part, side), f32),
            pltpu.VMEM((tract + 1, 8, side), f32),
        ],
        compiler_params=pltpu.CompilerParams(vmem_limit_bytes=16 * mib),
        name="combine",
    )(me, table, parts, var_sum, var_template)


def join_body(places, *refs, part, count):
    ins = refs[:count]
    out, held, sems = refs[-3:]
    copies = []
    for d, ref in enumerate(ins):
        held[d] = ref[...].astype(f32)
        row = pl.multiple_of(places[d] * part, part)
        copies.append(
            pltpu.make_async_copy(held.at[d], out.at[:, pl.ds(row, part), :], sems.at[d])
        )
        copies[-1].start()
    for copy in copies:
        copy.wait()


def join_parts(places, parts, whole, exps):
    tract, part, side = parts[0].shape
    count = len(parts)
    fresh = whole is None
    anywhere = pl.BlockSpec(memory_space=pl.ANY)
    return pl.pallas_call(
        functools.partial(join_body, part=part, count=count),
        out_shape=jax.ShapeDtypeStruct((tract, part * exps, side), f32),
        in_specs=[smem()] + [vmem()] * count + ([] if fresh else [anywhere]),
        out_specs=anywhere,
        scratch_shapes=[
            pltpu.VMEM((count, tract, part, side), f32),
            pltpu.SemaphoreType.DMA((count,)),
        ],
        input_output_aliases={} if fresh else {count + 1: 0},
        compiler_params=pltpu.CompilerParams(vmem_limit_bytes=16 * mib),
        cost_estimate=cost(0, 3_000_000 * count),
        name="join_parts",
    )(places, *parts, *([] if fresh else [whole]))


def local(
    template,
    template_var,
    science,
    science_var,
    routes_src,
    routes_blk,
    stamp_rows,
    stamp_cols,
    basis_col,
    basis_row,
    psf_col,
    psf_row,
):
    peers = lax.axis_size("det")
    exps = lax.axis_size("exp")
    me = lax.axis_index("exp").astype(jnp.int32)
    tract, side, _ = template.shape
    science_img = science[0]
    variance_img = science_var[0]
    blocks_dev = routes_src.shape[1]
    count, taps = basis_col.shape
    capacity = max(2, -(-blocks_dev // peers))
    slots = peers * capacity
    part = side // exps

    slot_of, sender, request = route_tables(routes_src, routes_blk, peers, capacity)
    asked = lax.all_to_all(request, "det", split_axis=0, concat_axis=0, tiled=True)
    picked = pick_blocks(asked, fetch(template), slots, capacity)
    var_parts, asked_late = prepare(
        sender, variance_img, science_img, asked, picked, side, exps, capacity
    )
    arrived = lax.all_to_all(picked, "det", split_axis=0, concat_axis=0, tiled=True)

    padded_k = up(count + 2, 16)
    col_t = jnp.pad(basis_col.T, ((0, up(taps, 16) - taps), (0, padded_k - count)))
    col = jnp.pad(basis_col.astype(f32), ((0, padded_k - count), (0, side - taps)))
    row_rev = jnp.pad(
        basis_row.astype(f32)[:, ::-1], ((0, padded_k - count), (side - taps, 0))
    )
    row_rev = jnp.roll(row_rev, 1, axis=1)
    over_rev = jnp.roll(jnp.pad(psf_row[:, ::-1], ((0, 0), (2 * side - taps, 0))), 1, axis=1)
    down = jnp.pad(psf_col, ((0, 0), (0, 2 * side - taps)))
    var_late, arrived = lax.optimization_barrier((var_parts, arrived))
    var_back = lax.all_to_all(
        var_late, ("det", "exp"), split_axis=0, concat_axis=0, tiled=True
    )
    tables = [asked_late] + [from_exposure(asked_late, g, exps) for g in range(1, exps)]
    table = jnp.stack(tables).reshape(exps, peers, capacity)

    high, wide = science_img.shape
    gram, frames = normal_matrix(
        slot_of,
        stamp_rows,
        stamp_cols,
        arrived,
        col,
        row_rev,
        science_img,
        variance_img,
        count,
        taps,
    )
    coef, payload = subtract(
        sender,
        gram,
        frames,
        science_img,
        col_t,
        row_rev,
        peers,
        exps,
        capacity,
        count,
        taps,
        stamp_rows.shape[1] * side * side,
    )
    diff_back = lax.all_to_all(payload, ("det", "exp"), split_axis=0, concat_axis=0, tiled=True)
    scored, var_sum = score(
        me[None],
        table,
        slot_of,
        payload,
        down,
        over_rev,
        var_back,
        high,
        wide,
        taps,
        tract,
        part,
        capacity,
    )
    var_template = lax.dynamic_slice_in_dim(template_var, me * part, part, 1)
    mine = combine(me[None], table, diff_back, var_sum, var_template, part, capacity)

    def swap(value, distance):
        return lax.ppermute(value, "exp", [(e, e ^ distance) for e in range(exps)])

    def put(parts, whole):
        places = jnp.stack([there for there, _ in parts])
        return join_parts(places, [held for _, held in parts], whole, exps)

    if exps == 4:
        far = swap(mine, 2)
        near = swap(mine, 1)
        last = swap(far, 1)
        whole = put([(me, mine), (me ^ 1, near), (me ^ 2, far)], None)
        significance = put([(me ^ 3, last)], whole)
    else:
        parts = [(me, mine)]
        for gap in range(1, exps):
            pairs = [(e, (e + gap) % exps) for e in range(exps)]
            parts.append(((me - gap) % exps, lax.ppermute(mine, "exp", pairs)))
        significance = put(parts, None)
    return (significance, scored[None], coef[:, : count + 1])


def solution(mesh):
    placed = (
        P("det", None, None),
        P("det", None, None),
        P("exp", "det", None),
        P("exp", "det", None),
        P("exp", "det"),
        P("exp", "det"),
        P("exp", "det"),
        P("exp", "det"),
        P(),
        P(),
        P("exp", None),
        P("exp", None),
    )
    return jax.shard_map(
        local,
        mesh=mesh,
        in_specs=placed,
        out_specs=(P("det", None, None), P("exp", "det", None), P("exp", "det")),
        check_vma=False,
    )
```

```python
import functools

import jax
import jax.numpy as jnp
from jax import lax
from jax.experimental import pallas as pl
from jax.experimental.pallas import tpu as pltpu
from jax.sharding import PartitionSpec as P

ridge_term = 0.01
bf16 = jnp.bfloat16
f32 = jnp.float32
vmem = functools.partial(pl.BlockSpec, memory_space=pltpu.VMEM)
smem = functools.partial(pl.BlockSpec, memory_space=pltpu.SMEM)
mib = 1024 * 1024
trailer_rows = 8


def up(value, step):
    return -(-value // step) * step


def cost(flops, moved):
    return pl.CostEstimate(flops=flops, bytes_accessed=moved, transcendentals=0)


def distance(here, there, exps):
    if exps & (exps - 1) == 0:
        return here ^ there
    return lax.rem(here - there + exps, exps)


def from_exposure(value, gap, exps):
    if exps & (exps - 1) == 0:
        pairs = [(e, e ^ gap) for e in range(exps)]
    else:
        pairs = [(e, (e + gap) % exps) for e in range(exps)]
    return lax.ppermute(value, "exp", pairs)


def route_body(src, blk, slot_of, sender, request, count, *, peers, capacity):
    def clear_count(p, carry):
        count[p] = 0
        return carry

    def clear_slot(s, carry):
        sender[s] = 0
        request[s // capacity, 0, s % capacity] = 0
        return carry

    lax.fori_loop(0, peers, clear_count, 0, unroll=peers <= 16)
    lax.fori_loop(0, peers * capacity, clear_slot, 0, unroll=peers <= 16)
    for b in range(src.shape[1]):
        owner = src[0, b]
        place = count[owner]
        count[owner] = place + 1
        slot_of[b] = owner * capacity + place
        sender[owner * capacity + place] = b
        request[owner, 0, place] = blk[0, b] + 1


def route_tables(routes_src, routes_blk, peers, capacity):
    return pl.pallas_call(
        functools.partial(route_body, peers=peers, capacity=capacity),
        out_shape=(
            jax.ShapeDtypeStruct((routes_src.shape[1],), jnp.int32),
            jax.ShapeDtypeStruct((peers * capacity,), jnp.int32),
            jax.ShapeDtypeStruct((peers, 1, capacity), jnp.int32),
        ),
        in_specs=[smem()] * 2,
        out_specs=(smem(),) * 3,
        scratch_shapes=[pltpu.SMEM((peers,), jnp.int32)],
        name="route_tables",
    )(routes_src, routes_blk)


def fetch_body(template, near, sem):
    copy = pltpu.make_async_copy(template, near, sem)
    copy.start()
    copy.wait()


def fetch(template):
    return pl.pallas_call(
        fetch_body,
        out_shape=jax.ShapeDtypeStruct(template.shape, template.dtype),
        in_specs=[pl.BlockSpec(memory_space=pl.ANY)],
        out_specs=vmem(),
        scratch_shapes=[pltpu.SemaphoreType.DMA(())],
        compiler_params=pltpu.CompilerParams(vmem_limit_bytes=16 * mib),
        cost_estimate=cost(0, 4_000_000),
        name="fetch",
    )(template)


def pick_body(asked, template, out, sems, *, capacity):
    copies = []
    for s in range(out.shape[0]):
        block = jnp.maximum(asked[s // capacity, 0, s % capacity] - 1, 0)
        copies.append(pltpu.make_async_copy(template.at[block], out.at[s], sems.at[s]))
        copies[-1].start()
    for copy in copies:
        copy.wait()


def pick_blocks(asked, template, slots, capacity):
    return pl.pallas_call(
        functools.partial(pick_body, capacity=capacity),
        out_shape=jax.ShapeDtypeStruct((slots,) + template.shape[1:], template.dtype),
        in_specs=[smem(), vmem()],
        out_specs=pl.BlockSpec(memory_space=pl.ANY),
        scratch_shapes=[pltpu.SemaphoreType.DMA((slots,))],
        compiler_params=pltpu.CompilerParams(vmem_limit_bytes=16 * mib),
        name="pick_blocks",
    )(asked, template)


def store_parts(sender, image, out, side, exps, capacity, across_blocks):
    part = side // exps
    slots = sender.shape[0]

    def one(s, carry):
        b = sender[s]
        top = pl.multiple_of((b // across_blocks) * side, side)
        left = pl.multiple_of((b % across_blocks) * side, side)
        block = image[pl.ds(top, side), pl.ds(left, side)].astype(bf16)
        row = pl.multiple_of((s % capacity) * part, part)
        for q in range(exps):
            out[(s // capacity) * exps + q, pl.ds(row, part), :] = block[q * part : (q + 1) * part]
        return carry

    lax.fori_loop(0, slots, one, 0, unroll=True if slots <= 32 else 4)


def cut(ref, top, left, height, side):
    down = pl.multiple_of((top // 8) * 8, 8)
    over = pl.multiple_of((left // side) * side, side)
    tile = ref[pl.ds(down, height), pl.ds(over, 3 * side)]
    tile = pltpu.roll(tile, lax.rem(3 * side - (left - over), 3 * side), 1)[:, : 2 * side]
    return pltpu.roll(tile, lax.rem(height - (top - down), height), 0)


def hold_body(asked, earlier, out):
    del earlier
    out[...] = asked[...]


def hold(asked, earlier):
    return pl.pallas_call(
        hold_body,
        out_shape=jax.ShapeDtypeStruct(asked.shape, asked.dtype),
        in_specs=[vmem(), pl.BlockSpec(memory_space=pl.ANY)],
        out_specs=vmem(),
        compiler_params=pltpu.CompilerParams(vmem_limit_bytes=16 * mib),
        name="hold",
    )(asked, earlier)


def prepare_body(sender, variance, science, earlier, out, *, side, exps, capacity):
    del earlier, science
    store_parts(sender, variance, out, side, exps, capacity, variance.shape[1] // side)


def prepare(sender, variance, science, earlier, side, exps, capacity):
    slots = sender.shape[0]
    part = side // exps
    return pl.pallas_call(
        functools.partial(prepare_body, side=side, exps=exps, capacity=capacity),
        out_shape=jax.ShapeDtypeStruct((slots // capacity * exps, capacity * part, side), bf16),
        in_specs=[smem()] + [vmem()] * 2 + [pl.BlockSpec(memory_space=pl.ANY)],
        out_specs=vmem(),
        compiler_params=pltpu.CompilerParams(vmem_limit_bytes=16 * mib),
        cost_estimate=cost(0, 6_000_000),
        name="prepare",
    )(sender, variance, science, earlier)


def normal_body(
    slot_of,
    rows_at,
    cols_at,
    arrived,
    col,
    row_rev,
    science,
    variance,
    gram_out,
    windows,
    frame,
    cuts,
    vert,
    design,
    roots,
    window,
    *,
    count,
    across_blocks,
    taps,
):
    side = row_rev.shape[1]
    margin = taps // 2
    stamps = rows_at.shape[1]
    span = up(side + taps - 1, 16)
    padded_k = gram_out.shape[1]
    pitch = (count + 2) | 1
    lines_all = stamps * side
    sub = lax.broadcasted_iota(jnp.int32, (side, side), 0)
    lane = lax.broadcasted_iota(jnp.int32, (side, side), 1)

    high, wide = science.shape
    rows_off = up(margin, 8)
    frame[:rows_off, :] = jnp.zeros((rows_off, frame.shape[1]), f32)
    below = rows_off + high
    frame[below:, :] = jnp.zeros((frame.shape[0] - below, frame.shape[1]), f32)
    frame[rows_off:below, :side] = jnp.zeros((high, side), f32)
    after = side + wide
    frame[rows_off:below, after:] = jnp.zeros((high, frame.shape[1] - after), f32)
    for b in range(slot_of.shape[0]):
        top = rows_off + (b // across_blocks) * side
        left = side + (b % across_blocks) * side
        frame[top : top + side, left : left + side] = arrived[slot_of[b]].astype(f32)
    first_row = rows_off - margin
    first_col = side - margin

    def cut_image(ref, top, left):
        tall = min(high, side + 16)
        down = pl.multiple_of(jnp.minimum((top // 16) * 16, high - tall), 16)
        over = pl.multiple_of(jnp.minimum((left // side) * side, wide - 2 * side), side)
        tile = ref[pl.ds(down, tall), pl.ds(over, 2 * side)].astype(f32)
        tile = pltpu.roll(tile, lax.rem(2 * side - (left - over), 2 * side), 1)[:, :side]
        return pltpu.roll(tile, lax.rem(tall - (top - down), tall), 0)[:side]

    for s in range(stamps):
        top = rows_at[0, s]
        left = cols_at[0, s]
        tile = cut(frame, top + first_row, left + first_col, span, side)
        cuts[s * span : (s + 1) * span, :] = tile.astype(bf16)
        root = lax.rsqrt(cut_image(variance, top, left))
        roots[s * side : (s + 1) * side, :] = root
        place = pl.ds(s * side * pitch + count, side, stride=pitch)
        design[place, :] = root
        place = pl.ds(s * side * pitch + count + 1, side, stride=pitch)
        design[place, :] = root * cut_image(science, top, left)
    design[lines_all * pitch :, :] = jnp.zeros((design.shape[0] - lines_all * pitch, side), f32)

    group = vert.shape[0]
    step = side - taps + 1
    starts = list(range(0, count, group))
    for turn, k in enumerate(starts):
        for c in range(turn, windows.shape[0], len(starts)):
            left = first_col + c * step
            window[...] = frame[first_row : first_row + window.shape[0], left : left + side]
            for parity in range(2):
                place = pl.ds(parity, windows.shape[2], stride=2)
                windows[c, parity] = window[place, :]
        filters = []
        for a in range(group):
            line = jnp.broadcast_to(col[k + a : k + a + 1, :], (side, side))
            line = pltpu.roll(line, 0, 1, stride=1, stride_axis=0)
            first = jnp.where(lane >= sub, line, 0.0).astype(bf16)
            second = jnp.where(lane < sub, line, 0.0).astype(bf16)
            filters.append(jnp.concatenate([first, second[:, : span - side]], axis=1))
        filters = jnp.concatenate(filters, axis=0)
        for s in range(stamps):
            out = jnp.dot(
                filters, cuts[s * span : (s + 1) * span, :], preferred_element_type=f32
            ).astype(bf16)
            for a in range(group):
                vert[a, s * side : (s + 1) * side, :] = out[a * side : (a + 1) * side]
        for a in range(group):
            line = jnp.broadcast_to(row_rev[k + a : k + a + 1, :], (side, side))
            line = pltpu.roll(line, 0, 1, stride=1, stride_axis=0)
            first = jnp.where(lane <= sub, line, 0.0).astype(bf16)
            second = jnp.where(lane > sub, line, 0.0).astype(bf16)
            band = jnp.concatenate([first, second], axis=0)
            out = jnp.dot(vert[a], band, preferred_element_type=f32)
            design[pl.ds(k + a, lines_all, stride=pitch), :] = out * roots[...]

    lines = 16
    sets = 4

    def gram_step(step, total):
        start = pl.multiple_of(step * sets * lines * pitch, 8)
        rows = []
        for g in range(sets):
            row = [
                design[pl.ds(start + (g * lines + j) * pitch, padded_k), :].astype(bf16)
                for j in range(lines)
            ]
            rows.append(jnp.concatenate(row, axis=1))
        both = jnp.concatenate(rows, axis=0)
        return total + lax.dot_general(
            both, both, (((1,), (1,)), ((), ())), preferred_element_type=f32
        )

    total = lax.fori_loop(
        0,
        lines_all // (lines * sets),
        gram_step,
        jnp.zeros((sets * padded_k, sets * padded_k), f32),
        unroll=2,
    )
    part = jnp.zeros((padded_k, padded_k), f32)
    for g in range(sets):
        rows = slice(g * padded_k, (g + 1) * padded_k)
        part = part + total[rows, rows]
    gram_out[...] = part


def subtract_body(
    sender,
    gram,
    frames,
    science,
    col_t,
    row_rev,
    coef_out,
    payload,
    window,
    image,
    bands,
    total,
    stacked,
    *,
    exps,
    capacity,
    count,
    taps,
    pixels,
):
    side = frames.shape[3]
    high, wide = science.shape
    padded_k = gram.shape[1]
    part = side // exps
    size = count + 1

    system = jnp.concatenate(
        [gram[...], jnp.zeros((padded_k, side - padded_k), f32)], axis=1
    ) / pixels
    sub = lax.broadcasted_iota(jnp.int32, (padded_k, side), 0)
    lane = lax.broadcasted_iota(jnp.int32, (padded_k, side), 1)
    system = jnp.where((sub < size) & (lane <= size), system, 0.0)
    system = system + jnp.where((sub == lane) & (sub < size), ridge_term, 0.0)

    pairs = (taps + 2) // 2
    rows_half = high // 2
    wins = frames.shape[0]

    def stack_rows(q):
        for c in range(wins):
            for a in range(2):
                stacked[q, c * rows_half : (c + 1) * rows_half, a * side : (a + 1) * side] = (
                    frames[c, a, q : q + rows_half, :].astype(bf16)
                )

    starts = list(range(0, size, 8))
    for step, k in enumerate(starts):
        for q in range(step, pairs, len(starts)):
            stack_rows(q)
        block = range(min(8, size - k))
        cols = [jnp.broadcast_to(system[:, k + j : k + j + 1], system.shape) for j in block]
        rows = [system[k + j : k + j + 1, :] for j in block]
        core = [[cols[j][k + i : k + i + 1, :] for j in block] for i in block]
        for j in block:
            inverse = 1.0 / core[j][j]
            factor = jnp.where(sub == k + j, 0.0, cols[j] * inverse)
            system = system - factor * rows[j]
            for i in block[j + 1 :]:
                scale = core[i][j] * inverse
                rows[i] = rows[i] - scale * rows[j]
                for l in block[j + 1 :]:
                    core[i][l] = core[i][l] - scale * core[j][l]
                cols[i] = cols[i] - factor * core[j][i]
    pivot = jnp.sum(jnp.where(sub == lane, system, 0.0), axis=1, keepdims=True)
    solved = system[:, size : size + 1] / jnp.where(sub[:, :1] < size, pivot, 1.0)
    coef_out[...] = jnp.sum(jnp.where(sub == lane, solved, 0.0), axis=0, keepdims=True)
    background = solved[count : count + 1, :]
    basis_coef = jnp.where(sub[:, :1] < count, solved, 0.0)

    scaled = basis_coef * row_rev[...]
    kernel = jnp.zeros((col_t.shape[0], side), f32)
    for _ in range(3):
        piece = scaled.astype(bf16)
        scaled = scaled - piece.astype(f32)
        kernel = kernel + jnp.dot(col_t[...], piece, preferred_element_type=f32)
    kernel_sum = jnp.sum(jnp.sum(kernel, axis=1, keepdims=True), axis=0, keepdims=True)
    rounded = kernel.astype(bf16).astype(f32)

    zero_band = jnp.zeros((side, side), bf16)

    def band(i):
        if i < 0 or i >= taps:
            return zero_band
        line = jnp.broadcast_to(rounded[i : i + 1, :], (side, side))
        return pltpu.roll(line, 0, 1, stride=1, stride_axis=0).astype(bf16)

    made = {i: band(i) for i in range(-1, 2 * pairs)}
    for q in range(pairs):
        for a in range(2):
            for b in range(2):
                bands[
                    q * 2 * side + a * side : q * 2 * side + (a + 1) * side,
                    b * side : (b + 1) * side,
                ] = made[2 * q + a - b]

    step = side - taps + 1
    for q in range(pairs):
        out = jnp.dot(
            stacked[q], bands[q * 2 * side : (q + 1) * 2 * side, :], preferred_element_type=f32
        )
        if q:
            out = out + total[...]
        if q < pairs - 1:
            total[...] = out
    for c in range(wins):
        rows = out[c * rows_half : (c + 1) * rows_half]
        window[c, pl.ds(0, rows_half, stride=2), :] = rows[:, :side]
        window[c, pl.ds(1, rows_half, stride=2), :] = rows[:, side:]
        keep = min(step, wide - c * step)
        image[:, c * step : c * step + keep] = window[c, :, :keep]
    image[...] = science[...].astype(f32) - image[...] - background

    store_parts(sender, image, payload, side, exps, capacity, wide // side)
    line_at = lax.broadcasted_iota(jnp.int32, (trailer_rows, side), 0)
    trailer = jnp.zeros((trailer_rows, side), f32)
    rest = kernel_sum
    for p in range(3):
        piece = rest.astype(bf16).astype(f32)
        rest = rest - piece
        trailer = jnp.where(line_at == p, piece, trailer)
    trailer = trailer.astype(bf16)

    def put(d, carry):
        payload[d, capacity * part :, :] = trailer
        return carry

    lax.fori_loop(0, payload.shape[0], put, 0, unroll=4)


def fit_body(
    slot_of,
    sender,
    rows_at,
    cols_at,
    arrived,
    col,
    row_rev,
    science,
    variance,
    col_t,
    coef_out,
    payload,
    *scratch,
    exps,
    capacity,
    count,
    taps,
):
    gram, windows = scratch[:2]
    stamps = rows_at.shape[1]
    side = row_rev.shape[1]
    normal_body(
        slot_of,
        rows_at,
        cols_at,
        arrived,
        col,
        row_rev,
        science,
        variance,
        gram,
        windows,
        *scratch[2:8],
        count=count,
        across_blocks=science.shape[1] // side,
        taps=taps,
    )
    subtract_body(
        sender,
        gram,
        windows,
        science,
        col_t,
        row_rev,
        coef_out,
        payload,
        *scratch[8:],
        exps=exps,
        capacity=capacity,
        count=count,
        taps=taps,
        pixels=stamps * side * side,
    )


def fit_and_subtract(
    slot_of,
    sender,
    rows_at,
    cols_at,
    arrived,
    col,
    row_rev,
    science,
    variance,
    col_t,
    exps,
    capacity,
    count,
    taps,
):
    high, wide = science.shape
    side = row_rev.shape[1]
    slots = sender.shape[0]
    stamps = rows_at.shape[1]
    padded_k = up(count + 2, 16)
    pairs = (taps + 2) // 2
    span = up(side + taps - 1, 16)
    half = up(high // 2 + pairs, 8)
    tall = up(taps // 2, 8) + max(high - side + span, 2 * half)
    wins = -(-wide // (side - taps + 1))
    group = next(g for g in (8, 4, 2, 1) if count % g == 0)
    return pl.pallas_call(
        functools.partial(fit_body, exps=exps, capacity=capacity, count=count, taps=taps),
        out_shape=(
            jax.ShapeDtypeStruct((1, side), f32),
            jax.ShapeDtypeStruct(
                (slots // capacity * exps, capacity * side // exps + trailer_rows, side), bf16
            ),
        ),
        in_specs=[smem()] * 4 + [vmem()] * 6,
        out_specs=(vmem(),) * 2,
        scratch_shapes=[
            pltpu.VMEM((padded_k, padded_k), f32),
            pltpu.VMEM((wins, 2, half, side), f32),
            pltpu.VMEM((tall, wide + 2 * side), f32),
            pltpu.VMEM((stamps * span, 2 * side), bf16),
            pltpu.VMEM((group, stamps * side, 2 * side), bf16),
            pltpu.VMEM((up(stamps * side * ((count + 2) | 1) + padded_k, 8), side), f32),
            pltpu.VMEM((stamps * side, side), f32),
            pltpu.VMEM((2 * half, side), f32),
            pltpu.VMEM((wins, high, side), f32),
            pltpu.VMEM((high, wide), f32),
            pltpu.VMEM((pairs * 2 * side, 2 * side), bf16),
            pltpu.VMEM((wins * high // 2, 2 * side), f32),
            pltpu.VMEM((pairs, wins * high // 2, 2 * side), bf16),
        ],
        compiler_params=pltpu.CompilerParams(vmem_limit_bytes=40 * mib),
        cost_estimate=cost(15_000_000_000, 8_000_000),
        name="fit_and_subtract",
    )(
        slot_of,
        sender,
        rows_at,
        cols_at,
        arrived,
        col,
        row_rev,
        science,
        variance,
        col_t,
    )


def split2(value):
    top = value.astype(bf16)
    return top, (value - top.astype(f32)).astype(bf16)


def score_body(
    me,
    table,
    slot_of,
    payload,
    down,
    over,
    parts,
    out,
    var_out,
    padded,
    sideways,
    var_total,
    *,
    side,
    taps,
    part,
    capacity,
):
    add_variance(me, table, parts, var_out, var_total, part, capacity)
    high, wide = out.shape
    margin = taps // 2
    span = up(side + taps - 1, 16)
    across_blocks = wide // side
    exps = side // part
    padded[...] = jnp.zeros(padded.shape, f32)
    for b in range(slot_of.shape[0]):
        slot = slot_of[b]
        row = pl.multiple_of((slot % capacity) * part, part)
        left = margin + (b % across_blocks) * side
        for q in range(exps):
            top = (b // across_blocks) * side + q * part
            block = payload[(slot // capacity) * exps + q, pl.ds(row, part), :]
            padded[top : top + part, left : left + side] = block.astype(f32)
    line = jnp.broadcast_to(over[...], (2 * side, 2 * side))
    band = pltpu.roll(line, 0, 1, stride=1, stride_axis=0)[:, :side]
    both = jnp.concatenate(split2(band), axis=1)
    sideways[...] = jnp.zeros(sideways.shape, f32)
    for c in range(wide // side):
        window = padded[:, c * side : (c + 2) * side].astype(bf16)
        got = jnp.dot(window, both, preferred_element_type=f32)
        sideways[margin : margin + high, c * side : (c + 1) * side] = got[:, :side] + got[:, side:]
    line = jnp.broadcast_to(down[...], (side, 2 * side))
    band = pltpu.roll(line, 0, 1, stride=1, stride_axis=0)[:, :span]
    top, low = split2(band)
    for r in range(high // side):
        data_top, data_low = split2(sideways[r * side : r * side + span, :])
        got = jnp.dot(top, data_top, preferred_element_type=f32)
        got = got + jnp.dot(top, data_low, preferred_element_type=f32)
        got = got + jnp.dot(low, data_top, preferred_element_type=f32)
        out[r * side : (r + 1) * side, :] = got


def score(
    me, table, slot_of, payload, down, over_rev, parts, high, wide, taps, tract, part, capacity
):
    side = payload.shape[2]
    span = up(side + taps - 1, 16)
    return pl.pallas_call(
        functools.partial(score_body, side=side, taps=taps, part=part, capacity=capacity),
        out_shape=(
            jax.ShapeDtypeStruct((high, wide), f32),
            jax.ShapeDtypeStruct((tract, part, side), f32),
        ),
        in_specs=[smem()] * 3 + [vmem()] * 4,
        out_specs=(vmem(),) * 2,
        scratch_shapes=[
            pltpu.VMEM((high, wide + side), f32),
            pltpu.VMEM((high - side + span, wide), f32),
            pltpu.VMEM((tract + 1, part, side), f32),
        ],
        compiler_params=pltpu.CompilerParams(vmem_limit_bytes=24 * mib),
        cost_estimate=cost(2_000_000_000, 2_000_000),
        name="score",
    )(me, table, slot_of, payload, down, over_rev, parts)


def wanted_block(me, table, d, c, tract):
    exps = table.shape[0]
    block = table[distance(me[0], lax.rem(d, exps), exps), d // exps, c] - 1
    return jnp.where(block < 0, tract, block)


def add_variance(me, table, parts, out, total, part, capacity):
    total[...] = jnp.zeros(total.shape, f32)
    tract = out.shape[0]

    def one(d, carry):
        for c in range(capacity):
            block = wanted_block(me, table, d, c, tract)
            total[block] += parts[d, c * part : (c + 1) * part, :].astype(f32)
        return carry

    lax.fori_loop(0, parts.shape[0], one, 0, unroll=4)
    out[...] = total[:tract]


def combine_body(
    me, table, parts, var_sum, var_template, out, total, gain, *, part, capacity
):
    total[...] = jnp.zeros(total.shape, f32)
    gain[...] = jnp.zeros(gain.shape, f32)
    tract = out.shape[0]

    def one(d, carry):
        tail = parts[d, capacity * part :, :].astype(f32)
        kernel_sum = tail[0:1] + tail[1:2] + tail[2:3]
        square = jnp.broadcast_to(kernel_sum * kernel_sum, gain.shape[1:])
        for c in range(capacity):
            block = wanted_block(me, table, d, c, tract)
            total[block] += parts[d, c * part : (c + 1) * part, :].astype(f32)
            gain[block] += square
        return carry

    lax.fori_loop(0, parts.shape[0], one, 0, unroll=4)
    for t in range(tract):
        variance = var_sum[t] + gain[t, 0:1, :] * var_template[t].astype(f32)
        out[t] = (total[t] * lax.rsqrt(jnp.maximum(variance, 1.0))).astype(bf16)


def combine(me, table, parts, var_sum, var_template, part, capacity):
    tract, _, side = var_sum.shape
    return pl.pallas_call(
        functools.partial(combine_body, part=part, capacity=capacity),
        out_shape=jax.ShapeDtypeStruct((tract, part, side), bf16),
        in_specs=[smem(), smem(), vmem(), vmem(), vmem()],
        out_specs=vmem(),
        scratch_shapes=[
            pltpu.VMEM((tract + 1, part, side), f32),
            pltpu.VMEM((tract + 1, 8, side), f32),
        ],
        compiler_params=pltpu.CompilerParams(vmem_limit_bytes=16 * mib),
        name="combine",
    )(me, table, parts, var_sum, var_template)


def join_body(places, *refs, part, count):
    ins = refs[:count]
    out, held, sems = refs[-3:]
    copies = []
    for d, ref in enumerate(ins):
        held[d] = ref[...].astype(f32)
        row = pl.multiple_of(places[d] * part, part)
        copies.append(
            pltpu.make_async_copy(held.at[d], out.at[:, pl.ds(row, part), :], sems.at[d])
        )
        copies[-1].start()
    for copy in copies:
        copy.wait()


def join_parts(places, parts, whole, exps):
    tract, part, side = parts[0].shape
    count = len(parts)
    fresh = whole is None
    anywhere = pl.BlockSpec(memory_space=pl.ANY)
    return pl.pallas_call(
        functools.partial(join_body, part=part, count=count),
        out_shape=jax.ShapeDtypeStruct((tract, part * exps, side), f32),
        in_specs=[smem()] + [vmem()] * count + ([] if fresh else [anywhere]),
        out_specs=anywhere,
        scratch_shapes=[
            pltpu.VMEM((count, tract, part, side), f32),
            pltpu.SemaphoreType.DMA((count,)),
        ],
        input_output_aliases={} if fresh else {count + 1: 0},
        compiler_params=pltpu.CompilerParams(vmem_limit_bytes=16 * mib),
        cost_estimate=cost(0, 3_000_000 * count),
        name="join_parts",
    )(places, *parts, *([] if fresh else [whole]))


def local(
    template,
    template_var,
    science,
    science_var,
    routes_src,
    routes_blk,
    stamp_rows,
    stamp_cols,
    basis_col,
    basis_row,
    psf_col,
    psf_row,
):
    peers = lax.axis_size("det")
    exps = lax.axis_size("exp")
    me = lax.axis_index("exp").astype(jnp.int32)
    tract, side, _ = template.shape
    science_img = science[0]
    variance_img = science_var[0]
    blocks_dev = routes_src.shape[1]
    count, taps = basis_col.shape
    capacity = max(2, -(-blocks_dev // peers))
    slots = peers * capacity
    part = side // exps

    slot_of, sender, request = route_tables(routes_src, routes_blk, peers, capacity)
    asked = lax.all_to_all(request, "det", split_axis=0, concat_axis=0, tiled=True)
    picked = pick_blocks(asked, fetch(template), slots, capacity)
    held = hold(asked, picked)
    tables = [held] + [from_exposure(held, g, exps) for g in range(1, exps)]
    table = jnp.stack(tables).reshape(exps, peers, capacity)
    var_parts = prepare(sender, variance_img, science_img, table, side, exps, capacity)
    arrived = lax.all_to_all(picked, "det", split_axis=0, concat_axis=0, tiled=True)

    padded_k = up(count + 2, 16)
    col_t = jnp.pad(basis_col.T, ((0, up(taps, 16) - taps), (0, padded_k - count)))
    col = jnp.pad(basis_col.astype(f32), ((0, padded_k - count), (0, side - taps)))
    row_rev = jnp.pad(
        basis_row.astype(f32)[:, ::-1], ((0, padded_k - count), (side - taps, 0))
    )
    row_rev = jnp.roll(row_rev, 1, axis=1)
    over_rev = jnp.roll(jnp.pad(psf_row[:, ::-1], ((0, 0), (2 * side - taps, 0))), 1, axis=1)
    down = jnp.pad(psf_col, ((0, 0), (0, 2 * side - taps)))
    var_late, arrived = lax.optimization_barrier((var_parts, arrived))
    var_back = lax.all_to_all(
        var_late, ("det", "exp"), split_axis=0, concat_axis=0, tiled=True
    )

    high, wide = science_img.shape
    coef, payload = fit_and_subtract(
        slot_of,
        sender,
        stamp_rows,
        stamp_cols,
        arrived,
        col,
        row_rev,
        science_img,
        variance_img,
        col_t,
        exps,
        capacity,
        count,
        taps,
    )
    diff_back = lax.all_to_all(payload, ("det", "exp"), split_axis=0, concat_axis=0, tiled=True)
    scored, var_sum = score(
        me[None],
        table,
        slot_of,
        payload,
        down,
        over_rev,
        var_back,
        high,
        wide,
        taps,
        tract,
        part,
        capacity,
    )
    var_template = lax.dynamic_slice_in_dim(template_var, me * part, part, 1)
    mine = combine(me[None], table, diff_back, var_sum, var_template, part, capacity)

    def swap(value, distance):
        return lax.ppermute(value, "exp", [(e, e ^ distance) for e in range(exps)])

    def put(parts, whole):
        places = jnp.stack([there for there, _ in parts])
        return join_parts(places, [held for _, held in parts], whole, exps)

    if exps == 4:
        far = swap(mine, 2)
        near = swap(mine, 1)
        last = swap(far, 1)
        whole = put([(me, mine), (me ^ 1, near), (me ^ 2, far)], None)
        significance = put([(me ^ 3, last)], whole)
    else:
        parts = [(me, mine)]
        for gap in range(1, exps):
            pairs = [(e, (e + gap) % exps) for e in range(exps)]
            parts.append(((me - gap) % exps, lax.ppermute(mine, "exp", pairs)))
        significance = put(parts, None)
    return (significance, scored[None], coef[:, : count + 1])


def solution(mesh):
    placed = (
        P("det", None, None),
        P("det", None, None),
        P("exp", "det", None),
        P("exp", "det", None),
        P("exp", "det"),
        P("exp", "det"),
        P("exp", "det"),
        P("exp", "det"),
        P(),
        P(),
        P("exp", None),
        P("exp", None),
    )
    return jax.shard_map(
        local,
        mesh=mesh,
        in_specs=placed,
        out_specs=(P("det", None, None), P("exp", "det", None), P("exp", "det")),
        check_vma=False,
    )
```

```python
import functools

import jax
import jax.numpy as jnp
from jax import lax
from jax.experimental import pallas as pl
from jax.experimental.pallas import tpu as pltpu
from jax.sharding import PartitionSpec as P

ridge_term = 0.01
bf16 = jnp.bfloat16
f32 = jnp.float32
vmem = functools.partial(pl.BlockSpec, memory_space=pltpu.VMEM)
smem = functools.partial(pl.BlockSpec, memory_space=pltpu.SMEM)
mib = 1024 * 1024
trailer_rows = 8


def up(value, step):
    return -(-value // step) * step


def cost(flops, moved):
    return pl.CostEstimate(flops=flops, bytes_accessed=moved, transcendentals=0)


def distance(here, there, exps):
    if exps & (exps - 1) == 0:
        return here ^ there
    return lax.rem(here - there + exps, exps)


def from_exposure(value, gap, exps):
    if exps & (exps - 1) == 0:
        pairs = [(e, e ^ gap) for e in range(exps)]
    else:
        pairs = [(e, (e + gap) % exps) for e in range(exps)]
    return lax.ppermute(value, "exp", pairs)


def route_body(src, blk, slot_of, sender, request, count, *, peers, capacity):
    def clear_count(p, carry):
        count[p] = 0
        return carry

    def clear_slot(s, carry):
        sender[s] = 0
        request[s // capacity, 0, s % capacity] = 0
        return carry

    lax.fori_loop(0, peers, clear_count, 0, unroll=peers <= 16)
    lax.fori_loop(0, peers * capacity, clear_slot, 0, unroll=peers <= 16)
    for b in range(src.shape[1]):
        owner = src[0, b]
        place = count[owner]
        count[owner] = place + 1
        slot_of[b] = owner * capacity + place
        sender[owner * capacity + place] = b
        request[owner, 0, place] = blk[0, b] + 1


def route_tables(routes_src, routes_blk, peers, capacity):
    return pl.pallas_call(
        functools.partial(route_body, peers=peers, capacity=capacity),
        out_shape=(
            jax.ShapeDtypeStruct((routes_src.shape[1],), jnp.int32),
            jax.ShapeDtypeStruct((peers * capacity,), jnp.int32),
            jax.ShapeDtypeStruct((peers, 1, capacity), jnp.int32),
        ),
        in_specs=[smem()] * 2,
        out_specs=(smem(),) * 3,
        scratch_shapes=[pltpu.SMEM((peers,), jnp.int32)],
        name="route_tables",
    )(routes_src, routes_blk)


def fetch_body(template, near, sem):
    copy = pltpu.make_async_copy(template, near, sem)
    copy.start()
    copy.wait()


def fetch(template):
    return pl.pallas_call(
        fetch_body,
        out_shape=jax.ShapeDtypeStruct(template.shape, template.dtype),
        in_specs=[pl.BlockSpec(memory_space=pl.ANY)],
        out_specs=vmem(),
        scratch_shapes=[pltpu.SemaphoreType.DMA(())],
        compiler_params=pltpu.CompilerParams(vmem_limit_bytes=16 * mib),
        cost_estimate=cost(0, 4_000_000),
        name="fetch",
    )(template)


def pick_body(asked, template, out, sems, *, capacity):
    copies = []
    for s in range(out.shape[0]):
        block = jnp.maximum(asked[s // capacity, 0, s % capacity] - 1, 0)
        copies.append(pltpu.make_async_copy(template.at[block], out.at[s], sems.at[s]))
        copies[-1].start()
    for copy in copies:
        copy.wait()


def pick_blocks(asked, template, slots, capacity):
    return pl.pallas_call(
        functools.partial(pick_body, capacity=capacity),
        out_shape=jax.ShapeDtypeStruct((slots,) + template.shape[1:], template.dtype),
        in_specs=[smem(), vmem()],
        out_specs=pl.BlockSpec(memory_space=pl.ANY),
        scratch_shapes=[pltpu.SemaphoreType.DMA((slots,))],
        compiler_params=pltpu.CompilerParams(vmem_limit_bytes=16 * mib),
        name="pick_blocks",
    )(asked, template)


def store_parts(sender, image, out, side, exps, capacity, across_blocks):
    part = side // exps
    slots = sender.shape[0]

    def one(s, carry):
        b = sender[s]
        top = pl.multiple_of((b // across_blocks) * side, side)
        left = pl.multiple_of((b % across_blocks) * side, side)
        block = image[pl.ds(top, side), pl.ds(left, side)].astype(bf16)
        row = pl.multiple_of((s % capacity) * part, part)
        for q in range(exps):
            out[(s // capacity) * exps + q, pl.ds(row, part), :] = block[q * part : (q + 1) * part]
        return carry

    lax.fori_loop(0, slots, one, 0, unroll=True if slots <= 32 else 4)


def cut(ref, top, left, height, side):
    down = pl.multiple_of((top // 8) * 8, 8)
    over = pl.multiple_of((left // side) * side, side)
    tile = ref[pl.ds(down, height), pl.ds(over, 3 * side)]
    tile = pltpu.roll(tile, lax.rem(3 * side - (left - over), 3 * side), 1)[:, : 2 * side]
    return pltpu.roll(tile, lax.rem(height - (top - down), height), 0)


def hold_body(asked, earlier, out):
    del earlier
    out[...] = asked[...]


def hold(asked, earlier):
    return pl.pallas_call(
        hold_body,
        out_shape=jax.ShapeDtypeStruct(asked.shape, asked.dtype),
        in_specs=[vmem(), pl.BlockSpec(memory_space=pl.ANY)],
        out_specs=vmem(),
        compiler_params=pltpu.CompilerParams(vmem_limit_bytes=16 * mib),
        name="hold",
    )(asked, earlier)


def prepare_body(sender, variance, science, earlier, out, *, side, exps, capacity):
    del earlier, science
    store_parts(sender, variance, out, side, exps, capacity, variance.shape[1] // side)


def prepare(sender, variance, science, earlier, side, exps, capacity):
    slots = sender.shape[0]
    part = side // exps
    return pl.pallas_call(
        functools.partial(prepare_body, side=side, exps=exps, capacity=capacity),
        out_shape=jax.ShapeDtypeStruct((slots // capacity * exps, capacity * part, side), bf16),
        in_specs=[smem()] + [vmem()] * 2 + [pl.BlockSpec(memory_space=pl.ANY)],
        out_specs=vmem(),
        compiler_params=pltpu.CompilerParams(vmem_limit_bytes=16 * mib),
        cost_estimate=cost(0, 6_000_000),
        name="prepare",
    )(sender, variance, science, earlier)


def normal_body(
    slot_of,
    rows_at,
    cols_at,
    arrived,
    col,
    row_rev,
    science,
    variance,
    gram_out,
    windows,
    frame,
    cuts,
    vert,
    design,
    roots,
    window,
    *,
    count,
    across_blocks,
    taps,
):
    side = row_rev.shape[1]
    margin = taps // 2
    stamps = rows_at.shape[1]
    span = up(side + taps - 1, 16)
    padded_k = gram_out.shape[1]
    pitch = (count + 2) | 1
    lines_all = stamps * side
    sub = lax.broadcasted_iota(jnp.int32, (side, side), 0)
    lane = lax.broadcasted_iota(jnp.int32, (side, side), 1)

    high, wide = science.shape
    rows_off = up(margin, 8)
    frame[:rows_off, :] = jnp.zeros((rows_off, frame.shape[1]), f32)
    below = rows_off + high
    frame[below:, :] = jnp.zeros((frame.shape[0] - below, frame.shape[1]), f32)
    frame[rows_off:below, :side] = jnp.zeros((high, side), f32)
    after = side + wide
    frame[rows_off:below, after:] = jnp.zeros((high, frame.shape[1] - after), f32)
    for b in range(slot_of.shape[0]):
        top = rows_off + (b // across_blocks) * side
        left = side + (b % across_blocks) * side
        frame[top : top + side, left : left + side] = arrived[slot_of[b]].astype(f32)
    first_row = rows_off - margin
    first_col = side - margin

    def cut_image(ref, top, left):
        tall = min(high, side + 16)
        down = pl.multiple_of(jnp.minimum((top // 16) * 16, high - tall), 16)
        over = pl.multiple_of(jnp.minimum((left // side) * side, wide - 2 * side), side)
        tile = ref[pl.ds(down, tall), pl.ds(over, 2 * side)].astype(f32)
        tile = pltpu.roll(tile, lax.rem(2 * side - (left - over), 2 * side), 1)[:, :side]
        return pltpu.roll(tile, lax.rem(tall - (top - down), tall), 0)[:side]

    for s in range(stamps):
        top = rows_at[0, s]
        left = cols_at[0, s]
        tile = cut(frame, top + first_row, left + first_col, span, side)
        cuts[s * span : (s + 1) * span, :] = tile.astype(bf16)
        root = lax.rsqrt(cut_image(variance, top, left))
        roots[s * side : (s + 1) * side, :] = root
        place = pl.ds(s * side * pitch + count, side, stride=pitch)
        design[place, :] = root
        place = pl.ds(s * side * pitch + count + 1, side, stride=pitch)
        design[place, :] = root * cut_image(science, top, left)
    design[lines_all * pitch :, :] = jnp.zeros((design.shape[0] - lines_all * pitch, side), f32)

    group = vert.shape[0]
    step = side - taps + 1
    starts = list(range(0, count, group))
    for turn, k in enumerate(starts):
        for c in range(turn, windows.shape[0], len(starts)):
            left = first_col + c * step
            window[...] = frame[first_row : first_row + window.shape[0], left : left + side]
            for parity in range(2):
                place = pl.ds(parity, windows.shape[2], stride=2)
                windows[c, parity] = window[place, :]
        filters = []
        for a in range(group):
            line = jnp.broadcast_to(col[k + a : k + a + 1, :], (side, side))
            line = pltpu.roll(line, 0, 1, stride=1, stride_axis=0)
            first = jnp.where(lane >= sub, line, 0.0).astype(bf16)
            second = jnp.where(lane < sub, line, 0.0).astype(bf16)
            filters.append(jnp.concatenate([first, second[:, : span - side]], axis=1))
        filters = jnp.concatenate(filters, axis=0)
        for s in range(stamps):
            out = jnp.dot(
                filters, cuts[s * span : (s + 1) * span, :], preferred_element_type=f32
            ).astype(bf16)
            for a in range(group):
                vert[a, s * side : (s + 1) * side, :] = out[a * side : (a + 1) * side]
        for a in range(group):
            line = jnp.broadcast_to(row_rev[k + a : k + a + 1, :], (side, side))
            line = pltpu.roll(line, 0, 1, stride=1, stride_axis=0)
            first = jnp.where(lane <= sub, line, 0.0).astype(bf16)
            second = jnp.where(lane > sub, line, 0.0).astype(bf16)
            band = jnp.concatenate([first, second], axis=0)
            out = jnp.dot(vert[a], band, preferred_element_type=f32)
            design[pl.ds(k + a, lines_all, stride=pitch), :] = out * roots[...]

    lines = 16
    sets = 4

    def gram_step(step, total):
        start = pl.multiple_of(step * sets * lines * pitch, 8)
        rows = []
        for g in range(sets):
            row = [
                design[pl.ds(start + (g * lines + j) * pitch, padded_k), :].astype(bf16)
                for j in range(lines)
            ]
            rows.append(jnp.concatenate(row, axis=1))
        both = jnp.concatenate(rows, axis=0)
        return total + lax.dot_general(
            both, both, (((1,), (1,)), ((), ())), preferred_element_type=f32
        )

    total = lax.fori_loop(
        0,
        lines_all // (lines * sets),
        gram_step,
        jnp.zeros((sets * padded_k, sets * padded_k), f32),
        unroll=2,
    )
    part = jnp.zeros((padded_k, padded_k), f32)
    for g in range(sets):
        rows = slice(g * padded_k, (g + 1) * padded_k)
        part = part + total[rows, rows]
    gram_out[...] = part


def subtract_body(
    sender,
    gram,
    frames,
    science,
    col_t,
    row_rev,
    coef_out,
    payload,
    window,
    image,
    bands,
    total,
    *,
    exps,
    capacity,
    count,
    taps,
    pixels,
):
    side = frames.shape[3]
    high, wide = science.shape
    padded_k = gram.shape[1]
    part = side // exps
    size = count + 1

    system = jnp.concatenate(
        [gram[...], jnp.zeros((padded_k, side - padded_k), f32)], axis=1
    ) / pixels
    sub = lax.broadcasted_iota(jnp.int32, (padded_k, side), 0)
    lane = lax.broadcasted_iota(jnp.int32, (padded_k, side), 1)
    system = jnp.where((sub < size) & (lane <= size), system, 0.0)
    system = system + jnp.where((sub == lane) & (sub < size), ridge_term, 0.0)

    pairs = (taps + 2) // 2
    rows_half = high // 2
    wins = frames.shape[0]

    for k in range(0, size, 8):
        block = range(min(8, size - k))
        cols = [jnp.broadcast_to(system[:, k + j : k + j + 1], system.shape) for j in block]
        rows = [system[k + j : k + j + 1, :] for j in block]
        core = [[cols[j][k + i : k + i + 1, :] for j in block] for i in block]
        for j in block:
            inverse = 1.0 / core[j][j]
            factor = jnp.where(sub == k + j, 0.0, cols[j] * inverse)
            system = system - factor * rows[j]
            for i in block[j + 1 :]:
                scale = core[i][j] * inverse
                rows[i] = rows[i] - scale * rows[j]
                for l in block[j + 1 :]:
                    core[i][l] = core[i][l] - scale * core[j][l]
                cols[i] = cols[i] - factor * core[j][i]
    pivot = jnp.sum(jnp.where(sub == lane, system, 0.0), axis=1, keepdims=True)
    solved = system[:, size : size + 1] / jnp.where(sub[:, :1] < size, pivot, 1.0)
    coef_out[...] = jnp.sum(jnp.where(sub == lane, solved, 0.0), axis=0, keepdims=True)
    background = solved[count : count + 1, :]
    basis_coef = jnp.where(sub[:, :1] < count, solved, 0.0)

    scaled = basis_coef * row_rev[...]
    kernel = jnp.zeros((col_t.shape[0], side), f32)
    for _ in range(3):
        piece = scaled.astype(bf16)
        scaled = scaled - piece.astype(f32)
        kernel = kernel + jnp.dot(col_t[...], piece, preferred_element_type=f32)
    kernel_sum = jnp.sum(jnp.sum(kernel, axis=1, keepdims=True), axis=0, keepdims=True)
    rounded = kernel.astype(bf16).astype(f32)

    zero_band = jnp.zeros((side, side), bf16)

    def band(i):
        if i < 0 or i >= taps:
            return zero_band
        line = jnp.broadcast_to(rounded[i : i + 1, :], (side, side))
        return pltpu.roll(line, 0, 1, stride=1, stride_axis=0).astype(bf16)

    made = {i: band(i) for i in range(-1, 2 * pairs)}
    for q in range(pairs):
        for a in range(2):
            for b in range(2):
                bands[
                    q * 2 * side + a * side : q * 2 * side + (a + 1) * side,
                    b * side : (b + 1) * side,
                ] = made[2 * q + a - b]

    step = side - taps + 1
    for q in range(pairs):
        lhs = jnp.concatenate(
            [
                jnp.concatenate(
                    [frames[c, a, q : q + rows_half, :].astype(bf16) for a in range(2)], axis=1
                )
                for c in range(wins)
            ],
            axis=0,
        )
        out = jnp.dot(
            lhs, bands[q * 2 * side : (q + 1) * 2 * side, :], preferred_element_type=f32
        )
        if q:
            out = out + total[...]
        if q < pairs - 1:
            total[...] = out
    for c in range(wins):
        rows = out[c * rows_half : (c + 1) * rows_half]
        window[c, pl.ds(0, rows_half, stride=2), :] = rows[:, :side]
        window[c, pl.ds(1, rows_half, stride=2), :] = rows[:, side:]
        keep = min(step, wide - c * step)
        image[:, c * step : c * step + keep] = window[c, :, :keep]
    image[...] = science[...].astype(f32) - image[...] - background

    store_parts(sender, image, payload, side, exps, capacity, wide // side)
    line_at = lax.broadcasted_iota(jnp.int32, (trailer_rows, side), 0)
    trailer = jnp.zeros((trailer_rows, side), f32)
    rest = kernel_sum
    for p in range(3):
        piece = rest.astype(bf16).astype(f32)
        rest = rest - piece
        trailer = jnp.where(line_at == p, piece, trailer)
    trailer = trailer.astype(bf16)

    def put(d, carry):
        payload[d, capacity * part :, :] = trailer
        return carry

    lax.fori_loop(0, payload.shape[0], put, 0, unroll=4)


def fit_body(
    slot_of,
    sender,
    rows_at,
    cols_at,
    arrived,
    col,
    row_rev,
    science,
    variance,
    col_t,
    coef_out,
    payload,
    *scratch,
    exps,
    capacity,
    count,
    taps,
):
    gram, windows = scratch[:2]
    stamps = rows_at.shape[1]
    side = row_rev.shape[1]
    normal_body(
        slot_of,
        rows_at,
        cols_at,
        arrived,
        col,
        row_rev,
        science,
        variance,
        gram,
        windows,
        *scratch[2:8],
        count=count,
        across_blocks=science.shape[1] // side,
        taps=taps,
    )
    subtract_body(
        sender,
        gram,
        windows,
        science,
        col_t,
        row_rev,
        coef_out,
        payload,
        *scratch[8:],
        exps=exps,
        capacity=capacity,
        count=count,
        taps=taps,
        pixels=stamps * side * side,
    )


def fit_and_subtract(
    slot_of,
    sender,
    rows_at,
    cols_at,
    arrived,
    col,
    row_rev,
    science,
    variance,
    col_t,
    exps,
    capacity,
    count,
    taps,
):
    high, wide = science.shape
    side = row_rev.shape[1]
    slots = sender.shape[0]
    stamps = rows_at.shape[1]
    padded_k = up(count + 2, 16)
    pairs = (taps + 2) // 2
    span = up(side + taps - 1, 16)
    half = up(high // 2 + pairs, 8)
    tall = up(taps // 2, 8) + max(high - side + span, 2 * half)
    wins = -(-wide // (side - taps + 1))
    group = next(g for g in (8, 4, 2, 1) if count % g == 0)
    return pl.pallas_call(
        functools.partial(fit_body, exps=exps, capacity=capacity, count=count, taps=taps),
        out_shape=(
            jax.ShapeDtypeStruct((1, side), f32),
            jax.ShapeDtypeStruct(
                (slots // capacity * exps, capacity * side // exps + trailer_rows, side), bf16
            ),
        ),
        in_specs=[smem()] * 4 + [vmem()] * 6,
        out_specs=(vmem(),) * 2,
        scratch_shapes=[
            pltpu.VMEM((padded_k, padded_k), f32),
            pltpu.VMEM((wins, 2, half, side), f32),
            pltpu.VMEM((tall, wide + 2 * side), f32),
            pltpu.VMEM((stamps * span, 2 * side), bf16),
            pltpu.VMEM((group, stamps * side, 2 * side), bf16),
            pltpu.VMEM((up(stamps * side * ((count + 2) | 1) + padded_k, 8), side), f32),
            pltpu.VMEM((stamps * side, side), f32),
            pltpu.VMEM((2 * half, side), f32),
            pltpu.VMEM((wins, high, side), f32),
            pltpu.VMEM((high, wide), f32),
            pltpu.VMEM((pairs * 2 * side, 2 * side), bf16),
            pltpu.VMEM((wins * high // 2, 2 * side), f32),
        ],
        compiler_params=pltpu.CompilerParams(vmem_limit_bytes=30 * mib),
        cost_estimate=cost(15_000_000_000, 8_000_000),
        name="fit_and_subtract",
    )(
        slot_of,
        sender,
        rows_at,
        cols_at,
        arrived,
        col,
        row_rev,
        science,
        variance,
        col_t,
    )


def split2(value):
    top = value.astype(bf16)
    return top, (value - top.astype(f32)).astype(bf16)


def score_body(
    me,
    table,
    slot_of,
    payload,
    down,
    over,
    parts,
    template_var,
    out,
    var_out,
    var_template,
    padded,
    sideways,
    var_total,
    sem,
    *,
    side,
    taps,
    part,
    capacity,
):
    mine = pl.ds(pl.multiple_of(me[0] * part, part), part)
    copy = pltpu.make_async_copy(template_var.at[:, mine, :], var_template, sem)
    copy.start()
    add_variance(me, table, parts, var_out, var_total, part, capacity)
    high, wide = out.shape
    margin = taps // 2
    span = up(side + taps - 1, 16)
    across_blocks = wide // side
    exps = side // part
    padded[...] = jnp.zeros(padded.shape, f32)
    for b in range(slot_of.shape[0]):
        slot = slot_of[b]
        row = pl.multiple_of((slot % capacity) * part, part)
        left = margin + (b % across_blocks) * side
        for q in range(exps):
            top = (b // across_blocks) * side + q * part
            block = payload[(slot // capacity) * exps + q, pl.ds(row, part), :]
            padded[top : top + part, left : left + side] = block.astype(f32)
    line = jnp.broadcast_to(over[...], (2 * side, 2 * side))
    band = pltpu.roll(line, 0, 1, stride=1, stride_axis=0)[:, :side]
    both = jnp.concatenate(split2(band), axis=1)
    sideways[...] = jnp.zeros(sideways.shape, f32)
    for c in range(wide // side):
        window = padded[:, c * side : (c + 2) * side].astype(bf16)
        got = jnp.dot(window, both, preferred_element_type=f32)
        sideways[margin : margin + high, c * side : (c + 1) * side] = got[:, :side] + got[:, side:]
    line = jnp.broadcast_to(down[...], (side, 2 * side))
    band = pltpu.roll(line, 0, 1, stride=1, stride_axis=0)[:, :span]
    top, low = split2(band)
    for r in range(high // side):
        data_top, data_low = split2(sideways[r * side : r * side + span, :])
        got = jnp.dot(top, data_top, preferred_element_type=f32)
        got = got + jnp.dot(top, data_low, preferred_element_type=f32)
        got = got + jnp.dot(low, data_top, preferred_element_type=f32)
        out[r * side : (r + 1) * side, :] = got
    copy.wait()


def score(
    me, table, slot_of, payload, down, over_rev, parts, template_var, high, wide, taps, capacity
):
    tract, side, _ = template_var.shape
    part = parts.shape[1] // capacity
    span = up(side + taps - 1, 16)
    return pl.pallas_call(
        functools.partial(score_body, side=side, taps=taps, part=part, capacity=capacity),
        out_shape=(
            jax.ShapeDtypeStruct((high, wide), f32),
            jax.ShapeDtypeStruct((tract, part, side), f32),
            jax.ShapeDtypeStruct((tract, part, side), template_var.dtype),
        ),
        in_specs=[smem()] * 3 + [vmem()] * 4 + [pl.BlockSpec(memory_space=pl.ANY)],
        out_specs=(vmem(),) * 3,
        scratch_shapes=[
            pltpu.VMEM((high, wide + side), f32),
            pltpu.VMEM((high - side + span, wide), f32),
            pltpu.VMEM((tract + 1, part, side), f32),
            pltpu.SemaphoreType.DMA(()),
        ],
        compiler_params=pltpu.CompilerParams(vmem_limit_bytes=20 * mib),
        cost_estimate=cost(2_000_000_000, 2_000_000),
        name="score",
    )(me, table, slot_of, payload, down, over_rev, parts, template_var)


def wanted_block(me, table, d, c, tract):
    exps = table.shape[0]
    block = table[distance(me[0], lax.rem(d, exps), exps), d // exps, c] - 1
    return jnp.where(block < 0, tract, block)


def add_variance(me, table, parts, out, total, part, capacity):
    total[...] = jnp.zeros(total.shape, f32)
    tract = out.shape[0]

    def one(d, carry):
        for c in range(capacity):
            block = wanted_block(me, table, d, c, tract)
            total[block] += parts[d, c * part : (c + 1) * part, :].astype(f32)
        return carry

    lax.fori_loop(0, parts.shape[0], one, 0, unroll=4)
    out[...] = total[:tract]


def combine_body(
    me, table, parts, var_sum, var_template, out, total, gain, *, part, capacity
):
    total[...] = jnp.zeros(total.shape, f32)
    gain[...] = jnp.zeros(gain.shape, f32)
    tract = out.shape[0]

    def one(d, carry):
        tail = parts[d, capacity * part :, :].astype(f32)
        kernel_sum = tail[0:1] + tail[1:2] + tail[2:3]
        square = jnp.broadcast_to(kernel_sum * kernel_sum, gain.shape[1:])
        for c in range(capacity):
            block = wanted_block(me, table, d, c, tract)
            total[block] += parts[d, c * part : (c + 1) * part, :].astype(f32)
            gain[block] += square
        return carry

    lax.fori_loop(0, parts.shape[0], one, 0, unroll=4)
    for t in range(tract):
        variance = var_sum[t] + gain[t, 0:1, :] * var_template[t].astype(f32)
        out[t] = (total[t] * lax.rsqrt(jnp.maximum(variance, 1.0))).astype(bf16)


def combine(me, table, parts, var_sum, var_template, part, capacity):
    tract, _, side = var_sum.shape
    return pl.pallas_call(
        functools.partial(combine_body, part=part, capacity=capacity),
        out_shape=jax.ShapeDtypeStruct((tract, part, side), bf16),
        in_specs=[smem(), smem(), vmem(), vmem(), vmem()],
        out_specs=vmem(),
        scratch_shapes=[
            pltpu.VMEM((tract + 1, part, side), f32),
            pltpu.VMEM((tract + 1, 8, side), f32),
        ],
        compiler_params=pltpu.CompilerParams(vmem_limit_bytes=16 * mib),
        name="combine",
    )(me, table, parts, var_sum, var_template)


def join_body(places, *refs, part, count):
    ins = refs[:count]
    out, held, sems = refs[-3:]
    copies = []
    for d, ref in enumerate(ins):
        held[d] = ref[...].astype(f32)
        row = pl.multiple_of(places[d] * part, part)
        copies.append(
            pltpu.make_async_copy(held.at[d], out.at[:, pl.ds(row, part), :], sems.at[d])
        )
        copies[-1].start()
    for copy in copies:
        copy.wait()


def join_parts(places, parts, whole, exps):
    tract, part, side = parts[0].shape
    count = len(parts)
    fresh = whole is None
    anywhere = pl.BlockSpec(memory_space=pl.ANY)
    return pl.pallas_call(
        functools.partial(join_body, part=part, count=count),
        out_shape=jax.ShapeDtypeStruct((tract, part * exps, side), f32),
        in_specs=[smem()] + [vmem()] * count + ([] if fresh else [anywhere]),
        out_specs=anywhere,
        scratch_shapes=[
            pltpu.VMEM((count, tract, part, side), f32),
            pltpu.SemaphoreType.DMA((count,)),
        ],
        input_output_aliases={} if fresh else {count + 1: 0},
        compiler_params=pltpu.CompilerParams(vmem_limit_bytes=16 * mib),
        cost_estimate=cost(0, 3_000_000 * count),
        name="join_parts",
    )(places, *parts, *([] if fresh else [whole]))


def local(
    template,
    template_var,
    science,
    science_var,
    routes_src,
    routes_blk,
    stamp_rows,
    stamp_cols,
    basis_col,
    basis_row,
    psf_col,
    psf_row,
):
    peers = lax.axis_size("det")
    exps = lax.axis_size("exp")
    me = lax.axis_index("exp").astype(jnp.int32)
    tract, side, _ = template.shape
    science_img = science[0]
    variance_img = science_var[0]
    blocks_dev = routes_src.shape[1]
    count, taps = basis_col.shape
    capacity = max(2, -(-blocks_dev // peers))
    slots = peers * capacity
    part = side // exps

    slot_of, sender, request = route_tables(routes_src, routes_blk, peers, capacity)
    asked = lax.all_to_all(request, "det", split_axis=0, concat_axis=0, tiled=True)
    picked = pick_blocks(asked, fetch(template), slots, capacity)
    held = hold(asked, picked)
    tables = [held] + [from_exposure(held, g, exps) for g in range(1, exps)]
    table = jnp.stack(tables).reshape(exps, peers, capacity)
    var_parts = prepare(sender, variance_img, science_img, table, side, exps, capacity)
    arrived = lax.all_to_all(picked, "det", split_axis=0, concat_axis=0, tiled=True)

    padded_k = up(count + 2, 16)
    col_t = jnp.pad(basis_col.T, ((0, up(taps, 16) - taps), (0, padded_k - count)))
    col = jnp.pad(basis_col.astype(f32), ((0, padded_k - count), (0, side - taps)))
    row_rev = jnp.pad(
        basis_row.astype(f32)[:, ::-1], ((0, padded_k - count), (side - taps, 0))
    )
    row_rev = jnp.roll(row_rev, 1, axis=1)
    over_rev = jnp.roll(jnp.pad(psf_row[:, ::-1], ((0, 0), (2 * side - taps, 0))), 1, axis=1)
    down = jnp.pad(psf_col, ((0, 0), (0, 2 * side - taps)))
    var_late, arrived = lax.optimization_barrier((var_parts, arrived))
    var_back = lax.all_to_all(
        var_late, ("det", "exp"), split_axis=0, concat_axis=0, tiled=True
    )

    high, wide = science_img.shape
    coef, payload = fit_and_subtract(
        slot_of,
        sender,
        stamp_rows,
        stamp_cols,
        arrived,
        col,
        row_rev,
        science_img,
        variance_img,
        col_t,
        exps,
        capacity,
        count,
        taps,
    )
    diff_back = lax.all_to_all(payload, ("det", "exp"), split_axis=0, concat_axis=0, tiled=True)
    scored, var_sum, var_template = score(
        me[None],
        table,
        slot_of,
        payload,
        down,
        over_rev,
        var_back,
        template_var,
        high,
        wide,
        taps,
        capacity,
    )
    mine = combine(me[None], table, diff_back, var_sum, var_template, part, capacity)

    def swap(value, distance):
        return lax.ppermute(value, "exp", [(e, e ^ distance) for e in range(exps)])

    def put(parts, whole):
        places = jnp.stack([there for there, _ in parts])
        return join_parts(places, [held for _, held in parts], whole, exps)

    if exps == 4:
        far = swap(mine, 2)
        near = swap(mine, 1)
        last = swap(far, 1)
        whole = put([(me, mine), (me ^ 1, near), (me ^ 2, far)], None)
        significance = put([(me ^ 3, last)], whole)
    else:
        parts = [(me, mine)]
        for gap in range(1, exps):
            pairs = [(e, (e + gap) % exps) for e in range(exps)]
            parts.append(((me - gap) % exps, lax.ppermute(mine, "exp", pairs)))
        significance = put(parts, None)
    return (significance, scored[None], coef[:, : count + 1])


def solution(mesh):
    placed = (
        P("det", None, None),
        P("det", None, None),
        P("exp", "det", None),
        P("exp", "det", None),
        P("exp", "det"),
        P("exp", "det"),
        P("exp", "det"),
        P("exp", "det"),
        P(),
        P(),
        P("exp", None),
        P("exp", None),
    )
    return jax.shard_map(
        local,
        mesh=mesh,
        in_specs=placed,
        out_specs=(P("det", None, None), P("exp", "det", None), P("exp", "det")),
        check_vma=False,
    )
```

```python
import functools

import jax
import jax.numpy as jnp
from jax import lax
from jax.experimental import pallas as pl
from jax.experimental.pallas import tpu as pltpu
from jax.sharding import PartitionSpec as P

ridge_term = 0.01
bf16 = jnp.bfloat16
f32 = jnp.float32
vmem = functools.partial(pl.BlockSpec, memory_space=pltpu.VMEM)
smem = functools.partial(pl.BlockSpec, memory_space=pltpu.SMEM)
mib = 1024 * 1024
trailer_rows = 8


def up(value, step):
    return -(-value // step) * step


def cost(flops, moved):
    return pl.CostEstimate(flops=flops, bytes_accessed=moved, transcendentals=0)


exposure_axes = ("far", "near")


def part_of(exposure, exps, nears):
    return lax.rem(exposure, nears) * (exps // nears) + exposure // nears


def distance(here, there, exps):
    if exps & (exps - 1) == 0:
        return here ^ there
    return lax.rem(here - there + exps, exps)


def from_exposure(value, gap, exps):
    if exps & (exps - 1) == 0:
        pairs = [(e, e ^ gap) for e in range(exps)]
    else:
        pairs = [(e, (e + gap) % exps) for e in range(exps)]
    return lax.ppermute(value, exposure_axes, pairs)


def route_body(src, blk, slot_of, sender, request, count, *, peers, capacity):
    def clear_count(p, carry):
        count[p] = 0
        return carry

    def clear_slot(s, carry):
        sender[s] = 0
        request[s // capacity, 0, s % capacity] = 0
        return carry

    lax.fori_loop(0, peers, clear_count, 0, unroll=peers <= 16)
    lax.fori_loop(0, peers * capacity, clear_slot, 0, unroll=peers <= 16)
    for b in range(src.shape[1]):
        owner = src[0, b]
        place = count[owner]
        count[owner] = place + 1
        slot_of[b] = owner * capacity + place
        sender[owner * capacity + place] = b
        request[owner, 0, place] = blk[0, b] + 1


def route_tables(routes_src, routes_blk, peers, capacity):
    return pl.pallas_call(
        functools.partial(route_body, peers=peers, capacity=capacity),
        out_shape=(
            jax.ShapeDtypeStruct((routes_src.shape[1],), jnp.int32),
            jax.ShapeDtypeStruct((peers * capacity,), jnp.int32),
            jax.ShapeDtypeStruct((peers, 1, capacity), jnp.int32),
        ),
        in_specs=[smem()] * 2,
        out_specs=(smem(),) * 3,
        scratch_shapes=[pltpu.SMEM((peers,), jnp.int32)],
        name="route_tables",
    )(routes_src, routes_blk)


def fetch_body(template, near, sem):
    copy = pltpu.make_async_copy(template, near, sem)
    copy.start()
    copy.wait()


def fetch(template):
    return pl.pallas_call(
        fetch_body,
        out_shape=jax.ShapeDtypeStruct(template.shape, template.dtype),
        in_specs=[pl.BlockSpec(memory_space=pl.ANY)],
        out_specs=vmem(),
        scratch_shapes=[pltpu.SemaphoreType.DMA(())],
        compiler_params=pltpu.CompilerParams(vmem_limit_bytes=16 * mib),
        cost_estimate=cost(0, 4_000_000),
        name="fetch",
    )(template)


def pick_body(asked, template, out, sems, *, capacity):
    copies = []
    for s in range(out.shape[0]):
        block = jnp.maximum(asked[s // capacity, 0, s % capacity] - 1, 0)
        copies.append(pltpu.make_async_copy(template.at[block], out.at[s], sems.at[s]))
        copies[-1].start()
    for copy in copies:
        copy.wait()


def pick_blocks(asked, template, slots, capacity):
    return pl.pallas_call(
        functools.partial(pick_body, capacity=capacity),
        out_shape=jax.ShapeDtypeStruct((slots,) + template.shape[1:], template.dtype),
        in_specs=[smem(), vmem()],
        out_specs=pl.BlockSpec(memory_space=pl.ANY),
        scratch_shapes=[pltpu.SemaphoreType.DMA((slots,))],
        compiler_params=pltpu.CompilerParams(vmem_limit_bytes=16 * mib),
        name="pick_blocks",
    )(asked, template)


def store_parts(sender, image, out, side, order, capacity, across_blocks):
    exps = len(order)
    part = side // exps
    slots = sender.shape[0]

    def one(s, carry):
        b = sender[s]
        top = pl.multiple_of((b // across_blocks) * side, side)
        left = pl.multiple_of((b % across_blocks) * side, side)
        block = image[pl.ds(top, side), pl.ds(left, side)].astype(bf16)
        row = pl.multiple_of((s % capacity) * part, part)
        for e, q in enumerate(order):
            out[(s // capacity) * exps + e, pl.ds(row, part), :] = block[q * part : (q + 1) * part]
        return carry

    lax.fori_loop(0, slots, one, 0, unroll=True if slots <= 32 else 4)


def cut(ref, top, left, height, side):
    down = pl.multiple_of((top // 8) * 8, 8)
    over = pl.multiple_of((left // side) * side, side)
    tile = ref[pl.ds(down, height), pl.ds(over, 3 * side)]
    tile = pltpu.roll(tile, lax.rem(3 * side - (left - over), 3 * side), 1)[:, : 2 * side]
    return pltpu.roll(tile, lax.rem(height - (top - down), height), 0)


def hold_body(asked, earlier, out):
    del earlier
    out[...] = asked[...]


def hold(asked, earlier):
    return pl.pallas_call(
        hold_body,
        out_shape=jax.ShapeDtypeStruct(asked.shape, asked.dtype),
        in_specs=[vmem(), pl.BlockSpec(memory_space=pl.ANY)],
        out_specs=vmem(),
        compiler_params=pltpu.CompilerParams(vmem_limit_bytes=16 * mib),
        name="hold",
    )(asked, earlier)


def prepare_body(sender, variance, science, earlier, out, *, side, nears, capacity):
    del earlier, science
    store_parts(sender, variance, out, side, range(nears), capacity, variance.shape[1] // side)


def prepare(sender, variance, science, earlier, side, nears, capacity):
    slots = sender.shape[0]
    part = side // nears
    return pl.pallas_call(
        functools.partial(prepare_body, side=side, nears=nears, capacity=capacity),
        out_shape=jax.ShapeDtypeStruct((slots // capacity * nears, capacity * part, side), bf16),
        in_specs=[smem()] + [vmem()] * 2 + [pl.BlockSpec(memory_space=pl.ANY)],
        out_specs=vmem(),
        compiler_params=pltpu.CompilerParams(vmem_limit_bytes=16 * mib),
        cost_estimate=cost(0, 6_000_000),
        name="prepare",
    )(sender, variance, science, earlier)


def normal_body(
    slot_of,
    rows_at,
    cols_at,
    arrived,
    col,
    row_rev,
    science,
    variance,
    gram_out,
    windows,
    frame,
    cuts,
    vert,
    design,
    roots,
    window,
    *,
    count,
    across_blocks,
    taps,
):
    side = row_rev.shape[1]
    margin = taps // 2
    stamps = rows_at.shape[1]
    span = up(side + taps - 1, 16)
    padded_k = gram_out.shape[1]
    pitch = (count + 2) | 1
    lines_all = stamps * side
    sub = lax.broadcasted_iota(jnp.int32, (side, side), 0)
    lane = lax.broadcasted_iota(jnp.int32, (side, side), 1)

    high, wide = science.shape
    rows_off = up(margin, 8)
    frame[:rows_off, :] = jnp.zeros((rows_off, frame.shape[1]), f32)
    below = rows_off + high
    frame[below:, :] = jnp.zeros((frame.shape[0] - below, frame.shape[1]), f32)
    frame[rows_off:below, :side] = jnp.zeros((high, side), f32)
    after = side + wide
    frame[rows_off:below, after:] = jnp.zeros((high, frame.shape[1] - after), f32)
    for b in range(slot_of.shape[0]):
        top = rows_off + (b // across_blocks) * side
        left = side + (b % across_blocks) * side
        frame[top : top + side, left : left + side] = arrived[slot_of[b]].astype(f32)
    first_row = rows_off - margin
    first_col = side - margin

    def cut_image(ref, top, left):
        tall = min(high, side + 16)
        down = pl.multiple_of(jnp.minimum((top // 16) * 16, high - tall), 16)
        over = pl.multiple_of(jnp.minimum((left // side) * side, wide - 2 * side), side)
        tile = ref[pl.ds(down, tall), pl.ds(over, 2 * side)].astype(f32)
        tile = pltpu.roll(tile, lax.rem(2 * side - (left - over), 2 * side), 1)[:, :side]
        return pltpu.roll(tile, lax.rem(tall - (top - down), tall), 0)[:side]

    for s in range(stamps):
        top = rows_at[0, s]
        left = cols_at[0, s]
        tile = cut(frame, top + first_row, left + first_col, span, side)
        cuts[s * span : (s + 1) * span, :] = tile.astype(bf16)
        root = lax.rsqrt(cut_image(variance, top, left))
        roots[s * side : (s + 1) * side, :] = root
        place = pl.ds(s * side * pitch + count, side, stride=pitch)
        design[place, :] = root
        place = pl.ds(s * side * pitch + count + 1, side, stride=pitch)
        design[place, :] = root * cut_image(science, top, left)
    design[lines_all * pitch :, :] = jnp.zeros((design.shape[0] - lines_all * pitch, side), f32)

    group = vert.shape[0]
    step = side - taps + 1
    starts = list(range(0, count, group))
    for turn, k in enumerate(starts):
        for c in range(turn, windows.shape[0], len(starts)):
            left = first_col + c * step
            window[...] = frame[first_row : first_row + window.shape[0], left : left + side]
            for parity in range(2):
                place = pl.ds(parity, windows.shape[2], stride=2)
                windows[c, parity] = window[place, :]
        filters = []
        for a in range(group):
            line = jnp.broadcast_to(col[k + a : k + a + 1, :], (side, side))
            line = pltpu.roll(line, 0, 1, stride=1, stride_axis=0)
            first = jnp.where(lane >= sub, line, 0.0).astype(bf16)
            second = jnp.where(lane < sub, line, 0.0).astype(bf16)
            filters.append(jnp.concatenate([first, second[:, : span - side]], axis=1))
        filters = jnp.concatenate(filters, axis=0)
        for s in range(stamps):
            out = jnp.dot(
                filters, cuts[s * span : (s + 1) * span, :], preferred_element_type=f32
            ).astype(bf16)
            for a in range(group):
                vert[a, s * side : (s + 1) * side, :] = out[a * side : (a + 1) * side]
        for a in range(group):
            line = jnp.broadcast_to(row_rev[k + a : k + a + 1, :], (side, side))
            line = pltpu.roll(line, 0, 1, stride=1, stride_axis=0)
            first = jnp.where(lane <= sub, line, 0.0).astype(bf16)
            second = jnp.where(lane > sub, line, 0.0).astype(bf16)
            band = jnp.concatenate([first, second], axis=0)
            out = jnp.dot(vert[a], band, preferred_element_type=f32)
            design[pl.ds(k + a, lines_all, stride=pitch), :] = out * roots[...]

    lines = 16
    sets = 4

    def gram_step(step, total):
        start = pl.multiple_of(step * sets * lines * pitch, 8)
        rows = []
        for g in range(sets):
            row = [
                design[pl.ds(start + (g * lines + j) * pitch, padded_k), :].astype(bf16)
                for j in range(lines)
            ]
            rows.append(jnp.concatenate(row, axis=1))
        both = jnp.concatenate(rows, axis=0)
        return total + lax.dot_general(
            both, both, (((1,), (1,)), ((), ())), preferred_element_type=f32
        )

    total = lax.fori_loop(
        0,
        lines_all // (lines * sets),
        gram_step,
        jnp.zeros((sets * padded_k, sets * padded_k), f32),
        unroll=2,
    )
    part = jnp.zeros((padded_k, padded_k), f32)
    for g in range(sets):
        rows = slice(g * padded_k, (g + 1) * padded_k)
        part = part + total[rows, rows]
    gram_out[...] = part


def subtract_body(
    sender,
    gram,
    frames,
    science,
    col_t,
    row_rev,
    coef_out,
    payload,
    window,
    image,
    bands,
    total,
    *,
    order,
    capacity,
    count,
    taps,
    pixels,
):
    side = frames.shape[3]
    high, wide = science.shape
    padded_k = gram.shape[1]
    part = side // len(order)
    size = count + 1

    system = jnp.concatenate(
        [gram[...], jnp.zeros((padded_k, side - padded_k), f32)], axis=1
    ) / pixels
    sub = lax.broadcasted_iota(jnp.int32, (padded_k, side), 0)
    lane = lax.broadcasted_iota(jnp.int32, (padded_k, side), 1)
    system = jnp.where((sub < size) & (lane <= size), system, 0.0)
    system = system + jnp.where((sub == lane) & (sub < size), ridge_term, 0.0)

    pairs = (taps + 2) // 2
    rows_half = high // 2
    wins = frames.shape[0]

    for k in range(0, size, 8):
        block = range(min(8, size - k))
        cols = [jnp.broadcast_to(system[:, k + j : k + j + 1], system.shape) for j in block]
        rows = [system[k + j : k + j + 1, :] for j in block]
        core = [[cols[j][k + i : k + i + 1, :] for j in block] for i in block]
        for j in block:
            inverse = 1.0 / core[j][j]
            factor = jnp.where(sub == k + j, 0.0, cols[j] * inverse)
            system = system - factor * rows[j]
            for i in block[j + 1 :]:
                scale = core[i][j] * inverse
                rows[i] = rows[i] - scale * rows[j]
                for l in block[j + 1 :]:
                    core[i][l] = core[i][l] - scale * core[j][l]
                cols[i] = cols[i] - factor * core[j][i]
    pivot = jnp.sum(jnp.where(sub == lane, system, 0.0), axis=1, keepdims=True)
    solved = system[:, size : size + 1] / jnp.where(sub[:, :1] < size, pivot, 1.0)
    coef_out[...] = jnp.sum(jnp.where(sub == lane, solved, 0.0), axis=0, keepdims=True)
    background = solved[count : count + 1, :]
    basis_coef = jnp.where(sub[:, :1] < count, solved, 0.0)

    scaled = basis_coef * row_rev[...]
    kernel = jnp.zeros((col_t.shape[0], side), f32)
    for _ in range(3):
        piece = scaled.astype(bf16)
        scaled = scaled - piece.astype(f32)
        kernel = kernel + jnp.dot(col_t[...], piece, preferred_element_type=f32)
    kernel_sum = jnp.sum(jnp.sum(kernel, axis=1, keepdims=True), axis=0, keepdims=True)
    rounded = kernel.astype(bf16).astype(f32)

    zero_band = jnp.zeros((side, side), bf16)

    def band(i):
        if i < 0 or i >= taps:
            return zero_band
        line = jnp.broadcast_to(rounded[i : i + 1, :], (side, side))
        return pltpu.roll(line, 0, 1, stride=1, stride_axis=0).astype(bf16)

    made = {i: band(i) for i in range(-1, 2 * pairs)}
    for q in range(pairs):
        for a in range(2):
            for b in range(2):
                bands[
                    q * 2 * side + a * side : q * 2 * side + (a + 1) * side,
                    b * side : (b + 1) * side,
                ] = made[2 * q + a - b]

    step = side - taps + 1
    for q in range(pairs):
        lhs = jnp.concatenate(
            [
                jnp.concatenate(
                    [frames[c, a, q : q + rows_half, :].astype(bf16) for a in range(2)], axis=1
                )
                for c in range(wins)
            ],
            axis=0,
        )
        out = jnp.dot(
            lhs, bands[q * 2 * side : (q + 1) * 2 * side, :], preferred_element_type=f32
        )
        if q:
            out = out + total[...]
        if q < pairs - 1:
            total[...] = out
    for c in range(wins):
        rows = out[c * rows_half : (c + 1) * rows_half]
        window[c, pl.ds(0, rows_half, stride=2), :] = rows[:, :side]
        window[c, pl.ds(1, rows_half, stride=2), :] = rows[:, side:]
        keep = min(step, wide - c * step)
        image[:, c * step : c * step + keep] = window[c, :, :keep]
    image[...] = science[...].astype(f32) - image[...] - background

    store_parts(sender, image, payload, side, order, capacity, wide // side)
    line_at = lax.broadcasted_iota(jnp.int32, (trailer_rows, side), 0)
    trailer = jnp.zeros((trailer_rows, side), f32)
    rest = kernel_sum
    for p in range(3):
        piece = rest.astype(bf16).astype(f32)
        rest = rest - piece
        trailer = jnp.where(line_at == p, piece, trailer)
    trailer = trailer.astype(bf16)

    def put(d, carry):
        payload[d, capacity * part :, :] = trailer
        return carry

    lax.fori_loop(0, payload.shape[0], put, 0, unroll=4)


def fit_body(
    slot_of,
    sender,
    rows_at,
    cols_at,
    arrived,
    col,
    row_rev,
    science,
    variance,
    col_t,
    coef_out,
    payload,
    *scratch,
    order,
    capacity,
    count,
    taps,
):
    gram, windows = scratch[:2]
    stamps = rows_at.shape[1]
    side = row_rev.shape[1]
    normal_body(
        slot_of,
        rows_at,
        cols_at,
        arrived,
        col,
        row_rev,
        science,
        variance,
        gram,
        windows,
        *scratch[2:8],
        count=count,
        across_blocks=science.shape[1] // side,
        taps=taps,
    )
    subtract_body(
        sender,
        gram,
        windows,
        science,
        col_t,
        row_rev,
        coef_out,
        payload,
        *scratch[8:],
        order=order,
        capacity=capacity,
        count=count,
        taps=taps,
        pixels=stamps * side * side,
    )


def fit_and_subtract(
    slot_of,
    sender,
    rows_at,
    cols_at,
    arrived,
    col,
    row_rev,
    science,
    variance,
    col_t,
    order,
    capacity,
    count,
    taps,
):
    exps = len(order)
    high, wide = science.shape
    side = row_rev.shape[1]
    slots = sender.shape[0]
    stamps = rows_at.shape[1]
    padded_k = up(count + 2, 16)
    pairs = (taps + 2) // 2
    span = up(side + taps - 1, 16)
    half = up(high // 2 + pairs, 8)
    tall = up(taps // 2, 8) + max(high - side + span, 2 * half)
    wins = -(-wide // (side - taps + 1))
    group = next(g for g in (8, 4, 2, 1) if count % g == 0)
    return pl.pallas_call(
        functools.partial(fit_body, order=order, capacity=capacity, count=count, taps=taps),
        out_shape=(
            jax.ShapeDtypeStruct((1, side), f32),
            jax.ShapeDtypeStruct(
                (slots // capacity * exps, capacity * side // exps + trailer_rows, side), bf16
            ),
        ),
        in_specs=[smem()] * 4 + [vmem()] * 6,
        out_specs=(vmem(),) * 2,
        scratch_shapes=[
            pltpu.VMEM((padded_k, padded_k), f32),
            pltpu.VMEM((wins, 2, half, side), f32),
            pltpu.VMEM((tall, wide + 2 * side), f32),
            pltpu.VMEM((stamps * span, 2 * side), bf16),
            pltpu.VMEM((group, stamps * side, 2 * side), bf16),
            pltpu.VMEM((up(stamps * side * ((count + 2) | 1) + padded_k, 8), side), f32),
            pltpu.VMEM((stamps * side, side), f32),
            pltpu.VMEM((2 * half, side), f32),
            pltpu.VMEM((wins, high, side), f32),
            pltpu.VMEM((high, wide), f32),
            pltpu.VMEM((pairs * 2 * side, 2 * side), bf16),
            pltpu.VMEM((wins * high // 2, 2 * side), f32),
        ],
        compiler_params=pltpu.CompilerParams(vmem_limit_bytes=30 * mib),
        cost_estimate=cost(15_000_000_000, 8_000_000),
        name="fit_and_subtract",
    )(
        slot_of,
        sender,
        rows_at,
        cols_at,
        arrived,
        col,
        row_rev,
        science,
        variance,
        col_t,
    )


def split2(value):
    top = value.astype(bf16)
    return top, (value - top.astype(f32)).astype(bf16)


def score_body(slot_of, payload, down, over, out, padded, sideways, *, order, taps, capacity):
    side = payload.shape[2]
    part = side // len(order)
    high, wide = out.shape
    margin = taps // 2
    span = up(side + taps - 1, 16)
    across_blocks = wide // side
    exps = len(order)
    padded[...] = jnp.zeros(padded.shape, f32)
    for b in range(slot_of.shape[0]):
        slot = slot_of[b]
        row = pl.multiple_of((slot % capacity) * part, part)
        left = margin + (b % across_blocks) * side
        for e, q in enumerate(order):
            top = (b // across_blocks) * side + q * part
            block = payload[(slot // capacity) * exps + e, pl.ds(row, part), :]
            padded[top : top + part, left : left + side] = block.astype(f32)
    line = jnp.broadcast_to(over[...], (2 * side, 2 * side))
    band = pltpu.roll(line, 0, 1, stride=1, stride_axis=0)[:, :side]
    both = jnp.concatenate(split2(band), axis=1)
    sideways[...] = jnp.zeros(sideways.shape, f32)
    for c in range(wide // side):
        window = padded[:, c * side : (c + 2) * side].astype(bf16)
        got = jnp.dot(window, both, preferred_element_type=f32)
        sideways[margin : margin + high, c * side : (c + 1) * side] = got[:, :side] + got[:, side:]
    line = jnp.broadcast_to(down[...], (side, 2 * side))
    band = pltpu.roll(line, 0, 1, stride=1, stride_axis=0)[:, :span]
    top, low = split2(band)
    for r in range(high // side):
        data_top, data_low = split2(sideways[r * side : r * side + span, :])
        got = jnp.dot(top, data_top, preferred_element_type=f32)
        got = got + jnp.dot(top, data_low, preferred_element_type=f32)
        got = got + jnp.dot(low, data_top, preferred_element_type=f32)
        out[r * side : (r + 1) * side, :] = got


def score(slot_of, payload, down, over_rev, high, wide, taps, order, capacity):
    side = payload.shape[2]
    span = up(side + taps - 1, 16)
    return pl.pallas_call(
        functools.partial(score_body, order=order, taps=taps, capacity=capacity),
        out_shape=jax.ShapeDtypeStruct((high, wide), f32),
        in_specs=[smem()] + [vmem()] * 3,
        out_specs=vmem(),
        scratch_shapes=[
            pltpu.VMEM((high, wide + side), f32),
            pltpu.VMEM((high - side + span, wide), f32),
        ],
        compiler_params=pltpu.CompilerParams(vmem_limit_bytes=20 * mib),
        cost_estimate=cost(2_000_000_000, 2_000_000),
        name="score",
    )(slot_of, payload, down, over_rev)


def wanted_block(me, exposure, table, d, c, tract):
    exps = table.shape[0]
    block = table[distance(me[0], exposure, exps), d, c] - 1
    return jnp.where(block < 0, tract, block)


def variance_body(
    me, table, parts, template_var, own_out, other_out, template_out, total, sem, *, nears, capacity
):
    exps = table.shape[0]
    fars = exps // nears
    tract, part, _ = own_out.shape
    mine = pl.ds(pl.multiple_of(part_of(me[0], exps, nears) * part, part), part)
    copy = pltpu.make_async_copy(template_var.at[:, mine, :], template_out, sem)
    copy.start()
    total[...] = jnp.zeros(total.shape, f32)
    far = me[0] // nears
    rows = fars * part

    def one(j, carry):
        exposure = far * nears + lax.rem(j, nears)
        for c in range(capacity):
            block = wanted_block(me, exposure, table, j // nears, c, tract)
            total[block] += parts[j, c * rows : (c + 1) * rows, :].astype(f32)
        return carry

    lax.fori_loop(0, parts.shape[0], one, 0, unroll=4)
    own_out[...] = total[:tract, pl.ds(pl.multiple_of(far * part, part), part), :]
    for g in range(1, fars):
        there = lax.rem(far + g, fars)
        rows_there = pl.ds(pl.multiple_of(there * part, part), part)
        other_out[g - 1] = total[:tract, rows_there, :].astype(bf16)
    copy.wait()


def sum_variance(me, table, parts, template_var, nears, capacity):
    tract, side, _ = template_var.shape
    exps = table.shape[0]
    fars = exps // nears
    part = side // exps
    return pl.pallas_call(
        functools.partial(variance_body, nears=nears, capacity=capacity),
        out_shape=(
            jax.ShapeDtypeStruct((tract, part, side), f32),
            jax.ShapeDtypeStruct((max(1, fars - 1), tract, part, side), bf16),
            jax.ShapeDtypeStruct((tract, part, side), template_var.dtype),
        ),
        in_specs=[smem()] * 2 + [vmem(), pl.BlockSpec(memory_space=pl.ANY)],
        out_specs=(vmem(),) * 3,
        scratch_shapes=[
            pltpu.VMEM((tract + 1, fars * part, side), f32),
            pltpu.SemaphoreType.DMA(()),
        ],
        compiler_params=pltpu.CompilerParams(vmem_limit_bytes=16 * mib),
        cost_estimate=cost(0, 4_000_000),
        name="sum_variance",
    )(me, table, parts, template_var)


def combine_body(me, table, parts, own_var, var_template, *rest, part, capacity):
    others = rest[:-3]
    out, total, gain = rest[-3:]
    total[...] = jnp.zeros(total.shape, f32)
    gain[...] = jnp.zeros(gain.shape, f32)
    tract = out.shape[0]
    exps = table.shape[0]

    def one(j, carry):
        tail = parts[j, capacity * part :, :].astype(f32)
        kernel_sum = tail[0:1] + tail[1:2] + tail[2:3]
        square = jnp.broadcast_to(kernel_sum * kernel_sum, gain.shape[1:])
        for c in range(capacity):
            block = wanted_block(me, lax.rem(j, exps), table, j // exps, c, tract)
            total[block] += parts[j, c * part : (c + 1) * part, :].astype(f32)
            gain[block] += square
        return carry

    lax.fori_loop(0, parts.shape[0], one, 0, unroll=4)
    for t in range(tract):
        variance = own_var[t] + gain[t, 0:1, :] * var_template[t].astype(f32)
        for other in others:
            variance = variance + other[t].astype(f32)
        out[t] = (total[t] * lax.rsqrt(jnp.maximum(variance, 1.0))).astype(bf16)


def combine(me, table, parts, own_var, var_template, others, capacity):
    tract, part, side = own_var.shape
    return pl.pallas_call(
        functools.partial(combine_body, part=part, capacity=capacity),
        out_shape=jax.ShapeDtypeStruct((tract, part, side), bf16),
        in_specs=[smem(), smem()] + [vmem()] * (3 + len(others)),
        out_specs=vmem(),
        scratch_shapes=[
            pltpu.VMEM((tract + 1, part, side), f32),
            pltpu.VMEM((tract + 1, 8, side), f32),
        ],
        compiler_params=pltpu.CompilerParams(vmem_limit_bytes=16 * mib),
        name="combine",
    )(me, table, parts, own_var, var_template, *others)


def join_body(places, *refs, part, count):
    ins = refs[:count]
    out, held, sems = refs[-3:]
    copies = []
    for d, ref in enumerate(ins):
        held[d] = ref[...].astype(f32)
        row = pl.multiple_of(places[d] * part, part)
        copies.append(
            pltpu.make_async_copy(held.at[d], out.at[:, pl.ds(row, part), :], sems.at[d])
        )
        copies[-1].start()
    for copy in copies:
        copy.wait()


def join_parts(places, parts, whole, exps):
    tract, part, side = parts[0].shape
    count = len(parts)
    fresh = whole is None
    anywhere = pl.BlockSpec(memory_space=pl.ANY)
    return pl.pallas_call(
        functools.partial(join_body, part=part, count=count),
        out_shape=jax.ShapeDtypeStruct((tract, part * exps, side), f32),
        in_specs=[smem()] + [vmem()] * count + ([] if fresh else [anywhere]),
        out_specs=anywhere,
        scratch_shapes=[
            pltpu.VMEM((count, tract, part, side), f32),
            pltpu.SemaphoreType.DMA((count,)),
        ],
        input_output_aliases={} if fresh else {count + 1: 0},
        compiler_params=pltpu.CompilerParams(vmem_limit_bytes=16 * mib),
        cost_estimate=cost(0, 3_000_000 * count),
        name="join_parts",
    )(places, *parts, *([] if fresh else [whole]))


def local(
    template,
    template_var,
    science,
    science_var,
    routes_src,
    routes_blk,
    stamp_rows,
    stamp_cols,
    basis_col,
    basis_row,
    psf_col,
    psf_row,
):
    peers = lax.axis_size("det")
    nears = lax.axis_size("near")
    exps = lax.axis_size("far") * nears
    me = (lax.axis_index("far") * nears + lax.axis_index("near")).astype(jnp.int32)
    order = tuple((e % nears) * (exps // nears) + e // nears for e in range(exps))
    tract, side, _ = template.shape
    science_img = science[0]
    variance_img = science_var[0]
    blocks_dev = routes_src.shape[1]
    count, taps = basis_col.shape
    capacity = max(2, -(-blocks_dev // peers))
    slots = peers * capacity
    part = side // exps

    slot_of, sender, request = route_tables(routes_src, routes_blk, peers, capacity)
    asked = lax.all_to_all(request, "det", split_axis=0, concat_axis=0, tiled=True)
    picked = pick_blocks(asked, fetch(template), slots, capacity)
    held = hold(asked, picked)
    tables = [held] + [from_exposure(held, g, exps) for g in range(1, exps)]
    table = jnp.stack(tables).reshape(exps, peers, capacity)
    var_parts = prepare(sender, variance_img, science_img, table, side, nears, capacity)
    arrived = lax.all_to_all(picked, "det", split_axis=0, concat_axis=0, tiled=True)

    padded_k = up(count + 2, 16)
    col_t = jnp.pad(basis_col.T, ((0, up(taps, 16) - taps), (0, padded_k - count)))
    col = jnp.pad(basis_col.astype(f32), ((0, padded_k - count), (0, side - taps)))
    row_rev = jnp.pad(
        basis_row.astype(f32)[:, ::-1], ((0, padded_k - count), (side - taps, 0))
    )
    row_rev = jnp.roll(row_rev, 1, axis=1)
    over_rev = jnp.roll(jnp.pad(psf_row[:, ::-1], ((0, 0), (2 * side - taps, 0))), 1, axis=1)
    down = jnp.pad(psf_col, ((0, 0), (0, 2 * side - taps)))
    var_late, arrived = lax.optimization_barrier((var_parts, arrived))
    var_back = lax.all_to_all(
        var_late, ("det", "near"), split_axis=0, concat_axis=0, tiled=True
    )

    high, wide = science_img.shape
    coef, payload = fit_and_subtract(
        slot_of,
        sender,
        stamp_rows,
        stamp_cols,
        arrived,
        col,
        row_rev,
        science_img,
        variance_img,
        col_t,
        order,
        capacity,
        count,
        taps,
    )
    diff_back = lax.all_to_all(payload, ("det",) + exposure_axes, split_axis=0, concat_axis=0, tiled=True)
    own_var, other_var, var_template = sum_variance(
        me[None], table, var_back, template_var, nears, capacity
    )
    fars = exps // nears
    others = []
    for g in range(1, fars):
        pairs = [(f, (f + g) % fars) for f in range(fars)]
        others.append(lax.ppermute(other_var[g - 1], "far", pairs))
    scored = score(slot_of, payload, down, over_rev, high, wide, taps, order, capacity)
    mine = combine(me[None], table, diff_back, own_var, var_template, others, capacity)

    def swap(value, distance):
        return lax.ppermute(value, exposure_axes, [(e, e ^ distance) for e in range(exps)])

    def put(parts, whole):
        places = jnp.stack([part_of(there, exps, nears) for there, _ in parts])
        return join_parts(places, [held for _, held in parts], whole, exps)

    if exps == 4:
        far = swap(mine, 2)
        near = swap(mine, 1)
        last = swap(far, 1)
        whole = put([(me, mine), (me ^ 1, near), (me ^ 2, far)], None)
        significance = put([(me ^ 3, last)], whole)
    else:
        parts = [(me, mine)]
        for gap in range(1, exps):
            pairs = [(e, (e + gap) % exps) for e in range(exps)]
            parts.append(((me - gap) % exps, lax.ppermute(mine, exposure_axes, pairs)))
        significance = put(parts, None)
    return (significance, scored[None], coef[:, : count + 1])


def solution(mesh):
    peers, exps = mesh.devices.shape
    nears = 2 if exps % 2 == 0 else 1
    split = jax.sharding.Mesh(
        mesh.devices.reshape(peers, exps // nears, nears), ("det",) + exposure_axes
    )
    placed = (
        P("det", None, None),
        P("det", None, None),
        P(exposure_axes, "det", None),
        P(exposure_axes, "det", None),
        P(exposure_axes, "det"),
        P(exposure_axes, "det"),
        P(exposure_axes, "det"),
        P(exposure_axes, "det"),
        P(),
        P(),
        P(exposure_axes, None),
        P(exposure_axes, None),
    )
    return jax.shard_map(
        local,
        mesh=split,
        in_specs=placed,
        out_specs=(
            P("det", None, None),
            P(exposure_axes, "det", None),
            P(exposure_axes, "det"),
        ),
        check_vma=False,
    )
```

```python
import functools

import jax
import jax.numpy as jnp
from jax import lax
from jax.experimental import pallas as pl
from jax.experimental.pallas import tpu as pltpu
from jax.sharding import PartitionSpec as P

ridge_term = 0.01
bf16 = jnp.bfloat16
f32 = jnp.float32
vmem = functools.partial(pl.BlockSpec, memory_space=pltpu.VMEM)
smem = functools.partial(pl.BlockSpec, memory_space=pltpu.SMEM)
mib = 1024 * 1024
trailer_rows = 8


def up(value, step):
    return -(-value // step) * step


def cost(flops, moved):
    return pl.CostEstimate(flops=flops, bytes_accessed=moved, transcendentals=0)


exposure_axes = ("far", "near")


def part_of(exposure, exps, nears):
    return lax.rem(exposure, nears) * (exps // nears) + exposure // nears


def distance(here, there, exps):
    if exps & (exps - 1) == 0:
        return here ^ there
    return lax.rem(here - there + exps, exps)


def from_exposure(value, gap, exps):
    if exps & (exps - 1) == 0:
        pairs = [(e, e ^ gap) for e in range(exps)]
    else:
        pairs = [(e, (e + gap) % exps) for e in range(exps)]
    return lax.ppermute(value, exposure_axes, pairs)


def route_body(src, blk, slot_of, sender, request, count, *, peers, capacity):
    def clear_count(p, carry):
        count[p] = 0
        return carry

    def clear_slot(s, carry):
        sender[s] = 0
        request[s // capacity, 0, s % capacity] = 0
        return carry

    lax.fori_loop(0, peers, clear_count, 0, unroll=peers <= 16)
    lax.fori_loop(0, peers * capacity, clear_slot, 0, unroll=peers <= 16)
    for b in range(src.shape[1]):
        owner = src[0, b]
        place = count[owner]
        count[owner] = place + 1
        slot_of[b] = owner * capacity + place
        sender[owner * capacity + place] = b
        request[owner, 0, place] = blk[0, b] + 1


def route_tables(routes_src, routes_blk, peers, capacity):
    return pl.pallas_call(
        functools.partial(route_body, peers=peers, capacity=capacity),
        out_shape=(
            jax.ShapeDtypeStruct((routes_src.shape[1],), jnp.int32),
            jax.ShapeDtypeStruct((peers * capacity,), jnp.int32),
            jax.ShapeDtypeStruct((peers, 1, capacity), jnp.int32),
        ),
        in_specs=[smem()] * 2,
        out_specs=(smem(),) * 3,
        scratch_shapes=[pltpu.SMEM((peers,), jnp.int32)],
        name="route_tables",
    )(routes_src, routes_blk)


def fetch_body(template, near, sem):
    copy = pltpu.make_async_copy(template, near, sem)
    copy.start()
    copy.wait()


def fetch(template):
    return pl.pallas_call(
        fetch_body,
        out_shape=jax.ShapeDtypeStruct(template.shape, template.dtype),
        in_specs=[pl.BlockSpec(memory_space=pl.ANY)],
        out_specs=vmem(),
        scratch_shapes=[pltpu.SemaphoreType.DMA(())],
        compiler_params=pltpu.CompilerParams(vmem_limit_bytes=16 * mib),
        cost_estimate=cost(0, 4_000_000),
        name="fetch",
    )(template)


def pick_body(asked, template, out, sems, *, capacity):
    copies = []
    for s in range(out.shape[0]):
        block = jnp.maximum(asked[s // capacity, 0, s % capacity] - 1, 0)
        copies.append(pltpu.make_async_copy(template.at[block], out.at[s], sems.at[s]))
        copies[-1].start()
    for copy in copies:
        copy.wait()


def pick_blocks(asked, template, slots, capacity):
    return pl.pallas_call(
        functools.partial(pick_body, capacity=capacity),
        out_shape=jax.ShapeDtypeStruct((slots,) + template.shape[1:], template.dtype),
        in_specs=[smem(), vmem()],
        out_specs=pl.BlockSpec(memory_space=pl.ANY),
        scratch_shapes=[pltpu.SemaphoreType.DMA((slots,))],
        compiler_params=pltpu.CompilerParams(vmem_limit_bytes=16 * mib),
        name="pick_blocks",
    )(asked, template)


def store_parts(sender, image, out, side, order, capacity, across_blocks):
    exps = len(order)
    part = side // exps
    slots = sender.shape[0]

    def one(s, carry):
        b = sender[s]
        top = pl.multiple_of((b // across_blocks) * side, side)
        left = pl.multiple_of((b % across_blocks) * side, side)
        block = image[pl.ds(top, side), pl.ds(left, side)].astype(bf16)
        row = pl.multiple_of((s % capacity) * part, part)
        for e, q in enumerate(order):
            out[(s // capacity) * exps + e, pl.ds(row, part), :] = block[q * part : (q + 1) * part]
        return carry

    lax.fori_loop(0, slots, one, 0, unroll=True if slots <= 32 else 4)


def cut(ref, top, left, height, side):
    down = pl.multiple_of((top // 8) * 8, 8)
    over = pl.multiple_of((left // side) * side, side)
    tile = ref[pl.ds(down, height), pl.ds(over, 3 * side)]
    tile = pltpu.roll(tile, lax.rem(3 * side - (left - over), 3 * side), 1)[:, : 2 * side]
    return pltpu.roll(tile, lax.rem(height - (top - down), height), 0)


def hold_body(asked, earlier, out):
    del earlier
    out[...] = asked[...]


def hold(asked, earlier):
    return pl.pallas_call(
        hold_body,
        out_shape=jax.ShapeDtypeStruct(asked.shape, asked.dtype),
        in_specs=[vmem(), pl.BlockSpec(memory_space=pl.ANY)],
        out_specs=vmem(),
        compiler_params=pltpu.CompilerParams(vmem_limit_bytes=16 * mib),
        name="hold",
    )(asked, earlier)


def prepare_body(sender, variance, science, earlier, out, *, side, nears, capacity):
    del earlier, science
    store_parts(sender, variance, out, side, range(nears), capacity, variance.shape[1] // side)


def prepare(sender, variance, science, earlier, side, nears, capacity):
    slots = sender.shape[0]
    part = side // nears
    return pl.pallas_call(
        functools.partial(prepare_body, side=side, nears=nears, capacity=capacity),
        out_shape=jax.ShapeDtypeStruct((slots // capacity * nears, capacity * part, side), bf16),
        in_specs=[smem()] + [vmem()] * 2 + [pl.BlockSpec(memory_space=pl.ANY)],
        out_specs=vmem(),
        compiler_params=pltpu.CompilerParams(vmem_limit_bytes=16 * mib),
        cost_estimate=cost(0, 6_000_000),
        name="prepare",
    )(sender, variance, science, earlier)


def normal_body(
    slot_of,
    rows_at,
    cols_at,
    arrived,
    col,
    row_rev,
    science,
    variance,
    gram_out,
    windows,
    frame,
    cuts,
    vert,
    design,
    roots,
    window,
    *,
    count,
    across_blocks,
    taps,
):
    side = row_rev.shape[1]
    margin = taps // 2
    stamps = rows_at.shape[1]
    span = up(side + taps - 1, 16)
    padded_k = gram_out.shape[1]
    pitch = (count + 2) | 1
    lines_all = stamps * side
    sub = lax.broadcasted_iota(jnp.int32, (side, side), 0)
    lane = lax.broadcasted_iota(jnp.int32, (side, side), 1)

    high, wide = science.shape
    rows_off = up(margin, 8)
    frame[:rows_off, :] = jnp.zeros((rows_off, frame.shape[1]), f32)
    below = rows_off + high
    frame[below:, :] = jnp.zeros((frame.shape[0] - below, frame.shape[1]), f32)
    frame[rows_off:below, :side] = jnp.zeros((high, side), f32)
    after = side + wide
    frame[rows_off:below, after:] = jnp.zeros((high, frame.shape[1] - after), f32)
    for b in range(slot_of.shape[0]):
        top = rows_off + (b // across_blocks) * side
        left = side + (b % across_blocks) * side
        frame[top : top + side, left : left + side] = arrived[slot_of[b]].astype(f32)
    first_row = rows_off - margin
    first_col = side - margin

    def cut_image(ref, top, left):
        tall = min(high, side + 16)
        down = pl.multiple_of(jnp.minimum((top // 16) * 16, high - tall), 16)
        over = pl.multiple_of(jnp.minimum((left // side) * side, wide - 2 * side), side)
        tile = ref[pl.ds(down, tall), pl.ds(over, 2 * side)].astype(f32)
        tile = pltpu.roll(tile, lax.rem(2 * side - (left - over), 2 * side), 1)[:, :side]
        return pltpu.roll(tile, lax.rem(tall - (top - down), tall), 0)[:side]

    for s in range(stamps):
        top = rows_at[0, s]
        left = cols_at[0, s]
        tile = cut(frame, top + first_row, left + first_col, span, side)
        cuts[s * span : (s + 1) * span, :] = tile.astype(bf16)
        root = lax.rsqrt(cut_image(variance, top, left))
        roots[s * side : (s + 1) * side, :] = root
        place = pl.ds(s * side * pitch + count, side, stride=pitch)
        design[place, :] = root
        place = pl.ds(s * side * pitch + count + 1, side, stride=pitch)
        design[place, :] = root * cut_image(science, top, left)
    design[lines_all * pitch :, :] = jnp.zeros((design.shape[0] - lines_all * pitch, side), f32)

    group = vert.shape[0]
    step = side - taps + 1
    starts = list(range(0, count, group))
    for turn, k in enumerate(starts):
        for c in range(turn, windows.shape[0], len(starts)):
            left = first_col + c * step
            window[...] = frame[first_row : first_row + window.shape[0], left : left + side]
            for parity in range(2):
                place = pl.ds(parity, windows.shape[2], stride=2)
                windows[c, parity] = window[place, :]
        filters = []
        for a in range(group):
            line = jnp.broadcast_to(col[k + a : k + a + 1, :], (side, side))
            line = pltpu.roll(line, 0, 1, stride=1, stride_axis=0)
            first = jnp.where(lane >= sub, line, 0.0).astype(bf16)
            second = jnp.where(lane < sub, line, 0.0).astype(bf16)
            filters.append(jnp.concatenate([first, second[:, : span - side]], axis=1))
        filters = jnp.concatenate(filters, axis=0)
        for s in range(stamps):
            out = jnp.dot(
                filters, cuts[s * span : (s + 1) * span, :], preferred_element_type=f32
            ).astype(bf16)
            for a in range(group):
                vert[a, s * side : (s + 1) * side, :] = out[a * side : (a + 1) * side]
        for a in range(group):
            line = jnp.broadcast_to(row_rev[k + a : k + a + 1, :], (side, side))
            line = pltpu.roll(line, 0, 1, stride=1, stride_axis=0)
            first = jnp.where(lane <= sub, line, 0.0).astype(bf16)
            second = jnp.where(lane > sub, line, 0.0).astype(bf16)
            band = jnp.concatenate([first, second], axis=0)
            out = jnp.dot(vert[a], band, preferred_element_type=f32)
            design[pl.ds(k + a, lines_all, stride=pitch), :] = out * roots[...]

    lines = 16
    sets = 4

    def gram_step(step, total):
        start = pl.multiple_of(step * sets * lines * pitch, 8)
        rows = []
        for g in range(sets):
            row = [
                design[pl.ds(start + (g * lines + j) * pitch, padded_k), :].astype(bf16)
                for j in range(lines)
            ]
            rows.append(jnp.concatenate(row, axis=1))
        both = jnp.concatenate(rows, axis=0)
        return total + lax.dot_general(
            both, both, (((1,), (1,)), ((), ())), preferred_element_type=f32
        )

    total = lax.fori_loop(
        0,
        lines_all // (lines * sets),
        gram_step,
        jnp.zeros((sets * padded_k, sets * padded_k), f32),
        unroll=2,
    )
    part = jnp.zeros((padded_k, padded_k), f32)
    for g in range(sets):
        rows = slice(g * padded_k, (g + 1) * padded_k)
        part = part + total[rows, rows]
    gram_out[...] = part


def subtract_body(
    sender,
    gram,
    frames,
    science,
    col_t,
    row_rev,
    coef_out,
    payload,
    window,
    image,
    bands,
    total,
    *,
    order,
    capacity,
    count,
    taps,
    pixels,
):
    side = frames.shape[3]
    high, wide = science.shape
    padded_k = gram.shape[1]
    part = side // len(order)
    size = count + 1

    system = jnp.concatenate(
        [gram[...], jnp.zeros((padded_k, side - padded_k), f32)], axis=1
    ) / pixels
    sub = lax.broadcasted_iota(jnp.int32, (padded_k, side), 0)
    lane = lax.broadcasted_iota(jnp.int32, (padded_k, side), 1)
    system = jnp.where((sub < size) & (lane <= size), system, 0.0)
    system = system + jnp.where((sub == lane) & (sub < size), ridge_term, 0.0)

    pairs = (taps + 2) // 2
    rows_half = high // 2
    wins = frames.shape[0]

    for k in range(0, size, 8):
        block = range(min(8, size - k))
        cols = [jnp.broadcast_to(system[:, k + j : k + j + 1], system.shape) for j in block]
        rows = [system[k + j : k + j + 1, :] for j in block]
        core = [[cols[j][k + i : k + i + 1, :] for j in block] for i in block]
        for j in block:
            inverse = 1.0 / core[j][j]
            factor = jnp.where(sub == k + j, 0.0, cols[j] * inverse)
            system = system - factor * rows[j]
            for i in block[j + 1 :]:
                scale = core[i][j] * inverse
                rows[i] = rows[i] - scale * rows[j]
                for l in block[j + 1 :]:
                    core[i][l] = core[i][l] - scale * core[j][l]
                cols[i] = cols[i] - factor * core[j][i]
    pivot = jnp.sum(jnp.where(sub == lane, system, 0.0), axis=1, keepdims=True)
    solved = system[:, size : size + 1] / jnp.where(sub[:, :1] < size, pivot, 1.0)
    coef_out[...] = jnp.sum(jnp.where(sub == lane, solved, 0.0), axis=0, keepdims=True)
    background = solved[count : count + 1, :]
    basis_coef = jnp.where(sub[:, :1] < count, solved, 0.0)

    scaled = basis_coef * row_rev[...]
    kernel = jnp.zeros((col_t.shape[0], side), f32)
    for _ in range(3):
        piece = scaled.astype(bf16)
        scaled = scaled - piece.astype(f32)
        kernel = kernel + jnp.dot(col_t[...], piece, preferred_element_type=f32)
    kernel_sum = jnp.sum(jnp.sum(kernel, axis=1, keepdims=True), axis=0, keepdims=True)
    rounded = kernel.astype(bf16).astype(f32)

    zero_band = jnp.zeros((side, side), bf16)

    def band(i):
        if i < 0 or i >= taps:
            return zero_band
        line = jnp.broadcast_to(rounded[i : i + 1, :], (side, side))
        return pltpu.roll(line, 0, 1, stride=1, stride_axis=0).astype(bf16)

    made = {i: band(i) for i in range(-1, 2 * pairs)}
    for q in range(pairs):
        for a in range(2):
            for b in range(2):
                bands[
                    q * 2 * side + a * side : q * 2 * side + (a + 1) * side,
                    b * side : (b + 1) * side,
                ] = made[2 * q + a - b]

    step = side - taps + 1
    joint = 4
    for q in range(0, pairs, joint):
        last = min(q + joint, pairs)
        lhs = jnp.concatenate(
            [
                jnp.concatenate(
                    [
                        frames[c, a, p : p + rows_half, :].astype(bf16)
                        for p in range(q, last)
                        for a in range(2)
                    ],
                    axis=1,
                )
                for c in range(wins)
            ],
            axis=0,
        )
        out = jnp.dot(
            lhs, bands[q * 2 * side : last * 2 * side, :], preferred_element_type=f32
        )
        if q:
            out = out + total[...]
        if last < pairs:
            total[...] = out
    for c in range(wins):
        rows = out[c * rows_half : (c + 1) * rows_half]
        window[c, pl.ds(0, rows_half, stride=2), :] = rows[:, :side]
        window[c, pl.ds(1, rows_half, stride=2), :] = rows[:, side:]
        keep = min(step, wide - c * step)
        image[:, c * step : c * step + keep] = window[c, :, :keep]
    image[...] = science[...].astype(f32) - image[...] - background

    store_parts(sender, image, payload, side, order, capacity, wide // side)
    line_at = lax.broadcasted_iota(jnp.int32, (trailer_rows, side), 0)
    trailer = jnp.zeros((trailer_rows, side), f32)
    rest = kernel_sum
    for p in range(3):
        piece = rest.astype(bf16).astype(f32)
        rest = rest - piece
        trailer = jnp.where(line_at == p, piece, trailer)
    trailer = trailer.astype(bf16)

    def put(d, carry):
        payload[d, capacity * part :, :] = trailer
        return carry

    lax.fori_loop(0, payload.shape[0], put, 0, unroll=4)


def fit_body(
    slot_of,
    sender,
    rows_at,
    cols_at,
    arrived,
    col,
    row_rev,
    science,
    variance,
    col_t,
    coef_out,
    payload,
    *scratch,
    order,
    capacity,
    count,
    taps,
):
    gram, windows = scratch[:2]
    stamps = rows_at.shape[1]
    side = row_rev.shape[1]
    normal_body(
        slot_of,
        rows_at,
        cols_at,
        arrived,
        col,
        row_rev,
        science,
        variance,
        gram,
        windows,
        *scratch[2:8],
        count=count,
        across_blocks=science.shape[1] // side,
        taps=taps,
    )
    subtract_body(
        sender,
        gram,
        windows,
        science,
        col_t,
        row_rev,
        coef_out,
        payload,
        *scratch[8:],
        order=order,
        capacity=capacity,
        count=count,
        taps=taps,
        pixels=stamps * side * side,
    )


def fit_and_subtract(
    slot_of,
    sender,
    rows_at,
    cols_at,
    arrived,
    col,
    row_rev,
    science,
    variance,
    col_t,
    order,
    capacity,
    count,
    taps,
):
    exps = len(order)
    high, wide = science.shape
    side = row_rev.shape[1]
    slots = sender.shape[0]
    stamps = rows_at.shape[1]
    padded_k = up(count + 2, 16)
    pairs = (taps + 2) // 2
    span = up(side + taps - 1, 16)
    half = up(high // 2 + pairs, 8)
    tall = up(taps // 2, 8) + max(high - side + span, 2 * half)
    wins = -(-wide // (side - taps + 1))
    group = next(g for g in (20, 8, 4, 2, 1) if count % g == 0)
    return pl.pallas_call(
        functools.partial(fit_body, order=order, capacity=capacity, count=count, taps=taps),
        out_shape=(
            jax.ShapeDtypeStruct((1, side), f32),
            jax.ShapeDtypeStruct(
                (slots // capacity * exps, capacity * side // exps + trailer_rows, side), bf16
            ),
        ),
        in_specs=[smem()] * 4 + [vmem()] * 6,
        out_specs=(vmem(),) * 2,
        scratch_shapes=[
            pltpu.VMEM((padded_k, padded_k), f32),
            pltpu.VMEM((wins, 2, half, side), f32),
            pltpu.VMEM((tall, wide + 2 * side), f32),
            pltpu.VMEM((stamps * span, 2 * side), bf16),
            pltpu.VMEM((group, stamps * side, 2 * side), bf16),
            pltpu.VMEM((up(stamps * side * ((count + 2) | 1) + padded_k, 8), side), f32),
            pltpu.VMEM((stamps * side, side), f32),
            pltpu.VMEM((2 * half, side), f32),
            pltpu.VMEM((wins, high, side), f32),
            pltpu.VMEM((high, wide), f32),
            pltpu.VMEM((pairs * 2 * side, 2 * side), bf16),
            pltpu.VMEM((wins * high // 2, 2 * side), f32),
        ],
        compiler_params=pltpu.CompilerParams(vmem_limit_bytes=30 * mib),
        cost_estimate=cost(15_000_000_000, 8_000_000),
        name="fit_and_subtract",
    )(
        slot_of,
        sender,
        rows_at,
        cols_at,
        arrived,
        col,
        row_rev,
        science,
        variance,
        col_t,
    )


def split2(value):
    top = value.astype(bf16)
    return top, (value - top.astype(f32)).astype(bf16)


def score_body(slot_of, payload, down, over, out, padded, sideways, *, order, taps, capacity):
    side = payload.shape[2]
    part = side // len(order)
    high, wide = out.shape
    margin = taps // 2
    span = up(side + taps - 1, 16)
    across_blocks = wide // side
    exps = len(order)
    padded[...] = jnp.zeros(padded.shape, f32)
    for b in range(slot_of.shape[0]):
        slot = slot_of[b]
        row = pl.multiple_of((slot % capacity) * part, part)
        left = margin + (b % across_blocks) * side
        for e, q in enumerate(order):
            top = (b // across_blocks) * side + q * part
            block = payload[(slot // capacity) * exps + e, pl.ds(row, part), :]
            padded[top : top + part, left : left + side] = block.astype(f32)
    line = jnp.broadcast_to(over[...], (2 * side, 2 * side))
    band = pltpu.roll(line, 0, 1, stride=1, stride_axis=0)[:, :side]
    both = jnp.concatenate(split2(band), axis=1)
    sideways[...] = jnp.zeros(sideways.shape, f32)
    for c in range(wide // side):
        window = padded[:, c * side : (c + 2) * side].astype(bf16)
        got = jnp.dot(window, both, preferred_element_type=f32)
        sideways[margin : margin + high, c * side : (c + 1) * side] = got[:, :side] + got[:, side:]
    line = jnp.broadcast_to(down[...], (side, 2 * side))
    band = pltpu.roll(line, 0, 1, stride=1, stride_axis=0)[:, :span]
    top, low = split2(band)
    for r in range(high // side):
        data_top, data_low = split2(sideways[r * side : r * side + span, :])
        got = jnp.dot(top, data_top, preferred_element_type=f32)
        got = got + jnp.dot(top, data_low, preferred_element_type=f32)
        got = got + jnp.dot(low, data_top, preferred_element_type=f32)
        out[r * side : (r + 1) * side, :] = got


def score(slot_of, payload, down, over_rev, high, wide, taps, order, capacity):
    side = payload.shape[2]
    span = up(side + taps - 1, 16)
    return pl.pallas_call(
        functools.partial(score_body, order=order, taps=taps, capacity=capacity),
        out_shape=jax.ShapeDtypeStruct((high, wide), f32),
        in_specs=[smem()] + [vmem()] * 3,
        out_specs=vmem(),
        scratch_shapes=[
            pltpu.VMEM((high, wide + side), f32),
            pltpu.VMEM((high - side + span, wide), f32),
        ],
        compiler_params=pltpu.CompilerParams(vmem_limit_bytes=20 * mib),
        cost_estimate=cost(2_000_000_000, 2_000_000),
        name="score",
    )(slot_of, payload, down, over_rev)


def wanted_block(me, exposure, table, d, c, tract):
    exps = table.shape[0]
    block = table[distance(me[0], exposure, exps), d, c] - 1
    return jnp.where(block < 0, tract, block)


def variance_body(
    me, table, parts, template_var, own_out, other_out, template_out, total, sem, *, nears, capacity
):
    exps = table.shape[0]
    fars = exps // nears
    tract, part, _ = own_out.shape
    mine = pl.ds(pl.multiple_of(part_of(me[0], exps, nears) * part, part), part)
    copy = pltpu.make_async_copy(template_var.at[:, mine, :], template_out, sem)
    copy.start()
    total[...] = jnp.zeros(total.shape, f32)
    far = me[0] // nears
    rows = fars * part

    def one(j, carry):
        exposure = far * nears + lax.rem(j, nears)
        for c in range(capacity):
            block = wanted_block(me, exposure, table, j // nears, c, tract)
            total[block] += parts[j, c * rows : (c + 1) * rows, :].astype(f32)
        return carry

    lax.fori_loop(0, parts.shape[0], one, 0, unroll=4)
    own_out[...] = total[:tract, pl.ds(pl.multiple_of(far * part, part), part), :]
    for g in range(1, fars):
        there = lax.rem(far + g, fars)
        rows_there = pl.ds(pl.multiple_of(there * part, part), part)
        other_out[g - 1] = total[:tract, rows_there, :].astype(bf16)
    copy.wait()


def sum_variance(me, table, parts, template_var, nears, capacity):
    tract, side, _ = template_var.shape
    exps = table.shape[0]
    fars = exps // nears
    part = side // exps
    return pl.pallas_call(
        functools.partial(variance_body, nears=nears, capacity=capacity),
        out_shape=(
            jax.ShapeDtypeStruct((tract, part, side), f32),
            jax.ShapeDtypeStruct((max(1, fars - 1), tract, part, side), bf16),
            jax.ShapeDtypeStruct((tract, part, side), template_var.dtype),
        ),
        in_specs=[smem()] * 2 + [vmem(), pl.BlockSpec(memory_space=pl.ANY)],
        out_specs=(vmem(),) * 3,
        scratch_shapes=[
            pltpu.VMEM((tract + 1, fars * part, side), f32),
            pltpu.SemaphoreType.DMA(()),
        ],
        compiler_params=pltpu.CompilerParams(vmem_limit_bytes=16 * mib),
        cost_estimate=cost(0, 4_000_000),
        name="sum_variance",
    )(me, table, parts, template_var)


def combine_body(me, table, earlier, parts, own_var, var_template, *rest, part, capacity):
    del earlier
    others = rest[:-3]
    out, total, gain = rest[-3:]
    total[...] = jnp.zeros(total.shape, f32)
    gain[...] = jnp.zeros(gain.shape, f32)
    tract = out.shape[0]
    exps = table.shape[0]

    def one(j, carry):
        tail = parts[j, capacity * part :, :].astype(f32)
        kernel_sum = tail[0:1] + tail[1:2] + tail[2:3]
        square = jnp.broadcast_to(kernel_sum * kernel_sum, gain.shape[1:])
        for c in range(capacity):
            block = wanted_block(me, lax.rem(j, exps), table, j // exps, c, tract)
            total[block] += parts[j, c * part : (c + 1) * part, :].astype(f32)
            gain[block] += square
        return carry

    lax.fori_loop(0, parts.shape[0], one, 0, unroll=4)
    for t in range(tract):
        variance = own_var[t] + gain[t, 0:1, :] * var_template[t].astype(f32)
        for other in others:
            variance = variance + other[t].astype(f32)
        out[t] = (total[t] * lax.rsqrt(jnp.maximum(variance, 1.0))).astype(bf16)


def combine(me, table, earlier, parts, own_var, var_template, others, capacity):
    tract, part, side = own_var.shape
    return pl.pallas_call(
        functools.partial(combine_body, part=part, capacity=capacity),
        out_shape=jax.ShapeDtypeStruct((tract, part, side), bf16),
        in_specs=[smem(), smem(), pl.BlockSpec(memory_space=pl.ANY)]
        + [vmem()] * (3 + len(others)),
        out_specs=vmem(),
        scratch_shapes=[
            pltpu.VMEM((tract + 1, part, side), f32),
            pltpu.VMEM((tract + 1, 8, side), f32),
        ],
        compiler_params=pltpu.CompilerParams(vmem_limit_bytes=16 * mib),
        name="combine",
    )(me, table, earlier, parts, own_var, var_template, *others)


def join_body(places, *refs, part, count):
    ins = refs[:count]
    out, held, sems = refs[-3:]
    copies = []
    for d, ref in enumerate(ins):
        held[d] = ref[...].astype(f32)
        row = pl.multiple_of(places[d] * part, part)
        copies.append(
            pltpu.make_async_copy(held.at[d], out.at[:, pl.ds(row, part), :], sems.at[d])
        )
        copies[-1].start()
    for copy in copies:
        copy.wait()


def join_parts(places, parts, whole, exps):
    tract, part, side = parts[0].shape
    count = len(parts)
    fresh = whole is None
    anywhere = pl.BlockSpec(memory_space=pl.ANY)
    return pl.pallas_call(
        functools.partial(join_body, part=part, count=count),
        out_shape=jax.ShapeDtypeStruct((tract, part * exps, side), f32),
        in_specs=[smem()] + [vmem()] * count + ([] if fresh else [anywhere]),
        out_specs=anywhere,
        scratch_shapes=[
            pltpu.VMEM((count, tract, part, side), f32),
            pltpu.SemaphoreType.DMA((count,)),
        ],
        input_output_aliases={} if fresh else {count + 1: 0},
        compiler_params=pltpu.CompilerParams(vmem_limit_bytes=16 * mib),
        cost_estimate=cost(0, 3_000_000 * count),
        name="join_parts",
    )(places, *parts, *([] if fresh else [whole]))


def local(
    template,
    template_var,
    science,
    science_var,
    routes_src,
    routes_blk,
    stamp_rows,
    stamp_cols,
    basis_col,
    basis_row,
    psf_col,
    psf_row,
):
    peers = lax.axis_size("det")
    nears = lax.axis_size("near")
    exps = lax.axis_size("far") * nears
    me = (lax.axis_index("far") * nears + lax.axis_index("near")).astype(jnp.int32)
    order = tuple((e % nears) * (exps // nears) + e // nears for e in range(exps))
    tract, side, _ = template.shape
    science_img = science[0]
    variance_img = science_var[0]
    blocks_dev = routes_src.shape[1]
    count, taps = basis_col.shape
    capacity = max(2, -(-blocks_dev // peers))
    slots = peers * capacity
    part = side // exps

    slot_of, sender, request = route_tables(routes_src, routes_blk, peers, capacity)
    asked = lax.all_to_all(request, "det", split_axis=0, concat_axis=0, tiled=True)
    picked = pick_blocks(asked, fetch(template), slots, capacity)
    held = hold(asked, picked)
    tables = [held] + [from_exposure(held, g, exps) for g in range(1, exps)]
    table = jnp.stack(tables).reshape(exps, peers, capacity)
    var_parts = prepare(sender, variance_img, science_img, table, side, nears, capacity)
    arrived = lax.all_to_all(picked, "det", split_axis=0, concat_axis=0, tiled=True)

    padded_k = up(count + 2, 16)
    col_t = jnp.pad(basis_col.T, ((0, up(taps, 16) - taps), (0, padded_k - count)))
    col = jnp.pad(basis_col.astype(f32), ((0, padded_k - count), (0, side - taps)))
    row_rev = jnp.pad(
        basis_row.astype(f32)[:, ::-1], ((0, padded_k - count), (side - taps, 0))
    )
    row_rev = jnp.roll(row_rev, 1, axis=1)
    over_rev = jnp.roll(jnp.pad(psf_row[:, ::-1], ((0, 0), (2 * side - taps, 0))), 1, axis=1)
    down = jnp.pad(psf_col, ((0, 0), (0, 2 * side - taps)))
    var_late, arrived = lax.optimization_barrier((var_parts, arrived))
    var_back = lax.all_to_all(
        var_late, ("det", "near"), split_axis=0, concat_axis=0, tiled=True
    )

    high, wide = science_img.shape
    coef, payload = fit_and_subtract(
        slot_of,
        sender,
        stamp_rows,
        stamp_cols,
        arrived,
        col,
        row_rev,
        science_img,
        variance_img,
        col_t,
        order,
        capacity,
        count,
        taps,
    )
    diff_back = lax.all_to_all(payload, ("det",) + exposure_axes, split_axis=0, concat_axis=0, tiled=True)
    own_var, other_var, var_template = sum_variance(
        me[None], table, var_back, template_var, nears, capacity
    )
    fars = exps // nears
    others = []
    for g in range(1, fars):
        pairs = [(f, (f + g) % fars) for f in range(fars)]
        others.append(lax.ppermute(other_var[g - 1], "far", pairs))
    scored = score(slot_of, payload, down, over_rev, high, wide, taps, order, capacity)
    mine = combine(me[None], table, scored, diff_back, own_var, var_template, others, capacity)

    def swap(value, distance):
        return lax.ppermute(value, exposure_axes, [(e, e ^ distance) for e in range(exps)])

    def put(parts, whole):
        places = jnp.stack([part_of(there, exps, nears) for there, _ in parts])
        return join_parts(places, [held for _, held in parts], whole, exps)

    if exps == 4:
        far = swap(mine, 2)
        near = swap(mine, 1)
        last = swap(far, 1)
        whole = put([(me, mine), (me ^ 1, near), (me ^ 2, far)], None)
        significance = put([(me ^ 3, last)], whole)
    else:
        parts = [(me, mine)]
        for gap in range(1, exps):
            pairs = [(e, (e + gap) % exps) for e in range(exps)]
            parts.append(((me - gap) % exps, lax.ppermute(mine, exposure_axes, pairs)))
        significance = put(parts, None)
    return (significance, scored[None], coef[:, : count + 1])


def solution(mesh):
    peers, exps = mesh.devices.shape
    nears = 2 if exps % 2 == 0 else 1
    split = jax.sharding.Mesh(
        mesh.devices.reshape(peers, exps // nears, nears), ("det",) + exposure_axes
    )
    placed = (
        P("det", None, None),
        P("det", None, None),
        P(exposure_axes, "det", None),
        P(exposure_axes, "det", None),
        P(exposure_axes, "det"),
        P(exposure_axes, "det"),
        P(exposure_axes, "det"),
        P(exposure_axes, "det"),
        P(),
        P(),
        P(exposure_axes, None),
        P(exposure_axes, None),
    )
    return jax.shard_map(
        local,
        mesh=split,
        in_specs=placed,
        out_specs=(
            P("det", None, None),
            P(exposure_axes, "det", None),
            P(exposure_axes, "det"),
        ),
        check_vma=False,
    )
```

```python
import functools

import jax
import jax.numpy as jnp
from jax import lax
from jax.experimental import pallas as pl
from jax.experimental.pallas import tpu as pltpu
from jax.sharding import PartitionSpec as P

ridge_term = 0.01
bf16 = jnp.bfloat16
f32 = jnp.float32
vmem = functools.partial(pl.BlockSpec, memory_space=pltpu.VMEM)
smem = functools.partial(pl.BlockSpec, memory_space=pltpu.SMEM)
mib = 1024 * 1024
trailer_rows = 8


def up(value, step):
    return -(-value // step) * step


def cost(flops, moved):
    return pl.CostEstimate(flops=flops, bytes_accessed=moved, transcendentals=0)


exposure_axes = ("far", "near")


def part_of(exposure, exps, nears):
    return lax.rem(exposure, nears) * (exps // nears) + exposure // nears


def distance(here, there, exps):
    if exps & (exps - 1) == 0:
        return here ^ there
    return lax.rem(here - there + exps, exps)


def from_exposure(value, gap, exps):
    if exps & (exps - 1) == 0:
        pairs = [(e, e ^ gap) for e in range(exps)]
    else:
        pairs = [(e, (e + gap) % exps) for e in range(exps)]
    return lax.ppermute(value, exposure_axes, pairs)


def route_body(src, blk, slot_of, sender, request, count, *, peers, capacity):
    def clear_count(p, carry):
        count[p] = 0
        return carry

    def clear_slot(s, carry):
        sender[s] = 0
        request[s // capacity, 0, s % capacity] = 0
        return carry

    lax.fori_loop(0, peers, clear_count, 0, unroll=peers <= 16)
    lax.fori_loop(0, peers * capacity, clear_slot, 0, unroll=peers <= 16)
    for b in range(src.shape[1]):
        owner = src[0, b]
        place = count[owner]
        count[owner] = place + 1
        slot_of[b] = owner * capacity + place
        sender[owner * capacity + place] = b
        request[owner, 0, place] = blk[0, b] + 1


def route_tables(routes_src, routes_blk, peers, capacity):
    return pl.pallas_call(
        functools.partial(route_body, peers=peers, capacity=capacity),
        out_shape=(
            jax.ShapeDtypeStruct((routes_src.shape[1],), jnp.int32),
            jax.ShapeDtypeStruct((peers * capacity,), jnp.int32),
            jax.ShapeDtypeStruct((peers, 1, capacity), jnp.int32),
        ),
        in_specs=[smem()] * 2,
        out_specs=(smem(),) * 3,
        scratch_shapes=[pltpu.SMEM((peers,), jnp.int32)],
        name="route_tables",
    )(routes_src, routes_blk)


def fetch_body(template, near, sem):
    copy = pltpu.make_async_copy(template, near, sem)
    copy.start()
    copy.wait()


def fetch(template):
    return pl.pallas_call(
        fetch_body,
        out_shape=jax.ShapeDtypeStruct(template.shape, template.dtype),
        in_specs=[pl.BlockSpec(memory_space=pl.ANY)],
        out_specs=vmem(),
        scratch_shapes=[pltpu.SemaphoreType.DMA(())],
        compiler_params=pltpu.CompilerParams(vmem_limit_bytes=16 * mib),
        cost_estimate=cost(0, 4_000_000),
        name="fetch",
    )(template)


def pick_body(asked, template, out, sems, *, capacity):
    copies = []
    for s in range(out.shape[0]):
        block = jnp.maximum(asked[s // capacity, 0, s % capacity] - 1, 0)
        copies.append(pltpu.make_async_copy(template.at[block], out.at[s], sems.at[s]))
        copies[-1].start()
    for copy in copies:
        copy.wait()


def pick_blocks(asked, template, slots, capacity):
    return pl.pallas_call(
        functools.partial(pick_body, capacity=capacity),
        out_shape=jax.ShapeDtypeStruct((slots,) + template.shape[1:], template.dtype),
        in_specs=[smem(), vmem()],
        out_specs=pl.BlockSpec(memory_space=pl.ANY),
        scratch_shapes=[pltpu.SemaphoreType.DMA((slots,))],
        compiler_params=pltpu.CompilerParams(vmem_limit_bytes=16 * mib),
        name="pick_blocks",
    )(asked, template)


def store_parts(sender, image, out, side, order, capacity, across_blocks):
    exps = len(order)
    part = side // exps
    slots = sender.shape[0]

    def one(s, carry):
        b = sender[s]
        top = pl.multiple_of((b // across_blocks) * side, side)
        left = pl.multiple_of((b % across_blocks) * side, side)
        block = image[pl.ds(top, side), pl.ds(left, side)].astype(bf16)
        row = pl.multiple_of((s % capacity) * part, part)
        for e, q in enumerate(order):
            out[(s // capacity) * exps + e, pl.ds(row, part), :] = block[q * part : (q + 1) * part]
        return carry

    lax.fori_loop(0, slots, one, 0, unroll=True if slots <= 32 else 4)


def cut(ref, top, left, height, side):
    down = pl.multiple_of((top // 8) * 8, 8)
    over = pl.multiple_of((left // side) * side, side)
    tile = ref[pl.ds(down, height), pl.ds(over, 3 * side)]
    tile = pltpu.roll(tile, lax.rem(3 * side - (left - over), 3 * side), 1)[:, : 2 * side]
    return pltpu.roll(tile, lax.rem(height - (top - down), height), 0)


def hold_body(asked, earlier, out):
    del earlier
    out[...] = asked[...]


def hold(asked, earlier):
    return pl.pallas_call(
        hold_body,
        out_shape=jax.ShapeDtypeStruct(asked.shape, asked.dtype),
        in_specs=[vmem(), pl.BlockSpec(memory_space=pl.ANY)],
        out_specs=vmem(),
        compiler_params=pltpu.CompilerParams(vmem_limit_bytes=16 * mib),
        name="hold",
    )(asked, earlier)


def prepare_body(sender, variance, science, earlier, out, *, side, nears, capacity):
    del earlier, science
    store_parts(sender, variance, out, side, range(nears), capacity, variance.shape[1] // side)


def prepare(sender, variance, science, earlier, side, nears, capacity):
    slots = sender.shape[0]
    part = side // nears
    return pl.pallas_call(
        functools.partial(prepare_body, side=side, nears=nears, capacity=capacity),
        out_shape=jax.ShapeDtypeStruct((slots // capacity * nears, capacity * part, side), bf16),
        in_specs=[smem()] + [vmem()] * 2 + [pl.BlockSpec(memory_space=pl.ANY)],
        out_specs=vmem(),
        compiler_params=pltpu.CompilerParams(vmem_limit_bytes=16 * mib),
        cost_estimate=cost(0, 6_000_000),
        name="prepare",
    )(sender, variance, science, earlier)


def normal_body(
    slot_of,
    rows_at,
    cols_at,
    arrived,
    col,
    row_rev,
    science,
    variance,
    gram_out,
    windows,
    frame,
    cuts,
    vert,
    design,
    roots,
    window,
    *,
    count,
    across_blocks,
    taps,
):
    side = row_rev.shape[1]
    margin = taps // 2
    stamps = rows_at.shape[1]
    span = up(side + taps - 1, 16)
    padded_k = gram_out.shape[1]
    pitch = (count + 2) | 1
    lines_all = stamps * side
    sub = lax.broadcasted_iota(jnp.int32, (side, side), 0)
    lane = lax.broadcasted_iota(jnp.int32, (side, side), 1)

    high, wide = science.shape
    rows_off = up(margin, 8)
    frame[:rows_off, :] = jnp.zeros((rows_off, frame.shape[1]), f32)
    below = rows_off + high
    frame[below:, :] = jnp.zeros((frame.shape[0] - below, frame.shape[1]), f32)
    frame[rows_off:below, :side] = jnp.zeros((high, side), f32)
    after = side + wide
    frame[rows_off:below, after:] = jnp.zeros((high, frame.shape[1] - after), f32)
    for b in range(slot_of.shape[0]):
        top = rows_off + (b // across_blocks) * side
        left = side + (b % across_blocks) * side
        frame[top : top + side, left : left + side] = arrived[slot_of[b]].astype(f32)
    first_row = rows_off - margin
    first_col = side - margin

    def cut_image(ref, top, left):
        tall = min(high, side + 16)
        down = pl.multiple_of(jnp.minimum((top // 16) * 16, high - tall), 16)
        over = pl.multiple_of(jnp.minimum((left // side) * side, wide - 2 * side), side)
        tile = ref[pl.ds(down, tall), pl.ds(over, 2 * side)].astype(f32)
        tile = pltpu.roll(tile, lax.rem(2 * side - (left - over), 2 * side), 1)[:, :side]
        return pltpu.roll(tile, lax.rem(tall - (top - down), tall), 0)[:side]

    for s in range(stamps):
        top = rows_at[0, s]
        left = cols_at[0, s]
        tile = cut(frame, top + first_row, left + first_col, span, side)
        cuts[s * span : (s + 1) * span, :] = tile.astype(bf16)
        root = lax.rsqrt(cut_image(variance, top, left))
        roots[s * side : (s + 1) * side, :] = root
        place = pl.ds(s * side * pitch + count, side, stride=pitch)
        design[place, :] = root
        place = pl.ds(s * side * pitch + count + 1, side, stride=pitch)
        design[place, :] = root * cut_image(science, top, left)
    design[lines_all * pitch :, :] = jnp.zeros((design.shape[0] - lines_all * pitch, side), f32)

    group = vert.shape[0]
    step = side - taps + 1
    starts = list(range(0, count, group))
    for turn, k in enumerate(starts):
        for c in range(turn, windows.shape[0], len(starts)):
            left = first_col + c * step
            window[...] = frame[first_row : first_row + window.shape[0], left : left + side]
            for parity in range(2):
                place = pl.ds(parity, windows.shape[2], stride=2)
                windows[c, parity] = window[place, :]
        filters = []
        for a in range(group):
            line = jnp.broadcast_to(col[k + a : k + a + 1, :], (side, side))
            line = pltpu.roll(line, 0, 1, stride=1, stride_axis=0)
            first = jnp.where(lane >= sub, line, 0.0).astype(bf16)
            second = jnp.where(lane < sub, line, 0.0).astype(bf16)
            filters.append(jnp.concatenate([first, second[:, : span - side]], axis=1))
        filters = jnp.concatenate(filters, axis=0)
        for s in range(stamps):
            out = jnp.dot(
                filters, cuts[s * span : (s + 1) * span, :], preferred_element_type=f32
            ).astype(bf16)
            for a in range(group):
                vert[a, s * side : (s + 1) * side, :] = out[a * side : (a + 1) * side]
        for a in range(group):
            line = jnp.broadcast_to(row_rev[k + a : k + a + 1, :], (side, side))
            line = pltpu.roll(line, 0, 1, stride=1, stride_axis=0)
            first = jnp.where(lane <= sub, line, 0.0).astype(bf16)
            second = jnp.where(lane > sub, line, 0.0).astype(bf16)
            band = jnp.concatenate([first, second], axis=0)
            out = jnp.dot(vert[a], band, preferred_element_type=f32)
            design[pl.ds(k + a, lines_all, stride=pitch), :] = out * roots[...]

    lines = 16
    sets = 4

    def gram_step(step, total):
        start = pl.multiple_of(step * sets * lines * pitch, 8)
        rows = []
        for g in range(sets):
            row = [
                design[pl.ds(start + (g * lines + j) * pitch, padded_k), :].astype(bf16)
                for j in range(lines)
            ]
            rows.append(jnp.concatenate(row, axis=1))
        both = jnp.concatenate(rows, axis=0)
        return total + lax.dot_general(
            both, both, (((1,), (1,)), ((), ())), preferred_element_type=f32
        )

    total = lax.fori_loop(
        0,
        lines_all // (lines * sets),
        gram_step,
        jnp.zeros((sets * padded_k, sets * padded_k), f32),
        unroll=2,
    )
    part = jnp.zeros((padded_k, padded_k), f32)
    for g in range(sets):
        rows = slice(g * padded_k, (g + 1) * padded_k)
        part = part + total[rows, rows]
    gram_out[...] = part


def subtract_body(
    sender,
    gram,
    frames,
    science,
    col_t,
    row_rev,
    coef_out,
    payload,
    window,
    image,
    bands,
    total,
    *,
    order,
    capacity,
    count,
    taps,
    pixels,
):
    side = frames.shape[3]
    high, wide = science.shape
    padded_k = gram.shape[1]
    part = side // len(order)
    size = count + 1

    system = jnp.concatenate(
        [gram[...], jnp.zeros((padded_k, side - padded_k), f32)], axis=1
    ) / pixels
    sub = lax.broadcasted_iota(jnp.int32, (padded_k, side), 0)
    lane = lax.broadcasted_iota(jnp.int32, (padded_k, side), 1)
    system = jnp.where((sub < size) & (lane <= size), system, 0.0)
    system = system + jnp.where((sub == lane) & (sub < size), ridge_term, 0.0)

    pairs = (taps + 2) // 2
    rows_half = high // 2
    wins = frames.shape[0]

    for k in range(0, size, 8):
        block = range(min(8, size - k))
        cols = [jnp.broadcast_to(system[:, k + j : k + j + 1], system.shape) for j in block]
        rows = [system[k + j : k + j + 1, :] for j in block]
        core = [[cols[j][k + i : k + i + 1, :] for j in block] for i in block]
        for j in block:
            inverse = 1.0 / core[j][j]
            factor = jnp.where(sub == k + j, 0.0, cols[j] * inverse)
            system = system - factor * rows[j]
            for i in block[j + 1 :]:
                scale = core[i][j] * inverse
                rows[i] = rows[i] - scale * rows[j]
                for l in block[j + 1 :]:
                    core[i][l] = core[i][l] - scale * core[j][l]
                cols[i] = cols[i] - factor * core[j][i]
    pivot = jnp.sum(jnp.where(sub == lane, system, 0.0), axis=1, keepdims=True)
    solved = system[:, size : size + 1] / jnp.where(sub[:, :1] < size, pivot, 1.0)
    coef_out[...] = jnp.sum(jnp.where(sub == lane, solved, 0.0), axis=0, keepdims=True)
    background = solved[count : count + 1, :]
    basis_coef = jnp.where(sub[:, :1] < count, solved, 0.0)

    scaled = basis_coef * row_rev[...]
    kernel = jnp.zeros((col_t.shape[0], side), f32)
    for _ in range(3):
        piece = scaled.astype(bf16)
        scaled = scaled - piece.astype(f32)
        kernel = kernel + jnp.dot(col_t[...], piece, preferred_element_type=f32)
    kernel_sum = jnp.sum(jnp.sum(kernel, axis=1, keepdims=True), axis=0, keepdims=True)
    rounded = kernel.astype(bf16).astype(f32)

    zero_band = jnp.zeros((side, side), bf16)

    def band(i):
        if i < 0 or i >= taps:
            return zero_band
        line = jnp.broadcast_to(rounded[i : i + 1, :], (side, side))
        return pltpu.roll(line, 0, 1, stride=1, stride_axis=0).astype(bf16)

    made = {i: band(i) for i in range(-1, 2 * pairs)}
    for q in range(pairs):
        for a in range(2):
            for b in range(2):
                bands[
                    q * 2 * side + a * side : q * 2 * side + (a + 1) * side,
                    b * side : (b + 1) * side,
                ] = made[2 * q + a - b]

    step = side - taps + 1
    joint = pairs
    for q in range(0, pairs, joint):
        last = min(q + joint, pairs)
        lhs = jnp.concatenate(
            [
                jnp.concatenate(
                    [
                        frames[c, a, p : p + rows_half, :].astype(bf16)
                        for p in range(q, last)
                        for a in range(2)
                    ],
                    axis=1,
                )
                for c in range(wins)
            ],
            axis=0,
        )
        out = jnp.dot(
            lhs, bands[q * 2 * side : last * 2 * side, :], preferred_element_type=f32
        )
        if q:
            out = out + total[...]
        if last < pairs:
            total[...] = out
    for c in range(wins):
        rows = out[c * rows_half : (c + 1) * rows_half]
        window[c, pl.ds(0, rows_half, stride=2), :] = rows[:, :side]
        window[c, pl.ds(1, rows_half, stride=2), :] = rows[:, side:]
        keep = min(step, wide - c * step)
        image[:, c * step : c * step + keep] = window[c, :, :keep]
    image[...] = science[...].astype(f32) - image[...] - background

    store_parts(sender, image, payload, side, order, capacity, wide // side)
    line_at = lax.broadcasted_iota(jnp.int32, (trailer_rows, side), 0)
    trailer = jnp.zeros((trailer_rows, side), f32)
    rest = kernel_sum
    for p in range(3):
        piece = rest.astype(bf16).astype(f32)
        rest = rest - piece
        trailer = jnp.where(line_at == p, piece, trailer)
    trailer = trailer.astype(bf16)

    def put(d, carry):
        payload[d, capacity * part :, :] = trailer
        return carry

    lax.fori_loop(0, payload.shape[0], put, 0, unroll=4)


def fit_body(
    slot_of,
    sender,
    rows_at,
    cols_at,
    arrived,
    col,
    row_rev,
    science,
    variance,
    col_t,
    coef_out,
    payload,
    *scratch,
    order,
    capacity,
    count,
    taps,
):
    gram, windows = scratch[:2]
    stamps = rows_at.shape[1]
    side = row_rev.shape[1]
    normal_body(
        slot_of,
        rows_at,
        cols_at,
        arrived,
        col,
        row_rev,
        science,
        variance,
        gram,
        windows,
        *scratch[2:8],
        count=count,
        across_blocks=science.shape[1] // side,
        taps=taps,
    )
    subtract_body(
        sender,
        gram,
        windows,
        science,
        col_t,
        row_rev,
        coef_out,
        payload,
        *scratch[8:],
        order=order,
        capacity=capacity,
        count=count,
        taps=taps,
        pixels=stamps * side * side,
    )


def fit_and_subtract(
    slot_of,
    sender,
    rows_at,
    cols_at,
    arrived,
    col,
    row_rev,
    science,
    variance,
    col_t,
    order,
    capacity,
    count,
    taps,
):
    exps = len(order)
    high, wide = science.shape
    side = row_rev.shape[1]
    slots = sender.shape[0]
    stamps = rows_at.shape[1]
    padded_k = up(count + 2, 16)
    pairs = (taps + 2) // 2
    span = up(side + taps - 1, 16)
    half = up(high // 2 + pairs, 8)
    tall = up(taps // 2, 8) + max(high - side + span, 2 * half)
    wins = -(-wide // (side - taps + 1))
    group = next(g for g in (20, 8, 4, 2, 1) if count % g == 0)
    return pl.pallas_call(
        functools.partial(fit_body, order=order, capacity=capacity, count=count, taps=taps),
        out_shape=(
            jax.ShapeDtypeStruct((1, side), f32),
            jax.ShapeDtypeStruct(
                (slots // capacity * exps, capacity * side // exps + trailer_rows, side), bf16
            ),
        ),
        in_specs=[smem()] * 4 + [vmem()] * 6,
        out_specs=(vmem(),) * 2,
        scratch_shapes=[
            pltpu.VMEM((padded_k, padded_k), f32),
            pltpu.VMEM((wins, 2, half, side), f32),
            pltpu.VMEM((tall, wide + 2 * side), f32),
            pltpu.VMEM((stamps * span, 2 * side), bf16),
            pltpu.VMEM((group, stamps * side, 2 * side), bf16),
            pltpu.VMEM((up(stamps * side * ((count + 2) | 1) + padded_k, 8), side), f32),
            pltpu.VMEM((stamps * side, side), f32),
            pltpu.VMEM((2 * half, side), f32),
            pltpu.VMEM((wins, high, side), f32),
            pltpu.VMEM((high, wide), f32),
            pltpu.VMEM((pairs * 2 * side, 2 * side), bf16),
            pltpu.VMEM((wins * high // 2, 2 * side), f32),
        ],
        compiler_params=pltpu.CompilerParams(vmem_limit_bytes=30 * mib),
        cost_estimate=cost(15_000_000_000, 8_000_000),
        name="fit_and_subtract",
    )(
        slot_of,
        sender,
        rows_at,
        cols_at,
        arrived,
        col,
        row_rev,
        science,
        variance,
        col_t,
    )


def split2(value):
    top = value.astype(bf16)
    return top, (value - top.astype(f32)).astype(bf16)


def score_body(
    slot_of, payload, down, over, out, token, padded, sideways, *, order, taps, capacity
):
    token[...] = jnp.zeros(token.shape, f32)
    side = payload.shape[2]
    part = side // len(order)
    high, wide = out.shape
    margin = taps // 2
    span = up(side + taps - 1, 16)
    across_blocks = wide // side
    exps = len(order)
    padded[...] = jnp.zeros(padded.shape, f32)
    for b in range(slot_of.shape[0]):
        slot = slot_of[b]
        row = pl.multiple_of((slot % capacity) * part, part)
        left = margin + (b % across_blocks) * side
        for e, q in enumerate(order):
            top = (b // across_blocks) * side + q * part
            block = payload[(slot // capacity) * exps + e, pl.ds(row, part), :]
            padded[top : top + part, left : left + side] = block.astype(f32)
    line = jnp.broadcast_to(over[...], (2 * side, 2 * side))
    band = pltpu.roll(line, 0, 1, stride=1, stride_axis=0)[:, :side]
    both = jnp.concatenate(split2(band), axis=1)
    sideways[...] = jnp.zeros(sideways.shape, f32)
    for c in range(wide // side):
        window = padded[:, c * side : (c + 2) * side].astype(bf16)
        got = jnp.dot(window, both, preferred_element_type=f32)
        sideways[margin : margin + high, c * side : (c + 1) * side] = got[:, :side] + got[:, side:]
    line = jnp.broadcast_to(down[...], (side, 2 * side))
    band = pltpu.roll(line, 0, 1, stride=1, stride_axis=0)[:, :span]
    top, low = split2(band)
    for r in range(high // side):
        data_top, data_low = split2(sideways[r * side : r * side + span, :])
        got = jnp.dot(top, data_top, preferred_element_type=f32)
        got = got + jnp.dot(top, data_low, preferred_element_type=f32)
        got = got + jnp.dot(low, data_top, preferred_element_type=f32)
        out[r * side : (r + 1) * side, :] = got


def score(slot_of, payload, down, over_rev, high, wide, taps, order, capacity):
    side = payload.shape[2]
    span = up(side + taps - 1, 16)
    return pl.pallas_call(
        functools.partial(score_body, order=order, taps=taps, capacity=capacity),
        out_shape=(
            jax.ShapeDtypeStruct((high, wide), f32),
            jax.ShapeDtypeStruct((8, 128), f32),
        ),
        in_specs=[smem()] + [vmem()] * 3,
        out_specs=(vmem(), vmem()),
        scratch_shapes=[
            pltpu.VMEM((high, wide + side), f32),
            pltpu.VMEM((high - side + span, wide), f32),
        ],
        compiler_params=pltpu.CompilerParams(vmem_limit_bytes=20 * mib),
        cost_estimate=cost(2_000_000_000, 2_000_000),
        name="score",
    )(slot_of, payload, down, over_rev)


def wanted_block(me, exposure, table, d, c, tract):
    exps = table.shape[0]
    block = table[distance(me[0], exposure, exps), d, c] - 1
    return jnp.where(block < 0, tract, block)


def variance_body(
    me, table, parts, template_var, own_out, other_out, template_out, total, sem, *, nears, capacity
):
    exps = table.shape[0]
    fars = exps // nears
    tract, part, _ = own_out.shape
    mine = pl.ds(pl.multiple_of(part_of(me[0], exps, nears) * part, part), part)
    copy = pltpu.make_async_copy(template_var.at[:, mine, :], template_out, sem)
    copy.start()
    total[...] = jnp.zeros(total.shape, f32)
    far = me[0] // nears
    rows = fars * part

    def one(j, carry):
        exposure = far * nears + lax.rem(j, nears)
        for c in range(capacity):
            block = wanted_block(me, exposure, table, j // nears, c, tract)
            total[block] += parts[j, c * rows : (c + 1) * rows, :].astype(f32)
        return carry

    lax.fori_loop(0, parts.shape[0], one, 0, unroll=4)
    own_out[...] = total[:tract, pl.ds(pl.multiple_of(far * part, part), part), :]
    for g in range(1, fars):
        there = lax.rem(far + g, fars)
        rows_there = pl.ds(pl.multiple_of(there * part, part), part)
        other_out[g - 1] = total[:tract, rows_there, :].astype(bf16)
    copy.wait()


def sum_variance(me, table, parts, template_var, nears, capacity):
    tract, side, _ = template_var.shape
    exps = table.shape[0]
    fars = exps // nears
    part = side // exps
    return pl.pallas_call(
        functools.partial(variance_body, nears=nears, capacity=capacity),
        out_shape=(
            jax.ShapeDtypeStruct((tract, part, side), f32),
            jax.ShapeDtypeStruct((max(1, fars - 1), tract, part, side), bf16),
            jax.ShapeDtypeStruct((tract, part, side), template_var.dtype),
        ),
        in_specs=[smem()] * 2 + [vmem(), pl.BlockSpec(memory_space=pl.ANY)],
        out_specs=(vmem(),) * 3,
        scratch_shapes=[
            pltpu.VMEM((tract + 1, fars * part, side), f32),
            pltpu.SemaphoreType.DMA(()),
        ],
        compiler_params=pltpu.CompilerParams(vmem_limit_bytes=16 * mib),
        cost_estimate=cost(0, 4_000_000),
        name="sum_variance",
    )(me, table, parts, template_var)


def combine_body(me, table, earlier, parts, own_var, var_template, *rest, part, capacity):
    del earlier
    others = rest[:-3]
    out, total, gain = rest[-3:]
    total[...] = jnp.zeros(total.shape, f32)
    gain[...] = jnp.zeros(gain.shape, f32)
    tract = out.shape[0]
    exps = table.shape[0]

    def one(j, carry):
        tail = parts[j, capacity * part :, :].astype(f32)
        kernel_sum = tail[0:1] + tail[1:2] + tail[2:3]
        square = jnp.broadcast_to(kernel_sum * kernel_sum, gain.shape[1:])
        for c in range(capacity):
            block = wanted_block(me, lax.rem(j, exps), table, j // exps, c, tract)
            total[block] += parts[j, c * part : (c + 1) * part, :].astype(f32)
            gain[block] += square
        return carry

    lax.fori_loop(0, parts.shape[0], one, 0, unroll=4)
    for t in range(tract):
        variance = own_var[t] + gain[t, 0:1, :] * var_template[t].astype(f32)
        for other in others:
            variance = variance + other[t].astype(f32)
        out[t] = (total[t] * lax.rsqrt(jnp.maximum(variance, 1.0))).astype(bf16)


def combine(me, table, earlier, parts, own_var, var_template, others, capacity):
    tract, part, side = own_var.shape
    return pl.pallas_call(
        functools.partial(combine_body, part=part, capacity=capacity),
        out_shape=jax.ShapeDtypeStruct((tract, part, side), bf16),
        in_specs=[smem(), smem(), pl.BlockSpec(memory_space=pl.ANY)]
        + [vmem()] * (3 + len(others)),
        out_specs=vmem(),
        scratch_shapes=[
            pltpu.VMEM((tract + 1, part, side), f32),
            pltpu.VMEM((tract + 1, 8, side), f32),
        ],
        compiler_params=pltpu.CompilerParams(vmem_limit_bytes=16 * mib),
        name="combine",
    )(me, table, earlier, parts, own_var, var_template, *others)


def join_body(places, *refs, part, count):
    ins = refs[:count]
    out, held, sems = refs[-3:]
    copies = []
    for d, ref in enumerate(ins):
        held[d] = ref[...].astype(f32)
        row = pl.multiple_of(places[d] * part, part)
        copies.append(
            pltpu.make_async_copy(held.at[d], out.at[:, pl.ds(row, part), :], sems.at[d])
        )
        copies[-1].start()
    for copy in copies:
        copy.wait()


def join_parts(places, parts, whole, exps):
    tract, part, side = parts[0].shape
    count = len(parts)
    fresh = whole is None
    anywhere = pl.BlockSpec(memory_space=pl.ANY)
    return pl.pallas_call(
        functools.partial(join_body, part=part, count=count),
        out_shape=jax.ShapeDtypeStruct((tract, part * exps, side), f32),
        in_specs=[smem()] + [vmem()] * count + ([] if fresh else [anywhere]),
        out_specs=anywhere,
        scratch_shapes=[
            pltpu.VMEM((count, tract, part, side), f32),
            pltpu.SemaphoreType.DMA((count,)),
        ],
        input_output_aliases={} if fresh else {count + 1: 0},
        compiler_params=pltpu.CompilerParams(vmem_limit_bytes=16 * mib),
        cost_estimate=cost(0, 3_000_000 * count),
        name="join_parts",
    )(places, *parts, *([] if fresh else [whole]))


def local(
    template,
    template_var,
    science,
    science_var,
    routes_src,
    routes_blk,
    stamp_rows,
    stamp_cols,
    basis_col,
    basis_row,
    psf_col,
    psf_row,
):
    peers = lax.axis_size("det")
    nears = lax.axis_size("near")
    exps = lax.axis_size("far") * nears
    me = (lax.axis_index("far") * nears + lax.axis_index("near")).astype(jnp.int32)
    order = tuple((e % nears) * (exps // nears) + e // nears for e in range(exps))
    tract, side, _ = template.shape
    science_img = science[0]
    variance_img = science_var[0]
    blocks_dev = routes_src.shape[1]
    count, taps = basis_col.shape
    capacity = max(2, -(-blocks_dev // peers))
    slots = peers * capacity
    part = side // exps

    slot_of, sender, request = route_tables(routes_src, routes_blk, peers, capacity)
    asked = lax.all_to_all(request, "det", split_axis=0, concat_axis=0, tiled=True)
    picked = pick_blocks(asked, fetch(template), slots, capacity)
    held = hold(asked, picked)
    tables = [held] + [from_exposure(held, g, exps) for g in range(1, exps)]
    table = jnp.stack(tables).reshape(exps, peers, capacity)
    var_parts = prepare(sender, variance_img, science_img, table, side, nears, capacity)
    arrived = lax.all_to_all(picked, "det", split_axis=0, concat_axis=0, tiled=True)

    padded_k = up(count + 2, 16)
    col_t = jnp.pad(basis_col.T, ((0, up(taps, 16) - taps), (0, padded_k - count)))
    col = jnp.pad(basis_col.astype(f32), ((0, padded_k - count), (0, side - taps)))
    row_rev = jnp.pad(
        basis_row.astype(f32)[:, ::-1], ((0, padded_k - count), (side - taps, 0))
    )
    row_rev = jnp.roll(row_rev, 1, axis=1)
    over_rev = jnp.roll(jnp.pad(psf_row[:, ::-1], ((0, 0), (2 * side - taps, 0))), 1, axis=1)
    down = jnp.pad(psf_col, ((0, 0), (0, 2 * side - taps)))
    var_late, arrived = lax.optimization_barrier((var_parts, arrived))
    var_back = lax.all_to_all(
        var_late, ("det", "near"), split_axis=0, concat_axis=0, tiled=True
    )

    high, wide = science_img.shape
    coef, payload = fit_and_subtract(
        slot_of,
        sender,
        stamp_rows,
        stamp_cols,
        arrived,
        col,
        row_rev,
        science_img,
        variance_img,
        col_t,
        order,
        capacity,
        count,
        taps,
    )
    diff_back = lax.all_to_all(payload, ("det",) + exposure_axes, split_axis=0, concat_axis=0, tiled=True)
    own_var, other_var, var_template = sum_variance(
        me[None], table, var_back, template_var, nears, capacity
    )
    fars = exps // nears
    others = []
    for g in range(1, fars):
        pairs = [(f, (f + g) % fars) for f in range(fars)]
        others.append(lax.ppermute(other_var[g - 1], "far", pairs))
    scored, token = score(
        slot_of, payload, down, over_rev, high, wide, taps, order, capacity
    )
    mine = combine(me[None], table, token, diff_back, own_var, var_template, others, capacity)

    def swap(value, distance):
        return lax.ppermute(value, exposure_axes, [(e, e ^ distance) for e in range(exps)])

    def put(parts, whole):
        places = jnp.stack([part_of(there, exps, nears) for there, _ in parts])
        return join_parts(places, [held for _, held in parts], whole, exps)

    if exps == 4:
        far = swap(mine, 2)
        near = swap(mine, 1)
        last = swap(far, 1)
        whole = put([(me, mine), (me ^ 1, near), (me ^ 2, far)], None)
        significance = put([(me ^ 3, last)], whole)
    else:
        parts = [(me, mine)]
        for gap in range(1, exps):
            pairs = [(e, (e + gap) % exps) for e in range(exps)]
            parts.append(((me - gap) % exps, lax.ppermute(mine, exposure_axes, pairs)))
        significance = put(parts, None)
    return (significance, scored[None], coef[:, : count + 1])


def solution(mesh):
    peers, exps = mesh.devices.shape
    nears = 2 if exps % 2 == 0 else 1
    split = jax.sharding.Mesh(
        mesh.devices.reshape(peers, exps // nears, nears), ("det",) + exposure_axes
    )
    placed = (
        P("det", None, None),
        P("det", None, None),
        P(exposure_axes, "det", None),
        P(exposure_axes, "det", None),
        P(exposure_axes, "det"),
        P(exposure_axes, "det"),
        P(exposure_axes, "det"),
        P(exposure_axes, "det"),
        P(),
        P(),
        P(exposure_axes, None),
        P(exposure_axes, None),
    )
    return jax.shard_map(
        local,
        mesh=split,
        in_specs=placed,
        out_specs=(
            P("det", None, None),
            P(exposure_axes, "det", None),
            P(exposure_axes, "det"),
        ),
        check_vma=False,
    )
```

```python
import functools

import jax
import jax.numpy as jnp
from jax import lax
from jax.experimental import pallas as pl
from jax.experimental.pallas import tpu as pltpu
from jax.sharding import PartitionSpec as P

ridge_term = 0.01
bf16 = jnp.bfloat16
f32 = jnp.float32
vmem = functools.partial(pl.BlockSpec, memory_space=pltpu.VMEM)
smem = functools.partial(pl.BlockSpec, memory_space=pltpu.SMEM)
mib = 1024 * 1024
trailer_rows = 8


def up(value, step):
    return -(-value // step) * step


def cost(flops, moved):
    return pl.CostEstimate(flops=flops, bytes_accessed=moved, transcendentals=0)


exposure_axes = ("far", "near")


def part_of(exposure, exps, nears):
    return lax.rem(exposure, nears) * (exps // nears) + exposure // nears


def distance(here, there, exps):
    if exps & (exps - 1) == 0:
        return here ^ there
    return lax.rem(here - there + exps, exps)


def from_exposure(value, gap, exps):
    if exps & (exps - 1) == 0:
        pairs = [(e, e ^ gap) for e in range(exps)]
    else:
        pairs = [(e, (e + gap) % exps) for e in range(exps)]
    return lax.ppermute(value, exposure_axes, pairs)


def route_body(src, blk, slot_of, sender, request, count, *, peers, capacity):
    def clear_count(p, carry):
        count[p] = 0
        return carry

    def clear_slot(s, carry):
        sender[s] = 0
        request[s // capacity, 0, s % capacity] = 0
        return carry

    lax.fori_loop(0, peers, clear_count, 0, unroll=peers <= 16)
    lax.fori_loop(0, peers * capacity, clear_slot, 0, unroll=peers <= 16)
    for b in range(src.shape[1]):
        owner = src[0, b]
        place = count[owner]
        count[owner] = place + 1
        slot_of[b] = owner * capacity + place
        sender[owner * capacity + place] = b
        request[owner, 0, place] = blk[0, b] + 1


def route_tables(routes_src, routes_blk, peers, capacity):
    return pl.pallas_call(
        functools.partial(route_body, peers=peers, capacity=capacity),
        out_shape=(
            jax.ShapeDtypeStruct((routes_src.shape[1],), jnp.int32),
            jax.ShapeDtypeStruct((peers * capacity,), jnp.int32),
            jax.ShapeDtypeStruct((peers, 1, capacity), jnp.int32),
        ),
        in_specs=[smem()] * 2,
        out_specs=(smem(),) * 3,
        scratch_shapes=[pltpu.SMEM((peers,), jnp.int32)],
        name="route_tables",
    )(routes_src, routes_blk)


def fetch_body(template, near, sem):
    copy = pltpu.make_async_copy(template, near, sem)
    copy.start()
    copy.wait()


def fetch(template):
    return pl.pallas_call(
        fetch_body,
        out_shape=jax.ShapeDtypeStruct(template.shape, template.dtype),
        in_specs=[pl.BlockSpec(memory_space=pl.ANY)],
        out_specs=vmem(),
        scratch_shapes=[pltpu.SemaphoreType.DMA(())],
        compiler_params=pltpu.CompilerParams(vmem_limit_bytes=16 * mib),
        cost_estimate=cost(0, 4_000_000),
        name="fetch",
    )(template)


def pick_body(asked, template, out, sems, *, capacity):
    copies = []
    for s in range(out.shape[0]):
        block = jnp.maximum(asked[s // capacity, 0, s % capacity] - 1, 0)
        copies.append(pltpu.make_async_copy(template.at[block], out.at[s], sems.at[s]))
        copies[-1].start()
    for copy in copies:
        copy.wait()


def pick_blocks(asked, template, slots, capacity):
    return pl.pallas_call(
        functools.partial(pick_body, capacity=capacity),
        out_shape=jax.ShapeDtypeStruct((slots,) + template.shape[1:], template.dtype),
        in_specs=[smem(), vmem()],
        out_specs=pl.BlockSpec(memory_space=pl.ANY),
        scratch_shapes=[pltpu.SemaphoreType.DMA((slots,))],
        compiler_params=pltpu.CompilerParams(vmem_limit_bytes=16 * mib),
        name="pick_blocks",
    )(asked, template)


def store_parts(sender, image, out, side, order, capacity, across_blocks):
    exps = len(order)
    part = side // exps
    slots = sender.shape[0]

    def one(s, carry):
        b = sender[s]
        top = pl.multiple_of((b // across_blocks) * side, side)
        left = pl.multiple_of((b % across_blocks) * side, side)
        block = image[pl.ds(top, side), pl.ds(left, side)].astype(bf16)
        row = pl.multiple_of((s % capacity) * part, part)
        for e, q in enumerate(order):
            out[(s // capacity) * exps + e, pl.ds(row, part), :] = block[q * part : (q + 1) * part]
        return carry

    lax.fori_loop(0, slots, one, 0, unroll=True if slots <= 32 else 4)


def cut(ref, top, left, height, side):
    down = pl.multiple_of((top // 8) * 8, 8)
    over = pl.multiple_of((left // side) * side, side)
    tile = ref[pl.ds(down, height), pl.ds(over, 3 * side)]
    tile = pltpu.roll(tile, lax.rem(3 * side - (left - over), 3 * side), 1)[:, : 2 * side]
    return pltpu.roll(tile, lax.rem(height - (top - down), height), 0)


def hold_body(asked, earlier, out):
    del earlier
    out[...] = asked[...]


def hold(asked, earlier):
    return pl.pallas_call(
        hold_body,
        out_shape=jax.ShapeDtypeStruct(asked.shape, asked.dtype),
        in_specs=[vmem(), pl.BlockSpec(memory_space=pl.ANY)],
        out_specs=vmem(),
        compiler_params=pltpu.CompilerParams(vmem_limit_bytes=16 * mib),
        name="hold",
    )(asked, earlier)


def prepare_body(sender, variance, science, earlier, out, *, side, nears, capacity):
    del earlier, science
    store_parts(sender, variance, out, side, range(nears), capacity, variance.shape[1] // side)


def prepare(sender, variance, science, earlier, side, nears, capacity):
    slots = sender.shape[0]
    part = side // nears
    return pl.pallas_call(
        functools.partial(prepare_body, side=side, nears=nears, capacity=capacity),
        out_shape=jax.ShapeDtypeStruct((slots // capacity * nears, capacity * part, side), bf16),
        in_specs=[smem()] + [vmem()] * 2 + [pl.BlockSpec(memory_space=pl.ANY)],
        out_specs=vmem(),
        compiler_params=pltpu.CompilerParams(vmem_limit_bytes=16 * mib),
        cost_estimate=cost(0, 6_000_000),
        name="prepare",
    )(sender, variance, science, earlier)


def normal_body(
    slot_of,
    rows_at,
    cols_at,
    arrived,
    col,
    row_rev,
    science,
    variance,
    gram_out,
    windows,
    frame,
    cuts,
    vert,
    design,
    roots,
    window,
    *,
    count,
    across_blocks,
    taps,
):
    side = row_rev.shape[1]
    margin = taps // 2
    stamps = rows_at.shape[1]
    span = up(side + taps - 1, 16)
    padded_k = gram_out.shape[1]
    pitch = (count + 2) | 1
    lines_all = stamps * side
    sub = lax.broadcasted_iota(jnp.int32, (side, side), 0)
    lane = lax.broadcasted_iota(jnp.int32, (side, side), 1)

    high, wide = science.shape
    rows_off = up(margin, 8)
    frame[:rows_off, :] = jnp.zeros((rows_off, frame.shape[1]), f32)
    below = rows_off + high
    frame[below:, :] = jnp.zeros((frame.shape[0] - below, frame.shape[1]), f32)
    frame[rows_off:below, :side] = jnp.zeros((high, side), f32)
    after = side + wide
    frame[rows_off:below, after:] = jnp.zeros((high, frame.shape[1] - after), f32)
    for b in range(slot_of.shape[0]):
        top = rows_off + (b // across_blocks) * side
        left = side + (b % across_blocks) * side
        frame[top : top + side, left : left + side] = arrived[slot_of[b]].astype(f32)
    first_row = rows_off - margin
    first_col = side - margin

    def cut_image(ref, top, left):
        tall = min(high, side + 16)
        down = pl.multiple_of(jnp.minimum((top // 16) * 16, high - tall), 16)
        over = pl.multiple_of(jnp.minimum((left // side) * side, wide - 2 * side), side)
        tile = ref[pl.ds(down, tall), pl.ds(over, 2 * side)].astype(f32)
        tile = pltpu.roll(tile, lax.rem(2 * side - (left - over), 2 * side), 1)[:, :side]
        return pltpu.roll(tile, lax.rem(tall - (top - down), tall), 0)[:side]

    for s in range(stamps):
        top = rows_at[0, s]
        left = cols_at[0, s]
        tile = cut(frame, top + first_row, left + first_col, span, side)
        cuts[s * span : (s + 1) * span, :] = tile.astype(bf16)
        root = lax.rsqrt(cut_image(variance, top, left))
        roots[s * side : (s + 1) * side, :] = root
        place = pl.ds(s * side * pitch + count, side, stride=pitch)
        design[place, :] = root
        place = pl.ds(s * side * pitch + count + 1, side, stride=pitch)
        design[place, :] = root * cut_image(science, top, left)
    design[lines_all * pitch :, :] = jnp.zeros((design.shape[0] - lines_all * pitch, side), f32)

    step = side - taps + 1
    for c in range(windows.shape[0]):
        left = first_col + c * step
        window[...] = frame[first_row : first_row + window.shape[0], left : left + side]
        for parity in range(2):
            place = pl.ds(parity, windows.shape[2], stride=2)
            windows[c, parity] = window[place, :]

    group = vert.shape[0]

    def passes(turn, carry):
        k = pl.multiple_of(turn * group, group)
        col_rows = col[pl.ds(k, group), :]
        row_rows = row_rev[pl.ds(k, group), :]
        filters = []
        for a in range(group):
            line = jnp.broadcast_to(col_rows[a : a + 1, :], (side, side))
            line = pltpu.roll(line, 0, 1, stride=1, stride_axis=0)
            first = jnp.where(lane >= sub, line, 0.0).astype(bf16)
            second = jnp.where(lane < sub, line, 0.0).astype(bf16)
            filters.append(jnp.concatenate([first, second[:, : span - side]], axis=1))
        filters = jnp.concatenate(filters, axis=0)
        for s in range(stamps):
            out = jnp.dot(
                filters, cuts[s * span : (s + 1) * span, :], preferred_element_type=f32
            ).astype(bf16)
            for a in range(group):
                vert[a, s * side : (s + 1) * side, :] = out[a * side : (a + 1) * side]
        for a in range(group):
            line = jnp.broadcast_to(row_rows[a : a + 1, :], (side, side))
            line = pltpu.roll(line, 0, 1, stride=1, stride_axis=0)
            first = jnp.where(lane <= sub, line, 0.0).astype(bf16)
            second = jnp.where(lane > sub, line, 0.0).astype(bf16)
            band = jnp.concatenate([first, second], axis=0)
            out = jnp.dot(vert[a], band, preferred_element_type=f32)
            design[pl.ds(k + a, lines_all, stride=pitch), :] = out * roots[...]
        return carry

    lax.fori_loop(0, count // group, passes, 0)

    lines = 16
    sets = 4

    def gram_step(step, total):
        start = pl.multiple_of(step * sets * lines * pitch, 8)
        rows = []
        for g in range(sets):
            row = [
                design[pl.ds(start + (g * lines + j) * pitch, padded_k), :].astype(bf16)
                for j in range(lines)
            ]
            rows.append(jnp.concatenate(row, axis=1))
        both = jnp.concatenate(rows, axis=0)
        return total + lax.dot_general(
            both, both, (((1,), (1,)), ((), ())), preferred_element_type=f32
        )

    total = lax.fori_loop(
        0,
        lines_all // (lines * sets),
        gram_step,
        jnp.zeros((sets * padded_k, sets * padded_k), f32),
        unroll=2,
    )
    part = jnp.zeros((padded_k, padded_k), f32)
    for g in range(sets):
        rows = slice(g * padded_k, (g + 1) * padded_k)
        part = part + total[rows, rows]
    gram_out[...] = part


def subtract_body(
    sender,
    gram,
    frames,
    science,
    col_t,
    row_rev,
    coef_out,
    payload,
    window,
    image,
    bands,
    total,
    *,
    order,
    capacity,
    count,
    taps,
    pixels,
):
    side = frames.shape[3]
    high, wide = science.shape
    padded_k = gram.shape[1]
    part = side // len(order)
    size = count + 1

    system = jnp.concatenate(
        [gram[...], jnp.zeros((padded_k, side - padded_k), f32)], axis=1
    ) / pixels
    sub = lax.broadcasted_iota(jnp.int32, (padded_k, side), 0)
    lane = lax.broadcasted_iota(jnp.int32, (padded_k, side), 1)
    system = jnp.where((sub < size) & (lane <= size), system, 0.0)
    system = system + jnp.where((sub == lane) & (sub < size), ridge_term, 0.0)

    pairs = (taps + 2) // 2
    rows_half = high // 2
    wins = frames.shape[0]

    for k in range(0, size, 8):
        block = range(min(8, size - k))
        cols = [jnp.broadcast_to(system[:, k + j : k + j + 1], system.shape) for j in block]
        rows = [system[k + j : k + j + 1, :] for j in block]
        core = [[cols[j][k + i : k + i + 1, :] for j in block] for i in block]
        for j in block:
            inverse = 1.0 / core[j][j]
            factor = jnp.where(sub == k + j, 0.0, cols[j] * inverse)
            system = system - factor * rows[j]
            for i in block[j + 1 :]:
                scale = core[i][j] * inverse
                rows[i] = rows[i] - scale * rows[j]
                for l in block[j + 1 :]:
                    core[i][l] = core[i][l] - scale * core[j][l]
                cols[i] = cols[i] - factor * core[j][i]
    pivot = jnp.sum(jnp.where(sub == lane, system, 0.0), axis=1, keepdims=True)
    solved = system[:, size : size + 1] / jnp.where(sub[:, :1] < size, pivot, 1.0)
    coef_out[...] = jnp.sum(jnp.where(sub == lane, solved, 0.0), axis=0, keepdims=True)
    background = solved[count : count + 1, :]
    basis_coef = jnp.where(sub[:, :1] < count, solved, 0.0)

    scaled = basis_coef * row_rev[...]
    kernel = jnp.zeros((col_t.shape[0], side), f32)
    for _ in range(3):
        piece = scaled.astype(bf16)
        scaled = scaled - piece.astype(f32)
        kernel = kernel + jnp.dot(col_t[...], piece, preferred_element_type=f32)
    kernel_sum = jnp.sum(jnp.sum(kernel, axis=1, keepdims=True), axis=0, keepdims=True)
    rounded = kernel.astype(bf16).astype(f32)

    zero_band = jnp.zeros((side, side), bf16)

    def band(i):
        if i < 0 or i >= taps:
            return zero_band
        line = jnp.broadcast_to(rounded[i : i + 1, :], (side, side))
        return pltpu.roll(line, 0, 1, stride=1, stride_axis=0).astype(bf16)

    made = {i: band(i) for i in range(-1, 2 * pairs)}
    for q in range(pairs):
        for a in range(2):
            for b in range(2):
                bands[
                    q * 2 * side + a * side : q * 2 * side + (a + 1) * side,
                    b * side : (b + 1) * side,
                ] = made[2 * q + a - b]

    step = side - taps + 1
    joint = 4
    for q in range(0, pairs, joint):
        last = min(q + joint, pairs)
        lhs = jnp.concatenate(
            [
                jnp.concatenate(
                    [
                        frames[c, a, p : p + rows_half, :].astype(bf16)
                        for p in range(q, last)
                        for a in range(2)
                    ],
                    axis=1,
                )
                for c in range(wins)
            ],
            axis=0,
        )
        out = jnp.dot(
            lhs, bands[q * 2 * side : last * 2 * side, :], preferred_element_type=f32
        )
        if q:
            out = out + total[...]
        if last < pairs:
            total[...] = out
    for c in range(wins):
        rows = out[c * rows_half : (c + 1) * rows_half]
        window[c, pl.ds(0, rows_half, stride=2), :] = rows[:, :side]
        window[c, pl.ds(1, rows_half, stride=2), :] = rows[:, side:]
        keep = min(step, wide - c * step)
        image[:, c * step : c * step + keep] = window[c, :, :keep]
    image[...] = science[...].astype(f32) - image[...] - background

    store_parts(sender, image, payload, side, order, capacity, wide // side)
    line_at = lax.broadcasted_iota(jnp.int32, (trailer_rows, side), 0)
    trailer = jnp.zeros((trailer_rows, side), f32)
    rest = kernel_sum
    for p in range(3):
        piece = rest.astype(bf16).astype(f32)
        rest = rest - piece
        trailer = jnp.where(line_at == p, piece, trailer)
    trailer = trailer.astype(bf16)

    def put(d, carry):
        payload[d, capacity * part :, :] = trailer
        return carry

    lax.fori_loop(0, payload.shape[0], put, 0, unroll=4)


def fit_body(
    slot_of,
    sender,
    rows_at,
    cols_at,
    arrived,
    col,
    row_rev,
    science,
    variance,
    col_t,
    coef_out,
    payload,
    *scratch,
    order,
    capacity,
    count,
    taps,
):
    gram, windows = scratch[:2]
    stamps = rows_at.shape[1]
    side = row_rev.shape[1]
    normal_body(
        slot_of,
        rows_at,
        cols_at,
        arrived,
        col,
        row_rev,
        science,
        variance,
        gram,
        windows,
        *scratch[2:8],
        count=count,
        across_blocks=science.shape[1] // side,
        taps=taps,
    )
    subtract_body(
        sender,
        gram,
        windows,
        science,
        col_t,
        row_rev,
        coef_out,
        payload,
        *scratch[8:],
        order=order,
        capacity=capacity,
        count=count,
        taps=taps,
        pixels=stamps * side * side,
    )


def fit_and_subtract(
    slot_of,
    sender,
    rows_at,
    cols_at,
    arrived,
    col,
    row_rev,
    science,
    variance,
    col_t,
    order,
    capacity,
    count,
    taps,
):
    exps = len(order)
    high, wide = science.shape
    side = row_rev.shape[1]
    slots = sender.shape[0]
    stamps = rows_at.shape[1]
    padded_k = up(count + 2, 16)
    pairs = (taps + 2) // 2
    span = up(side + taps - 1, 16)
    half = up(high // 2 + pairs, 8)
    tall = up(taps // 2, 8) + max(high - side + span, 2 * half)
    wins = -(-wide // (side - taps + 1))
    group = next(g for g in (8, 4, 2, 1) if count % g == 0)
    return pl.pallas_call(
        functools.partial(fit_body, order=order, capacity=capacity, count=count, taps=taps),
        out_shape=(
            jax.ShapeDtypeStruct((1, side), f32),
            jax.ShapeDtypeStruct(
                (slots // capacity * exps, capacity * side // exps + trailer_rows, side), bf16
            ),
        ),
        in_specs=[smem()] * 4 + [vmem()] * 6,
        out_specs=(vmem(),) * 2,
        scratch_shapes=[
            pltpu.VMEM((padded_k, padded_k), f32),
            pltpu.VMEM((wins, 2, half, side), f32),
            pltpu.VMEM((tall, wide + 2 * side), f32),
            pltpu.VMEM((stamps * span, 2 * side), bf16),
            pltpu.VMEM((group, stamps * side, 2 * side), bf16),
            pltpu.VMEM((up(stamps * side * ((count + 2) | 1) + padded_k, 8), side), f32),
            pltpu.VMEM((stamps * side, side), f32),
            pltpu.VMEM((2 * half, side), f32),
            pltpu.VMEM((wins, high, side), f32),
            pltpu.VMEM((high, wide), f32),
            pltpu.VMEM((pairs * 2 * side, 2 * side), bf16),
            pltpu.VMEM((wins * high // 2, 2 * side), f32),
        ],
        compiler_params=pltpu.CompilerParams(vmem_limit_bytes=30 * mib),
        cost_estimate=cost(15_000_000_000, 8_000_000),
        name="fit_and_subtract",
    )(
        slot_of,
        sender,
        rows_at,
        cols_at,
        arrived,
        col,
        row_rev,
        science,
        variance,
        col_t,
    )


def split2(value):
    top = value.astype(bf16)
    return top, (value - top.astype(f32)).astype(bf16)


def score_body(
    slot_of, payload, down, over, out, token, padded, sideways, *, order, taps, capacity
):
    token[...] = jnp.zeros(token.shape, f32)
    side = payload.shape[2]
    part = side // len(order)
    high, wide = out.shape
    margin = taps // 2
    span = up(side + taps - 1, 16)
    across_blocks = wide // side
    exps = len(order)
    padded[...] = jnp.zeros(padded.shape, f32)
    for b in range(slot_of.shape[0]):
        slot = slot_of[b]
        row = pl.multiple_of((slot % capacity) * part, part)
        left = margin + (b % across_blocks) * side
        for e, q in enumerate(order):
            top = (b // across_blocks) * side + q * part
            block = payload[(slot // capacity) * exps + e, pl.ds(row, part), :]
            padded[top : top + part, left : left + side] = block.astype(f32)
    line = jnp.broadcast_to(over[...], (2 * side, 2 * side))
    band = pltpu.roll(line, 0, 1, stride=1, stride_axis=0)[:, :side]
    both = jnp.concatenate(split2(band), axis=1)
    sideways[...] = jnp.zeros(sideways.shape, f32)
    for c in range(wide // side):
        window = padded[:, c * side : (c + 2) * side].astype(bf16)
        got = jnp.dot(window, both, preferred_element_type=f32)
        sideways[margin : margin + high, c * side : (c + 1) * side] = got[:, :side] + got[:, side:]
    line = jnp.broadcast_to(down[...], (side, 2 * side))
    band = pltpu.roll(line, 0, 1, stride=1, stride_axis=0)[:, :span]
    top, low = split2(band)
    for r in range(high // side):
        data_top, data_low = split2(sideways[r * side : r * side + span, :])
        got = jnp.dot(top, data_top, preferred_element_type=f32)
        got = got + jnp.dot(top, data_low, preferred_element_type=f32)
        got = got + jnp.dot(low, data_top, preferred_element_type=f32)
        out[r * side : (r + 1) * side, :] = got


def score(slot_of, payload, down, over_rev, high, wide, taps, order, capacity):
    side = payload.shape[2]
    span = up(side + taps - 1, 16)
    return pl.pallas_call(
        functools.partial(score_body, order=order, taps=taps, capacity=capacity),
        out_shape=(
            jax.ShapeDtypeStruct((high, wide), f32),
            jax.ShapeDtypeStruct((8, 128), f32),
        ),
        in_specs=[smem()] + [vmem()] * 3,
        out_specs=(vmem(), vmem()),
        scratch_shapes=[
            pltpu.VMEM((high, wide + side), f32),
            pltpu.VMEM((high - side + span, wide), f32),
        ],
        compiler_params=pltpu.CompilerParams(vmem_limit_bytes=20 * mib),
        cost_estimate=cost(2_000_000_000, 2_000_000),
        name="score",
    )(slot_of, payload, down, over_rev)


def wanted_block(me, exposure, table, d, c, tract):
    exps = table.shape[0]
    block = table[distance(me[0], exposure, exps), d, c] - 1
    return jnp.where(block < 0, tract, block)


def variance_body(
    me, table, parts, template_var, own_out, other_out, template_out, total, sem, *, nears, capacity
):
    exps = table.shape[0]
    fars = exps // nears
    tract, part, _ = own_out.shape
    mine = pl.ds(pl.multiple_of(part_of(me[0], exps, nears) * part, part), part)
    copy = pltpu.make_async_copy(template_var.at[:, mine, :], template_out, sem)
    copy.start()
    total[...] = jnp.zeros(total.shape, f32)
    far = me[0] // nears
    rows = fars * part

    def one(j, carry):
        exposure = far * nears + lax.rem(j, nears)
        for c in range(capacity):
            block = wanted_block(me, exposure, table, j // nears, c, tract)
            total[block] += parts[j, c * rows : (c + 1) * rows, :].astype(f32)
        return carry

    lax.fori_loop(0, parts.shape[0], one, 0, unroll=4)
    own_out[...] = total[:tract, pl.ds(pl.multiple_of(far * part, part), part), :]
    for g in range(1, fars):
        there = lax.rem(far + g, fars)
        rows_there = pl.ds(pl.multiple_of(there * part, part), part)
        other_out[g - 1] = total[:tract, rows_there, :].astype(bf16)
    copy.wait()


def sum_variance(me, table, parts, template_var, nears, capacity):
    tract, side, _ = template_var.shape
    exps = table.shape[0]
    fars = exps // nears
    part = side // exps
    return pl.pallas_call(
        functools.partial(variance_body, nears=nears, capacity=capacity),
        out_shape=(
            jax.ShapeDtypeStruct((tract, part, side), f32),
            jax.ShapeDtypeStruct((max(1, fars - 1), tract, part, side), bf16),
            jax.ShapeDtypeStruct((tract, part, side), template_var.dtype),
        ),
        in_specs=[smem()] * 2 + [vmem(), pl.BlockSpec(memory_space=pl.ANY)],
        out_specs=(vmem(),) * 3,
        scratch_shapes=[
            pltpu.VMEM((tract + 1, fars * part, side), f32),
            pltpu.SemaphoreType.DMA(()),
        ],
        compiler_params=pltpu.CompilerParams(vmem_limit_bytes=16 * mib),
        cost_estimate=cost(0, 4_000_000),
        name="sum_variance",
    )(me, table, parts, template_var)


def combine_body(me, table, earlier, parts, own_var, var_template, *rest, part, capacity):
    del earlier
    others = rest[:-3]
    out, total, gain = rest[-3:]
    total[...] = jnp.zeros(total.shape, f32)
    gain[...] = jnp.zeros(gain.shape, f32)
    tract = out.shape[0]
    exps = table.shape[0]

    def one(j, carry):
        tail = parts[j, capacity * part :, :].astype(f32)
        kernel_sum = tail[0:1] + tail[1:2] + tail[2:3]
        square = jnp.broadcast_to(kernel_sum * kernel_sum, gain.shape[1:])
        for c in range(capacity):
            block = wanted_block(me, lax.rem(j, exps), table, j // exps, c, tract)
            total[block] += parts[j, c * part : (c + 1) * part, :].astype(f32)
            gain[block] += square
        return carry

    lax.fori_loop(0, parts.shape[0], one, 0, unroll=4)
    for t in range(tract):
        variance = own_var[t] + gain[t, 0:1, :] * var_template[t].astype(f32)
        for other in others:
            variance = variance + other[t].astype(f32)
        out[t] = (total[t] * lax.rsqrt(jnp.maximum(variance, 1.0))).astype(bf16)


def combine(me, table, earlier, parts, own_var, var_template, others, capacity):
    tract, part, side = own_var.shape
    return pl.pallas_call(
        functools.partial(combine_body, part=part, capacity=capacity),
        out_shape=jax.ShapeDtypeStruct((tract, part, side), bf16),
        in_specs=[smem(), smem(), pl.BlockSpec(memory_space=pl.ANY)]
        + [vmem()] * (3 + len(others)),
        out_specs=vmem(),
        scratch_shapes=[
            pltpu.VMEM((tract + 1, part, side), f32),
            pltpu.VMEM((tract + 1, 8, side), f32),
        ],
        compiler_params=pltpu.CompilerParams(vmem_limit_bytes=16 * mib),
        name="combine",
    )(me, table, earlier, parts, own_var, var_template, *others)


def join_body(places, *refs, part, count):
    ins = refs[:count]
    out, held, sems = refs[-3:]
    copies = []
    for d, ref in enumerate(ins):
        held[d] = ref[...].astype(f32)
        row = pl.multiple_of(places[d] * part, part)
        copies.append(
            pltpu.make_async_copy(held.at[d], out.at[:, pl.ds(row, part), :], sems.at[d])
        )
        copies[-1].start()
    for copy in copies:
        copy.wait()


def join_parts(places, parts, whole, exps):
    tract, part, side = parts[0].shape
    count = len(parts)
    fresh = whole is None
    anywhere = pl.BlockSpec(memory_space=pl.ANY)
    return pl.pallas_call(
        functools.partial(join_body, part=part, count=count),
        out_shape=jax.ShapeDtypeStruct((tract, part * exps, side), f32),
        in_specs=[smem()] + [vmem()] * count + ([] if fresh else [anywhere]),
        out_specs=anywhere,
        scratch_shapes=[
            pltpu.VMEM((count, tract, part, side), f32),
            pltpu.SemaphoreType.DMA((count,)),
        ],
        input_output_aliases={} if fresh else {count + 1: 0},
        compiler_params=pltpu.CompilerParams(vmem_limit_bytes=16 * mib),
        cost_estimate=cost(0, 3_000_000 * count),
        name="join_parts",
    )(places, *parts, *([] if fresh else [whole]))


def local(
    template,
    template_var,
    science,
    science_var,
    routes_src,
    routes_blk,
    stamp_rows,
    stamp_cols,
    basis_col,
    basis_row,
    psf_col,
    psf_row,
):
    peers = lax.axis_size("det")
    nears = lax.axis_size("near")
    exps = lax.axis_size("far") * nears
    me = (lax.axis_index("far") * nears + lax.axis_index("near")).astype(jnp.int32)
    order = tuple((e % nears) * (exps // nears) + e // nears for e in range(exps))
    tract, side, _ = template.shape
    science_img = science[0]
    variance_img = science_var[0]
    blocks_dev = routes_src.shape[1]
    count, taps = basis_col.shape
    capacity = max(2, -(-blocks_dev // peers))
    slots = peers * capacity
    part = side // exps

    slot_of, sender, request = route_tables(routes_src, routes_blk, peers, capacity)
    asked = lax.all_to_all(request, "det", split_axis=0, concat_axis=0, tiled=True)
    picked = pick_blocks(asked, fetch(template), slots, capacity)
    held = hold(asked, picked)
    tables = [held] + [from_exposure(held, g, exps) for g in range(1, exps)]
    table = jnp.stack(tables).reshape(exps, peers, capacity)
    var_parts = prepare(sender, variance_img, science_img, table, side, nears, capacity)
    arrived = lax.all_to_all(picked, "det", split_axis=0, concat_axis=0, tiled=True)

    padded_k = up(count + 2, 16)
    col_t = jnp.pad(basis_col.T, ((0, up(taps, 16) - taps), (0, padded_k - count)))
    col = jnp.pad(basis_col.astype(f32), ((0, padded_k - count), (0, side - taps)))
    row_rev = jnp.pad(
        basis_row.astype(f32)[:, ::-1], ((0, padded_k - count), (side - taps, 0))
    )
    row_rev = jnp.roll(row_rev, 1, axis=1)
    over_rev = jnp.roll(jnp.pad(psf_row[:, ::-1], ((0, 0), (2 * side - taps, 0))), 1, axis=1)
    down = jnp.pad(psf_col, ((0, 0), (0, 2 * side - taps)))
    var_late, arrived = lax.optimization_barrier((var_parts, arrived))
    var_back = lax.all_to_all(
        var_late, ("det", "near"), split_axis=0, concat_axis=0, tiled=True
    )

    high, wide = science_img.shape
    coef, payload = fit_and_subtract(
        slot_of,
        sender,
        stamp_rows,
        stamp_cols,
        arrived,
        col,
        row_rev,
        science_img,
        variance_img,
        col_t,
        order,
        capacity,
        count,
        taps,
    )
    diff_back = lax.all_to_all(payload, ("det",) + exposure_axes, split_axis=0, concat_axis=0, tiled=True)
    own_var, other_var, var_template = sum_variance(
        me[None], table, var_back, template_var, nears, capacity
    )
    fars = exps // nears
    others = []
    for g in range(1, fars):
        pairs = [(f, (f + g) % fars) for f in range(fars)]
        others.append(lax.ppermute(other_var[g - 1], "far", pairs))
    scored, token = score(
        slot_of, payload, down, over_rev, high, wide, taps, order, capacity
    )
    mine = combine(me[None], table, token, diff_back, own_var, var_template, others, capacity)

    def swap(value, distance):
        return lax.ppermute(value, exposure_axes, [(e, e ^ distance) for e in range(exps)])

    def put(parts, whole):
        places = jnp.stack([part_of(there, exps, nears) for there, _ in parts])
        return join_parts(places, [held for _, held in parts], whole, exps)

    if exps == 4:
        far = swap(mine, 2)
        near = swap(mine, 1)
        last = swap(far, 1)
        whole = put([(me, mine), (me ^ 1, near), (me ^ 2, far)], None)
        significance = put([(me ^ 3, last)], whole)
    else:
        parts = [(me, mine)]
        for gap in range(1, exps):
            pairs = [(e, (e + gap) % exps) for e in range(exps)]
            parts.append(((me - gap) % exps, lax.ppermute(mine, exposure_axes, pairs)))
        significance = put(parts, None)
    return (significance, scored[None], coef[:, : count + 1])


def solution(mesh):
    peers, exps = mesh.devices.shape
    nears = 2 if exps % 2 == 0 else 1
    split = jax.sharding.Mesh(
        mesh.devices.reshape(peers, exps // nears, nears), ("det",) + exposure_axes
    )
    placed = (
        P("det", None, None),
        P("det", None, None),
        P(exposure_axes, "det", None),
        P(exposure_axes, "det", None),
        P(exposure_axes, "det"),
        P(exposure_axes, "det"),
        P(exposure_axes, "det"),
        P(exposure_axes, "det"),
        P(),
        P(),
        P(exposure_axes, None),
        P(exposure_axes, None),
    )
    return jax.shard_map(
        local,
        mesh=split,
        in_specs=placed,
        out_specs=(
            P("det", None, None),
            P(exposure_axes, "det", None),
            P(exposure_axes, "det"),
        ),
        check_vma=False,
    )
```

```python
import functools

import jax
import jax.numpy as jnp
from jax import lax
from jax.experimental import pallas as pl
from jax.experimental.pallas import tpu as pltpu
from jax.sharding import PartitionSpec as P

ridge_term = 0.01
bf16 = jnp.bfloat16
f32 = jnp.float32
vmem = functools.partial(pl.BlockSpec, memory_space=pltpu.VMEM)
smem = functools.partial(pl.BlockSpec, memory_space=pltpu.SMEM)
mib = 1024 * 1024
trailer_rows = 8


def up(value, step):
    return -(-value // step) * step


def cost(flops, moved):
    return pl.CostEstimate(flops=flops, bytes_accessed=moved, transcendentals=0)


exposure_axes = ("far", "near")


def part_of(exposure, exps, nears):
    return lax.rem(exposure, nears) * (exps // nears) + exposure // nears


def distance(here, there, exps):
    if exps & (exps - 1) == 0:
        return here ^ there
    return lax.rem(here - there + exps, exps)


def from_exposure(value, gap, exps):
    if exps & (exps - 1) == 0:
        pairs = [(e, e ^ gap) for e in range(exps)]
    else:
        pairs = [(e, (e + gap) % exps) for e in range(exps)]
    return lax.ppermute(value, exposure_axes, pairs)


def route_body(src, blk, slot_of, sender, request, count, *, peers, capacity):
    def clear_count(p, carry):
        count[p] = 0
        return carry

    def clear_slot(s, carry):
        sender[s] = 0
        request[s // capacity, 0, s % capacity] = 0
        return carry

    lax.fori_loop(0, peers, clear_count, 0, unroll=peers <= 16)
    lax.fori_loop(0, peers * capacity, clear_slot, 0, unroll=peers <= 16)
    for b in range(src.shape[1]):
        owner = src[0, b]
        place = count[owner]
        count[owner] = place + 1
        slot_of[b] = owner * capacity + place
        sender[owner * capacity + place] = b
        request[owner, 0, place] = blk[0, b] + 1


def route_tables(routes_src, routes_blk, peers, capacity):
    return pl.pallas_call(
        functools.partial(route_body, peers=peers, capacity=capacity),
        out_shape=(
            jax.ShapeDtypeStruct((routes_src.shape[1],), jnp.int32),
            jax.ShapeDtypeStruct((peers * capacity,), jnp.int32),
            jax.ShapeDtypeStruct((peers, 1, capacity), jnp.int32),
        ),
        in_specs=[smem()] * 2,
        out_specs=(smem(),) * 3,
        scratch_shapes=[pltpu.SMEM((peers,), jnp.int32)],
        name="route_tables",
    )(routes_src, routes_blk)


def fetch_body(template, near, sem):
    copy = pltpu.make_async_copy(template, near, sem)
    copy.start()
    copy.wait()


def fetch(template):
    return pl.pallas_call(
        fetch_body,
        out_shape=jax.ShapeDtypeStruct(template.shape, template.dtype),
        in_specs=[pl.BlockSpec(memory_space=pl.ANY)],
        out_specs=vmem(),
        scratch_shapes=[pltpu.SemaphoreType.DMA(())],
        compiler_params=pltpu.CompilerParams(vmem_limit_bytes=16 * mib),
        cost_estimate=cost(0, 4_000_000),
        name="fetch",
    )(template)


def pick_body(asked, template, out, sems, *, capacity):
    copies = []
    for s in range(out.shape[0]):
        block = jnp.maximum(asked[s // capacity, 0, s % capacity] - 1, 0)
        copies.append(pltpu.make_async_copy(template.at[block], out.at[s], sems.at[s]))
        copies[-1].start()
    for copy in copies:
        copy.wait()


def pick_blocks(asked, template, slots, capacity):
    return pl.pallas_call(
        functools.partial(pick_body, capacity=capacity),
        out_shape=jax.ShapeDtypeStruct((slots,) + template.shape[1:], template.dtype),
        in_specs=[smem(), vmem()],
        out_specs=pl.BlockSpec(memory_space=pl.ANY),
        scratch_shapes=[pltpu.SemaphoreType.DMA((slots,))],
        compiler_params=pltpu.CompilerParams(vmem_limit_bytes=16 * mib),
        name="pick_blocks",
    )(asked, template)


def store_parts(sender, image, out, side, order, capacity, across_blocks):
    exps = len(order)
    part = side // exps
    slots = sender.shape[0]

    def one(s, carry):
        b = sender[s]
        top = pl.multiple_of((b // across_blocks) * side, side)
        left = pl.multiple_of((b % across_blocks) * side, side)
        block = image[pl.ds(top, side), pl.ds(left, side)].astype(bf16)
        row = pl.multiple_of((s % capacity) * part, part)
        for e, q in enumerate(order):
            out[(s // capacity) * exps + e, pl.ds(row, part), :] = block[q * part : (q + 1) * part]
        return carry

    lax.fori_loop(0, slots, one, 0, unroll=True if slots <= 32 else 4)


def cut(ref, top, left, height, side):
    down = pl.multiple_of((top // 8) * 8, 8)
    over = pl.multiple_of((left // side) * side, side)
    tile = ref[pl.ds(down, height), pl.ds(over, 3 * side)]
    tile = pltpu.roll(tile, lax.rem(3 * side - (left - over), 3 * side), 1)[:, : 2 * side]
    return pltpu.roll(tile, lax.rem(height - (top - down), height), 0)


def hold_body(asked, earlier, out):
    del earlier
    out[...] = asked[...]


def hold(asked, earlier):
    return pl.pallas_call(
        hold_body,
        out_shape=jax.ShapeDtypeStruct(asked.shape, asked.dtype),
        in_specs=[vmem(), pl.BlockSpec(memory_space=pl.ANY)],
        out_specs=vmem(),
        compiler_params=pltpu.CompilerParams(vmem_limit_bytes=16 * mib),
        name="hold",
    )(asked, earlier)


def prepare_body(sender, variance, science, earlier, out, *, side, nears, capacity):
    del earlier, science
    store_parts(sender, variance, out, side, range(nears), capacity, variance.shape[1] // side)


def prepare(sender, variance, science, earlier, side, nears, capacity):
    slots = sender.shape[0]
    part = side // nears
    return pl.pallas_call(
        functools.partial(prepare_body, side=side, nears=nears, capacity=capacity),
        out_shape=jax.ShapeDtypeStruct((slots // capacity * nears, capacity * part, side), bf16),
        in_specs=[smem()] + [vmem()] * 2 + [pl.BlockSpec(memory_space=pl.ANY)],
        out_specs=vmem(),
        compiler_params=pltpu.CompilerParams(vmem_limit_bytes=16 * mib),
        cost_estimate=cost(0, 6_000_000),
        name="prepare",
    )(sender, variance, science, earlier)


def normal_body(
    slot_of,
    rows_at,
    cols_at,
    arrived,
    col,
    row_rev,
    science,
    variance,
    gram_out,
    windows,
    frame,
    cuts,
    vert,
    design,
    roots,
    window,
    *,
    count,
    across_blocks,
    taps,
):
    side = row_rev.shape[1]
    margin = taps // 2
    stamps = rows_at.shape[1]
    span = up(side + taps - 1, 16)
    padded_k = gram_out.shape[1]
    pitch = (count + 2) | 1
    lines_all = stamps * side
    sub = lax.broadcasted_iota(jnp.int32, (side, side), 0)
    lane = lax.broadcasted_iota(jnp.int32, (side, side), 1)

    high, wide = science.shape
    rows_off = up(margin, 8)
    frame[:rows_off, :] = jnp.zeros((rows_off, frame.shape[1]), f32)
    below = rows_off + high
    frame[below:, :] = jnp.zeros((frame.shape[0] - below, frame.shape[1]), f32)
    frame[rows_off:below, :side] = jnp.zeros((high, side), f32)
    after = side + wide
    frame[rows_off:below, after:] = jnp.zeros((high, frame.shape[1] - after), f32)
    for b in range(slot_of.shape[0]):
        top = rows_off + (b // across_blocks) * side
        left = side + (b % across_blocks) * side
        frame[top : top + side, left : left + side] = arrived[slot_of[b]].astype(f32)
    first_row = rows_off - margin
    first_col = side - margin

    def cut_image(ref, top, left):
        tall = min(high, side + 16)
        down = pl.multiple_of(jnp.minimum((top // 16) * 16, high - tall), 16)
        over = pl.multiple_of(jnp.minimum((left // side) * side, wide - 2 * side), side)
        tile = ref[pl.ds(down, tall), pl.ds(over, 2 * side)].astype(f32)
        tile = pltpu.roll(tile, lax.rem(2 * side - (left - over), 2 * side), 1)[:, :side]
        return pltpu.roll(tile, lax.rem(tall - (top - down), tall), 0)[:side]

    for s in range(stamps):
        top = rows_at[0, s]
        left = cols_at[0, s]
        tile = cut(frame, top + first_row, left + first_col, span, side)
        cuts[s * span : (s + 1) * span, :] = tile.astype(bf16)
        root = lax.rsqrt(cut_image(variance, top, left))
        roots[s * side : (s + 1) * side, :] = root
        place = pl.ds(s * side * pitch + count, side, stride=pitch)
        design[place, :] = root
        place = pl.ds(s * side * pitch + count + 1, side, stride=pitch)
        design[place, :] = root * cut_image(science, top, left)
    design[lines_all * pitch :, :] = jnp.zeros((design.shape[0] - lines_all * pitch, side), f32)

    group = vert.shape[0]
    step = side - taps + 1
    starts = list(range(0, count, group))
    for turn, k in enumerate(starts):
        for c in range(turn, windows.shape[0], len(starts)):
            left = first_col + c * step
            window[...] = frame[first_row : first_row + window.shape[0], left : left + side]
            for parity in range(2):
                place = pl.ds(parity, windows.shape[2], stride=2)
                windows[c, parity] = window[place, :]
        filters = []
        for a in range(group):
            line = jnp.broadcast_to(col[k + a : k + a + 1, :], (side, side))
            line = pltpu.roll(line, 0, 1, stride=1, stride_axis=0)
            first = jnp.where(lane >= sub, line, 0.0).astype(bf16)
            second = jnp.where(lane < sub, line, 0.0).astype(bf16)
            filters.append(jnp.concatenate([first, second[:, : span - side]], axis=1))
        filters = jnp.concatenate(filters, axis=0)
        for s in range(stamps):
            out = jnp.dot(
                filters, cuts[s * span : (s + 1) * span, :], preferred_element_type=f32
            ).astype(bf16)
            for a in range(group):
                vert[a, s * side : (s + 1) * side, :] = out[a * side : (a + 1) * side]
        for a in range(group):
            line = jnp.broadcast_to(row_rev[k + a : k + a + 1, :], (side, side))
            line = pltpu.roll(line, 0, 1, stride=1, stride_axis=0)
            first = jnp.where(lane <= sub, line, 0.0).astype(bf16)
            second = jnp.where(lane > sub, line, 0.0).astype(bf16)
            band = jnp.concatenate([first, second], axis=0)
            out = jnp.dot(vert[a], band, preferred_element_type=f32)
            design[pl.ds(k + a, lines_all, stride=pitch), :] = out * roots[...]

    lines = 16
    sets = 4

    def gram_step(step, total):
        start = pl.multiple_of(step * sets * lines * pitch, 8)
        rows = []
        for g in range(sets):
            row = [
                design[pl.ds(start + (g * lines + j) * pitch, padded_k), :].astype(bf16)
                for j in range(lines)
            ]
            rows.append(jnp.concatenate(row, axis=1))
        both = jnp.concatenate(rows, axis=0)
        return total + lax.dot_general(
            both, both, (((1,), (1,)), ((), ())), preferred_element_type=f32
        )

    total = lax.fori_loop(
        0,
        lines_all // (lines * sets),
        gram_step,
        jnp.zeros((sets * padded_k, sets * padded_k), f32),
        unroll=4,
    )
    part = jnp.zeros((padded_k, padded_k), f32)
    for g in range(sets):
        rows = slice(g * padded_k, (g + 1) * padded_k)
        part = part + total[rows, rows]
    gram_out[...] = part


def subtract_body(
    sender,
    gram,
    frames,
    science,
    col_t,
    row_rev,
    coef_out,
    payload,
    window,
    image,
    bands,
    total,
    *,
    order,
    capacity,
    count,
    taps,
    pixels,
):
    side = frames.shape[3]
    high, wide = science.shape
    padded_k = gram.shape[1]
    part = side // len(order)
    size = count + 1

    system = jnp.concatenate(
        [gram[...], jnp.zeros((padded_k, side - padded_k), f32)], axis=1
    ) / pixels
    sub = lax.broadcasted_iota(jnp.int32, (padded_k, side), 0)
    lane = lax.broadcasted_iota(jnp.int32, (padded_k, side), 1)
    system = jnp.where((sub < size) & (lane <= size), system, 0.0)
    system = system + jnp.where((sub == lane) & (sub < size), ridge_term, 0.0)

    pairs = (taps + 2) // 2
    rows_half = high // 2
    wins = frames.shape[0]

    for k in range(0, size, 8):
        block = range(min(8, size - k))
        cols = [jnp.broadcast_to(system[:, k + j : k + j + 1], system.shape) for j in block]
        rows = [system[k + j : k + j + 1, :] for j in block]
        core = [[cols[j][k + i : k + i + 1, :] for j in block] for i in block]
        for j in block:
            inverse = 1.0 / core[j][j]
            factor = jnp.where(sub == k + j, 0.0, cols[j] * inverse)
            system = system - factor * rows[j]
            for i in block[j + 1 :]:
                scale = core[i][j] * inverse
                rows[i] = rows[i] - scale * rows[j]
                for l in block[j + 1 :]:
                    core[i][l] = core[i][l] - scale * core[j][l]
                cols[i] = cols[i] - factor * core[j][i]
    pivot = jnp.sum(jnp.where(sub == lane, system, 0.0), axis=1, keepdims=True)
    solved = system[:, size : size + 1] / jnp.where(sub[:, :1] < size, pivot, 1.0)
    coef_out[...] = jnp.sum(jnp.where(sub == lane, solved, 0.0), axis=0, keepdims=True)
    background = solved[count : count + 1, :]
    basis_coef = jnp.where(sub[:, :1] < count, solved, 0.0)

    scaled = basis_coef * row_rev[...]
    kernel = jnp.zeros((col_t.shape[0], side), f32)
    for _ in range(3):
        piece = scaled.astype(bf16)
        scaled = scaled - piece.astype(f32)
        kernel = kernel + jnp.dot(col_t[...], piece, preferred_element_type=f32)
    kernel_sum = jnp.sum(jnp.sum(kernel, axis=1, keepdims=True), axis=0, keepdims=True)
    rounded = kernel.astype(bf16).astype(f32)

    zero_band = jnp.zeros((side, side), bf16)

    def band(i):
        if i < 0 or i >= taps:
            return zero_band
        line = jnp.broadcast_to(rounded[i : i + 1, :], (side, side))
        return pltpu.roll(line, 0, 1, stride=1, stride_axis=0).astype(bf16)

    made = {i: band(i) for i in range(-1, 2 * pairs)}
    for q in range(pairs):
        for a in range(2):
            for b in range(2):
                bands[
                    q * 2 * side + a * side : q * 2 * side + (a + 1) * side,
                    b * side : (b + 1) * side,
                ] = made[2 * q + a - b]

    step = side - taps + 1
    joint = 4
    for q in range(0, pairs, joint):
        last = min(q + joint, pairs)
        lhs = jnp.concatenate(
            [
                jnp.concatenate(
                    [
                        frames[c, a, p : p + rows_half, :].astype(bf16)
                        for p in range(q, last)
                        for a in range(2)
                    ],
                    axis=1,
                )
                for c in range(wins)
            ],
            axis=0,
        )
        out = jnp.dot(
            lhs, bands[q * 2 * side : last * 2 * side, :], preferred_element_type=f32
        )
        if q:
            out = out + total[...]
        if last < pairs:
            total[...] = out
    for c in range(wins):
        rows = out[c * rows_half : (c + 1) * rows_half]
        window[c, pl.ds(0, rows_half, stride=2), :] = rows[:, :side]
        window[c, pl.ds(1, rows_half, stride=2), :] = rows[:, side:]
        keep = min(step, wide - c * step)
        image[:, c * step : c * step + keep] = window[c, :, :keep]
    image[...] = science[...].astype(f32) - image[...] - background

    store_parts(sender, image, payload, side, order, capacity, wide // side)
    line_at = lax.broadcasted_iota(jnp.int32, (trailer_rows, side), 0)
    trailer = jnp.zeros((trailer_rows, side), f32)
    rest = kernel_sum
    for p in range(3):
        piece = rest.astype(bf16).astype(f32)
        rest = rest - piece
        trailer = jnp.where(line_at == p, piece, trailer)
    trailer = trailer.astype(bf16)

    def put(d, carry):
        payload[d, capacity * part :, :] = trailer
        return carry

    lax.fori_loop(0, payload.shape[0], put, 0, unroll=4)


def fit_body(
    slot_of,
    sender,
    rows_at,
    cols_at,
    arrived,
    col,
    row_rev,
    science,
    variance,
    col_t,
    coef_out,
    payload,
    *scratch,
    order,
    capacity,
    count,
    taps,
):
    gram, windows = scratch[:2]
    stamps = rows_at.shape[1]
    side = row_rev.shape[1]
    normal_body(
        slot_of,
        rows_at,
        cols_at,
        arrived,
        col,
        row_rev,
        science,
        variance,
        gram,
        windows,
        *scratch[2:8],
        count=count,
        across_blocks=science.shape[1] // side,
        taps=taps,
    )
    subtract_body(
        sender,
        gram,
        windows,
        science,
        col_t,
        row_rev,
        coef_out,
        payload,
        *scratch[8:],
        order=order,
        capacity=capacity,
        count=count,
        taps=taps,
        pixels=stamps * side * side,
    )


def fit_and_subtract(
    slot_of,
    sender,
    rows_at,
    cols_at,
    arrived,
    col,
    row_rev,
    science,
    variance,
    col_t,
    order,
    capacity,
    count,
    taps,
):
    exps = len(order)
    high, wide = science.shape
    side = row_rev.shape[1]
    slots = sender.shape[0]
    stamps = rows_at.shape[1]
    padded_k = up(count + 2, 16)
    pairs = (taps + 2) // 2
    span = up(side + taps - 1, 16)
    half = up(high // 2 + pairs, 8)
    tall = up(taps // 2, 8) + max(high - side + span, 2 * half)
    wins = -(-wide // (side - taps + 1))
    group = next(g for g in (20, 8, 4, 2, 1) if count % g == 0)
    return pl.pallas_call(
        functools.partial(fit_body, order=order, capacity=capacity, count=count, taps=taps),
        out_shape=(
            jax.ShapeDtypeStruct((1, side), f32),
            jax.ShapeDtypeStruct(
                (slots // capacity * exps, capacity * side // exps + trailer_rows, side), bf16
            ),
        ),
        in_specs=[smem()] * 4 + [vmem()] * 6,
        out_specs=(vmem(),) * 2,
        scratch_shapes=[
            pltpu.VMEM((padded_k, padded_k), f32),
            pltpu.VMEM((wins, 2, half, side), f32),
            pltpu.VMEM((tall, wide + 2 * side), f32),
            pltpu.VMEM((stamps * span, 2 * side), bf16),
            pltpu.VMEM((group, stamps * side, 2 * side), bf16),
            pltpu.VMEM((up(stamps * side * ((count + 2) | 1) + padded_k, 8), side), f32),
            pltpu.VMEM((stamps * side, side), f32),
            pltpu.VMEM((2 * half, side), f32),
            pltpu.VMEM((wins, high, side), f32),
            pltpu.VMEM((high, wide), f32),
            pltpu.VMEM((pairs * 2 * side, 2 * side), bf16),
            pltpu.VMEM((wins * high // 2, 2 * side), f32),
        ],
        compiler_params=pltpu.CompilerParams(vmem_limit_bytes=34 * mib),
        cost_estimate=cost(15_000_000_000, 8_000_000),
        name="fit_and_subtract",
    )(
        slot_of,
        sender,
        rows_at,
        cols_at,
        arrived,
        col,
        row_rev,
        science,
        variance,
        col_t,
    )


def split2(value):
    top = value.astype(bf16)
    return top, (value - top.astype(f32)).astype(bf16)


def score_body(
    slot_of, payload, down, over, out, token, padded, sideways, *, order, taps, capacity
):
    token[...] = jnp.zeros(token.shape, f32)
    side = payload.shape[2]
    part = side // len(order)
    high, wide = out.shape
    margin = taps // 2
    span = up(side + taps - 1, 16)
    across_blocks = wide // side
    exps = len(order)
    padded[...] = jnp.zeros(padded.shape, f32)
    for b in range(slot_of.shape[0]):
        slot = slot_of[b]
        row = pl.multiple_of((slot % capacity) * part, part)
        left = margin + (b % across_blocks) * side
        for e, q in enumerate(order):
            top = (b // across_blocks) * side + q * part
            block = payload[(slot // capacity) * exps + e, pl.ds(row, part), :]
            padded[top : top + part, left : left + side] = block.astype(f32)
    line = jnp.broadcast_to(over[...], (2 * side, 2 * side))
    band = pltpu.roll(line, 0, 1, stride=1, stride_axis=0)[:, :side]
    both = jnp.concatenate(split2(band), axis=1)
    sideways[...] = jnp.zeros(sideways.shape, f32)
    for c in range(wide // side):
        window = padded[:, c * side : (c + 2) * side].astype(bf16)
        got = jnp.dot(window, both, preferred_element_type=f32)
        sideways[margin : margin + high, c * side : (c + 1) * side] = got[:, :side] + got[:, side:]
    line = jnp.broadcast_to(down[...], (side, 2 * side))
    band = pltpu.roll(line, 0, 1, stride=1, stride_axis=0)[:, :span]
    top, low = split2(band)
    for r in range(high // side):
        data_top, data_low = split2(sideways[r * side : r * side + span, :])
        got = jnp.dot(top, data_top, preferred_element_type=f32)
        got = got + jnp.dot(top, data_low, preferred_element_type=f32)
        got = got + jnp.dot(low, data_top, preferred_element_type=f32)
        out[r * side : (r + 1) * side, :] = got


def score(slot_of, payload, down, over_rev, high, wide, taps, order, capacity):
    side = payload.shape[2]
    span = up(side + taps - 1, 16)
    return pl.pallas_call(
        functools.partial(score_body, order=order, taps=taps, capacity=capacity),
        out_shape=(
            jax.ShapeDtypeStruct((high, wide), f32),
            jax.ShapeDtypeStruct((8, 128), f32),
        ),
        in_specs=[smem()] + [vmem()] * 3,
        out_specs=(vmem(), vmem()),
        scratch_shapes=[
            pltpu.VMEM((high, wide + side), f32),
            pltpu.VMEM((high - side + span, wide), f32),
        ],
        compiler_params=pltpu.CompilerParams(vmem_limit_bytes=20 * mib),
        cost_estimate=cost(2_000_000_000, 2_000_000),
        name="score",
    )(slot_of, payload, down, over_rev)


def wanted_block(me, exposure, table, d, c, tract):
    exps = table.shape[0]
    block = table[distance(me[0], exposure, exps), d, c] - 1
    return jnp.where(block < 0, tract, block)


def variance_body(
    me, table, parts, template_var, own_out, other_out, template_out, total, sem, *, nears, capacity
):
    exps = table.shape[0]
    fars = exps // nears
    tract, part, _ = own_out.shape
    mine = pl.ds(pl.multiple_of(part_of(me[0], exps, nears) * part, part), part)
    copy = pltpu.make_async_copy(template_var.at[:, mine, :], template_out, sem)
    copy.start()
    total[...] = jnp.zeros(total.shape, f32)
    far = me[0] // nears
    rows = fars * part

    def one(j, carry):
        exposure = far * nears + lax.rem(j, nears)
        for c in range(capacity):
            block = wanted_block(me, exposure, table, j // nears, c, tract)
            total[block] += parts[j, c * rows : (c + 1) * rows, :].astype(f32)
        return carry

    lax.fori_loop(0, parts.shape[0], one, 0, unroll=4)
    own_out[...] = total[:tract, pl.ds(pl.multiple_of(far * part, part), part), :]
    for g in range(1, fars):
        there = lax.rem(far + g, fars)
        rows_there = pl.ds(pl.multiple_of(there * part, part), part)
        other_out[g - 1] = total[:tract, rows_there, :].astype(bf16)
    copy.wait()


def sum_variance(me, table, parts, template_var, nears, capacity):
    tract, side, _ = template_var.shape
    exps = table.shape[0]
    fars = exps // nears
    part = side // exps
    return pl.pallas_call(
        functools.partial(variance_body, nears=nears, capacity=capacity),
        out_shape=(
            jax.ShapeDtypeStruct((tract, part, side), f32),
            jax.ShapeDtypeStruct((max(1, fars - 1), tract, part, side), bf16),
            jax.ShapeDtypeStruct((tract, part, side), template_var.dtype),
        ),
        in_specs=[smem()] * 2 + [vmem(), pl.BlockSpec(memory_space=pl.ANY)],
        out_specs=(vmem(),) * 3,
        scratch_shapes=[
            pltpu.VMEM((tract + 1, fars * part, side), f32),
            pltpu.SemaphoreType.DMA(()),
        ],
        compiler_params=pltpu.CompilerParams(vmem_limit_bytes=16 * mib),
        cost_estimate=cost(0, 4_000_000),
        name="sum_variance",
    )(me, table, parts, template_var)


def combine_body(me, table, earlier, parts, own_var, var_template, *rest, part, capacity):
    del earlier
    others = rest[:-3]
    out, total, gain = rest[-3:]
    total[...] = jnp.zeros(total.shape, f32)
    gain[...] = jnp.zeros(gain.shape, f32)
    tract = out.shape[0]
    exps = table.shape[0]

    def one(j, carry):
        tail = parts[j, capacity * part :, :].astype(f32)
        kernel_sum = tail[0:1] + tail[1:2] + tail[2:3]
        square = jnp.broadcast_to(kernel_sum * kernel_sum, gain.shape[1:])
        for c in range(capacity):
            block = wanted_block(me, lax.rem(j, exps), table, j // exps, c, tract)
            total[block] += parts[j, c * part : (c + 1) * part, :].astype(f32)
            gain[block] += square
        return carry

    lax.fori_loop(0, parts.shape[0], one, 0, unroll=4)
    for t in range(tract):
        variance = own_var[t] + gain[t, 0:1, :] * var_template[t].astype(f32)
        for other in others:
            variance = variance + other[t].astype(f32)
        out[t] = (total[t] * lax.rsqrt(jnp.maximum(variance, 1.0))).astype(bf16)


def combine(me, table, earlier, parts, own_var, var_template, others, capacity):
    tract, part, side = own_var.shape
    return pl.pallas_call(
        functools.partial(combine_body, part=part, capacity=capacity),
        out_shape=jax.ShapeDtypeStruct((tract, part, side), bf16),
        in_specs=[smem(), smem(), pl.BlockSpec(memory_space=pl.ANY)]
        + [vmem()] * (3 + len(others)),
        out_specs=vmem(),
        scratch_shapes=[
            pltpu.VMEM((tract + 1, part, side), f32),
            pltpu.VMEM((tract + 1, 8, side), f32),
        ],
        compiler_params=pltpu.CompilerParams(vmem_limit_bytes=16 * mib),
        name="combine",
    )(me, table, earlier, parts, own_var, var_template, *others)


def join_body(places, *refs, part, count):
    ins = refs[:count]
    out, held, sems = refs[-3:]
    copies = []
    for d, ref in enumerate(ins):
        held[d] = ref[...].astype(f32)
        row = pl.multiple_of(places[d] * part, part)
        copies.append(
            pltpu.make_async_copy(held.at[d], out.at[:, pl.ds(row, part), :], sems.at[d])
        )
        copies[-1].start()
    for copy in copies:
        copy.wait()


def join_parts(places, parts, whole, exps):
    tract, part, side = parts[0].shape
    count = len(parts)
    fresh = whole is None
    anywhere = pl.BlockSpec(memory_space=pl.ANY)
    return pl.pallas_call(
        functools.partial(join_body, part=part, count=count),
        out_shape=jax.ShapeDtypeStruct((tract, part * exps, side), f32),
        in_specs=[smem()] + [vmem()] * count + ([] if fresh else [anywhere]),
        out_specs=anywhere,
        scratch_shapes=[
            pltpu.VMEM((count, tract, part, side), f32),
            pltpu.SemaphoreType.DMA((count,)),
        ],
        input_output_aliases={} if fresh else {count + 1: 0},
        compiler_params=pltpu.CompilerParams(vmem_limit_bytes=16 * mib),
        cost_estimate=cost(0, 3_000_000 * count),
        name="join_parts",
    )(places, *parts, *([] if fresh else [whole]))


def local(
    template,
    template_var,
    science,
    science_var,
    routes_src,
    routes_blk,
    stamp_rows,
    stamp_cols,
    basis_col,
    basis_row,
    psf_col,
    psf_row,
):
    peers = lax.axis_size("det")
    nears = lax.axis_size("near")
    exps = lax.axis_size("far") * nears
    me = (lax.axis_index("far") * nears + lax.axis_index("near")).astype(jnp.int32)
    order = tuple((e % nears) * (exps // nears) + e // nears for e in range(exps))
    tract, side, _ = template.shape
    science_img = science[0]
    variance_img = science_var[0]
    blocks_dev = routes_src.shape[1]
    count, taps = basis_col.shape
    capacity = max(2, -(-blocks_dev // peers))
    slots = peers * capacity
    part = side // exps

    slot_of, sender, request = route_tables(routes_src, routes_blk, peers, capacity)
    asked = lax.all_to_all(request, "det", split_axis=0, concat_axis=0, tiled=True)
    picked = pick_blocks(asked, fetch(template), slots, capacity)
    held = hold(asked, picked)
    tables = [held] + [from_exposure(held, g, exps) for g in range(1, exps)]
    table = jnp.stack(tables).reshape(exps, peers, capacity)
    var_parts = prepare(sender, variance_img, science_img, table, side, nears, capacity)
    arrived = lax.all_to_all(picked, "det", split_axis=0, concat_axis=0, tiled=True)

    padded_k = up(count + 2, 16)
    col_t = jnp.pad(basis_col.T, ((0, up(taps, 16) - taps), (0, padded_k - count)))
    col = jnp.pad(basis_col.astype(f32), ((0, padded_k - count), (0, side - taps)))
    row_rev = jnp.pad(
        basis_row.astype(f32)[:, ::-1], ((0, padded_k - count), (side - taps, 0))
    )
    row_rev = jnp.roll(row_rev, 1, axis=1)
    over_rev = jnp.roll(jnp.pad(psf_row[:, ::-1], ((0, 0), (2 * side - taps, 0))), 1, axis=1)
    down = jnp.pad(psf_col, ((0, 0), (0, 2 * side - taps)))
    var_late, arrived = lax.optimization_barrier((var_parts, arrived))
    var_back = lax.all_to_all(
        var_late, ("det", "near"), split_axis=0, concat_axis=0, tiled=True
    )

    high, wide = science_img.shape
    coef, payload = fit_and_subtract(
        slot_of,
        sender,
        stamp_rows,
        stamp_cols,
        arrived,
        col,
        row_rev,
        science_img,
        variance_img,
        col_t,
        order,
        capacity,
        count,
        taps,
    )
    diff_back = lax.all_to_all(payload, ("det",) + exposure_axes, split_axis=0, concat_axis=0, tiled=True)
    own_var, other_var, var_template = sum_variance(
        me[None], table, var_back, template_var, nears, capacity
    )
    fars = exps // nears
    others = []
    for g in range(1, fars):
        pairs = [(f, (f + g) % fars) for f in range(fars)]
        others.append(lax.ppermute(other_var[g - 1], "far", pairs))
    scored, token = score(
        slot_of, payload, down, over_rev, high, wide, taps, order, capacity
    )
    mine = combine(me[None], table, token, diff_back, own_var, var_template, others, capacity)

    def swap(value, distance):
        return lax.ppermute(value, exposure_axes, [(e, e ^ distance) for e in range(exps)])

    def put(parts, whole):
        places = jnp.stack([part_of(there, exps, nears) for there, _ in parts])
        return join_parts(places, [held for _, held in parts], whole, exps)

    if exps == 4:
        far = swap(mine, 2)
        near = swap(mine, 1)
        last = swap(far, 1)
        whole = put([(me, mine), (me ^ 1, near), (me ^ 2, far)], None)
        significance = put([(me ^ 3, last)], whole)
    else:
        parts = [(me, mine)]
        for gap in range(1, exps):
            pairs = [(e, (e + gap) % exps) for e in range(exps)]
            parts.append(((me - gap) % exps, lax.ppermute(mine, exposure_axes, pairs)))
        significance = put(parts, None)
    return (significance, scored[None], coef[:, : count + 1])


def solution(mesh):
    peers, exps = mesh.devices.shape
    nears = 2 if exps % 2 == 0 else 1
    split = jax.sharding.Mesh(
        mesh.devices.reshape(peers, exps // nears, nears), ("det",) + exposure_axes
    )
    placed = (
        P("det", None, None),
        P("det", None, None),
        P(exposure_axes, "det", None),
        P(exposure_axes, "det", None),
        P(exposure_axes, "det"),
        P(exposure_axes, "det"),
        P(exposure_axes, "det"),
        P(exposure_axes, "det"),
        P(),
        P(),
        P(exposure_axes, None),
        P(exposure_axes, None),
    )
    return jax.shard_map(
        local,
        mesh=split,
        in_specs=placed,
        out_specs=(
            P("det", None, None),
            P(exposure_axes, "det", None),
            P(exposure_axes, "det"),
        ),
        check_vma=False,
    )
```

```python
import functools

import jax
import jax.numpy as jnp
from jax import lax
from jax.experimental import pallas as pl
from jax.experimental.pallas import tpu as pltpu
from jax.sharding import PartitionSpec as P

ridge_term = 0.01
bf16 = jnp.bfloat16
f32 = jnp.float32
vmem = functools.partial(pl.BlockSpec, memory_space=pltpu.VMEM)
smem = functools.partial(pl.BlockSpec, memory_space=pltpu.SMEM)
mib = 1024 * 1024
trailer_rows = 8


def up(value, step):
    return -(-value // step) * step


def cost(flops, moved):
    return pl.CostEstimate(flops=flops, bytes_accessed=moved, transcendentals=0)


exposure_axes = ("far", "near")


def part_of(exposure, exps, nears):
    return lax.rem(exposure, nears) * (exps // nears) + exposure // nears


def distance(here, there, exps):
    if exps & (exps - 1) == 0:
        return here ^ there
    return lax.rem(here - there + exps, exps)


def from_exposure(value, gap, exps):
    if exps & (exps - 1) == 0:
        pairs = [(e, e ^ gap) for e in range(exps)]
    else:
        pairs = [(e, (e + gap) % exps) for e in range(exps)]
    return lax.ppermute(value, exposure_axes, pairs)


def route_body(src, blk, slot_of, sender, request, count, *, peers, capacity):
    def clear_count(p, carry):
        count[p] = 0
        return carry

    def clear_slot(s, carry):
        sender[s] = 0
        request[s // capacity, 0, s % capacity] = 0
        return carry

    lax.fori_loop(0, peers, clear_count, 0, unroll=peers <= 16)
    lax.fori_loop(0, peers * capacity, clear_slot, 0, unroll=peers <= 16)
    for b in range(src.shape[1]):
        owner = src[0, b]
        place = count[owner]
        count[owner] = place + 1
        slot_of[b] = owner * capacity + place
        sender[owner * capacity + place] = b
        request[owner, 0, place] = blk[0, b] + 1


def route_tables(routes_src, routes_blk, peers, capacity):
    return pl.pallas_call(
        functools.partial(route_body, peers=peers, capacity=capacity),
        out_shape=(
            jax.ShapeDtypeStruct((routes_src.shape[1],), jnp.int32),
            jax.ShapeDtypeStruct((peers * capacity,), jnp.int32),
            jax.ShapeDtypeStruct((peers, 1, capacity), jnp.int32),
        ),
        in_specs=[smem()] * 2,
        out_specs=(smem(),) * 3,
        scratch_shapes=[pltpu.SMEM((peers,), jnp.int32)],
        name="route_tables",
    )(routes_src, routes_blk)


def fetch_body(template, near, sem):
    copy = pltpu.make_async_copy(template, near, sem)
    copy.start()
    copy.wait()


def fetch(template):
    return pl.pallas_call(
        fetch_body,
        out_shape=jax.ShapeDtypeStruct(template.shape, template.dtype),
        in_specs=[pl.BlockSpec(memory_space=pl.ANY)],
        out_specs=vmem(),
        scratch_shapes=[pltpu.SemaphoreType.DMA(())],
        compiler_params=pltpu.CompilerParams(vmem_limit_bytes=16 * mib),
        cost_estimate=cost(0, 4_000_000),
        name="fetch",
    )(template)


def pick_body(asked, template, out, sems, *, capacity):
    copies = []
    for s in range(out.shape[0]):
        block = jnp.maximum(asked[s // capacity, 0, s % capacity] - 1, 0)
        copies.append(pltpu.make_async_copy(template.at[block], out.at[s], sems.at[s]))
        copies[-1].start()
    for copy in copies:
        copy.wait()


def pick_blocks(asked, template, slots, capacity):
    return pl.pallas_call(
        functools.partial(pick_body, capacity=capacity),
        out_shape=jax.ShapeDtypeStruct((slots,) + template.shape[1:], template.dtype),
        in_specs=[smem(), vmem()],
        out_specs=pl.BlockSpec(memory_space=pl.ANY),
        scratch_shapes=[pltpu.SemaphoreType.DMA((slots,))],
        compiler_params=pltpu.CompilerParams(vmem_limit_bytes=16 * mib),
        name="pick_blocks",
    )(asked, template)


def store_parts(sender, image, out, side, order, capacity, across_blocks):
    exps = len(order)
    part = side // exps
    slots = sender.shape[0]

    def one(s, carry):
        b = sender[s]
        top = pl.multiple_of((b // across_blocks) * side, side)
        left = pl.multiple_of((b % across_blocks) * side, side)
        block = image[pl.ds(top, side), pl.ds(left, side)].astype(bf16)
        row = pl.multiple_of((s % capacity) * part, part)
        for e, q in enumerate(order):
            out[(s // capacity) * exps + e, pl.ds(row, part), :] = block[q * part : (q + 1) * part]
        return carry

    lax.fori_loop(0, slots, one, 0, unroll=True if slots <= 32 else 4)


def cut(ref, top, left, height, side):
    down = pl.multiple_of((top // 8) * 8, 8)
    over = pl.multiple_of((left // side) * side, side)
    tile = ref[pl.ds(down, height), pl.ds(over, 3 * side)]
    tile = pltpu.roll(tile, lax.rem(3 * side - (left - over), 3 * side), 1)[:, : 2 * side]
    return pltpu.roll(tile, lax.rem(height - (top - down), height), 0)


def hold_body(asked, earlier, out):
    del earlier
    out[...] = asked[...]


def hold(asked, earlier):
    return pl.pallas_call(
        hold_body,
        out_shape=jax.ShapeDtypeStruct(asked.shape, asked.dtype),
        in_specs=[vmem(), pl.BlockSpec(memory_space=pl.ANY)],
        out_specs=vmem(),
        compiler_params=pltpu.CompilerParams(vmem_limit_bytes=16 * mib),
        name="hold",
    )(asked, earlier)


def prepare_body(sender, variance, science, earlier, out, *, side, nears, capacity):
    del earlier, science
    store_parts(sender, variance, out, side, range(nears), capacity, variance.shape[1] // side)


def prepare(sender, variance, science, earlier, side, nears, capacity):
    slots = sender.shape[0]
    part = side // nears
    return pl.pallas_call(
        functools.partial(prepare_body, side=side, nears=nears, capacity=capacity),
        out_shape=jax.ShapeDtypeStruct((slots // capacity * nears, capacity * part, side), bf16),
        in_specs=[smem()] + [vmem()] * 2 + [pl.BlockSpec(memory_space=pl.ANY)],
        out_specs=vmem(),
        compiler_params=pltpu.CompilerParams(vmem_limit_bytes=16 * mib),
        cost_estimate=cost(0, 6_000_000),
        name="prepare",
    )(sender, variance, science, earlier)


def normal_body(
    slot_of,
    rows_at,
    cols_at,
    arrived,
    col,
    row_rev,
    science,
    variance,
    gram_out,
    windows,
    frame,
    cuts,
    vert,
    design,
    roots,
    window,
    *,
    count,
    across_blocks,
    taps,
):
    side = row_rev.shape[1]
    margin = taps // 2
    stamps = rows_at.shape[1]
    span = up(side + taps - 1, 16)
    padded_k = gram_out.shape[1]
    pitch = (count + 2) | 1
    lines_all = stamps * side
    sub = lax.broadcasted_iota(jnp.int32, (side, side), 0)
    lane = lax.broadcasted_iota(jnp.int32, (side, side), 1)

    high, wide = science.shape
    rows_off = up(margin, 8)
    frame[:rows_off, :] = jnp.zeros((rows_off, frame.shape[1]), f32)
    below = rows_off + high
    frame[below:, :] = jnp.zeros((frame.shape[0] - below, frame.shape[1]), f32)
    frame[rows_off:below, :side] = jnp.zeros((high, side), f32)
    after = side + wide
    frame[rows_off:below, after:] = jnp.zeros((high, frame.shape[1] - after), f32)
    for b in range(slot_of.shape[0]):
        top = rows_off + (b // across_blocks) * side
        left = side + (b % across_blocks) * side
        frame[top : top + side, left : left + side] = arrived[slot_of[b]].astype(f32)
    first_row = rows_off - margin
    first_col = side - margin

    def cut_image(ref, top, left):
        tall = min(high, side + 16)
        down = pl.multiple_of(jnp.minimum((top // 16) * 16, high - tall), 16)
        over = pl.multiple_of(jnp.minimum((left // side) * side, wide - 2 * side), side)
        tile = ref[pl.ds(down, tall), pl.ds(over, 2 * side)].astype(f32)
        tile = pltpu.roll(tile, lax.rem(2 * side - (left - over), 2 * side), 1)[:, :side]
        return pltpu.roll(tile, lax.rem(tall - (top - down), tall), 0)[:side]

    for s in range(stamps):
        top = rows_at[0, s]
        left = cols_at[0, s]
        tile = cut(frame, top + first_row, left + first_col, span, side)
        cuts[s * span : (s + 1) * span, :] = tile.astype(bf16)
        root = lax.rsqrt(cut_image(variance, top, left))
        roots[s * side : (s + 1) * side, :] = root
        place = pl.ds(s * side * pitch + count, side, stride=pitch)
        design[place, :] = root
        place = pl.ds(s * side * pitch + count + 1, side, stride=pitch)
        design[place, :] = root * cut_image(science, top, left)
    design[lines_all * pitch :, :] = jnp.zeros((design.shape[0] - lines_all * pitch, side), f32)

    group = vert.shape[0]
    step = side - taps + 1
    starts = list(range(0, count, group))
    for turn, k in enumerate(starts):
        for c in range(turn, windows.shape[0], len(starts)):
            left = first_col + c * step
            window[...] = frame[first_row : first_row + window.shape[0], left : left + side]
            for parity in range(2):
                place = pl.ds(parity, windows.shape[2], stride=2)
                windows[c, parity] = window[place, :]
        filters = []
        for a in range(group):
            line = jnp.broadcast_to(col[k + a : k + a + 1, :], (side, side))
            line = pltpu.roll(line, 0, 1, stride=1, stride_axis=0)
            first = jnp.where(lane >= sub, line, 0.0).astype(bf16)
            second = jnp.where(lane < sub, line, 0.0).astype(bf16)
            filters.append(jnp.concatenate([first, second[:, : span - side]], axis=1))
        filters = jnp.concatenate(filters, axis=0)
        for s in range(stamps):
            out = jnp.dot(
                filters, cuts[s * span : (s + 1) * span, :], preferred_element_type=f32
            ).astype(bf16)
            for a in range(group):
                vert[a, s * side : (s + 1) * side, :] = out[a * side : (a + 1) * side]
        for a in range(group):
            line = jnp.broadcast_to(row_rev[k + a : k + a + 1, :], (side, side))
            line = pltpu.roll(line, 0, 1, stride=1, stride_axis=0)
            first = jnp.where(lane <= sub, line, 0.0).astype(bf16)
            second = jnp.where(lane > sub, line, 0.0).astype(bf16)
            band = jnp.concatenate([first, second], axis=0)
            out = jnp.dot(vert[a], band, preferred_element_type=f32)
            design[pl.ds(k + a, lines_all, stride=pitch), :] = out * roots[...]

    lines = 16
    sets = 4

    def gram_step(step, total):
        start = pl.multiple_of(step * sets * lines * pitch, 8)
        rows = []
        for g in range(sets):
            row = [
                design[pl.ds(start + (g * lines + j) * pitch, padded_k), :].astype(bf16)
                for j in range(lines)
            ]
            rows.append(jnp.concatenate(row, axis=1))
        both = jnp.concatenate(rows, axis=0)
        return total + lax.dot_general(
            both, both, (((1,), (1,)), ((), ())), preferred_element_type=f32
        )

    total = lax.fori_loop(
        0,
        lines_all // (lines * sets),
        gram_step,
        jnp.zeros((sets * padded_k, sets * padded_k), f32),
        unroll=4,
    )
    part = jnp.zeros((padded_k, padded_k), f32)
    for g in range(sets):
        rows = slice(g * padded_k, (g + 1) * padded_k)
        part = part + total[rows, rows]
    gram_out[...] = part


def subtract_body(
    sender,
    gram,
    frames,
    science,
    col_t,
    row_rev,
    coef_out,
    payload,
    window,
    image,
    bands,
    total,
    *,
    order,
    capacity,
    count,
    taps,
    pixels,
):
    side = frames.shape[3]
    high, wide = science.shape
    padded_k = gram.shape[1]
    part = side // len(order)
    size = count + 1

    system = jnp.concatenate(
        [gram[...], jnp.zeros((padded_k, side - padded_k), f32)], axis=1
    ) / pixels
    sub = lax.broadcasted_iota(jnp.int32, (padded_k, side), 0)
    lane = lax.broadcasted_iota(jnp.int32, (padded_k, side), 1)
    system = jnp.where((sub < size) & (lane <= size), system, 0.0)
    system = system + jnp.where((sub == lane) & (sub < size), ridge_term, 0.0)

    pairs = (taps + 2) // 2
    rows_half = high // 2
    wins = frames.shape[0]

    for k in range(0, size, 8):
        block = range(min(8, size - k))
        cols = [jnp.broadcast_to(system[:, k + j : k + j + 1], system.shape) for j in block]
        rows = [system[k + j : k + j + 1, :] for j in block]
        core = [[cols[j][k + i : k + i + 1, :] for j in block] for i in block]
        for j in block:
            inverse = 1.0 / core[j][j]
            factor = jnp.where(sub == k + j, 0.0, cols[j] * inverse)
            system = system - factor * rows[j]
            for i in block[j + 1 :]:
                scale = core[i][j] * inverse
                rows[i] = rows[i] - scale * rows[j]
                for l in block[j + 1 :]:
                    core[i][l] = core[i][l] - scale * core[j][l]
                cols[i] = cols[i] - factor * core[j][i]
    pivot = jnp.sum(jnp.where(sub == lane, system, 0.0), axis=1, keepdims=True)
    solved = system[:, size : size + 1] / jnp.where(sub[:, :1] < size, pivot, 1.0)
    coef_out[...] = jnp.sum(jnp.where(sub == lane, solved, 0.0), axis=0, keepdims=True)
    background = solved[count : count + 1, :]
    basis_coef = jnp.where(sub[:, :1] < count, solved, 0.0)

    scaled = basis_coef * row_rev[...]
    kernel = jnp.zeros((col_t.shape[0], side), f32)
    for _ in range(3):
        piece = scaled.astype(bf16)
        scaled = scaled - piece.astype(f32)
        kernel = kernel + jnp.dot(col_t[...], piece, preferred_element_type=f32)
    kernel_sum = jnp.sum(jnp.sum(kernel, axis=1, keepdims=True), axis=0, keepdims=True)
    rounded = kernel.astype(bf16).astype(f32)

    zero_band = jnp.zeros((side, side), bf16)

    def band(i):
        if i < 0 or i >= taps:
            return zero_band
        line = jnp.broadcast_to(rounded[i : i + 1, :], (side, side))
        return pltpu.roll(line, 0, 1, stride=1, stride_axis=0).astype(bf16)

    made = {i: band(i) for i in range(-1, 2 * pairs)}
    for q in range(pairs):
        for a in range(2):
            for b in range(2):
                bands[
                    q * 2 * side + a * side : q * 2 * side + (a + 1) * side,
                    b * side : (b + 1) * side,
                ] = made[2 * q + a - b]

    step = side - taps + 1
    joint = 4
    for q in range(0, pairs, joint):
        last = min(q + joint, pairs)
        lhs = jnp.concatenate(
            [
                jnp.concatenate(
                    [
                        frames[c, a, p : p + rows_half, :].astype(bf16)
                        for p in range(q, last)
                        for a in range(2)
                    ],
                    axis=1,
                )
                for c in range(wins)
            ],
            axis=0,
        )
        out = jnp.dot(
            lhs, bands[q * 2 * side : last * 2 * side, :], preferred_element_type=f32
        )
        if q:
            out = out + total[...]
        if last < pairs:
            total[...] = out
    for c in range(wins):
        rows = out[c * rows_half : (c + 1) * rows_half]
        window[c, pl.ds(0, rows_half, stride=2), :] = rows[:, :side]
        window[c, pl.ds(1, rows_half, stride=2), :] = rows[:, side:]
        keep = min(step, wide - c * step)
        image[:, c * step : c * step + keep] = window[c, :, :keep]
    image[...] = science[...].astype(f32) - image[...] - background

    store_parts(sender, image, payload, side, order, capacity, wide // side)
    line_at = lax.broadcasted_iota(jnp.int32, (trailer_rows, side), 0)
    trailer = jnp.zeros((trailer_rows, side), f32)
    rest = kernel_sum
    for p in range(3):
        piece = rest.astype(bf16).astype(f32)
        rest = rest - piece
        trailer = jnp.where(line_at == p, piece, trailer)
    trailer = trailer.astype(bf16)

    def put(d, carry):
        payload[d, capacity * part :, :] = trailer
        return carry

    lax.fori_loop(0, payload.shape[0], put, 0, unroll=4)


def fit_body(
    slot_of,
    sender,
    rows_at,
    cols_at,
    arrived,
    col,
    row_rev,
    science,
    variance,
    col_t,
    coef_out,
    payload,
    *scratch,
    order,
    capacity,
    count,
    taps,
):
    gram, windows = scratch[:2]
    stamps = rows_at.shape[1]
    side = row_rev.shape[1]
    normal_body(
        slot_of,
        rows_at,
        cols_at,
        arrived,
        col,
        row_rev,
        science,
        variance,
        gram,
        windows,
        *scratch[2:8],
        count=count,
        across_blocks=science.shape[1] // side,
        taps=taps,
    )
    subtract_body(
        sender,
        gram,
        windows,
        science,
        col_t,
        row_rev,
        coef_out,
        payload,
        *scratch[8:],
        order=order,
        capacity=capacity,
        count=count,
        taps=taps,
        pixels=stamps * side * side,
    )


def fit_and_subtract(
    slot_of,
    sender,
    rows_at,
    cols_at,
    arrived,
    col,
    row_rev,
    science,
    variance,
    col_t,
    order,
    capacity,
    count,
    taps,
):
    exps = len(order)
    high, wide = science.shape
    side = row_rev.shape[1]
    slots = sender.shape[0]
    stamps = rows_at.shape[1]
    padded_k = up(count + 2, 16)
    pairs = (taps + 2) // 2
    span = up(side + taps - 1, 16)
    half = up(high // 2 + pairs, 8)
    tall = up(taps // 2, 8) + max(high - side + span, 2 * half)
    wins = -(-wide // (side - taps + 1))
    group = next(g for g in (20, 8, 4, 2, 1) if count % g == 0)
    return pl.pallas_call(
        functools.partial(fit_body, order=order, capacity=capacity, count=count, taps=taps),
        out_shape=(
            jax.ShapeDtypeStruct((1, side), f32),
            jax.ShapeDtypeStruct(
                (slots // capacity * exps, capacity * side // exps + trailer_rows, side), bf16
            ),
        ),
        in_specs=[smem()] * 4 + [vmem()] * 6,
        out_specs=(vmem(),) * 2,
        scratch_shapes=[
            pltpu.VMEM((padded_k, padded_k), f32),
            pltpu.VMEM((wins, 2, half, side), f32),
            pltpu.VMEM((tall, wide + 2 * side), f32),
            pltpu.VMEM((stamps * span, 2 * side), bf16),
            pltpu.VMEM((group, stamps * side, 2 * side), bf16),
            pltpu.VMEM((up(stamps * side * ((count + 2) | 1) + padded_k, 8), side), f32),
            pltpu.VMEM((stamps * side, side), f32),
            pltpu.VMEM((2 * half, side), f32),
            pltpu.VMEM((wins, high, side), f32),
            pltpu.VMEM((high, wide), f32),
            pltpu.VMEM((pairs * 2 * side, 2 * side), bf16),
            pltpu.VMEM((wins * high // 2, 2 * side), f32),
        ],
        compiler_params=pltpu.CompilerParams(vmem_limit_bytes=34 * mib),
        cost_estimate=cost(15_000_000_000, 8_000_000),
        name="fit_and_subtract",
    )(
        slot_of,
        sender,
        rows_at,
        cols_at,
        arrived,
        col,
        row_rev,
        science,
        variance,
        col_t,
    )


def split2(value):
    top = value.astype(bf16)
    return top, (value - top.astype(f32)).astype(bf16)


def score_body(
    slot_of, payload, down, over, out, token, padded, sideways, *, order, taps, capacity
):
    token[...] = jnp.zeros(token.shape, f32)
    side = payload.shape[2]
    part = side // len(order)
    high, wide = out.shape
    margin = taps // 2
    span = up(side + taps - 1, 16)
    across_blocks = wide // side
    exps = len(order)
    padded[...] = jnp.zeros(padded.shape, f32)
    for b in range(slot_of.shape[0]):
        slot = slot_of[b]
        row = pl.multiple_of((slot % capacity) * part, part)
        left = margin + (b % across_blocks) * side
        for e, q in enumerate(order):
            top = (b // across_blocks) * side + q * part
            block = payload[(slot // capacity) * exps + e, pl.ds(row, part), :]
            padded[top : top + part, left : left + side] = block.astype(f32)
    line = jnp.broadcast_to(over[...], (2 * side, 2 * side))
    band = pltpu.roll(line, 0, 1, stride=1, stride_axis=0)[:, :side]
    both = jnp.concatenate(split2(band), axis=1)
    sideways[...] = jnp.zeros(sideways.shape, f32)
    for c in range(wide // side):
        window = padded[:, c * side : (c + 2) * side].astype(bf16)
        got = jnp.dot(window, both, preferred_element_type=f32)
        sideways[margin : margin + high, c * side : (c + 1) * side] = got[:, :side] + got[:, side:]
    line = jnp.broadcast_to(down[...], (side, 2 * side))
    band = pltpu.roll(line, 0, 1, stride=1, stride_axis=0)[:, :span]
    top, low = split2(band)
    for r in range(high // side):
        data_top, data_low = split2(sideways[r * side : r * side + span, :])
        got = jnp.dot(top, data_top, preferred_element_type=f32)
        got = got + jnp.dot(top, data_low, preferred_element_type=f32)
        got = got + jnp.dot(low, data_top, preferred_element_type=f32)
        out[r * side : (r + 1) * side, :] = got


def score(slot_of, payload, down, over_rev, high, wide, taps, order, capacity):
    side = payload.shape[2]
    span = up(side + taps - 1, 16)
    return pl.pallas_call(
        functools.partial(score_body, order=order, taps=taps, capacity=capacity),
        out_shape=(
            jax.ShapeDtypeStruct((high, wide), f32),
            jax.ShapeDtypeStruct((8, 128), f32),
        ),
        in_specs=[smem()] + [vmem()] * 3,
        out_specs=(vmem(), vmem()),
        scratch_shapes=[
            pltpu.VMEM((high, wide + side), f32),
            pltpu.VMEM((high - side + span, wide), f32),
        ],
        compiler_params=pltpu.CompilerParams(vmem_limit_bytes=20 * mib),
        cost_estimate=cost(2_000_000_000, 2_000_000),
        name="score",
    )(slot_of, payload, down, over_rev)


def wanted_block(me, exposure, table, d, c, tract):
    exps = table.shape[0]
    block = table[distance(me[0], exposure, exps), d, c] - 1
    return jnp.where(block < 0, tract, block)


def variance_body(
    me, table, parts, template_var, own_out, other_out, template_out, total, sem, *, nears, capacity
):
    exps = table.shape[0]
    fars = exps // nears
    tract, part, _ = own_out.shape
    mine = pl.ds(pl.multiple_of(part_of(me[0], exps, nears) * part, part), part)
    copy = pltpu.make_async_copy(template_var.at[:, mine, :], template_out, sem)
    copy.start()
    total[...] = jnp.zeros(total.shape, f32)
    far = me[0] // nears
    rows = fars * part

    def one(j, carry):
        exposure = far * nears + lax.rem(j, nears)
        for c in range(capacity):
            block = wanted_block(me, exposure, table, j // nears, c, tract)
            total[block] += parts[j, c * rows : (c + 1) * rows, :].astype(f32)
        return carry

    lax.fori_loop(0, parts.shape[0], one, 0, unroll=4)
    own_out[...] = total[:tract, pl.ds(pl.multiple_of(far * part, part), part), :]
    for g in range(1, fars):
        there = lax.rem(far + g, fars)
        rows_there = pl.ds(pl.multiple_of(there * part, part), part)
        other_out[g - 1] = total[:tract, rows_there, :].astype(bf16)
    copy.wait()


def sum_variance(me, table, parts, template_var, nears, capacity):
    tract, side, _ = template_var.shape
    exps = table.shape[0]
    fars = exps // nears
    part = side // exps
    return pl.pallas_call(
        functools.partial(variance_body, nears=nears, capacity=capacity),
        out_shape=(
            jax.ShapeDtypeStruct((tract, part, side), f32),
            jax.ShapeDtypeStruct((max(1, fars - 1), tract, part, side), bf16),
            jax.ShapeDtypeStruct((tract, part, side), template_var.dtype),
        ),
        in_specs=[smem()] * 2 + [vmem(), pl.BlockSpec(memory_space=pl.ANY)],
        out_specs=(vmem(),) * 3,
        scratch_shapes=[
            pltpu.VMEM((tract + 1, fars * part, side), f32),
            pltpu.SemaphoreType.DMA(()),
        ],
        compiler_params=pltpu.CompilerParams(vmem_limit_bytes=16 * mib),
        cost_estimate=cost(0, 4_000_000),
        name="sum_variance",
    )(me, table, parts, template_var)


def combine_body(
    me, table, earlier, parts, own_var, var_template, *rest, part, nears, capacity
):
    del earlier
    others = rest[:-3]
    out, total, gain = rest[-3:]
    total[...] = jnp.zeros(total.shape, f32)
    gain[...] = jnp.zeros(gain.shape, f32)
    tract = out.shape[0]
    exps = table.shape[0]

    def one(j, carry):
        place = lax.rem(j, exps)
        exposure = lax.rem(place, exps // nears) * nears + place // (exps // nears)
        tail = parts[j, capacity * part :, :].astype(f32)
        kernel_sum = tail[0:1] + tail[1:2] + tail[2:3]
        square = jnp.broadcast_to(kernel_sum * kernel_sum, gain.shape[1:])
        for c in range(capacity):
            block = wanted_block(me, exposure, table, j // exps, c, tract)
            total[block] += parts[j, c * part : (c + 1) * part, :].astype(f32)
            gain[block] += square
        return carry

    lax.fori_loop(0, parts.shape[0], one, 0, unroll=4)
    for t in range(tract):
        variance = own_var[t] + gain[t, 0:1, :] * var_template[t].astype(f32)
        for other in others:
            variance = variance + other[t].astype(f32)
        out[t] = (total[t] * lax.rsqrt(jnp.maximum(variance, 1.0))).astype(bf16)


def combine(me, table, earlier, parts, own_var, var_template, others, nears, capacity):
    tract, part, side = own_var.shape
    return pl.pallas_call(
        functools.partial(combine_body, part=part, nears=nears, capacity=capacity),
        out_shape=jax.ShapeDtypeStruct((tract, part, side), bf16),
        in_specs=[smem(), smem(), pl.BlockSpec(memory_space=pl.ANY)]
        + [vmem()] * (3 + len(others)),
        out_specs=vmem(),
        scratch_shapes=[
            pltpu.VMEM((tract + 1, part, side), f32),
            pltpu.VMEM((tract + 1, 8, side), f32),
        ],
        compiler_params=pltpu.CompilerParams(vmem_limit_bytes=16 * mib),
        name="combine",
    )(me, table, earlier, parts, own_var, var_template, *others)


def join_body(places, *refs, part, count):
    ins = refs[:count]
    out, held, sems = refs[-3:]
    copies = []
    for d, ref in enumerate(ins):
        held[d] = ref[...].astype(f32)
        row = pl.multiple_of(places[d] * part, part)
        copies.append(
            pltpu.make_async_copy(held.at[d], out.at[:, pl.ds(row, part), :], sems.at[d])
        )
        copies[-1].start()
    for copy in copies:
        copy.wait()


def join_parts(places, parts, whole, exps, moved):
    tract, part, side = parts[0].shape
    count = len(parts)
    fresh = whole is None
    anywhere = pl.BlockSpec(memory_space=pl.ANY)
    return pl.pallas_call(
        functools.partial(join_body, part=part, count=count),
        out_shape=jax.ShapeDtypeStruct((tract, part * exps, side), f32),
        in_specs=[smem()] + [vmem()] * count + ([] if fresh else [anywhere]),
        out_specs=anywhere,
        scratch_shapes=[
            pltpu.VMEM((count, tract, part, side), f32),
            pltpu.SemaphoreType.DMA((count,)),
        ],
        input_output_aliases={} if fresh else {count + 1: 0},
        compiler_params=pltpu.CompilerParams(vmem_limit_bytes=16 * mib),
        cost_estimate=cost(0, moved),
        name="join_parts",
    )(places, *parts, *([] if fresh else [whole]))


def local(
    template,
    template_var,
    science,
    science_var,
    routes_src,
    routes_blk,
    stamp_rows,
    stamp_cols,
    basis_col,
    basis_row,
    psf_col,
    psf_row,
):
    peers = lax.axis_size("det")
    nears = lax.axis_size("near")
    exps = lax.axis_size("far") * nears
    me = (lax.axis_index("far") * nears + lax.axis_index("near")).astype(jnp.int32)
    order = tuple(range(exps))
    tract, side, _ = template.shape
    science_img = science[0]
    variance_img = science_var[0]
    blocks_dev = routes_src.shape[1]
    count, taps = basis_col.shape
    capacity = max(2, -(-blocks_dev // peers))
    slots = peers * capacity
    part = side // exps

    slot_of, sender, request = route_tables(routes_src, routes_blk, peers, capacity)
    asked = lax.all_to_all(request, "det", split_axis=0, concat_axis=0, tiled=True)
    picked = pick_blocks(asked, fetch(template), slots, capacity)
    held = hold(asked, picked)
    tables = [held] + [from_exposure(held, g, exps) for g in range(1, exps)]
    table = jnp.stack(tables).reshape(exps, peers, capacity)
    var_parts = prepare(sender, variance_img, science_img, table, side, nears, capacity)
    arrived = lax.all_to_all(picked, "det", split_axis=0, concat_axis=0, tiled=True)

    padded_k = up(count + 2, 16)
    col_t = jnp.pad(basis_col.T, ((0, up(taps, 16) - taps), (0, padded_k - count)))
    col = jnp.pad(basis_col.astype(f32), ((0, padded_k - count), (0, side - taps)))
    row_rev = jnp.pad(
        basis_row.astype(f32)[:, ::-1], ((0, padded_k - count), (side - taps, 0))
    )
    row_rev = jnp.roll(row_rev, 1, axis=1)
    over_rev = jnp.roll(jnp.pad(psf_row[:, ::-1], ((0, 0), (2 * side - taps, 0))), 1, axis=1)
    down = jnp.pad(psf_col, ((0, 0), (0, 2 * side - taps)))
    var_late, arrived = lax.optimization_barrier((var_parts, arrived))
    var_back = lax.all_to_all(
        var_late, ("det", "near"), split_axis=0, concat_axis=0, tiled=True
    )

    high, wide = science_img.shape
    coef, payload = fit_and_subtract(
        slot_of,
        sender,
        stamp_rows,
        stamp_cols,
        arrived,
        col,
        row_rev,
        science_img,
        variance_img,
        col_t,
        order,
        capacity,
        count,
        taps,
    )
    diff_back = lax.all_to_all(payload, ("det", "near", "far"), split_axis=0, concat_axis=0, tiled=True)
    own_var, other_var, var_template = sum_variance(
        me[None], table, var_back, template_var, nears, capacity
    )
    fars = exps // nears
    others = []
    for g in range(1, fars):
        pairs = [(f, (f + g) % fars) for f in range(fars)]
        others.append(lax.ppermute(other_var[g - 1], "far", pairs))
    scored, token = score(
        slot_of, payload, down, over_rev, high, wide, taps, order, capacity
    )
    mine = combine(
        me[None], table, token, diff_back, own_var, var_template, others, nears, capacity
    )

    def swap(value, distance):
        return lax.ppermute(value, exposure_axes, [(e, e ^ distance) for e in range(exps)])

    def put(parts, whole, moved=3_000_000):
        places = jnp.stack([part_of(there, exps, nears) for there, _ in parts])
        return join_parts(places, [held for _, held in parts], whole, exps, moved)

    if exps == 4:
        far = swap(mine, 2)
        near = swap(mine, 1)
        last = swap(far, 1)
        whole = put([(me, mine), (me ^ 1, near)], None, 1_000_000)
        whole = put([(me ^ 2, far)], whole, 100_000_000)
        significance = put([(me ^ 3, last)], whole)
    else:
        parts = [(me, mine)]
        for gap in range(1, exps):
            pairs = [(e, (e + gap) % exps) for e in range(exps)]
            parts.append(((me - gap) % exps, lax.ppermute(mine, exposure_axes, pairs)))
        significance = put(parts, None)
    return (significance, scored[None], coef[:, : count + 1])


def solution(mesh):
    peers, exps = mesh.devices.shape
    nears = 2 if exps % 2 == 0 else 1
    split = jax.sharding.Mesh(
        mesh.devices.reshape(peers, exps // nears, nears), ("det",) + exposure_axes
    )
    placed = (
        P("det", None, None),
        P("det", None, None),
        P(exposure_axes, "det", None),
        P(exposure_axes, "det", None),
        P(exposure_axes, "det"),
        P(exposure_axes, "det"),
        P(exposure_axes, "det"),
        P(exposure_axes, "det"),
        P(),
        P(),
        P(exposure_axes, None),
        P(exposure_axes, None),
    )
    return jax.shard_map(
        local,
        mesh=split,
        in_specs=placed,
        out_specs=(
            P("det", None, None),
            P(exposure_axes, "det", None),
            P(exposure_axes, "det"),
        ),
        check_vma=False,
    )
```

```python
import functools

import jax
import jax.numpy as jnp
from jax import lax
from jax.experimental import pallas as pl
from jax.experimental.pallas import tpu as pltpu
from jax.sharding import PartitionSpec as P

ridge_term = 0.01
bf16 = jnp.bfloat16
f32 = jnp.float32
vmem = functools.partial(pl.BlockSpec, memory_space=pltpu.VMEM)
smem = functools.partial(pl.BlockSpec, memory_space=pltpu.SMEM)
mib = 1024 * 1024
trailer_rows = 8


def up(value, step):
    return -(-value // step) * step


def cost(flops, moved):
    return pl.CostEstimate(flops=flops, bytes_accessed=moved, transcendentals=0)


exposure_axes = ("far", "near")


def part_of(exposure, exps, nears):
    return lax.rem(exposure, nears) * (exps // nears) + exposure // nears


def distance(here, there, exps):
    if exps & (exps - 1) == 0:
        return here ^ there
    return lax.rem(here - there + exps, exps)


def from_exposure(value, gap, exps):
    if exps & (exps - 1) == 0:
        pairs = [(e, e ^ gap) for e in range(exps)]
    else:
        pairs = [(e, (e + gap) % exps) for e in range(exps)]
    return lax.ppermute(value, exposure_axes, pairs)


def route_body(src, blk, earlier, slot_of, sender, count, *, peers, capacity):
    del earlier

    def clear_count(p, carry):
        count[p] = 0
        return carry

    def clear_slot(s, carry):
        sender[s] = 0
        return carry

    lax.fori_loop(0, peers, clear_count, 0, unroll=peers <= 16)
    lax.fori_loop(0, peers * capacity, clear_slot, 0, unroll=peers <= 16)
    for b in range(src.shape[1]):
        owner = src[0, b]
        place = count[owner]
        count[owner] = place + 1
        slot_of[b] = owner * capacity + place
        sender[owner * capacity + place] = b


def route_tables(routes_src, routes_blk, earlier, peers, capacity):
    return pl.pallas_call(
        functools.partial(route_body, peers=peers, capacity=capacity),
        out_shape=(
            jax.ShapeDtypeStruct((routes_src.shape[1],), jnp.int32),
            jax.ShapeDtypeStruct((peers * capacity,), jnp.int32),
        ),
        in_specs=[smem()] * 2 + [pl.BlockSpec(memory_space=pl.ANY)],
        out_specs=(smem(),) * 2,
        scratch_shapes=[pltpu.SMEM((peers,), jnp.int32)],
        name="route_tables",
    )(routes_src, routes_blk, earlier)


def request_body(src, blk, request, count, *, peers, capacity):
    for p in range(peers):
        count[p] = 0
        for c in range(capacity):
            request[p, 0, c] = 0
    for b in range(src.shape[1]):
        owner = src[0, b]
        place = count[owner]
        count[owner] = place + 1
        request[owner, 0, place] = blk[0, b] + 1


def request_table(routes_src, routes_blk, peers, capacity):
    return pl.pallas_call(
        functools.partial(request_body, peers=peers, capacity=capacity),
        out_shape=jax.ShapeDtypeStruct((peers, 1, capacity), jnp.int32),
        in_specs=[smem()] * 2,
        out_specs=smem(),
        scratch_shapes=[pltpu.SMEM((peers,), jnp.int32)],
        name="request_table",
    )(routes_src, routes_blk)


def fetch_body(template, near, sem):
    copy = pltpu.make_async_copy(template, near, sem)
    copy.start()
    copy.wait()


def fetch(template):
    return pl.pallas_call(
        fetch_body,
        out_shape=jax.ShapeDtypeStruct(template.shape, template.dtype),
        in_specs=[pl.BlockSpec(memory_space=pl.ANY)],
        out_specs=vmem(),
        scratch_shapes=[pltpu.SemaphoreType.DMA(())],
        compiler_params=pltpu.CompilerParams(vmem_limit_bytes=16 * mib),
        cost_estimate=cost(0, 4_000_000),
        name="fetch",
    )(template)


def pick_body(asked, template, out, sems, *, capacity):
    copies = []
    for s in range(out.shape[0]):
        block = jnp.maximum(asked[s // capacity, 0, s % capacity] - 1, 0)
        copies.append(pltpu.make_async_copy(template.at[block], out.at[s], sems.at[s]))
        copies[-1].start()
    for copy in copies:
        copy.wait()


def pick_blocks(asked, template, slots, capacity):
    return pl.pallas_call(
        functools.partial(pick_body, capacity=capacity),
        out_shape=jax.ShapeDtypeStruct((slots,) + template.shape[1:], template.dtype),
        in_specs=[smem(), vmem()],
        out_specs=pl.BlockSpec(memory_space=pl.ANY),
        scratch_shapes=[pltpu.SemaphoreType.DMA((slots,))],
        compiler_params=pltpu.CompilerParams(vmem_limit_bytes=16 * mib),
        name="pick_blocks",
    )(asked, template)


def store_parts(sender, image, out, side, order, capacity, across_blocks):
    exps = len(order)
    part = side // exps
    slots = sender.shape[0]

    def one(s, carry):
        b = sender[s]
        top = pl.multiple_of((b // across_blocks) * side, side)
        left = pl.multiple_of((b % across_blocks) * side, side)
        block = image[pl.ds(top, side), pl.ds(left, side)].astype(bf16)
        row = pl.multiple_of((s % capacity) * part, part)
        for e, q in enumerate(order):
            out[(s // capacity) * exps + e, pl.ds(row, part), :] = block[q * part : (q + 1) * part]
        return carry

    lax.fori_loop(0, slots, one, 0, unroll=True if slots <= 32 else 4)


def cut(ref, top, left, height, side):
    down = pl.multiple_of((top // 8) * 8, 8)
    over = pl.multiple_of((left // side) * side, side)
    tile = ref[pl.ds(down, height), pl.ds(over, 3 * side)]
    tile = pltpu.roll(tile, lax.rem(3 * side - (left - over), 3 * side), 1)[:, : 2 * side]
    return pltpu.roll(tile, lax.rem(height - (top - down), height), 0)


def hold_body(asked, earlier, out):
    del earlier
    out[...] = asked[...]


def hold(asked, earlier):
    return pl.pallas_call(
        hold_body,
        out_shape=jax.ShapeDtypeStruct(asked.shape, asked.dtype),
        in_specs=[vmem(), pl.BlockSpec(memory_space=pl.ANY)],
        out_specs=vmem(),
        compiler_params=pltpu.CompilerParams(vmem_limit_bytes=16 * mib),
        name="hold",
    )(asked, earlier)


def prepare_body(sender, variance, science, earlier, out, *, side, nears, capacity):
    del earlier, science
    store_parts(sender, variance, out, side, range(nears), capacity, variance.shape[1] // side)


def prepare(sender, variance, science, earlier, side, nears, capacity):
    slots = sender.shape[0]
    part = side // nears
    return pl.pallas_call(
        functools.partial(prepare_body, side=side, nears=nears, capacity=capacity),
        out_shape=jax.ShapeDtypeStruct((slots // capacity * nears, capacity * part, side), bf16),
        in_specs=[smem()] + [vmem()] * 2 + [pl.BlockSpec(memory_space=pl.ANY)],
        out_specs=vmem(),
        compiler_params=pltpu.CompilerParams(vmem_limit_bytes=16 * mib),
        cost_estimate=cost(0, 6_000_000),
        name="prepare",
    )(sender, variance, science, earlier)


def normal_body(
    slot_of,
    rows_at,
    cols_at,
    arrived,
    col,
    row_rev,
    science,
    variance,
    gram_out,
    windows,
    frame,
    cuts,
    vert,
    design,
    roots,
    window,
    *,
    count,
    across_blocks,
    taps,
):
    side = row_rev.shape[1]
    margin = taps // 2
    stamps = rows_at.shape[1]
    span = up(side + taps - 1, 16)
    padded_k = gram_out.shape[1]
    pitch = (count + 2) | 1
    lines_all = stamps * side
    sub = lax.broadcasted_iota(jnp.int32, (side, side), 0)
    lane = lax.broadcasted_iota(jnp.int32, (side, side), 1)

    high, wide = science.shape
    rows_off = up(margin, 8)
    frame[:rows_off, :] = jnp.zeros((rows_off, frame.shape[1]), f32)
    below = rows_off + high
    frame[below:, :] = jnp.zeros((frame.shape[0] - below, frame.shape[1]), f32)
    frame[rows_off:below, :side] = jnp.zeros((high, side), f32)
    after = side + wide
    frame[rows_off:below, after:] = jnp.zeros((high, frame.shape[1] - after), f32)
    for b in range(slot_of.shape[0]):
        top = rows_off + (b // across_blocks) * side
        left = side + (b % across_blocks) * side
        frame[top : top + side, left : left + side] = arrived[slot_of[b]].astype(f32)
    first_row = rows_off - margin
    first_col = side - margin

    def cut_image(ref, top, left):
        tall = min(high, side + 16)
        down = pl.multiple_of(jnp.minimum((top // 16) * 16, high - tall), 16)
        over = pl.multiple_of(jnp.minimum((left // side) * side, wide - 2 * side), side)
        tile = ref[pl.ds(down, tall), pl.ds(over, 2 * side)].astype(f32)
        tile = pltpu.roll(tile, lax.rem(2 * side - (left - over), 2 * side), 1)[:, :side]
        return pltpu.roll(tile, lax.rem(tall - (top - down), tall), 0)[:side]

    for s in range(stamps):
        top = rows_at[0, s]
        left = cols_at[0, s]
        tile = cut(frame, top + first_row, left + first_col, span, side)
        cuts[s * span : (s + 1) * span, :] = tile.astype(bf16)
        root = lax.rsqrt(cut_image(variance, top, left))
        roots[s * side : (s + 1) * side, :] = root
        place = pl.ds(s * side * pitch + count, side, stride=pitch)
        design[place, :] = root
        place = pl.ds(s * side * pitch + count + 1, side, stride=pitch)
        design[place, :] = root * cut_image(science, top, left)
    design[lines_all * pitch :, :] = jnp.zeros((design.shape[0] - lines_all * pitch, side), f32)

    group = vert.shape[0]
    step = side - taps + 1
    starts = list(range(0, count, group))
    for turn, k in enumerate(starts):
        for c in range(turn, windows.shape[0], len(starts)):
            left = first_col + c * step
            window[...] = frame[first_row : first_row + window.shape[0], left : left + side]
            for parity in range(2):
                place = pl.ds(parity, windows.shape[2], stride=2)
                windows[c, parity] = window[place, :]
        filters = []
        for a in range(group):
            line = jnp.broadcast_to(col[k + a : k + a + 1, :], (side, side))
            line = pltpu.roll(line, 0, 1, stride=1, stride_axis=0)
            first = jnp.where(lane >= sub, line, 0.0).astype(bf16)
            second = jnp.where(lane < sub, line, 0.0).astype(bf16)
            filters.append(jnp.concatenate([first, second[:, : span - side]], axis=1))
        filters = jnp.concatenate(filters, axis=0)
        for s in range(stamps):
            out = jnp.dot(
                filters, cuts[s * span : (s + 1) * span, :], preferred_element_type=f32
            ).astype(bf16)
            for a in range(group):
                vert[a, s * side : (s + 1) * side, :] = out[a * side : (a + 1) * side]
        for a in range(group):
            line = jnp.broadcast_to(row_rev[k + a : k + a + 1, :], (side, side))
            line = pltpu.roll(line, 0, 1, stride=1, stride_axis=0)
            first = jnp.where(lane <= sub, line, 0.0).astype(bf16)
            second = jnp.where(lane > sub, line, 0.0).astype(bf16)
            band = jnp.concatenate([first, second], axis=0)
            out = jnp.dot(vert[a], band, preferred_element_type=f32)
            design[pl.ds(k + a, lines_all, stride=pitch), :] = out * roots[...]

    lines = 16
    sets = 4

    def gram_step(step, total):
        start = pl.multiple_of(step * sets * lines * pitch, 8)
        rows = []
        for g in range(sets):
            row = [
                design[pl.ds(start + (g * lines + j) * pitch, padded_k), :].astype(bf16)
                for j in range(lines)
            ]
            rows.append(jnp.concatenate(row, axis=1))
        both = jnp.concatenate(rows, axis=0)
        return total + lax.dot_general(
            both, both, (((1,), (1,)), ((), ())), preferred_element_type=f32
        )

    total = lax.fori_loop(
        0,
        lines_all // (lines * sets),
        gram_step,
        jnp.zeros((sets * padded_k, sets * padded_k), f32),
        unroll=4,
    )
    part = jnp.zeros((padded_k, padded_k), f32)
    for g in range(sets):
        rows = slice(g * padded_k, (g + 1) * padded_k)
        part = part + total[rows, rows]
    gram_out[...] = part


def subtract_body(
    sender,
    gram,
    frames,
    science,
    col_t,
    row_rev,
    coef_out,
    payload,
    window,
    image,
    bands,
    total,
    *,
    order,
    capacity,
    count,
    taps,
    pixels,
):
    side = frames.shape[3]
    high, wide = science.shape
    padded_k = gram.shape[1]
    part = side // len(order)
    size = count + 1

    system = jnp.concatenate(
        [gram[...], jnp.zeros((padded_k, side - padded_k), f32)], axis=1
    ) / pixels
    sub = lax.broadcasted_iota(jnp.int32, (padded_k, side), 0)
    lane = lax.broadcasted_iota(jnp.int32, (padded_k, side), 1)
    system = jnp.where((sub < size) & (lane <= size), system, 0.0)
    system = system + jnp.where((sub == lane) & (sub < size), ridge_term, 0.0)

    pairs = (taps + 2) // 2
    rows_half = high // 2
    wins = frames.shape[0]

    for k in range(0, size, 8):
        block = range(min(8, size - k))
        cols = [jnp.broadcast_to(system[:, k + j : k + j + 1], system.shape) for j in block]
        rows = [system[k + j : k + j + 1, :] for j in block]
        core = [[cols[j][k + i : k + i + 1, :] for j in block] for i in block]
        for j in block:
            inverse = 1.0 / core[j][j]
            factor = jnp.where(sub == k + j, 0.0, cols[j] * inverse)
            system = system - factor * rows[j]
            for i in block[j + 1 :]:
                scale = core[i][j] * inverse
                rows[i] = rows[i] - scale * rows[j]
                for l in block[j + 1 :]:
                    core[i][l] = core[i][l] - scale * core[j][l]
                cols[i] = cols[i] - factor * core[j][i]
    pivot = jnp.sum(jnp.where(sub == lane, system, 0.0), axis=1, keepdims=True)
    solved = system[:, size : size + 1] / jnp.where(sub[:, :1] < size, pivot, 1.0)
    coef_out[...] = jnp.sum(jnp.where(sub == lane, solved, 0.0), axis=0, keepdims=True)
    background = solved[count : count + 1, :]
    basis_coef = jnp.where(sub[:, :1] < count, solved, 0.0)

    scaled = basis_coef * row_rev[...]
    kernel = jnp.zeros((col_t.shape[0], side), f32)
    for _ in range(3):
        piece = scaled.astype(bf16)
        scaled = scaled - piece.astype(f32)
        kernel = kernel + jnp.dot(col_t[...], piece, preferred_element_type=f32)
    kernel_sum = jnp.sum(jnp.sum(kernel, axis=1, keepdims=True), axis=0, keepdims=True)
    rounded = kernel.astype(bf16).astype(f32)

    zero_band = jnp.zeros((side, side), bf16)

    def band(i):
        if i < 0 or i >= taps:
            return zero_band
        line = jnp.broadcast_to(rounded[i : i + 1, :], (side, side))
        return pltpu.roll(line, 0, 1, stride=1, stride_axis=0).astype(bf16)

    made = {i: band(i) for i in range(-1, 2 * pairs)}
    for q in range(pairs):
        for a in range(2):
            for b in range(2):
                bands[
                    q * 2 * side + a * side : q * 2 * side + (a + 1) * side,
                    b * side : (b + 1) * side,
                ] = made[2 * q + a - b]

    step = side - taps + 1
    joint = 4
    for q in range(0, pairs, joint):
        last = min(q + joint, pairs)
        lhs = jnp.concatenate(
            [
                jnp.concatenate(
                    [
                        frames[c, a, p : p + rows_half, :].astype(bf16)
                        for p in range(q, last)
                        for a in range(2)
                    ],
                    axis=1,
                )
                for c in range(wins)
            ],
            axis=0,
        )
        out = jnp.dot(
            lhs, bands[q * 2 * side : last * 2 * side, :], preferred_element_type=f32
        )
        if q:
            out = out + total[...]
        if last < pairs:
            total[...] = out
    for c in range(wins):
        rows = out[c * rows_half : (c + 1) * rows_half]
        window[c, pl.ds(0, rows_half, stride=2), :] = rows[:, :side]
        window[c, pl.ds(1, rows_half, stride=2), :] = rows[:, side:]
        keep = min(step, wide - c * step)
        image[:, c * step : c * step + keep] = window[c, :, :keep]
    image[...] = science[...].astype(f32) - image[...] - background

    store_parts(sender, image, payload, side, order, capacity, wide // side)
    line_at = lax.broadcasted_iota(jnp.int32, (trailer_rows, side), 0)
    trailer = jnp.zeros((trailer_rows, side), f32)
    rest = kernel_sum
    for p in range(3):
        piece = rest.astype(bf16).astype(f32)
        rest = rest - piece
        trailer = jnp.where(line_at == p, piece, trailer)
    trailer = trailer.astype(bf16)

    def put(d, carry):
        payload[d, capacity * part :, :] = trailer
        return carry

    lax.fori_loop(0, payload.shape[0], put, 0, unroll=4)


def fit_body(
    slot_of,
    sender,
    rows_at,
    cols_at,
    arrived,
    col,
    row_rev,
    science,
    variance,
    col_t,
    coef_out,
    payload,
    *scratch,
    order,
    capacity,
    count,
    taps,
):
    gram, windows = scratch[:2]
    stamps = rows_at.shape[1]
    side = row_rev.shape[1]
    normal_body(
        slot_of,
        rows_at,
        cols_at,
        arrived,
        col,
        row_rev,
        science,
        variance,
        gram,
        windows,
        *scratch[2:8],
        count=count,
        across_blocks=science.shape[1] // side,
        taps=taps,
    )
    subtract_body(
        sender,
        gram,
        windows,
        science,
        col_t,
        row_rev,
        coef_out,
        payload,
        *scratch[8:],
        order=order,
        capacity=capacity,
        count=count,
        taps=taps,
        pixels=stamps * side * side,
    )


def fit_and_subtract(
    slot_of,
    sender,
    rows_at,
    cols_at,
    arrived,
    col,
    row_rev,
    science,
    variance,
    col_t,
    order,
    capacity,
    count,
    taps,
):
    exps = len(order)
    high, wide = science.shape
    side = row_rev.shape[1]
    slots = sender.shape[0]
    stamps = rows_at.shape[1]
    padded_k = up(count + 2, 16)
    pairs = (taps + 2) // 2
    span = up(side + taps - 1, 16)
    half = up(high // 2 + pairs, 8)
    tall = up(taps // 2, 8) + max(high - side + span, 2 * half)
    wins = -(-wide // (side - taps + 1))
    group = next(g for g in (20, 8, 4, 2, 1) if count % g == 0)
    return pl.pallas_call(
        functools.partial(fit_body, order=order, capacity=capacity, count=count, taps=taps),
        out_shape=(
            jax.ShapeDtypeStruct((1, side), f32),
            jax.ShapeDtypeStruct(
                (slots // capacity * exps, capacity * side // exps + trailer_rows, side), bf16
            ),
        ),
        in_specs=[smem()] * 4 + [vmem()] * 6,
        out_specs=(vmem(),) * 2,
        scratch_shapes=[
            pltpu.VMEM((padded_k, padded_k), f32),
            pltpu.VMEM((wins, 2, half, side), f32),
            pltpu.VMEM((tall, wide + 2 * side), f32),
            pltpu.VMEM((stamps * span, 2 * side), bf16),
            pltpu.VMEM((group, stamps * side, 2 * side), bf16),
            pltpu.VMEM((up(stamps * side * ((count + 2) | 1) + padded_k, 8), side), f32),
            pltpu.VMEM((stamps * side, side), f32),
            pltpu.VMEM((2 * half, side), f32),
            pltpu.VMEM((wins, high, side), f32),
            pltpu.VMEM((high, wide), f32),
            pltpu.VMEM((pairs * 2 * side, 2 * side), bf16),
            pltpu.VMEM((wins * high // 2, 2 * side), f32),
        ],
        compiler_params=pltpu.CompilerParams(vmem_limit_bytes=34 * mib),
        cost_estimate=cost(15_000_000_000, 8_000_000),
        name="fit_and_subtract",
    )(
        slot_of,
        sender,
        rows_at,
        cols_at,
        arrived,
        col,
        row_rev,
        science,
        variance,
        col_t,
    )


def split2(value):
    top = value.astype(bf16)
    return top, (value - top.astype(f32)).astype(bf16)


def score_body(
    slot_of, payload, down, over, out, token, padded, sideways, *, order, taps, capacity
):
    token[...] = jnp.zeros(token.shape, f32)
    side = payload.shape[2]
    part = side // len(order)
    high, wide = out.shape
    margin = taps // 2
    span = up(side + taps - 1, 16)
    across_blocks = wide // side
    exps = len(order)
    padded[...] = jnp.zeros(padded.shape, f32)
    for b in range(slot_of.shape[0]):
        slot = slot_of[b]
        row = pl.multiple_of((slot % capacity) * part, part)
        left = margin + (b % across_blocks) * side
        for e, q in enumerate(order):
            top = (b // across_blocks) * side + q * part
            block = payload[(slot // capacity) * exps + e, pl.ds(row, part), :]
            padded[top : top + part, left : left + side] = block.astype(f32)
    line = jnp.broadcast_to(over[...], (2 * side, 2 * side))
    band = pltpu.roll(line, 0, 1, stride=1, stride_axis=0)[:, :side]
    both = jnp.concatenate(split2(band), axis=1)
    sideways[...] = jnp.zeros(sideways.shape, f32)
    for c in range(wide // side):
        window = padded[:, c * side : (c + 2) * side].astype(bf16)
        got = jnp.dot(window, both, preferred_element_type=f32)
        sideways[margin : margin + high, c * side : (c + 1) * side] = got[:, :side] + got[:, side:]
    line = jnp.broadcast_to(down[...], (side, 2 * side))
    band = pltpu.roll(line, 0, 1, stride=1, stride_axis=0)[:, :span]
    top, low = split2(band)
    for r in range(high // side):
        data_top, data_low = split2(sideways[r * side : r * side + span, :])
        got = jnp.dot(top, data_top, preferred_element_type=f32)
        got = got + jnp.dot(top, data_low, preferred_element_type=f32)
        got = got + jnp.dot(low, data_top, preferred_element_type=f32)
        out[r * side : (r + 1) * side, :] = got


def score(slot_of, payload, down, over_rev, high, wide, taps, order, capacity):
    side = payload.shape[2]
    span = up(side + taps - 1, 16)
    return pl.pallas_call(
        functools.partial(score_body, order=order, taps=taps, capacity=capacity),
        out_shape=(
            jax.ShapeDtypeStruct((high, wide), f32),
            jax.ShapeDtypeStruct((8, 128), f32),
        ),
        in_specs=[smem()] + [vmem()] * 3,
        out_specs=(vmem(), vmem()),
        scratch_shapes=[
            pltpu.VMEM((high, wide + side), f32),
            pltpu.VMEM((high - side + span, wide), f32),
        ],
        compiler_params=pltpu.CompilerParams(vmem_limit_bytes=20 * mib),
        cost_estimate=cost(2_000_000_000, 2_000_000),
        name="score",
    )(slot_of, payload, down, over_rev)


def wanted_block(me, exposure, table, d, c, tract):
    exps = table.shape[0]
    block = table[distance(me[0], exposure, exps), d, c] - 1
    return jnp.where(block < 0, tract, block)


def variance_body(
    me, table, parts, template_var, own_out, other_out, template_out, total, sem, *, nears, capacity
):
    exps = table.shape[0]
    fars = exps // nears
    tract, part, _ = own_out.shape
    mine = pl.ds(pl.multiple_of(part_of(me[0], exps, nears) * part, part), part)
    copy = pltpu.make_async_copy(template_var.at[:, mine, :], template_out, sem)
    copy.start()
    total[...] = jnp.zeros(total.shape, f32)
    far = me[0] // nears
    rows = fars * part

    def one(j, carry):
        exposure = far * nears + lax.rem(j, nears)
        for c in range(capacity):
            block = wanted_block(me, exposure, table, j // nears, c, tract)
            total[block] += parts[j, c * rows : (c + 1) * rows, :].astype(f32)
        return carry

    lax.fori_loop(0, parts.shape[0], one, 0, unroll=4)
    own_out[...] = total[:tract, pl.ds(pl.multiple_of(far * part, part), part), :]
    for g in range(1, fars):
        there = lax.rem(far + g, fars)
        rows_there = pl.ds(pl.multiple_of(there * part, part), part)
        other_out[g - 1] = total[:tract, rows_there, :].astype(bf16)
    copy.wait()


def sum_variance(me, table, parts, template_var, nears, capacity):
    tract, side, _ = template_var.shape
    exps = table.shape[0]
    fars = exps // nears
    part = side // exps
    return pl.pallas_call(
        functools.partial(variance_body, nears=nears, capacity=capacity),
        out_shape=(
            jax.ShapeDtypeStruct((tract, part, side), f32),
            jax.ShapeDtypeStruct((max(1, fars - 1), tract, part, side), bf16),
            jax.ShapeDtypeStruct((tract, part, side), template_var.dtype),
        ),
        in_specs=[smem()] * 2 + [vmem(), pl.BlockSpec(memory_space=pl.ANY)],
        out_specs=(vmem(),) * 3,
        scratch_shapes=[
            pltpu.VMEM((tract + 1, fars * part, side), f32),
            pltpu.SemaphoreType.DMA(()),
        ],
        compiler_params=pltpu.CompilerParams(vmem_limit_bytes=16 * mib),
        cost_estimate=cost(0, 4_000_000),
        name="sum_variance",
    )(me, table, parts, template_var)


def combine_body(me, table, earlier, parts, own_var, var_template, *rest, part, capacity):
    del earlier
    others = rest[:-3]
    out, total, gain = rest[-3:]
    total[...] = jnp.zeros(total.shape, f32)
    gain[...] = jnp.zeros(gain.shape, f32)
    tract = out.shape[0]
    exps = table.shape[0]

    def one(j, carry):
        tail = parts[j, capacity * part :, :].astype(f32)
        kernel_sum = tail[0:1] + tail[1:2] + tail[2:3]
        square = jnp.broadcast_to(kernel_sum * kernel_sum, gain.shape[1:])
        for c in range(capacity):
            block = wanted_block(me, lax.rem(j, exps), table, j // exps, c, tract)
            total[block] += parts[j, c * part : (c + 1) * part, :].astype(f32)
            gain[block] += square
        return carry

    lax.fori_loop(0, parts.shape[0], one, 0, unroll=4)
    for t in range(tract):
        variance = own_var[t] + gain[t, 0:1, :] * var_template[t].astype(f32)
        for other in others:
            variance = variance + other[t].astype(f32)
        out[t] = (total[t] * lax.rsqrt(jnp.maximum(variance, 1.0))).astype(bf16)


def combine(me, table, earlier, parts, own_var, var_template, others, capacity):
    tract, part, side = own_var.shape
    return pl.pallas_call(
        functools.partial(combine_body, part=part, capacity=capacity),
        out_shape=jax.ShapeDtypeStruct((tract, part, side), bf16),
        in_specs=[smem(), smem(), pl.BlockSpec(memory_space=pl.ANY)]
        + [vmem()] * (3 + len(others)),
        out_specs=vmem(),
        scratch_shapes=[
            pltpu.VMEM((tract + 1, part, side), f32),
            pltpu.VMEM((tract + 1, 8, side), f32),
        ],
        compiler_params=pltpu.CompilerParams(vmem_limit_bytes=16 * mib),
        name="combine",
    )(me, table, earlier, parts, own_var, var_template, *others)


def join_body(places, *refs, part, count):
    ins = refs[:count]
    out, held, sems = refs[-3:]
    copies = []
    for d, ref in enumerate(ins):
        held[d] = ref[...].astype(f32)
        row = pl.multiple_of(places[d] * part, part)
        copies.append(
            pltpu.make_async_copy(held.at[d], out.at[:, pl.ds(row, part), :], sems.at[d])
        )
        copies[-1].start()
    for copy in copies:
        copy.wait()


def join_parts(places, parts, whole, exps):
    tract, part, side = parts[0].shape
    count = len(parts)
    fresh = whole is None
    anywhere = pl.BlockSpec(memory_space=pl.ANY)
    return pl.pallas_call(
        functools.partial(join_body, part=part, count=count),
        out_shape=jax.ShapeDtypeStruct((tract, part * exps, side), f32),
        in_specs=[smem()] + [vmem()] * count + ([] if fresh else [anywhere]),
        out_specs=anywhere,
        scratch_shapes=[
            pltpu.VMEM((count, tract, part, side), f32),
            pltpu.SemaphoreType.DMA((count,)),
        ],
        input_output_aliases={} if fresh else {count + 1: 0},
        compiler_params=pltpu.CompilerParams(vmem_limit_bytes=16 * mib),
        cost_estimate=cost(0, 3_000_000 * count),
        name="join_parts",
    )(places, *parts, *([] if fresh else [whole]))


def local(
    template,
    template_var,
    science,
    science_var,
    routes_src,
    routes_blk,
    stamp_rows,
    stamp_cols,
    basis_col,
    basis_row,
    psf_col,
    psf_row,
):
    peers = lax.axis_size("det")
    nears = lax.axis_size("near")
    exps = lax.axis_size("far") * nears
    me = (lax.axis_index("far") * nears + lax.axis_index("near")).astype(jnp.int32)
    order = tuple((e % nears) * (exps // nears) + e // nears for e in range(exps))
    tract, side, _ = template.shape
    science_img = science[0]
    variance_img = science_var[0]
    blocks_dev = routes_src.shape[1]
    count, taps = basis_col.shape
    capacity = max(2, -(-blocks_dev // peers))
    slots = peers * capacity
    part = side // exps

    request = request_table(routes_src, routes_blk, peers, capacity)
    asked = lax.all_to_all(request, "det", split_axis=0, concat_axis=0, tiled=True)
    picked = pick_blocks(asked, fetch(template), slots, capacity)
    slot_of, sender = route_tables(routes_src, routes_blk, picked, peers, capacity)
    held = hold(asked, picked)
    tables = [held] + [from_exposure(held, g, exps) for g in range(1, exps)]
    table = jnp.stack(tables).reshape(exps, peers, capacity)
    var_parts = prepare(sender, variance_img, science_img, table, side, nears, capacity)
    arrived = lax.all_to_all(picked, "det", split_axis=0, concat_axis=0, tiled=True)

    padded_k = up(count + 2, 16)
    col_t = jnp.pad(basis_col.T, ((0, up(taps, 16) - taps), (0, padded_k - count)))
    col = jnp.pad(basis_col.astype(f32), ((0, padded_k - count), (0, side - taps)))
    row_rev = jnp.pad(
        basis_row.astype(f32)[:, ::-1], ((0, padded_k - count), (side - taps, 0))
    )
    row_rev = jnp.roll(row_rev, 1, axis=1)
    over_rev = jnp.roll(jnp.pad(psf_row[:, ::-1], ((0, 0), (2 * side - taps, 0))), 1, axis=1)
    down = jnp.pad(psf_col, ((0, 0), (0, 2 * side - taps)))
    var_late, arrived = lax.optimization_barrier((var_parts, arrived))
    var_back = lax.all_to_all(
        var_late, ("det", "near"), split_axis=0, concat_axis=0, tiled=True
    )

    high, wide = science_img.shape
    coef, payload = fit_and_subtract(
        slot_of,
        sender,
        stamp_rows,
        stamp_cols,
        arrived,
        col,
        row_rev,
        science_img,
        variance_img,
        col_t,
        order,
        capacity,
        count,
        taps,
    )
    diff_back = lax.all_to_all(payload, ("det",) + exposure_axes, split_axis=0, concat_axis=0, tiled=True)
    own_var, other_var, var_template = sum_variance(
        me[None], table, var_back, template_var, nears, capacity
    )
    fars = exps // nears
    others = []
    for g in range(1, fars):
        pairs = [(f, (f + g) % fars) for f in range(fars)]
        others.append(lax.ppermute(other_var[g - 1], "far", pairs))
    scored, token = score(
        slot_of, payload, down, over_rev, high, wide, taps, order, capacity
    )
    mine = combine(me[None], table, token, diff_back, own_var, var_template, others, capacity)

    def swap(value, distance):
        return lax.ppermute(value, exposure_axes, [(e, e ^ distance) for e in range(exps)])

    def put(parts, whole):
        places = jnp.stack([part_of(there, exps, nears) for there, _ in parts])
        return join_parts(places, [held for _, held in parts], whole, exps)

    if exps == 4:
        far = swap(mine, 2)
        near = swap(mine, 1)
        last = swap(far, 1)
        whole = put([(me, mine), (me ^ 1, near), (me ^ 2, far)], None)
        significance = put([(me ^ 3, last)], whole)
    else:
        parts = [(me, mine)]
        for gap in range(1, exps):
            pairs = [(e, (e + gap) % exps) for e in range(exps)]
            parts.append(((me - gap) % exps, lax.ppermute(mine, exposure_axes, pairs)))
        significance = put(parts, None)
    return (significance, scored[None], coef[:, : count + 1])


def solution(mesh):
    peers, exps = mesh.devices.shape
    nears = 2 if exps % 2 == 0 else 1
    split = jax.sharding.Mesh(
        mesh.devices.reshape(peers, exps // nears, nears), ("det",) + exposure_axes
    )
    placed = (
        P("det", None, None),
        P("det", None, None),
        P(exposure_axes, "det", None),
        P(exposure_axes, "det", None),
        P(exposure_axes, "det"),
        P(exposure_axes, "det"),
        P(exposure_axes, "det"),
        P(exposure_axes, "det"),
        P(),
        P(),
        P(exposure_axes, None),
        P(exposure_axes, None),
    )
    return jax.shard_map(
        local,
        mesh=split,
        in_specs=placed,
        out_specs=(
            P("det", None, None),
            P(exposure_axes, "det", None),
            P(exposure_axes, "det"),
        ),
        check_vma=False,
    )
```
